32 devices in a mesh: seq: 8 (over y, x, core), tp: 4 (over z).
Axes of the slice: x: 2, y: 2, z: 4, core: 2. Of those that a mesh axis runs over, the one named last changes fastest.
Arguments:
- tokens: bfloat16 [4096, 2048], P('seq'), may hold values from -6 to 6
- w_zx: float32 [2048, 8192], P(('seq', 'tp')), may hold values from -0.125 to 0.125
- w_dt: float32 [2048, 64], P(('seq', 'tp')), may hold values from -0.26516503 to 0.26516503
- w_bc: float32 [2048, 256], P(('seq', 'tp')), may hold values from -0.125 to 0.125
- conv_x_weight: float32 [4, 4096], P(None, 'tp'), may hold values from -3 to 3
- conv_x_bias: float32 [4096], P('tp'), may hold values from -1.8 to 1.8
- conv_bc_weight: float32 [4, 256], replicated, may hold values from -3 to 3
- conv_bc_bias: float32 [256], replicated, may hold values from -1.8 to 1.8
- dt_bias: float32 [64], P('tp'), may hold values from -11 to -2
- a_log: float32 [64], P('tp'), may hold values from 0 to 2.77
- skip: float32 [64], P('tp'), may hold values from 0.5 to 2
- norm_weight: float32 [4096], P('tp'), may hold values from 0.1 to 1.9
- w_out: float32 [4096, 2048], P('tp', 'seq'), may hold values from -0.09375 to 0.09375
- lengths: int32 [8], replicated, may hold values from 1 to 2048, 4096 in all
- request_group: int32 [16], replicated, may hold values from 0 to 15
Outputs:
- mixed: bfloat16 [4096, 2048], P(('seq', 'tp'))
- request_states: float32 [16, 64, 64, 128], P('seq', 'tp')
The draws below stay inside these ranges and needn't reach their ends.
Inputs may be any that keep to these rules, and one draw needn't show every extreme that they name: 8 prompts packed end to end in this order; the lengths sum to 4096 and the longest is exactly 2048.
All inputs are finite; a program needn't handle non-finite values.
Results may differ from the reference program's by a relative error of at most 0.011.
Values may be sent and summed in bfloat16 or wider, within the bound.
No kernel may reach another device: no remote copies, remote signals or barrier semaphores. Data moves between devices by JAX's collectives and lax.ppermute only.
A program may use at most 128 MiB of HBM per device.

```python
import math
import jax
import jax.numpy as jnp
import numpy as np
from jax import lax

D = 2048
INNER = 4096
HEADS = 64
HEAD_DIM = 64
STATE = 128
CONV = 4
GROUP = 256
PROMPTS = 8
TOKENS = 4096
GROUPS = 16
REQUESTS = 16
PROMPT_MAX = 2048


def set_ends(entries, own_key, low, largest):
    longest = entries.shape.index(max(entries.shape))
    spots = []
    for shift in (0, 1):
        where = [jax.random.randint(jax.random.fold_in(own_key, axis), (), 0, length) for axis, length in enumerate(entries.shape)]
        where[longest] = (where[longest] + shift) % entries.shape[longest]
        spots.append(tuple(where))
    return entries.at[spots[0]].set(low).at[spots[1]].set(largest)


def steps_of(stream_key, shape, shards, low, largest):
    gain, own = 1.0, jax.random.fold_in(stream_key, 6)
    for dim, blocks in shards:
        draws = jnp.exp(jax.random.uniform(jax.random.fold_in(own, dim), (blocks,), jnp.float32, low / len(shards), largest / len(shards)))
        gain = gain * jnp.repeat(draws, shape[dim] // blocks).reshape([-1 if axis == dim else 1 for axis in range(len(shape))])
    return gain


def profile(count, total, limit, skew):
    portions = [(1 << 20) // math.isqrt(grade ** skew) + 1 for grade in range(2, count + 1)]
    spare, holding = total - limit - (count - 1), [1] * (count - 1)
    while spare > 0:
        movable = [i for i in range(count - 1) if holding[i] < limit]
        mass, budget = sum([portions[i] for i in movable]), spare
        for i in movable:
            extra = min(limit - holding[i], max(1, budget * portions[i] // mass), spare)
            holding[i] = holding[i] + extra
            spare = spare - extra
    return np.array([limit] + holding)


def ragged(key, count, total, most, lean):
    if count == 2:
        one = jax.random.randint(key, (), max(1, total - most), min(most, total - 1) + 1)
        return jnp.stack([one, total - one])
    tallies = jnp.asarray(profile(count, total, most, lean), jnp.int32)
    twos = (count - 1) // 2
    donor, taker = tallies[1:1 + 2 * twos:2], tallies[2:2 + 2 * twos:2]
    margin = jnp.minimum(donor - 1, most - taker)
    passed = jax.random.randint(jax.random.fold_in(key, 1), (twos,), 0, 1 << 20) % (margin + 1)
    tallies = tallies.at[1:1 + 2 * twos:2].set(donor - passed).at[2:2 + 2 * twos:2].set(taker + passed)
    return tallies[jax.random.permutation(jax.random.fold_in(key, 2), count)]


def normal_values(key, dims, scale, bound, pieces=(), held_as=jnp.bfloat16):
    array = jax.random.normal(key, dims, jnp.float32) * scale
    if len(pieces) > 0:
        array = steps_of(key, dims, pieces, -0.22, 0.18) * array
    return jnp.clip(array, min=-bound, max=bound).astype(held_as)


def setup_inputs(seed: int = 0) -> dict:
    streams_of = jax.random.split(jax.random.key(seed), 16)
    return {
        "tokens": normal_values(streams_of[0], (TOKENS, D), 1.0, 6.0, ((0, 8),)),
        "w_zx": normal_values(streams_of[1], (D, 2 * INNER), D ** -0.5, 0.125, ((0, 32),), jnp.float32),
        "w_dt": normal_values(streams_of[2], (D, HEADS), (2.0 / D ** 0.5), 0.26516503, ((0, 32),), jnp.float32),
        "w_bc": normal_values(streams_of[3], (D, 2 * STATE), D ** -0.5, 0.125, ((0, 32),), jnp.float32),
        "conv_x_weight": normal_values(streams_of[4], (CONV, INNER), CONV ** -0.5, 3.0, ((1, 4),), jnp.float32),
        "conv_x_bias": normal_values(streams_of[5], (INNER,), 0.3, 1.8, ((0, 4),), jnp.float32),
        "conv_bc_weight": normal_values(streams_of[6], (CONV, 2 * STATE), CONV ** -0.5, 3.0, (), jnp.float32),
        "conv_bc_bias": normal_values(streams_of[7], (2 * STATE,), 0.3, 1.8, (), jnp.float32),
        "dt_bias": jnp.clip(-11.0 + 9.0 * jax.random.uniform(streams_of[8], (HEADS,), jnp.float32) ** steps_of(streams_of[8], (HEADS,), ((0, 4),), -0.2, 0.2), -11.0, -2.0),
        "a_log": jnp.clip(2.77 * jax.random.uniform(streams_of[9], (HEADS,), jnp.float32) ** steps_of(streams_of[9], (HEADS,), ((0, 4),), -0.2, 0.2), 0.0, 2.77),
        "skip": jnp.clip(0.5 + 1.5 * jax.random.uniform(streams_of[10], (HEADS,), jnp.float32) ** steps_of(streams_of[10], (HEADS,), ((0, 4),), -0.2, 0.2), 0.5, 2.0),
        "norm_weight": jnp.clip(1.0 + 0.18 * jax.random.normal(streams_of[11], (INNER,), jnp.float32), 0.1, 1.9),
        "w_out": normal_values(streams_of[12], (INNER, D), INNER ** -0.5, 0.09375, ((0, 4), (1, 8)), jnp.float32),
        "lengths": ragged(streams_of[13], PROMPTS, TOKENS, PROMPT_MAX, 2).astype(jnp.int32),
        "request_group": set_ends(jax.random.randint(streams_of[14], (REQUESTS,), 0, GROUPS), jax.random.fold_in(streams_of[14], 1), 0, GROUPS - 1).astype(jnp.int32),
    }


epsilon = 1e-05

def segment_of(position, lengths):
    prompt_ends = jnp.cumsum(lengths).astype(jnp.int32)
    return lax.optimization_barrier(jnp.sum((position[:, None] >= prompt_ends[None, :]).astype(jnp.int32), axis=1))

def group_scan(carry_state, group_item, decay_rate, skip):
    inputs, b_matrix, c_matrix, step_size, segments, seg_before = group_item
    cumul_heads = jnp.cumsum(step_size * decay_rate[None, :], axis=0).T
    within = jnp.arange(GROUP, dtype=jnp.int32)
    same_prompt = (segments[:, None] == segments[None, :]) & (within[:, None] >= within[None, :])
    log_decay = cumul_heads[:, :, None] - cumul_heads[:, None, :]
    decay_matrix = jnp.where(same_prompt[None], jnp.exp(jnp.where(same_prompt[None], log_decay, 0.0)), 0.0)
    scores = jnp.dot(c_matrix, b_matrix.T, preferred_element_type=jnp.float32)
    step_heads = step_size.T
    mix_weights = lax.optimization_barrier((decay_matrix * scores[None] * step_heads[:, None, :]).astype(jnp.bfloat16))
    inputs_wide = inputs.astype(jnp.float32)
    diag_out = jnp.einsum('hij,jhp->ihp', mix_weights.astype(jnp.float32), inputs_wide)
    last_segment = segments[-1]
    tail_weight = jnp.where((segments == last_segment)[None, :], jnp.exp(cumul_heads[:, -1:] - cumul_heads), 0.0) * step_heads
    b_weighted = lax.optimization_barrier((b_matrix.astype(jnp.float32)[None] * tail_weight[:, :, None]).astype(jnp.bfloat16))
    contrib = jnp.einsum('jhp,hjn->hpn', inputs_wide, b_weighted.astype(jnp.float32))
    carry_keep = jnp.where((segments == seg_before)[None, :], jnp.exp(cumul_heads), 0.0)
    state_low = lax.optimization_barrier(carry_state.astype(jnp.bfloat16))
    carry_out = jnp.einsum('in,hpn->ihp', c_matrix.astype(jnp.float32), state_low.astype(jnp.float32)) * carry_keep.T[:, :, None]
    pass_gate = jnp.where(last_segment == seg_before, jnp.exp(cumul_heads[:, -1]), 0.0)
    next_state = pass_gate[:, None, None] * carry_state + contrib
    output = diag_out + carry_out + skip[None, :, None] * inputs_wide
    return (next_state, (output, next_state))

def reference(tokens, w_zx, w_dt, w_bc, conv_x_weight, conv_x_bias, conv_bc_weight, conv_bc_bias, dt_bias, a_log, skip, norm_weight, w_out, lengths, request_group):
    zx = jnp.dot(tokens, w_zx.astype(jnp.bfloat16), preferred_element_type=jnp.float32).astype(jnp.bfloat16)
    gate_z = zx[:, :INNER]
    x_raw = zx[:, INNER:]
    dt_pre = jnp.dot(tokens, w_dt.astype(jnp.bfloat16), preferred_element_type=jnp.float32)
    bc_raw = jnp.dot(tokens, w_bc.astype(jnp.bfloat16), preferred_element_type=jnp.float32).astype(jnp.bfloat16)
    raw_mix = jnp.concatenate([x_raw, bc_raw], axis=1)
    conv_weight = jnp.concatenate([conv_x_weight, conv_bc_weight], axis=1)
    conv_bias = jnp.concatenate([conv_x_bias, conv_bc_bias], axis=0)
    padded = jnp.concatenate([jnp.zeros((CONV - 1, raw_mix.shape[1]), jnp.bfloat16), raw_mix], axis=0)
    seg_pad = segment_of(jnp.arange(TOKENS + CONV - 1, dtype=jnp.int32) - (CONV - 1), lengths)
    seg_tok = seg_pad[CONV - 1:]
    conv_sum = jnp.zeros((TOKENS, raw_mix.shape[1]), jnp.float32) + conv_bias[None, :]
    for offset_tap in range(CONV):
        rows_wide = padded[offset_tap:offset_tap + TOKENS].astype(jnp.float32)
        keep_tap = seg_pad[offset_tap:offset_tap + TOKENS] == seg_tok
        conv_sum = conv_sum + jnp.where(keep_tap[:, None], rows_wide * conv_weight[offset_tap][None, :], 0.0)
    convolved = jax.nn.silu(conv_sum).astype(jnp.bfloat16)
    inputs = convolved[:, :INNER].reshape(GROUPS, GROUP, HEADS, HEAD_DIM)
    b_matrix = convolved[:, INNER:INNER + STATE].reshape(GROUPS, GROUP, STATE)
    c_matrix = convolved[:, INNER + STATE:].reshape(GROUPS, GROUP, STATE)
    step_size = jax.nn.softplus(dt_pre + dt_bias[None, :]).reshape(GROUPS, GROUP, HEADS)
    segments = seg_tok.reshape(GROUPS, GROUP)
    seg_before = segment_of(jnp.arange(GROUPS, dtype=jnp.int32) * GROUP - 1, lengths)
    decay_rate = -jnp.exp(a_log)

    def scan_step(carry_state, group_item):
        return group_scan(carry_state, group_item, decay_rate, skip)
    start_state = jnp.zeros((HEADS, HEAD_DIM, STATE), jnp.float32)
    _, (outputs, end_states) = lax.scan(scan_step, start_state, (inputs, b_matrix, c_matrix, step_size, segments, seg_before))
    y_full = outputs.reshape(TOKENS, INNER)
    gated = y_full * jax.nn.silu(gate_z.astype(jnp.float32))
    mean_square = lax.optimization_barrier(jnp.mean(gated * gated, axis=1))
    normed = (gated * lax.rsqrt(mean_square + epsilon)[:, None] * norm_weight[None, :]).astype(jnp.bfloat16)
    mixed = jnp.dot(normed, w_out.astype(jnp.bfloat16), preferred_element_type=jnp.float32).astype(jnp.bfloat16)
    request_states = end_states[request_group]
    return (mixed, request_states)
```

```python
import jax
import jax.numpy as jnp
from jax import lax
from jax.sharding import PartitionSpec as P

GROUP = 256
HALO = 16
LANES = 128

epsilon = 1e-05


def flip(x, bits):
    count = lax.axis_size("seq")
    return lax.ppermute(x, "seq", [(i, i ^ bits) for i in range(count)])


def shift(x, by):
    count = lax.axis_size("tp")
    return lax.ppermute(x, "tp", [(i, (i + by) % count) for i in range(count)])


def plane_gather(block):
    chips = lax.axis_size("seq") // 2
    half = block.shape[0] // 2
    blocks = [block]
    for k in range(1, chips):
        low = k & -k
        high = 1 << (k.bit_length() - 1)
        if low == high:
            blocks.append(flip(block, 2 * k))
        else:
            first = flip(blocks[k ^ low][:half], 2 * low)
            second = flip(blocks[k ^ high][half:], 2 * high)
            blocks.append(jnp.concatenate([first, second], axis=0))
    return blocks


def split_terms(x):
    high = x.astype(jnp.bfloat16)
    rest = x - high.astype(jnp.float32)
    mid = rest.astype(jnp.bfloat16)
    low = (rest - mid.astype(jnp.float32)).astype(jnp.bfloat16)
    return high, mid, low


def on_device(
    tokens,
    w_zx,
    w_dt,
    w_bc,
    conv_x_weight,
    conv_x_bias,
    conv_bc_weight,
    conv_bc_bias,
    dt_bias,
    a_log,
    skip,
    norm_weight,
    w_out,
    lengths,
    request_group,
):
    tp_count, seq_count = lax.axis_size("tp"), lax.axis_size("seq")
    t, s = lax.axis_index("tp"), lax.axis_index("seq")
    chips = seq_count // 2
    p, c = s // 2, s % 2
    tok_dev, width = tokens.shape
    rows = w_zx.shape[0]
    taps = conv_x_weight.shape[0]
    inner_all = w_zx.shape[1] // 2
    inner = conv_x_weight.shape[1] // 2
    heads = dt_bias.shape[0] // 2
    head_width = inner // heads
    bc_width = w_bc.shape[1]
    state_width = bc_width // 2
    tok = 2 * tok_dev
    groups = tok // GROUP
    mm = jnp.bfloat16

    def core_part(x):
        size = x.shape[-1] // 2
        return lax.dynamic_slice_in_dim(x, c * size, size, x.ndim - 1)

    conv_weight = jnp.concatenate([core_part(conv_x_weight), conv_bc_weight], axis=1)
    conv_bias = jnp.concatenate([core_part(conv_x_bias), conv_bc_bias], axis=0)
    dt_bias, a_log, skip, norm_weight = (core_part(x) for x in (dt_bias, a_log, skip, norm_weight))

    gate_part = w_zx[:, :inner_all].astype(mm).reshape(rows, tp_count, 2, inner).transpose(2, 1, 0, 3)
    x_part = w_zx[:, inner_all:].astype(mm).reshape(rows, tp_count, 2, inner).transpose(2, 1, 0, 3)
    dt_part = w_dt.astype(mm).reshape(rows, tp_count, 2, heads).transpose(2, 1, 0, 3)
    dt_part = jnp.pad(dt_part, ((0, 0), (0, 0), (0, 0), (0, LANES - heads)))
    bc_part = jnp.broadcast_to(w_bc.astype(mm)[None, None], (2, tp_count, rows, bc_width))
    x_part = jnp.concatenate([x_part, bc_part, dt_part], axis=-1)

    def owners(part):
        mine = lax.dynamic_index_in_dim(part, c, 0, False)
        theirs = flip(lax.dynamic_index_in_dim(part, 1 - c, 0, False), 1)
        both = jnp.zeros((tp_count, 2) + mine.shape[1:], mm)
        both = lax.dynamic_update_index_in_dim(both, mine, c, 1)
        return lax.dynamic_update_index_in_dim(both, theirs, 1 - c, 1)

    def over_tp(both):
        own = jnp.zeros((2, tp_count) + both.shape[2:], mm)
        own = lax.dynamic_update_index_in_dim(
            own, lax.dynamic_index_in_dim(both, t, 0, False), t, 1
        )
        for by in range(1, tp_count):
            to, source = (t + by) % tp_count, (t - by) % tp_count
            got = shift(lax.dynamic_index_in_dim(both, to, 0, False), by)
            own = lax.dynamic_update_index_in_dim(own, got, source, 1)
        return own.reshape(2 * tp_count * rows, both.shape[-1])

    x_blocks = plane_gather(over_tp(owners(x_part)))
    z_blocks = plane_gather(over_tp(owners(gate_part)))
    out_blocks = plane_gather(w_out.astype(mm))
    out_blocks = [(b, flip(b, 1)) for b in out_blocks]

    own_tok = jnp.zeros((tok, width), mm)
    own_tok = lax.dynamic_update_slice(own_tok, tokens, (c * tok_dev, 0))
    own_tok = lax.dynamic_update_slice(own_tok, flip(tokens, 1), ((1 - c) * tok_dev, 0))
    before = lax.ppermute(
        own_tok[tok - HALO :], "seq", [(i, i + 2) for i in range(seq_count - 2)]
    )
    all_tok = jnp.concatenate([before, own_tok], axis=0)

    def project(x, blocks):
        depth = blocks[0].shape[0]
        total = 0.0
        for k, block in enumerate(blocks):
            columns = lax.dynamic_slice_in_dim(x, (p ^ k) * depth, depth, 1)
            total = total + jnp.dot(columns, block, preferred_element_type=jnp.float32)
        return total

    x_sum = project(all_tok, x_blocks)
    raw = x_sum[:, : inner + bc_width].astype(mm)
    dt_pre = x_sum[HALO:, inner + bc_width : inner + bc_width + heads]

    base = p * tok
    ends = jnp.cumsum(lengths)
    position = base + jnp.arange(tok, dtype=jnp.int32)
    start = jnp.max(jnp.where(ends[None, :] <= position[:, None], ends[None, :], 0), axis=1)
    behind = position - start

    conv_sum = jnp.zeros((tok, raw.shape[1]), jnp.float32) + conv_bias[None, :]
    for lag in range(taps):
        wide = raw[HALO - lag : HALO - lag + tok].astype(jnp.float32)
        conv_sum = conv_sum + jnp.where(
            (behind >= lag)[:, None], wide * conv_weight[taps - 1 - lag][None, :], 0.0
        )
    convolved = jax.nn.silu(conv_sum).astype(mm)
    xs = convolved[:, :inner].reshape(groups, GROUP, heads, head_width)
    b_matrix = convolved[:, inner : inner + state_width].reshape(groups, GROUP, state_width)
    c_matrix = convolved[:, inner + state_width :].reshape(groups, GROUP, state_width)

    step = jax.nn.softplus(dt_pre + dt_bias[None, :]).reshape(groups, GROUP, heads)
    step_heads = step.transpose(0, 2, 1)
    decay_rate = -jnp.exp(a_log)
    cumul = jnp.cumsum(step * decay_rate[None, None, :], axis=1).transpose(0, 2, 1)
    start = start.reshape(groups, GROUP)
    position = position.reshape(groups, GROUP)
    first = base + jnp.arange(groups, dtype=jnp.int32) * GROUP

    tail = (
        jnp.where(
            (position >= start[:, -1:])[:, None, :], jnp.exp(cumul[:, :, -1:] - cumul), 0.0
        )
        * step_heads
    )
    b_weighted = (b_matrix.astype(jnp.float32)[:, None] * tail[:, :, :, None]).astype(mm)
    contrib = jnp.einsum("cjhp,chjn->chpn", xs, b_weighted, preferred_element_type=jnp.float32)
    gate = jnp.where((start[:, -1] < first)[:, None], jnp.exp(cumul[:, :, -1]), 0.0)

    state_rows = heads * head_width
    gate_rows = jnp.concatenate(
        [jnp.broadcast_to(g[:, :, None], g.shape + (state_width,)) for g in split_terms(gate)], axis=1
    )
    spare = -gate_rows.shape[1] % 16
    gate_rows = jnp.pad(gate_rows, ((0, 0), (0, spare), (0, 0)))
    message = jnp.concatenate(
        [contrib.astype(mm).reshape(groups, state_rows, state_width), gate_rows], axis=1
    )
    parts = plane_gather(message)
    everything = jnp.zeros((chips,) + message.shape, mm)
    for k, part in enumerate(parts):
        everything = lax.dynamic_update_index_in_dim(everything, part, p ^ k, 0)
    everything = everything.reshape((chips * groups,) + message.shape[1:])
    all_contrib = everything[:, :state_rows].reshape(-1, heads, head_width, state_width)
    all_gates = everything[:, state_rows : state_rows + 3 * heads].astype(jnp.float32)
    all_gates = all_gates.reshape(-1, 3, heads, state_width).sum(axis=1)

    def one(state, item):
        factor, source = item
        new = factor[:, None, :] * state + source.astype(jnp.float32)
        return new, (state.astype(mm), new.astype(mm))

    zero_state = jnp.zeros((heads, head_width, state_width), jnp.float32)
    _, (entering, leaving) = lax.scan(one, zero_state, (all_gates, all_contrib))
    state_low = lax.dynamic_slice_in_dim(entering, p * groups, groups, 0)

    within = jnp.arange(GROUP, dtype=jnp.int32)
    same = (position[:, None, :] >= start[:, :, None]) & (within[:, None] >= within[None, :])[None]
    log_decay = cumul[:, :, :, None] - cumul[:, :, None, :]
    decay = jnp.exp(jnp.where(same[:, None], log_decay, -jnp.inf))
    scores = jnp.einsum("cin,cjn->cij", c_matrix, b_matrix, preferred_element_type=jnp.float32)
    mix = (decay * scores[:, None] * step_heads[:, :, None, :]).astype(mm)
    y = jnp.einsum("chij,cjhp->cihp", mix, xs, preferred_element_type=jnp.float32)
    carried = jnp.einsum("cin,chpn->cihp", c_matrix, state_low, preferred_element_type=jnp.float32)
    keep = jnp.where((start < first[:, None])[:, None, :], jnp.exp(cumul), 0.0)
    y = y + carried * keep.transpose(0, 2, 1)[:, :, :, None]
    y = y + skip[None, None, :, None] * xs.astype(jnp.float32)
    y = y.reshape(tok, inner)
    gate_z = project(own_tok, z_blocks).astype(mm)
    gated = y * jax.nn.silu(gate_z.astype(jnp.float32))
    squares = jnp.sum(gated * gated, axis=1)
    terms = [h[:, None] for h in split_terms(squares)]
    gated = (gated * norm_weight[None, :]).astype(mm)
    extra = jnp.concatenate(terms + [jnp.zeros((tok, LANES - 3), mm)], axis=1)
    gated = jnp.concatenate([gated, extra], axis=1)

    mine = lax.dynamic_slice_in_dim(gated, c * tok_dev, tok_dev, 0)
    theirs = flip(lax.dynamic_slice_in_dim(gated, (1 - c) * tok_dev, tok_dev, 0), 1)
    both = jnp.zeros((tok_dev, 2 * inner), mm)
    both = lax.dynamic_update_slice(both, mine[:, :inner], (0, c * inner))
    both = lax.dynamic_update_slice(both, theirs[:, :inner], (0, (1 - c) * inner))

    def three(x):
        return jnp.sum(x[:, :3].astype(jnp.float32), axis=1)

    squares = three(mine[:, inner:]) + three(theirs[:, inner:])
    out_block = jnp.zeros((2 * inner, seq_count * w_out.shape[1]), mm)
    for k, pair in enumerate(out_blocks):
        for f, block in enumerate(pair):
            out_block = lax.dynamic_update_slice(
                out_block, block, (0, ((p ^ k) * 2 + (c ^ f)) * w_out.shape[1])
            )
    terms = [h[:, None] for h in split_terms(squares)]
    extra = jnp.concatenate(terms + [jnp.zeros((tok_dev, LANES - 3), mm)], axis=1)
    piece = tok_dev // tp_count

    def partial(to):
        a = lax.dynamic_slice_in_dim(both, to * piece, piece, 0)
        return jnp.dot(a, out_block, preferred_element_type=jnp.float32)

    total = None
    received = []
    for by in range(1, tp_count):
        to = (t + by) % tp_count
        low = jnp.concatenate(
            [partial(to).astype(mm), lax.dynamic_slice_in_dim(extra, to * piece, piece, 0)], axis=1
        )
        received.append(shift(low, by))
    total = partial(t)
    squares = lax.dynamic_slice_in_dim(squares, t * piece, piece, 0)
    for got in received:
        total = total + got[:, :width].astype(jnp.float32)
        squares = squares + three(got[:, width:])
    mixed = (total * lax.rsqrt(squares / inner_all + epsilon)[:, None]).astype(mm)

    per = request_group.shape[0] // seq_count
    def pick(who):
        wanted = lax.dynamic_slice_in_dim(request_group, who * per, per, 0)
        return jnp.stack([lax.dynamic_index_in_dim(leaving, wanted[i], 0, False) for i in range(per)])

    other_heads = flip(pick(s ^ 1), 1)
    states = jnp.zeros((per, 2 * heads, head_width, state_width), jnp.float32)
    states = lax.dynamic_update_slice(states, pick(s).astype(jnp.float32), (0, c * heads, 0, 0))
    states = lax.dynamic_update_slice(
        states, other_heads.astype(jnp.float32), (0, (1 - c) * heads, 0, 0)
    )
    return (mixed, states)


def solution(mesh):
    return jax.shard_map(
        on_device,
        mesh=mesh,
        in_specs=(
            P("seq", None),
            P(("seq", "tp"), None),
            P(("seq", "tp"), None),
            P(("seq", "tp"), None),
            P(None, "tp"),
            P("tp"),
            P(),
            P(),
            P("tp"),
            P("tp"),
            P("tp"),
            P("tp"),
            P("tp", "seq"),
            P(),
            P(),
        ),
        out_specs=(P(("seq", "tp"), None), P("seq", "tp", None, None)),
        check_vma=False,
    )
```

```python
import functools

import jax
import jax.numpy as jnp
from jax import lax
from jax.experimental import pallas as pl
from jax.experimental.pallas import tpu as pltpu
from jax.sharding import PartitionSpec as P

GROUP = 256
HALO = 16
LANES = 128
TERMS = 32
MM = jnp.bfloat16
F32 = jnp.float32
NEGATIVE = -1e30
VMEM_BYTES = 40 * 1024 * 1024

epsilon = 1e-05

ANY = pl.BlockSpec(memory_space=pl.ANY)
SMEM = pl.BlockSpec(memory_space=pltpu.SMEM)
VMEM = pl.BlockSpec(memory_space=pltpu.VMEM)


def flip(x, bits):
    count = lax.axis_size("seq")
    return lax.ppermute(x, "seq", [(i, i ^ bits) for i in range(count)])


def shift(x, by):
    count = lax.axis_size("tp")
    return lax.ppermute(x, "tp", [(i, (i + by) % count) for i in range(count)])


def plane_gather(halves):
    chips = lax.axis_size("seq") // 2
    blocks = [tuple(halves)]
    for k in range(1, chips):
        low = k & -k
        high = 1 << (k.bit_length() - 1)
        second = flip(blocks[k ^ high][1], 2 * high)
        first = flip(blocks[k ^ low][0], 2 * low)
        blocks.append((first, second))
    return blocks


def with_other_core(blocks):
    own = [piece for pair in blocks for piece in pair]
    return own + [flip(piece, 1) for piece in own]


def call(kernel, outs, in_specs, scratch=(), flops=0, moved=0, out_specs=None, name=None):
    return pl.pallas_call(
        kernel,
        out_shape=outs,
        in_specs=in_specs,
        out_specs=[VMEM] * len(outs) if out_specs is None else out_specs,
        scratch_shapes=list(scratch),
        compiler_params=pltpu.CompilerParams(vmem_limit_bytes=VMEM_BYTES),
        cost_estimate=pl.CostEstimate(flops=flops, bytes_accessed=moved, transcendentals=0),
        name=name,
    )


def split_terms(x):
    high = x.astype(MM).astype(F32)
    rest = x - high
    mid = rest.astype(MM).astype(F32)
    return high, mid, (rest - mid).astype(MM).astype(F32)


def run_all(copies):
    for copy in copies:
        copy.start()
    for copy in copies:
        copy.wait()


def starts_of(position, lengths_ref):
    start, end = jnp.zeros_like(position), 0
    for i in range(lengths_ref.shape[0]):
        end = end + lengths_ref[i]
        start = jnp.where(position >= end, end, start)
    return start


def pack_x_kernel(tp_count, place, w_ref, bc_ref, dt_ref, *outs):
    t = place[0]
    pair = w_ref.shape[1] // tp_count
    inner = pair // 2
    bc_width = bc_ref.shape[1]
    heads = dt_ref.shape[1] // tp_count
    low_bc = bc_ref[...].astype(MM)
    for j, out in enumerate(outs):
        owner = lax.rem(t + j, tp_count)
        at = pl.multiple_of(owner * pair, LANES)
        out[:, :inner] = w_ref[:, pl.ds(at, inner)].astype(MM)
        out[:, inner : inner + bc_width] = low_bc
        steps = jnp.zeros((dt_ref.shape[0], heads), F32)
        for u in range(tp_count):
            steps = jnp.where(owner == u, dt_ref[:, u * heads : (u + 1) * heads], steps)
        steps = jnp.concatenate(
            [steps, jnp.zeros((dt_ref.shape[0], LANES - heads), F32)], axis=1
        )
        out[:, inner + bc_width : inner + bc_width + LANES] = steps.astype(MM)
        at = pl.multiple_of(owner * pair + inner, LANES)
        out[:, inner + bc_width + LANES :] = w_ref[:, pl.ds(at, inner)].astype(MM)


def pack_z_kernel(tp_count, place, w_ref, *outs):
    t = place[0]
    pair = w_ref.shape[1] // tp_count
    for j, out in enumerate(outs):
        at = pl.multiple_of(lax.rem(t + j, tp_count) * pair, LANES)
        out[...] = w_ref[:, pl.ds(at, pair)].astype(MM)


def assemble_kernel(tp_count, place, *refs):
    t = place[0]
    pieces, low, high = refs[:tp_count], refs[tp_count], refs[tp_count + 1]
    rows = pieces[0].shape[0]
    for j, piece in enumerate(pieces):
        source = lax.rem(t + tp_count - j, tp_count)
        for half, out in ((0, low), (1, high)):

            @pl.when(source // (tp_count // 2) == half)
            def _():
                at = pl.multiple_of(lax.rem(source, tp_count // 2) * rows, 16)
                out[pl.ds(at, rows), :] = piece[...]


def halves_kernel(w_ref, low, high):
    half = w_ref.shape[0] // 2
    low[...] = w_ref[:half].astype(MM)
    high[...] = w_ref[half:].astype(MM)


def weight_copies(place, pieces, sems, target, columns):
    p, c = place[1], place[2]
    count = len(pieces) // 2
    half = pieces[0].shape[0]
    copies = []
    for i, piece in enumerate(pieces):
        k, side = (i % count) // 2, i % 2
        core = c if i < count else 1 - c
        row = pl.multiple_of(((p ^ k) * 2 + core) * (2 * half) + side * half, 16)
        for source, goal, size in columns:
            copies.append(
                pltpu.make_async_copy(
                    piece.at[:, pl.ds(source, size)],
                    target.at[pl.ds(row, half), pl.ds(goal, size)],
                    sems.at[len(copies)],
                )
            )
    return copies


def front_kernel(sizes, place, lengths_ref, tok_ref, cw_ref, cb_ref, hp_ref, *refs):
    inner, bc_width, heads, n_pieces, groups = sizes
    pieces = refs[:n_pieces]
    xs_ref, bc_ref, cum_ref, step_ref, low_ref, high_ref, weights, raw, sems = refs[n_pieces:]
    c = place[2]
    conv = inner + bc_width
    state = bc_width // 2
    head_width = inner // heads
    taps = cw_ref.shape[0]
    start_x = pl.multiple_of(c * (conv + LANES), LANES)
    run_all(
        weight_copies(
            place,
            pieces,
            sems,
            weights,
            ((start_x, 0, inner), (inner, inner, bc_width + LANES)),
        )
    )
    lower = (
        lax.broadcasted_iota(jnp.int32, (GROUP, GROUP), 0)
        >= lax.broadcasted_iota(jnp.int32, (GROUP, GROUP), 1)
    ).astype(F32)
    within = lax.broadcasted_iota(jnp.int32, (GROUP, LANES), 0)
    base = place[1] * (groups * GROUP)

    def one(g, out, at):
        row = pl.multiple_of(g * GROUP, 16)
        raw[...] = jnp.dot(
            tok_ref[pl.ds(row, HALO + GROUP), :], weights[...], preferred_element_type=F32
        )
        first = base + g * GROUP
        position = first + within
        behind = position - starts_of(position, lengths_ref)
        keeps = [(behind >= lag).astype(F32) for lag in range(1, taps)]
        for block in range(0, conv, LANES):
            lanes = slice(block, block + LANES)
            total = cb_ref[:, lanes] + jnp.zeros((GROUP, LANES), F32)
            for lag in range(taps):
                wide = raw[HALO - lag : HALO - lag + GROUP, lanes].astype(MM).astype(F32)
                term = wide * cw_ref[taps - 1 - lag : taps - lag, lanes]
                total = total + (term if lag == 0 else term * keeps[lag - 1])
            value = (total * (1.0 / (1.0 + jnp.exp(-total)))).astype(MM)
            if block < inner:
                xs_ref[pl.ds(row, GROUP), lanes] = value
            else:
                bc_ref[pl.ds(row, GROUP), block - inner : block - inner + LANES] = value
        dt = raw[HALO : HALO + GROUP, conv:]
        dt = jnp.where(c == 0, dt, pltpu.roll(dt, LANES - heads, 1)) + hp_ref[0:1, :]
        step = jnp.maximum(dt, 0.0) + jnp.log1p(jnp.exp(-jnp.abs(dt)))
        cum = jnp.dot(
            lower,
            step * -jnp.exp(hp_ref[1:2, :]),
            precision=lax.Precision.HIGHEST,
            preferred_element_type=F32,
        )
        cum_ref[pl.ds(row, GROUP), :] = cum
        step_ref[pl.ds(row, GROUP), :] = step
        last = cum[GROUP - 1 : GROUP, :]
        start_last = starts_of(first + (GROUP - 1), lengths_ref)
        tail = jnp.where(position >= start_last, jnp.exp(last - cum), 0.0) * step
        b_wide = bc_ref[pl.ds(row, GROUP), :state].astype(F32)
        for h in range(0, heads, 2):
            weighted = jnp.concatenate(
                [(b_wide * tail[:, h + i : h + i + 1]).astype(MM) for i in range(2)], axis=1
            )
            both = lax.dot_general(
                xs_ref[pl.ds(row, GROUP), h * head_width : (h + 2) * head_width],
                weighted,
                (((0,), (0,)), ((), ())),
                preferred_element_type=F32,
            )
            out[at, h * head_width : (h + 1) * head_width, :] = both[:head_width, :state].astype(MM)
            out[at, (h + 1) * head_width : (h + 2) * head_width, :] = both[
                head_width:, state:
            ].astype(MM)
        spread = jnp.broadcast_to(jnp.exp(last), (8, LANES))
        diagonal = lax.broadcasted_iota(jnp.int32, (8, LANES), 0) == lax.broadcasted_iota(
            jnp.int32, (8, LANES), 1
        )
        gates = jnp.sum(jnp.where(diagonal, spread, 0.0), axis=1, keepdims=True)
        gates = jnp.where(start_last < first, jnp.broadcast_to(gates, (8, LANES)), 0.0)
        rows = jnp.concatenate(list(split_terms(gates)) + [jnp.zeros_like(gates)], axis=0)
        out[at, inner : inner + TERMS, :] = rows.astype(MM)

    half = groups // 2
    for side, out in ((0, low_ref), (1, high_ref)):

        @pl.loop(0, half)
        def _(i):
            one(side * half + i, out, i)


def mid_kernel(sizes, place, lengths_ref, xs_ref, bc_ref, cum_ref, step_ref, skip_ref, y_ref):
    inner, heads, groups = sizes
    state = bc_ref.shape[1] // 2
    head_width = inner // heads
    base = place[1] * (groups * GROUP)
    within_i = lax.broadcasted_iota(jnp.int32, (GROUP, GROUP), 0)
    within_j = lax.broadcasted_iota(jnp.int32, (GROUP, GROUP), 1)
    lane = lax.broadcasted_iota(jnp.int32, (GROUP, LANES), 1)

    @pl.loop(0, groups)
    def _(g):
        row = pl.multiple_of(g * GROUP, 16)
        rows = pl.ds(row, GROUP)
        first = base + g * GROUP
        start = starts_of(first + within_i, lengths_ref)
        seen = (within_j <= within_i) & (first + within_j >= start)
        scores = lax.dot_general(
            bc_ref[rows, state:],
            bc_ref[rows, :state],
            (((1,), (1,)), ((), ())),
            preferred_element_type=F32,
        )
        cum = cum_ref[rows, :]
        cum_t = cum.T
        step_t = step_ref[rows, :].T
        for h in range(0, heads, 2):
            lanes = slice(h * head_width, (h + 2) * head_width)
            pair = xs_ref[rows, lanes]
            total = skip_ref[:, lanes] * pair.astype(F32)
            for i in range(2):
                log_decay = cum[:, h + i : h + i + 1] - cum_t[h + i : h + i + 1, :]
                decay = jnp.exp(jnp.where(seen, log_decay, NEGATIVE))
                mix = (decay * scores * step_t[h + i : h + i + 1, :]).astype(MM)
                own = jnp.where((lane < head_width) == (i == 0), pair, jnp.zeros_like(pair))
                total = total + jnp.dot(mix, own, preferred_element_type=F32)
            y_ref[rows, lanes] = total


def gate_kernel(sizes, place, tok_ref, *refs):
    inner, n_pieces = sizes
    pieces = refs[:n_pieces]
    out_ref, weights, sems = refs[n_pieces:]
    start = pl.multiple_of(place[2] * inner, LANES)
    run_all(weight_copies(place, pieces, sems, weights, ((start, 0, inner),)))
    count = out_ref.shape[0] // GROUP

    @pl.loop(0, count)
    def _(g):
        row = pl.multiple_of(g * GROUP, 16)
        out_ref[pl.ds(row, GROUP), :] = jnp.dot(
            tok_ref[pl.ds(row + HALO, GROUP), :], weights[...], preferred_element_type=F32
        ).astype(MM)


def back_kernel(
    sizes, place, lengths_ref, wanted, y_ref, gate_ref, bc_ref, cum_ref, norm_ref, *refs
):
    inner, heads, groups, n_pieces, per = sizes
    pieces = refs[:n_pieces]
    theirs, mine, asked, own_asked, parts, states, sems = refs[n_pieces:]
    p, c = place[1], place[2]
    state = bc_ref.shape[1] // 2
    head_width = inner // heads
    half = groups // 2
    copies = []
    for i, piece in enumerate(pieces):
        k, side = i // 2, i % 2
        at = (p ^ k) * groups + side * half
        copies.append(pltpu.make_async_copy(piece, parts.at[pl.ds(at, half)], sems.at[i]))
    run_all(copies)
    blocks = parts.shape[0]
    states[0] = jnp.zeros(states.shape[1:], F32)

    @pl.loop(0, blocks)
    def _(b):
        terms = parts[b, inner : inner + TERMS, :].astype(F32)
        gates = terms[0:8] + terms[8:16] + terms[16:24]
        for h in range(heads):
            rows = slice(h * head_width, (h + 1) * head_width)
            states[b + 1, rows, :] = gates[h : h + 1, :] * states[b, rows, :] + parts[
                b, rows, :
            ].astype(F32)

    chip = place[1] * 2
    for i in range(per):
        own_asked[i] = states[wanted[(chip + c) * per + i] + 1]
        asked[i] = states[wanted[(chip + 1 - c) * per + i] + 1].astype(MM)

    lane = lax.broadcasted_iota(jnp.int32, (GROUP, LANES), 1)
    within = lax.broadcasted_iota(jnp.int32, (GROUP, LANES), 0)
    for core, out in ((1 - c, theirs), (c, mine)):

        @pl.loop(0, half)
        def _(i):
            g = core * half + i
            rows = pl.ds(pl.multiple_of(g * GROUP, 16), GROUP)
            to = pl.ds(pl.multiple_of(i * GROUP, 16), GROUP)
            first = p * (groups * GROUP) + g * GROUP
            start = starts_of(first + within, lengths_ref)
            keep = jnp.where(start < first, jnp.exp(cum_ref[rows, :]), 0.0)
            low_state = states[p * groups + g].astype(MM)
            carried = lax.dot_general(
                bc_ref[rows, state:],
                low_state,
                (((1,), (1,)), ((), ())),
                preferred_element_type=F32,
            )
            squares = jnp.zeros((GROUP, LANES), F32)
            for h in range(0, heads, 2):
                lanes = slice(h * head_width, (h + 2) * head_width)
                factor = jnp.where(lane < head_width, keep[:, h : h + 1], keep[:, h + 1 : h + 2])
                y = y_ref[rows, lanes] + carried[:, lanes] * factor
                z = gate_ref[rows, lanes].astype(F32)
                gated = y * (z * (1.0 / (1.0 + jnp.exp(-z))))
                squares = squares + gated * gated
                out[to, lanes] = (gated * norm_ref[:, lanes]).astype(MM)
            total = jnp.broadcast_to(jnp.sum(squares, axis=1, keepdims=True), (GROUP, LANES))
            high, mid, low = split_terms(total)
            out[to, inner:] = jnp.where(
                lane == 0, high, jnp.where(lane == 1, mid, jnp.where(lane == 2, low, 0.0))
            ).astype(MM)


def out_kernel(sizes, place, mine, theirs, *refs):
    inner, n_pieces, tp_count = sizes
    pieces = refs[:n_pieces]
    outs = refs[n_pieces : n_pieces + tp_count]
    weights, sems = refs[n_pieces + tp_count :]
    t, p, c = place[0], place[1], place[2]
    count = n_pieces // 2
    half, columns = pieces[0].shape
    copies = []
    for i, piece in enumerate(pieces):
        k, side = (i % count) // 2, i % 2
        core = c if i < count else 1 - c
        at = pl.multiple_of(((p ^ k) * 2 + core) * columns, LANES)
        copies.append(
            pltpu.make_async_copy(
                piece,
                weights.at[pl.ds(side * half, half), pl.ds(at, columns)],
                sems.at[i],
            )
        )
    run_all(copies)
    width = weights.shape[1]
    piece_rows = mine.shape[0] // tp_count
    own_rows = pl.ds(pl.multiple_of(c * inner, 16), inner)
    other_rows = pl.ds(pl.multiple_of((1 - c) * inner, 16), inner)
    lane = lax.broadcasted_iota(jnp.int32, (piece_rows, LANES), 1)
    for j in list(range(1, tp_count)) + [0]:
        to = lax.rem(t + j, tp_count)
        rows = pl.ds(pl.multiple_of(to * piece_rows, 16), piece_rows)
        sums = jnp.sum(
            mine[rows, inner:].astype(F32) + theirs[rows, inner:].astype(F32), axis=1, keepdims=True
        )
        sums = jnp.broadcast_to(sums, (piece_rows, LANES))
        if j:
            high, mid, low = split_terms(sums)
            sums = jnp.where(
                lane == 0, high, jnp.where(lane == 1, mid, jnp.where(lane == 2, low, 0.0))
            )
        outs[j][:, width:] = sums.astype(outs[j].dtype)
        for at in range(0, width, 512):
            lanes = slice(at, at + 512)
            value = jnp.dot(mine[rows, :inner], weights[own_rows, lanes], preferred_element_type=F32)
            value = value + jnp.dot(
                theirs[rows, :inner], weights[other_rows, lanes], preferred_element_type=F32
            )
            outs[j][:, lanes] = value.astype(outs[j].dtype)


def final_kernel(channels, own, *refs):
    received, out = refs[:-1], refs[-1]
    width = out.shape[1]
    squares = own[:, width : width + 1]
    for got in received:
        squares = squares + jnp.sum(got[:, width:].astype(F32), axis=1, keepdims=True)
    factor = lax.rsqrt(squares / channels + epsilon)
    for at in range(0, width, 512):
        lanes = slice(at, at + 512)
        total = own[:, lanes]
        for got in received:
            total = total + got[:, lanes].astype(F32)
        out[:, lanes] = (total * factor).astype(out.dtype)


def on_device(
    tokens,
    w_zx,
    w_dt,
    w_bc,
    conv_x_weight,
    conv_x_bias,
    conv_bc_weight,
    conv_bc_bias,
    dt_bias,
    a_log,
    skip,
    norm_weight,
    w_out,
    lengths,
    request_group,
):
    tp_count, seq_count = lax.axis_size("tp"), lax.axis_size("seq")
    t, s = lax.axis_index("tp"), lax.axis_index("seq")
    chips = seq_count // 2
    p, c = s // 2, s % 2
    place = jnp.stack([t, p, c]).astype(jnp.int32)
    tok_dev, width = tokens.shape
    rows = w_zx.shape[0]
    taps = conv_x_weight.shape[0]
    inner_all = w_zx.shape[1] // 2
    inner = conv_x_weight.shape[1] // 2
    heads = dt_bias.shape[0] // 2
    head_width = inner // heads
    bc_width = w_bc.shape[1]
    state = bc_width // 2
    tok = 2 * tok_dev
    groups = tok // GROUP
    half = groups // 2
    conv = inner + bc_width
    sds = jax.ShapeDtypeStruct

    def core_part(x):
        size = x.shape[-1] // 2
        return lax.dynamic_slice_in_dim(x, c * size, size, x.ndim - 1)

    conv_weight = jnp.concatenate([core_part(conv_x_weight), conv_bc_weight], axis=1)
    conv_bias = jnp.concatenate([core_part(conv_x_bias), conv_bc_bias], axis=0)[None, :]
    head_params = jnp.stack([core_part(dt_bias), core_part(a_log)])
    head_params = jnp.pad(head_params, ((0, 0), (0, LANES - heads)))
    skip_row = jnp.repeat(core_part(skip), head_width)[None, :]
    norm_row = core_part(norm_weight)[None, :]

    half_rows = w_out.shape[0] // 2
    out_halves = call(
        halves_kernel, [sds((half_rows, w_out.shape[1]), MM)] * 2, [VMEM], name="out_halves"
    )(w_out)
    out_pieces = with_other_core(plane_gather(out_halves))

    x_width = 2 * inner + bc_width + LANES

    def packed(kernel, operands, specs, wide, name):
        return pl.pallas_call(
            functools.partial(kernel, tp_count),
            grid=(1,),
            out_shape=[sds((rows, wide), MM)] * tp_count,
            in_specs=specs,
            out_specs=[pl.BlockSpec((rows, wide), lambda i: (0, 0))] * tp_count,
            compiler_params=pltpu.CompilerParams(vmem_limit_bytes=VMEM_BYTES),
            name=name,
        )(*operands)

    def whole(x):
        return pl.BlockSpec(x.shape, lambda i: (0, 0))

    def assembled(pieces, name):
        pieces = [pieces[0]] + [shift(x, j) for j, x in enumerate(pieces) if j]
        wide = pieces[0].shape[1]
        return call(
            functools.partial(assemble_kernel, tp_count),
            [sds((tp_count * rows // 2, wide), MM)] * 2,
            [SMEM] + [VMEM] * tp_count,
            name=name,
        )(place, *pieces)

    x_sent = packed(
        pack_x_kernel,
        (place, w_zx, w_bc, w_dt),
        [SMEM, pl.BlockSpec((rows, inner_all), lambda i: (0, 1)), whole(w_bc), whole(w_dt)],
        x_width,
        "pack_x",
    )
    x_halves = assembled(x_sent, "assemble_x")
    place_z, *x_halves = lax.optimization_barrier((place, *x_halves))
    x_pieces = with_other_core(plane_gather(x_halves))

    z_sent = packed(
        pack_z_kernel,
        (place_z, w_zx),
        [SMEM, pl.BlockSpec((rows, inner_all), lambda i: (0, 0))],
        2 * inner,
        "pack_z",
    )
    z_pieces = with_other_core(plane_gather(assembled(z_sent, "assemble_z")))

    other = flip(tokens, 1)
    first_tok = jnp.where(c == 0, tokens, other)
    second_tok = jnp.where(c == 0, other, tokens)
    before = lax.ppermute(
        second_tok[tok_dev - HALO :], "seq", [(i, i + 2) for i in range(seq_count - 2)]
    )
    all_tok = jnp.concatenate([before, first_tok, second_tok], axis=0)

    n_pieces = len(x_pieces)
    message = sds((half, inner + TERMS, state), MM)
    xs, bc, cum, step, low, high = call(
        functools.partial(front_kernel, (inner, bc_width, heads, n_pieces, groups)),
        [
            sds((tok, inner), MM),
            sds((tok, bc_width), MM),
            sds((tok, LANES), F32),
            sds((tok, LANES), F32),
            message,
            message,
        ],
        [SMEM, SMEM, VMEM, VMEM, VMEM, VMEM] + [ANY] * n_pieces,
        [
            pltpu.VMEM((width, conv + LANES), MM),
            pltpu.VMEM((HALO + GROUP, conv + LANES), F32),
            pltpu.SemaphoreType.DMA((2 * n_pieces,)),
        ],
        flops=2 * (tok + HALO) * width * (conv + LANES),
        moved=12_000_000,
        name="front",
    )(place, lengths, all_tok, conv_weight, conv_bias, head_params, *x_pieces)

    parts = [piece for pair in plane_gather((low, high)) for piece in pair]

    (y,) = call(
        functools.partial(mid_kernel, (inner, heads, groups)),
        [sds((tok, inner), F32)],
        [SMEM, SMEM] + [VMEM] * 5,
        flops=2 * tok * GROUP * inner * 8,
        moved=8_000_000,
        name="mid",
    )(place, lengths, xs, bc, cum, step, skip_row)

    (gate,) = call(
        functools.partial(gate_kernel, (inner, n_pieces)),
        [sds((tok, inner), MM)],
        [SMEM, VMEM] + [ANY] * n_pieces,
        [pltpu.VMEM((width, inner), MM), pltpu.SemaphoreType.DMA((n_pieces,))],
        flops=2 * tok * width * inner,
        moved=8_000_000,
        name="gate",
    )(place, all_tok, *z_pieces)

    per = request_group.shape[0] // seq_count
    sent = sds((tok_dev, inner + LANES), MM)
    theirs, mine, asked, own_asked = call(
        functools.partial(back_kernel, (inner, heads, groups, len(parts), per)),
        [sent, sent, sds((per, inner, state), MM), sds((per, inner, state), F32)],
        [SMEM, SMEM, SMEM] + [VMEM] * 5 + [ANY] * len(parts),
        [
            pltpu.VMEM((chips * groups, inner + TERMS, state), MM),
            pltpu.VMEM((chips * groups + 1, inner, state), F32),
            pltpu.SemaphoreType.DMA((len(parts),)),
        ],
        flops=2 * tok * state * inner,
        moved=12_000_000,
        name="back",
    )(place, lengths, request_group, y, gate, bc, cum, norm_row, *parts)

    theirs = flip(theirs, 1)
    out_width = seq_count * w_out.shape[1]
    piece = tok_dev // tp_count
    partial = call(
        functools.partial(out_kernel, (inner, len(out_pieces), tp_count)),
        [sds((piece, out_width + LANES), F32 if j == 0 else MM) for j in range(tp_count)],
        [SMEM, VMEM, VMEM] + [ANY] * len(out_pieces),
        [
            pltpu.VMEM((2 * inner, out_width), MM),
            pltpu.SemaphoreType.DMA((len(out_pieces),)),
        ],
        flops=4 * tok_dev * inner * out_width,
        moved=8_000_000,
        name="out",
    )(place, mine, theirs, *out_pieces)
    received = [shift(x, j) for j, x in enumerate(partial) if j]
    (mixed,) = call(
        functools.partial(final_kernel, float(inner_all)),
        [sds((piece, out_width), MM)],
        [VMEM] * tp_count,
        name="final",
    )(partial[0], *received)

    other_asked = flip(asked, 1).astype(F32)
    states = jnp.where(
        c == 0,
        jnp.concatenate([own_asked, other_asked], axis=1),
        jnp.concatenate([other_asked, own_asked], axis=1),
    )
    return (mixed, states.reshape(per, 2 * heads, head_width, state))


def solution(mesh):
    return jax.shard_map(
        on_device,
        mesh=mesh,
        in_specs=(
            P("seq", None),
            P(("seq", "tp"), None),
            P(("seq", "tp"), None),
            P(("seq", "tp"), None),
            P(None, "tp"),
            P("tp"),
            P(),
            P(),
            P("tp"),
            P("tp"),
            P("tp"),
            P("tp"),
            P("tp", "seq"),
            P(),
            P(),
        ),
        out_specs=(P(("seq", "tp"), None), P("seq", "tp", None, None)),
        check_vma=False,
    )
```

```python
import functools

import jax
import jax.numpy as jnp
from jax import lax
from jax.experimental import pallas as pl
from jax.experimental.pallas import tpu as pltpu
from jax.sharding import PartitionSpec as P

GROUP = 256
HALO = 16
LANES = 128
TERMS = 32
MM = jnp.bfloat16
F32 = jnp.float32
NEGATIVE = -1e30
VMEM_BYTES = 20 * 1024 * 1024

epsilon = 1e-05

ANY = pl.BlockSpec(memory_space=pl.ANY)
SMEM = pl.BlockSpec(memory_space=pltpu.SMEM)
VMEM = pl.BlockSpec(memory_space=pltpu.VMEM)


def flip(x, bits):
    count = lax.axis_size("seq")
    return lax.ppermute(x, "seq", [(i, i ^ bits) for i in range(count)])


def shift(x, by):
    count = lax.axis_size("tp")
    return lax.ppermute(x, "tp", [(i, (i + by) % count) for i in range(count)])


def plane_gather(halves):
    chips = lax.axis_size("seq") // 2
    blocks = [tuple(halves)]
    for k in range(1, chips):
        low = k & -k
        high = 1 << (k.bit_length() - 1)
        second = flip(blocks[k ^ high][1], 2 * high)
        first = flip(blocks[k ^ low][0], 2 * low)
        blocks.append((first, second))
    return blocks


def plane_near(block):
    chips = lax.axis_size("seq") // 2
    return {k: (block if k == 0 else flip(block, 2 * k),) for k in range(chips) if k & (k - 1) == 0}


def plane_far(blocks):
    chips = lax.axis_size("seq") // 2
    blocks = dict(blocks)

    def half(k, side):
        if len(blocks[k]) == 2:
            return blocks[k][side]
        size = blocks[k][0].shape[0] // 2
        return blocks[k][0][side * size : (side + 1) * size]

    for k in range(1, chips):
        if k not in blocks:
            low = k & -k
            high = 1 << (k.bit_length() - 1)
            first = flip(half(k ^ low, 0), 2 * low)
            second = flip(half(k ^ high, 1), 2 * high)
            blocks[k] = (first, second)
    return blocks


def call(kernel, outs, in_specs, scratch=(), flops=0, moved=0, out_specs=None, name=None):
    return pl.pallas_call(
        kernel,
        out_shape=outs,
        in_specs=in_specs,
        out_specs=[VMEM] * len(outs) if out_specs is None else out_specs,
        scratch_shapes=list(scratch),
        compiler_params=pltpu.CompilerParams(vmem_limit_bytes=VMEM_BYTES),
        cost_estimate=pl.CostEstimate(flops=flops, bytes_accessed=moved, transcendentals=0),
        name=name,
    )


def split_terms(x):
    high = x.astype(MM).astype(F32)
    rest = x - high
    mid = rest.astype(MM).astype(F32)
    return high, mid, (rest - mid).astype(MM).astype(F32)


def silu(x):
    half = 0.5 * x
    return half + half * jnp.tanh(half)


def run_all(copies):
    for copy in copies:
        copy.start()
    for copy in copies:
        copy.wait()


def starts_of(position, lengths_ref):
    start, end = jnp.zeros_like(position), 0
    for i in range(lengths_ref.shape[0]):
        end = end + lengths_ref[i]
        start = jnp.where(position >= end, end, start)
    return start


def pack_x_kernel(tp_count, place, w_ref, bc_ref, dt_ref, *outs):
    t = place[0]
    pair = w_ref.shape[1] // tp_count
    inner = pair // 2
    bc_width = bc_ref.shape[1]
    heads = dt_ref.shape[1] // tp_count
    low_bc = bc_ref[...].astype(MM)
    for j, out in enumerate(outs):
        owner = lax.rem(t + j, tp_count)
        at = pl.multiple_of(owner * pair, LANES)
        out[:, :inner] = w_ref[:, pl.ds(at, inner)].astype(MM)
        out[:, inner : inner + bc_width] = low_bc
        steps = jnp.zeros((dt_ref.shape[0], heads), F32)
        for u in range(tp_count):
            steps = jnp.where(owner == u, dt_ref[:, u * heads : (u + 1) * heads], steps)
        steps = jnp.concatenate(
            [steps, jnp.zeros((dt_ref.shape[0], LANES - heads), F32)], axis=1
        )
        out[:, inner + bc_width : inner + bc_width + LANES] = steps.astype(MM)
        at = pl.multiple_of(owner * pair + inner, LANES)
        out[:, inner + bc_width + LANES :] = w_ref[:, pl.ds(at, inner)].astype(MM)


def pack_z_kernel(tp_count, place, w_ref, *outs):
    t = place[0]
    pair = w_ref.shape[1] // tp_count
    for j, out in enumerate(outs):
        at = pl.multiple_of(lax.rem(t + j, tp_count) * pair, LANES)
        out[...] = w_ref[:, pl.ds(at, pair)].astype(MM)


def assemble_kernel(tp_count, place, *refs):
    pieces, out = refs[:tp_count], refs[tp_count]
    rows = pieces[0].shape[0]
    for j, piece in enumerate(pieces):
        source = lax.rem(place[0] + tp_count - j, tp_count)
        out[pl.ds(pl.multiple_of(source * rows, 16), rows), :] = piece[...]


def weight_copies(place, pieces, where, depth, sems, target, columns):
    p, c = place[1], place[2]
    copies = []
    for piece, (k, other, first) in zip(pieces, where):
        core = 1 - c if other else c
        row = pl.multiple_of(((p ^ k) * 2 + core) * depth + first, 16)
        for source, goal, size in columns:
            copies.append(
                pltpu.make_async_copy(
                    piece.at[:, pl.ds(source, size)],
                    target.at[pl.ds(row, piece.shape[0]), pl.ds(goal, size)],
                    sems.at[len(copies)],
                )
            )
    return copies


def lane_row(ref, first, count):
    lane = lax.broadcasted_iota(jnp.int32, (1, LANES), 1)
    row = jnp.zeros((1, LANES), F32)
    for i in range(count):
        row = jnp.where(lane == i, ref[first + i], row)
    return row


def front_kernel(
    sizes, place, lengths_ref, bias_ref, decay_ref, tok_ref, cx_ref, bx_ref, cbc_ref, bbc_ref, *refs
):
    inner, bc_width, heads, where, depth, groups = sizes
    n_pieces = len(where)
    pieces = refs[:n_pieces]
    xs_ref, bc_ref, cum_ref, step_ref, low_ref, high_ref, weights, raw, sems = refs[n_pieces:]
    c = place[2]
    conv = inner + bc_width
    state = bc_width // 2
    head_width = inner // heads
    taps = cx_ref.shape[0]
    start_x = pl.multiple_of(c * (conv + LANES), LANES)
    run_all(
        weight_copies(
            place,
            pieces,
            where,
            depth,
            sems,
            weights,
            ((start_x, 0, inner), (inner, inner, bc_width + LANES)),
        )
    )
    lower = (
        lax.broadcasted_iota(jnp.int32, (GROUP, GROUP), 0)
        >= lax.broadcasted_iota(jnp.int32, (GROUP, GROUP), 1)
    ).astype(F32)
    within = lax.broadcasted_iota(jnp.int32, (GROUP, LANES), 0)
    base = place[1] * (groups * GROUP)
    bias = lane_row(bias_ref, c * heads, heads)
    rate = -jnp.exp(lane_row(decay_ref, c * heads, heads))

    def project(g):
        value = jnp.dot(
            tok_ref[g * GROUP : (g + 1) * GROUP + HALO, :],
            weights[...],
            preferred_element_type=F32,
        )
        raw[g % 2, :, :conv] = value[:, :conv].astype(MM).astype(F32)
        raw[g % 2, :, conv:] = value[:, conv:]

    def one(g, out, at):
        rows = slice(g * GROUP, (g + 1) * GROUP)
        slot = g % 2
        first = base + g * GROUP
        position = first + within
        behind = position - starts_of(position, lengths_ref)
        keeps = [(behind >= lag).astype(F32) for lag in range(1, taps)]
        for block in range(0, conv, LANES):
            lanes = slice(block, block + LANES)
            if block < inner:
                here = pl.ds(pl.multiple_of(c * inner + block, LANES), LANES)
                weight, offset = cx_ref[:, here], bx_ref[:, here]
            else:
                here = slice(block - inner, block - inner + LANES)
                weight, offset = cbc_ref[:, here], bbc_ref[:, here]
            total = offset + raw[slot, HALO : HALO + GROUP, lanes] * weight[taps - 1 : taps]
            for lag in range(1, taps):
                term = raw[slot, HALO - lag : HALO - lag + GROUP, lanes] * keeps[lag - 1]
                total = total + term * weight[taps - 1 - lag : taps - lag]
            value = silu(total).astype(MM)
            if block < inner:
                xs_ref[rows, lanes] = value
            else:
                bc_ref[rows, here] = value
        dt = raw[slot, HALO : HALO + GROUP, conv:]
        dt = jnp.where(c == 0, dt, pltpu.roll(dt, LANES - heads, 1)) + bias
        step = jnp.maximum(dt, 0.0) + jnp.log1p(jnp.exp(-jnp.abs(dt)))
        cum = jnp.dot(
            lower, step * rate, precision=lax.Precision.HIGHEST, preferred_element_type=F32
        )
        cum_ref[rows, :] = cum
        step_ref[rows, :] = step
        last = cum[GROUP - 1 : GROUP, :]
        start_last = starts_of(first + (GROUP - 1), lengths_ref)
        tail = jnp.where(position >= start_last, jnp.exp(last - cum), 0.0) * step
        b_wide = bc_ref[rows, :state].astype(F32)
        for h in range(0, heads, 2):
            weighted = jnp.concatenate(
                [(b_wide * tail[:, h + i : h + i + 1]).astype(MM) for i in range(2)], axis=1
            )
            both = lax.dot_general(
                xs_ref[rows, h * head_width : (h + 2) * head_width],
                weighted,
                (((0,), (0,)), ((), ())),
                preferred_element_type=F32,
            )
            out[at, h * head_width : (h + 1) * head_width, :] = both[:head_width, :state].astype(MM)
            out[at, (h + 1) * head_width : (h + 2) * head_width, :] = both[
                head_width:, state:
            ].astype(MM)
        spread = jnp.broadcast_to(jnp.exp(last), (8, LANES))
        diagonal = lax.broadcasted_iota(jnp.int32, (8, LANES), 0) == lax.broadcasted_iota(
            jnp.int32, (8, LANES), 1
        )
        gates = jnp.sum(jnp.where(diagonal, spread, 0.0), axis=1, keepdims=True)
        gates = jnp.where(start_last < first, jnp.broadcast_to(gates, (8, LANES)), 0.0)
        terms = jnp.concatenate(list(split_terms(gates)) + [jnp.zeros_like(gates)], axis=0)
        out[at, inner : inner + TERMS, :] = terms.astype(MM)

    half = groups // 2
    project(0)
    for g in range(groups):
        if g + 1 < groups:
            project(g + 1)
        one(g, (low_ref, high_ref)[g // half], g % half)


def mid_kernel(sizes, place, lengths_ref, skip_ref, xs_ref, bc_ref, cum_ref, step_ref, y_ref):
    inner, heads, groups = sizes
    state = bc_ref.shape[1] // 2
    head_width = inner // heads
    base = place[1] * (groups * GROUP)
    within_i = lax.broadcasted_iota(jnp.int32, (GROUP, GROUP), 0)
    within_j = lax.broadcasted_iota(jnp.int32, (GROUP, GROUP), 1)
    lane = lax.broadcasted_iota(jnp.int32, (GROUP, LANES), 1)

    @pl.loop(0, groups)
    def _(g):
        row = pl.multiple_of(g * GROUP, 16)
        rows = pl.ds(row, GROUP)
        first = base + g * GROUP
        start = starts_of(first + within_i, lengths_ref)
        seen = (within_j <= within_i) & (first + within_j >= start)
        scores = lax.dot_general(
            bc_ref[rows, state:],
            bc_ref[rows, :state],
            (((1,), (1,)), ((), ())),
            preferred_element_type=F32,
        )
        cum = cum_ref[rows, :]
        cum_t = cum.T
        step_t = step_ref[rows, :].T
        for h in range(0, heads, 2):
            lanes = slice(h * head_width, (h + 2) * head_width)
            pair = xs_ref[rows, lanes]
            first_skip, second_skip = (skip_ref[place[2] * heads + h + i] for i in range(2))
            total = jnp.where(lane < head_width, first_skip, second_skip) * pair.astype(F32)
            for i in range(2):
                log_decay = cum[:, h + i : h + i + 1] - cum_t[h + i : h + i + 1, :]
                decay = jnp.exp(jnp.where(seen, log_decay, NEGATIVE))
                mix = (decay * scores * step_t[h + i : h + i + 1, :]).astype(MM)
                own = jnp.where((lane < head_width) == (i == 0), pair, jnp.zeros_like(pair))
                total = total + jnp.dot(mix, own, preferred_element_type=F32)
            y_ref[rows, lanes] = total


def gate_kernel(inner, place, tok_ref, all_ref, out_ref, weights, sem):
    start = pl.multiple_of(place[2] * inner, LANES)
    run_all([pltpu.make_async_copy(all_ref.at[:, :, pl.ds(start, inner)], weights, sem)])
    count = out_ref.shape[0] // GROUP
    depth = weights.shape[0] * weights.shape[1]

    @pl.loop(0, count)
    def _(g):
        row = pl.multiple_of(g * GROUP, 16)
        out_ref[pl.ds(row, GROUP), :] = jnp.dot(
            tok_ref[pl.ds(row + HALO, GROUP), :],
            weights[...].reshape(depth, inner),
            preferred_element_type=F32,
        ).astype(MM)


def back_kernel(
    sizes, place, lengths_ref, wanted, y_ref, gate_ref, bc_ref, cum_ref, norm_ref, *refs
):
    inner, heads, groups, n_pieces, per = sizes
    pieces = refs[:n_pieces]
    theirs, mine, asked, own_asked, parts, states, sems = refs[n_pieces:]
    p, c = place[1], place[2]
    state = bc_ref.shape[1] // 2
    head_width = inner // heads
    half = groups // 2
    copies = []
    for i, piece in enumerate(pieces):
        k, side = i // 2, i % 2
        at = (p ^ k) * groups + side * half
        copies.append(pltpu.make_async_copy(piece, parts.at[pl.ds(at, half)], sems.at[i]))
    run_all(copies)
    blocks = parts.shape[0]
    states[0] = jnp.zeros(states.shape[1:], F32)

    @pl.loop(0, blocks)
    def _(b):
        terms = parts[b, inner : inner + TERMS, :].astype(F32)
        gates = terms[0:8] + terms[8:16] + terms[16:24]
        for h in range(heads):
            rows = slice(h * head_width, (h + 1) * head_width)
            states[b + 1, rows, :] = gates[h : h + 1, :] * states[b, rows, :] + parts[
                b, rows, :
            ].astype(F32)

    chip = place[1] * 2
    for i in range(per):
        own_asked[i] = states[wanted[(chip + c) * per + i] + 1]
        asked[i] = states[wanted[(chip + 1 - c) * per + i] + 1].astype(MM)

    lane = lax.broadcasted_iota(jnp.int32, (GROUP, LANES), 1)
    within = lax.broadcasted_iota(jnp.int32, (GROUP, LANES), 0)
    for core, out in ((1 - c, theirs), (c, mine)):

        @pl.loop(0, half)
        def _(i):
            g = core * half + i
            rows = pl.ds(pl.multiple_of(g * GROUP, 16), GROUP)
            to = pl.ds(pl.multiple_of(i * GROUP, 16), GROUP)
            first = p * (groups * GROUP) + g * GROUP
            start = starts_of(first + within, lengths_ref)
            keep = jnp.where(start < first, jnp.exp(cum_ref[rows, :]), 0.0)
            low_state = states[p * groups + g].astype(MM)
            carried = lax.dot_general(
                bc_ref[rows, state:],
                low_state,
                (((1,), (1,)), ((), ())),
                preferred_element_type=F32,
            )
            squares = jnp.zeros((GROUP, LANES), F32)
            for h in range(0, heads, 2):
                lanes = slice(h * head_width, (h + 2) * head_width)
                factor = jnp.where(lane < head_width, keep[:, h : h + 1], keep[:, h + 1 : h + 2])
                y = y_ref[rows, lanes] + carried[:, lanes] * factor
                z = gate_ref[rows, lanes].astype(F32)
                gated = y * silu(z)
                squares = squares + gated * gated
                here = pl.ds(pl.multiple_of(c * inner + h * head_width, LANES), LANES)
                out[to, lanes] = (gated * norm_ref[:, here]).astype(MM)
            total = jnp.broadcast_to(jnp.sum(squares, axis=1, keepdims=True), (GROUP, LANES))
            high, mid, low = split_terms(total)
            out[to, inner:] = jnp.where(
                lane == 0, high, jnp.where(lane == 1, mid, jnp.where(lane == 2, low, 0.0))
            ).astype(MM)


def out_kernel(sizes, place, mine, theirs, all_ref, *refs):
    inner, tp_count = sizes
    outs = refs[:tp_count]
    weights, sems = refs[tp_count:]
    t, c = place[0], place[2]
    count, _, columns = all_ref.shape
    run_all(
        [
            pltpu.make_async_copy(
                all_ref.at[i], weights.at[:, pl.ds(i * columns, columns)], sems.at[i]
            )
            for i in range(count)
        ]
    )
    width = weights.shape[1]
    piece_rows = mine.shape[0] // tp_count
    own_rows = pl.ds(pl.multiple_of(c * inner, 16), inner)
    other_rows = pl.ds(pl.multiple_of((1 - c) * inner, 16), inner)
    lane = lax.broadcasted_iota(jnp.int32, (piece_rows, LANES), 1)
    for j in list(range(1, tp_count)) + [0]:
        to = lax.rem(t + j, tp_count)
        rows = pl.ds(pl.multiple_of(to * piece_rows, 16), piece_rows)
        sums = jnp.sum(
            mine[rows, inner:].astype(F32) + theirs[rows, inner:].astype(F32), axis=1, keepdims=True
        )
        sums = jnp.broadcast_to(sums, (piece_rows, LANES))
        if j:
            high, mid, low = split_terms(sums)
            sums = jnp.where(
                lane == 0, high, jnp.where(lane == 1, mid, jnp.where(lane == 2, low, 0.0))
            )
        outs[j][:, width:] = sums.astype(outs[j].dtype)
        for at in range(0, width, 512):
            lanes = slice(at, at + 512)
            value = jnp.dot(mine[rows, :inner], weights[own_rows, lanes], preferred_element_type=F32)
            value = value + jnp.dot(
                theirs[rows, :inner], weights[other_rows, lanes], preferred_element_type=F32
            )
            outs[j][:, lanes] = value.astype(outs[j].dtype)


def final_kernel(channels, own, *refs):
    received, out = refs[:-1], refs[-1]
    width = out.shape[1]
    squares = own[:, width : width + 1]
    for got in received:
        squares = squares + jnp.sum(got[:, width:].astype(F32), axis=1, keepdims=True)
    factor = lax.rsqrt(squares / channels + epsilon)
    for at in range(0, width, 512):
        lanes = slice(at, at + 512)
        total = own[:, lanes]
        for got in received:
            total = total + got[:, lanes].astype(F32)
        out[:, lanes] = (total * factor).astype(out.dtype)


def on_device(
    tokens,
    w_zx,
    w_dt,
    w_bc,
    conv_x_weight,
    conv_x_bias,
    conv_bc_weight,
    conv_bc_bias,
    dt_bias,
    a_log,
    skip,
    norm_weight,
    w_out,
    lengths,
    request_group,
):
    tp_count, seq_count = lax.axis_size("tp"), lax.axis_size("seq")
    t, s = lax.axis_index("tp"), lax.axis_index("seq")
    chips = seq_count // 2
    p, c = s // 2, s % 2
    place = jnp.stack([t, p, c]).astype(jnp.int32)
    tok_dev, width = tokens.shape
    rows = w_zx.shape[0]
    inner_all = w_zx.shape[1] // 2
    inner = conv_x_weight.shape[1] // 2
    heads = dt_bias.shape[0] // 2
    head_width = inner // heads
    bc_width = w_bc.shape[1]
    state = bc_width // 2
    tok = 2 * tok_dev
    groups = tok // GROUP
    half = groups // 2
    conv = inner + bc_width
    sds = jax.ShapeDtypeStruct

    def packed(kernel, operands, specs, wide, name):
        return pl.pallas_call(
            functools.partial(kernel, tp_count),
            grid=(1,),
            out_shape=[sds((rows, wide), MM)] * tp_count,
            in_specs=specs,
            out_specs=[pl.BlockSpec((rows, wide), lambda i: (0, 0))] * tp_count,
            compiler_params=pltpu.CompilerParams(vmem_limit_bytes=VMEM_BYTES),
            name=name,
        )(*operands)

    def whole(x):
        return pl.BlockSpec(x.shape, lambda i: (0, 0))

    def sent_over_tp(pieces):
        return [pieces[0]] + [shift(x, j) for j, x in enumerate(pieces) if j]

    def assembled(pieces, name):
        wide = pieces[0].shape[1]
        return call(
            functools.partial(assemble_kernel, tp_count),
            [sds((tp_count * rows, wide), MM)],
            [SMEM] + [VMEM] * tp_count,
            name=name,
        )(place, *pieces)[0]

    def after(first, then):
        joined = lax.optimization_barrier((tuple(first), tuple(then)))
        return list(joined[0]), list(joined[1])

    out_low = w_out.astype(MM)
    out_all = lax.all_gather(out_low, "seq")

    x_width = 2 * inner + bc_width + LANES
    x_sent = packed(
        pack_x_kernel,
        (place, w_zx, w_bc, w_dt),
        [SMEM, pl.BlockSpec((rows, inner_all), lambda i: (0, 1)), whole(w_bc), whole(w_dt)],
        x_width,
        "pack_x",
    )
    x_block = assembled(sent_over_tp(x_sent), "assemble_x")

    other = flip(tokens, 1)
    first_tok = jnp.where(c == 0, tokens, other)
    second_tok = jnp.where(c == 0, other, tokens)
    before = lax.ppermute(
        second_tok[tok_dev - HALO :], "seq", [(i, i + 2) for i in range(seq_count - 2)]
    )
    all_tok = jnp.concatenate([before, first_tok, second_tok], axis=0)

    x_block, all_tok, place_z = lax.optimization_barrier((x_block, all_tok, place))
    z_sent = packed(
        pack_z_kernel,
        (place_z, w_zx),
        [SMEM, pl.BlockSpec((rows, inner_all), lambda i: (0, 0))],
        2 * inner,
        "pack_z",
    )
    near = plane_near(x_block)
    z_got = sent_over_tp(z_sent)
    blocks, (out_all, *z_got) = after([near[k][0] for k in near], [out_all, *z_got])
    z_all = lax.all_gather(assembled(z_got, "assemble_z"), "seq")
    far = plane_far({k: (block,) for k, block in zip(near, blocks)})
    depth = x_block.shape[0]
    where = [(k, 0, i * depth // 2) for k in far for i in range(len(far[k]))]
    x_pieces = [piece for k in far for piece in far[k]]
    x_pieces += [flip(piece, 1) for piece in x_pieces]
    where = tuple(where + [(k, 1, first) for k, _, first in where])

    n_pieces = len(x_pieces)
    message = sds((half, inner + TERMS, state), MM)
    xs, bc, cum, step, low, high = call(
        functools.partial(front_kernel, (inner, bc_width, heads, where, depth, groups)),
        [
            sds((tok, inner), MM),
            sds((tok, bc_width), MM),
            sds((tok, LANES), F32),
            sds((tok, LANES), F32),
            message,
            message,
        ],
        [SMEM] * 4 + [VMEM] * 5 + [ANY] * n_pieces,
        [
            pltpu.VMEM((width, conv + LANES), MM),
            pltpu.VMEM((2, HALO + GROUP, conv + LANES), F32),
            pltpu.SemaphoreType.DMA((2 * n_pieces,)),
        ],
        flops=2 * (tok + HALO) * width * (conv + LANES),
        moved=12_000_000,
        name="front",
    )(
        place,
        lengths,
        dt_bias,
        a_log,
        all_tok,
        conv_x_weight,
        conv_x_bias[None, :],
        conv_bc_weight,
        conv_bc_bias[None, :],
        *x_pieces,
    )

    parts = [piece for pair in plane_gather((low, high)) for piece in pair]

    (y,) = call(
        functools.partial(mid_kernel, (inner, heads, groups)),
        [sds((tok, inner), F32)],
        [SMEM] * 3 + [VMEM] * 4,
        flops=2 * tok * GROUP * inner * 8,
        moved=8_000_000,
        name="mid",
    )(place, lengths, skip, xs, bc, cum, step)

    (gate,) = call(
        functools.partial(gate_kernel, inner),
        [sds((tok, inner), MM)],
        [SMEM, VMEM, ANY],
        [pltpu.VMEM((seq_count, depth, inner), MM), pltpu.SemaphoreType.DMA(())],
        flops=2 * tok * width * inner,
        moved=8_000_000,
        name="gate",
    )(place, all_tok, z_all)

    per = request_group.shape[0] // seq_count
    sent = sds((tok_dev, inner + LANES), MM)
    theirs, mine, asked, own_asked = call(
        functools.partial(back_kernel, (inner, heads, groups, len(parts), per)),
        [sent, sent, sds((per, inner, state), MM), sds((per, inner, state), F32)],
        [SMEM, SMEM, SMEM] + [VMEM] * 5 + [ANY] * len(parts),
        [
            pltpu.VMEM((chips * groups, inner + TERMS, state), MM),
            pltpu.VMEM((chips * groups + 1, inner, state), F32),
            pltpu.SemaphoreType.DMA((len(parts),)),
        ],
        flops=2 * tok * state * inner,
        moved=12_000_000,
        name="back",
    )(place, lengths, request_group, y, gate, bc, cum, norm_weight[None, :], *parts)

    theirs = flip(theirs, 1)
    out_width = seq_count * w_out.shape[1]
    piece = tok_dev // tp_count
    partial = call(
        functools.partial(out_kernel, (inner, tp_count)),
        [sds((piece, out_width + LANES), F32 if j == 0 else MM) for j in range(tp_count)],
        [SMEM, VMEM, VMEM, ANY],
        [
            pltpu.VMEM((2 * inner, out_width), MM),
            pltpu.SemaphoreType.DMA((seq_count,)),
        ],
        flops=4 * tok_dev * inner * out_width,
        moved=8_000_000,
        name="out",
    )(place, mine, theirs, out_all)
    received = [shift(x, j) for j, x in enumerate(partial) if j]
    (mixed,) = call(
        functools.partial(final_kernel, float(inner_all)),
        [sds((piece, out_width), MM)],
        [VMEM] * tp_count,
        name="final",
    )(partial[0], *received)

    other_asked = flip(asked, 1).astype(F32)
    states = jnp.where(
        c == 0,
        jnp.concatenate([own_asked, other_asked], axis=1),
        jnp.concatenate([other_asked, own_asked], axis=1),
    )
    return (mixed, states.reshape(per, 2 * heads, head_width, state))


def solution(mesh):
    return jax.shard_map(
        on_device,
        mesh=mesh,
        in_specs=(
            P("seq", None),
            P(("seq", "tp"), None),
            P(("seq", "tp"), None),
            P(("seq", "tp"), None),
            P(None, "tp"),
            P("tp"),
            P(),
            P(),
            P("tp"),
            P("tp"),
            P("tp"),
            P("tp"),
            P("tp", "seq"),
            P(),
            P(),
        ),
        out_specs=(P(("seq", "tp"), None), P("seq", "tp", None, None)),
        check_vma=False,
    )
```

```python
import functools

import jax
import jax.numpy as jnp
from jax import lax
from jax.experimental import pallas as pl
from jax.experimental.pallas import tpu as pltpu
from jax.sharding import PartitionSpec as P

GROUP = 256
HALO = 16
LANES = 128
TERMS = 32
MM = jnp.bfloat16
F32 = jnp.float32
NEGATIVE = -1e30
sds = jax.ShapeDtypeStruct
VMEM_BYTES = 20 * 1024 * 1024

epsilon = 1e-05

ANY = pl.BlockSpec(memory_space=pl.ANY)
SMEM = pl.BlockSpec(memory_space=pltpu.SMEM)
VMEM = pl.BlockSpec(memory_space=pltpu.VMEM)


def flip(x, bits):
    count = lax.axis_size("seq")
    return lax.ppermute(x, "seq", [(i, i ^ bits) for i in range(count)])


def shift(x, by):
    count = lax.axis_size("tp")
    return lax.ppermute(x, "tp", [(i, (i + by) % count) for i in range(count)])


def plane_near(block):
    chips = lax.axis_size("seq") // 2
    return {k: (block if k == 0 else flip(block, 2 * k),) for k in range(chips) if k & (k - 1) == 0}


def plane_far(blocks):
    chips = lax.axis_size("seq") // 2
    blocks = dict(blocks)

    def half(k, side):
        if len(blocks[k]) == 2:
            return blocks[k][side]
        size = blocks[k][0].shape[0] // 2
        return blocks[k][0][side * size : (side + 1) * size]

    for k in range(1, chips):
        if k not in blocks:
            low = k & -k
            high = 1 << (k.bit_length() - 1)
            first = flip(half(k ^ low, 0), 2 * low)
            second = flip(half(k ^ high, 1), 2 * high)
            blocks[k] = (first, second)
    return blocks


def call(kernel, outs, in_specs, scratch=(), flops=0, moved=0, out_specs=None, name=None):
    return pl.pallas_call(
        kernel,
        out_shape=outs,
        in_specs=in_specs,
        out_specs=[VMEM] * len(outs) if out_specs is None else out_specs,
        scratch_shapes=list(scratch),
        compiler_params=pltpu.CompilerParams(vmem_limit_bytes=VMEM_BYTES),
        cost_estimate=pl.CostEstimate(flops=flops, bytes_accessed=moved, transcendentals=0),
        name=name,
    )


def split_terms(x):
    high = x.astype(MM).astype(F32)
    rest = x - high
    mid = rest.astype(MM).astype(F32)
    return high, mid, (rest - mid).astype(MM).astype(F32)


def silu(x):
    half = 0.5 * x
    return half + half * jnp.tanh(half)


def run_all(copies):
    for copy in copies:
        copy.start()
    for copy in copies:
        copy.wait()


def starts_of(position, ints):
    start, end = jnp.zeros_like(position), 0
    for i in range(ints.prompts):
        end = end + ints.ref[3 + i]
        start = jnp.where(position >= end, end, start)
    return start


class Ints:
    def __init__(self, ref, prompts):
        self.ref, self.prompts = ref, prompts
        self.t, self.p, self.c = ref[0], ref[1], ref[2]

    def wanted(self, i):
        return self.ref[3 + self.prompts + i]


def rows_at(first, size):
    return pl.ds(pl.multiple_of(first, 16), size)


def pack_x_kernel(tp_count, ints, w_ref, bc_ref, dt_ref, *outs):
    t = ints[0]
    pair = w_ref.shape[1] // tp_count
    inner = pair // 2
    bc_width = bc_ref.shape[1]
    heads = dt_ref.shape[1] // tp_count
    low_bc = bc_ref[...].astype(MM)
    for j, out in enumerate(outs):
        owner = lax.rem(t + j, tp_count)
        at = pl.multiple_of(owner * pair, LANES)
        out[:, :inner] = w_ref[:, pl.ds(at, inner)].astype(MM)
        out[:, inner : inner + bc_width] = low_bc
        steps = jnp.zeros((dt_ref.shape[0], heads), F32)
        for u in range(tp_count):
            steps = jnp.where(owner == u, dt_ref[:, u * heads : (u + 1) * heads], steps)
        steps = jnp.concatenate(
            [steps, jnp.zeros((dt_ref.shape[0], LANES - heads), F32)], axis=1
        )
        out[:, inner + bc_width : inner + bc_width + LANES] = steps.astype(MM)
        at = pl.multiple_of(owner * pair + inner, LANES)
        out[:, inner + bc_width + LANES :] = w_ref[:, pl.ds(at, inner)].astype(MM)


def pack_z_kernel(tp_count, ints, w_ref, *outs):
    pair = w_ref.shape[1] // tp_count
    for j, out in enumerate(outs):
        at = pl.multiple_of(lax.rem(ints[0] + j, tp_count) * pair, LANES)
        out[...] = w_ref[:, pl.ds(at, pair)].astype(MM)


def assemble_x_kernel(tp_count, ints, *refs):
    pieces, out = refs[:tp_count], refs[tp_count]
    rows = pieces[0].shape[0]
    for j, piece in enumerate(pieces):
        source = lax.rem(ints[0] + tp_count - j, tp_count)
        out[rows_at(source * rows, rows), :] = piece[...]


def assemble_z_kernel(tp_count, ints, *refs):
    pieces, (mine, theirs) = refs[:tp_count], refs[tp_count:]
    rows, inner = pieces[0].shape[0], mine.shape[1]
    c = ints[2]
    for j, piece in enumerate(pieces):
        at = rows_at(lax.rem(ints[0] + tp_count - j, tp_count) * rows, rows)
        mine[at, :] = piece[:, pl.ds(pl.multiple_of(c * inner, LANES), inner)]
        theirs[at, :] = piece[:, pl.ds(pl.multiple_of((1 - c) * inner, LANES), inner)]


def merge_kernel(ints, mine, theirs, out):
    rows = mine.shape[0]
    out[rows_at(ints[2] * rows, rows), :] = mine[...]
    out[rows_at((1 - ints[2]) * rows, rows), :] = theirs[...]


def lane_row(ref, first, count):
    lane = lax.broadcasted_iota(jnp.int32, (1, LANES), 1)
    row = jnp.zeros((1, LANES), F32)
    for i in range(count):
        row = jnp.where(lane == i, ref[first + i], row)
    return row


def front_kernel(sizes, ints_ref, floats, vecs, tok_ref, *refs):
    inner, bc_width, heads, prompts, where, depth, groups, side = sizes
    ints = Ints(ints_ref, prompts)
    c = ints.c
    conv = inner + bc_width
    state = bc_width // 2
    head_width = inner // heads
    half = groups // 2
    if where:
        pieces = refs[: len(where)]
        xs_ref, bc_ref, cum_ref, step_ref, message, weights, raw, sems = refs[len(where) :]
        start_x = pl.multiple_of(c * (conv + LANES), LANES)
        copies = []
        for piece, (k, other, first) in zip(pieces, where):
            core = 1 - c if other else c
            rows = rows_at(((ints.p ^ k) * 2 + core) * depth + first, piece.shape[0])
            for source, goal, size in ((start_x, 0, inner), (inner, inner, bc_width + LANES)):
                copies.append(
                    pltpu.make_async_copy(
                        piece.at[:, pl.ds(source, size)],
                        weights.at[rows, pl.ds(goal, size)],
                        sems.at[len(copies)],
                    )
                )
        run_all(copies)
    else:
        weights, xs_ref, bc_ref, cum_ref, step_ref, message, raw = refs
    taps = 4
    lower = (
        lax.broadcasted_iota(jnp.int32, (GROUP, GROUP), 0)
        >= lax.broadcasted_iota(jnp.int32, (GROUP, GROUP), 1)
    ).astype(F32)
    within = lax.broadcasted_iota(jnp.int32, (GROUP, LANES), 0)
    base = ints.p * (groups * GROUP) + side * half * GROUP
    all_heads = 2 * heads
    bias = lane_row(floats, c * heads, heads)
    rate = -jnp.exp(lane_row(floats, all_heads + c * heads, heads))

    def project(g):
        at = (side * half + g) * GROUP
        value = jnp.dot(
            tok_ref[at : at + GROUP + HALO, :], weights[...], preferred_element_type=F32
        )
        raw[g % 2, :, :conv] = value[:, :conv].astype(MM).astype(F32)
        raw[g % 2, :, conv:] = value[:, conv:]

    def one(g):
        rows = slice(g * GROUP, (g + 1) * GROUP)
        slot = g % 2
        first = base + g * GROUP
        position = first + within
        behind = position - starts_of(position, ints)
        keeps = [(behind >= lag).astype(F32) for lag in range(1, taps)]
        for block in range(0, conv, LANES):
            lanes = slice(block, block + LANES)
            if block < inner:
                here = pl.ds(pl.multiple_of(c * inner + block, LANES), LANES)
                weight, offset = vecs[0:taps, here], vecs[taps : taps + 1, here]
            else:
                here = slice(block - inner, block - inner + LANES)
                weight, offset = vecs[8 : 8 + taps, here], vecs[8 + taps : 9 + taps, here]
            total = offset + raw[slot, HALO : HALO + GROUP, lanes] * weight[taps - 1 : taps]
            for lag in range(1, taps):
                term = raw[slot, HALO - lag : HALO - lag + GROUP, lanes] * keeps[lag - 1]
                total = total + term * weight[taps - 1 - lag : taps - lag]
            value = silu(total).astype(MM)
            if block < inner:
                xs_ref[rows, lanes] = value
            else:
                bc_ref[rows, here] = value
        dt = raw[slot, HALO : HALO + GROUP, conv:]
        dt = jnp.where(c == 0, dt, pltpu.roll(dt, LANES - heads, 1)) + bias
        step = jnp.maximum(dt, 0.0) + jnp.log1p(jnp.exp(-jnp.abs(dt)))
        cum = jnp.dot(
            lower, step * rate, precision=lax.Precision.HIGHEST, preferred_element_type=F32
        )
        cum_ref[rows, :] = cum
        step_ref[rows, :] = step
        last = cum[GROUP - 1 : GROUP, :]
        start_last = starts_of(first + (GROUP - 1), ints)
        tail = jnp.where(position >= start_last, jnp.exp(last - cum), 0.0) * step
        b_wide = bc_ref[rows, :state].astype(F32)
        for h in range(0, heads, 2):
            weighted = jnp.concatenate(
                [(b_wide * tail[:, h + i : h + i + 1]).astype(MM) for i in range(2)], axis=1
            )
            both = lax.dot_general(
                xs_ref[rows, h * head_width : (h + 2) * head_width],
                weighted,
                (((0,), (0,)), ((), ())),
                preferred_element_type=F32,
            )
            at = h * head_width
            message[g, at : at + head_width, :] = both[:head_width, :state].astype(MM)
            at = at + head_width
            message[g, at : at + head_width, :] = both[head_width:, state:].astype(MM)
        spread = jnp.broadcast_to(jnp.exp(last), (8, LANES))
        diagonal = lax.broadcasted_iota(jnp.int32, (8, LANES), 0) == lax.broadcasted_iota(
            jnp.int32, (8, LANES), 1
        )
        gates = jnp.sum(jnp.where(diagonal, spread, 0.0), axis=1, keepdims=True)
        gates = jnp.where(start_last < first, jnp.broadcast_to(gates, (8, LANES)), 0.0)
        terms = jnp.concatenate(list(split_terms(gates)) + [jnp.zeros_like(gates)], axis=0)
        message[g, inner : inner + TERMS, :] = terms.astype(MM)

    project(0)
    for g in range(half):
        if g + 1 < half:
            project(g + 1)
        one(g)


def mid_kernel(sizes, ints_ref, floats, xs_ref, bc_ref, cum_ref, step_ref, y_ref, keep_ref):
    inner, heads, prompts, groups, side = sizes
    ints = Ints(ints_ref, prompts)
    state = bc_ref.shape[1] // 2
    head_width = inner // heads
    half = groups // 2
    base = ints.p * (groups * GROUP) + side * half * GROUP
    within_i = lax.broadcasted_iota(jnp.int32, (GROUP, GROUP), 0)
    within_j = lax.broadcasted_iota(jnp.int32, (GROUP, GROUP), 1)
    lane = lax.broadcasted_iota(jnp.int32, (GROUP, LANES), 1)
    skip_at = 4 * heads + ints.c * heads

    @pl.loop(0, half)
    def _(g):
        rows = rows_at(g * GROUP, GROUP)
        first = base + g * GROUP
        start = starts_of(first + within_i, ints)
        seen = (within_j <= within_i) & (first + within_j >= start)
        scores = lax.dot_general(
            bc_ref[rows, state:],
            bc_ref[rows, :state],
            (((1,), (1,)), ((), ())),
            preferred_element_type=F32,
        )
        cum = cum_ref[rows, :]
        cum_t = cum.T
        step_t = step_ref[rows, :].T
        keep = jnp.where(start[:, :LANES] < first, jnp.exp(cum), 0.0)
        for h in range(0, heads, 2):
            lanes = slice(h * head_width, (h + 2) * head_width)
            pair = xs_ref[rows, lanes]
            first_skip, second_skip = (floats[skip_at + h + i] for i in range(2))
            total = jnp.where(lane < head_width, first_skip, second_skip) * pair.astype(F32)
            for i in range(2):
                log_decay = cum[:, h + i : h + i + 1] - cum_t[h + i : h + i + 1, :]
                decay = jnp.exp(jnp.where(seen, log_decay, NEGATIVE))
                mix = (decay * scores * step_t[h + i : h + i + 1, :]).astype(MM)
                own = jnp.where((lane < head_width) == (i == 0), pair, jnp.zeros_like(pair))
                total = total + jnp.dot(mix, own, preferred_element_type=F32)
            y_ref[rows, lanes] = total
            keep_ref[rows, lanes] = jnp.where(
                lane < head_width, keep[:, h : h + 1], keep[:, h + 1 : h + 2]
            )


def gate_kernel(sizes, ints, tok_ref, *refs):
    inner, where, depth = sizes
    pieces = refs[: len(where)]
    low, high, weights, sems = refs[len(where) :]
    copies = []
    for i, (piece, (k, first)) in enumerate(zip(pieces, where)):
        rows = rows_at((ints[1] ^ k) * depth + first, piece.shape[0])
        copies.append(pltpu.make_async_copy(piece, weights.at[rows, :], sems.at[i]))
    run_all(copies)
    count = low.shape[0] // GROUP
    for side, out in enumerate((low, high)):

        @pl.loop(0, count)
        def _(g):
            row = (side * count + g) * GROUP + HALO
            value = jnp.dot(
                tok_ref[rows_at(row, GROUP), :], weights[...], preferred_element_type=F32
            )
            out[rows_at(g * GROUP, GROUP), :] = silu(value.astype(MM).astype(F32))


def gating(sizes, ints, low_states, vecs, side, y_ref, keep_ref, gate_ref, bc_ref, out):
    inner, heads, groups = sizes
    half = groups // 2
    state = bc_ref.shape[1] // 2
    lane = lax.broadcasted_iota(jnp.int32, (GROUP, LANES), 1)
    for g in range(half):
        rows = slice(g * GROUP, (g + 1) * GROUP)
        carried = lax.dot_general(
            bc_ref[rows, state:],
            low_states[side * half + g],
            (((1,), (1,)), ((), ())),
            preferred_element_type=F32,
        )
        squares = jnp.zeros((GROUP, LANES), F32)
        for at in range(0, inner, LANES):
            lanes = slice(at, at + LANES)
            y = y_ref[rows, lanes] + carried[:, lanes] * keep_ref[rows, lanes]
            gated = y * gate_ref[rows, lanes]
            squares = squares + gated * gated
            here = pl.ds(pl.multiple_of(ints[2] * inner + at, LANES), LANES)
            out[rows, lanes] = (gated * vecs[5:6, here]).astype(MM)
        total = jnp.broadcast_to(jnp.sum(squares, axis=1, keepdims=True), (GROUP, LANES))
        out[rows, inner:] = spread_terms(total).astype(MM)


def spread_terms(total):
    lane = lax.broadcasted_iota(jnp.int32, total.shape, 1)
    high, mid, low = split_terms(total)
    return jnp.where(lane == 0, high, jnp.where(lane == 1, mid, jnp.where(lane == 2, low, 0.0)))


def added_terms(ref, at):
    value = ref[:, at:].astype(F32)
    return jnp.broadcast_to(jnp.sum(value, axis=1, keepdims=True), value.shape)


def back_kernel(sizes, ints_ref, vecs, *refs):
    inner, heads, prompts, groups, n_pieces, per = sizes
    pieces = refs[:n_pieces]
    sides = (refs[n_pieces : n_pieces + 4], refs[n_pieces + 4 : n_pieces + 8])
    theirs, low_states, asked, own_asked, parts, states, sems = refs[n_pieces + 8 :]
    ints = Ints(ints_ref, prompts)
    p, c = ints.p, ints.c
    head_width = inner // heads
    half = groups // 2
    copies = []
    for i, piece in enumerate(pieces):
        k, side = i // 2, i % 2
        at = (p ^ k) * groups + side * half
        copies.append(pltpu.make_async_copy(piece, parts.at[pl.ds(at, half)], sems.at[i]))
    run_all(copies)
    blocks = parts.shape[0]
    states[0] = jnp.zeros(states.shape[1:], F32)

    @pl.loop(0, blocks)
    def _(b):
        terms = parts[b, inner : inner + TERMS, :].astype(F32)
        gates = terms[0:8] + terms[8:16] + terms[16:24]
        for h in range(heads):
            rows = slice(h * head_width, (h + 1) * head_width)
            states[b + 1, rows, :] = gates[h : h + 1, :] * states[b, rows, :] + parts[
                b, rows, :
            ].astype(F32)

    for g in range(groups):
        low_states[g] = states[p * groups + g].astype(MM)
    for side in range(2):

        @pl.when(c != side)
        def _():
            gating((inner, heads, groups), ints_ref, low_states, vecs, side, *sides[side], theirs)

    for i in range(per):
        own_asked[i] = states[ints.wanted((p * 2 + c) * per + i) + 1]
        asked[i] = states[ints.wanted((p * 2 + 1 - c) * per + i) + 1].astype(MM)


def back_own_kernel(sizes, ints_ref, vecs, low_states, *refs):
    sides = (refs[:4], refs[4:8])
    mine = refs[8]
    for side in range(2):

        @pl.when(ints_ref[2] == side)
        def _():
            gating(sizes, ints_ref, low_states, vecs, side, *sides[side], mine)


def block_places(t, tp_count):
    if tp_count == 4:
        return [jnp.where(t < 2, 3, 0), jnp.where(t < 2, 2, 1), t ^ 1, t]
    return [lax.rem(t + j, tp_count) for j in range(1, tp_count)] + [t]


def out_kernel(sizes, ints, mine, theirs, *refs):
    inner, tp_count, chosen, where = sizes
    t, p, c = ints[0], ints[1], ints[2]
    if where:
        pieces = refs[: len(where)]
        outs = refs[len(where) : len(where) + len(chosen)]
        weights, sems = refs[len(where) + len(chosen) :]
        copies = []
        for i, (piece, (k, other, first)) in enumerate(zip(pieces, where)):
            rows, columns = piece.shape
            core = 1 - c if other else c
            at = pl.multiple_of(((p ^ k) * 2 + core) * columns, LANES)
            copies.append(
                pltpu.make_async_copy(
                    piece, weights.at[pl.ds(first, rows), pl.ds(at, columns)], sems.at[i]
                )
            )
        run_all(copies)
    else:
        weights, outs = refs[0], refs[1:]
    width = weights.shape[1]
    piece_rows = mine.shape[0] // tp_count
    own_rows = rows_at(c * inner, inner)
    other_rows = rows_at((1 - c) * inner, inner)
    for i, out in zip(chosen, outs):
        rows = rows_at(block_places(t, tp_count)[i] * piece_rows, piece_rows)
        sums = jnp.sum(
            mine[rows, inner:].astype(F32) + theirs[rows, inner:].astype(F32), axis=1, keepdims=True
        )
        out[:, width:] = spread_terms(jnp.broadcast_to(sums, (piece_rows, LANES))).astype(out.dtype)
        for at in range(0, width, 512):
            lanes = slice(at, at + 512)
            value = jnp.dot(mine[rows, :inner], weights[own_rows, lanes], preferred_element_type=F32)
            value = value + jnp.dot(
                theirs[rows, :inner], weights[other_rows, lanes], preferred_element_type=F32
            )
            out[:, lanes] = value.astype(out.dtype)


def add_kernel(got, own, out):
    width = out.shape[1] - LANES
    for at in range(0, width, 512):
        lanes = slice(at, at + 512)
        out[:, lanes] = (got[:, lanes].astype(F32) + own[:, lanes].astype(F32)).astype(MM)
    out[:, width:] = spread_terms(added_terms(got, width) + added_terms(own, width)).astype(MM)


def final_kernel(channels, own, *refs):
    received, out = refs[:-1], refs[-1]
    width = out.shape[1]
    squares = added_terms(own, width)
    for got in received:
        squares = squares + added_terms(got, width)
    factor = lax.rsqrt(squares[:, :1] / channels + epsilon)
    for at in range(0, width, 512):
        lanes = slice(at, at + 512)
        total = own[:, lanes]
        for got in received:
            total = total + got[:, lanes].astype(F32)
        out[:, lanes] = (total * factor).astype(out.dtype)


def sum_over_tp(blocks, own):
    tp_count = lax.axis_size("tp")
    if tp_count != 4:
        return [shift(x, j + 1) for j, x in enumerate(blocks)]

    def send(x, pairs):
        return lax.ppermute(x, "tp", pairs)

    def add(got, x, name):
        return call(add_kernel, [sds(x.shape, MM)], [VMEM] * 2, moved=1_700_000, name=name)(got, x)[0]

    far, mid, near = blocks
    far_got = send(far, [(0, 1), (3, 2)])
    mid_got = send(mid, [(0, 1), (3, 2)])
    near_got = send(near, [(0, 1), (1, 0), (2, 3), (3, 2)])
    far_sum = send(add(far_got, far, "add_far"), [(1, 3), (2, 0)])
    mid_sum = send(add(mid_got, mid, "add_mid"), [(1, 2), (2, 1)])
    return [near_got, far_sum, mid_sum]


def on_device(
    tokens,
    w_zx,
    w_dt,
    w_bc,
    conv_x_weight,
    conv_x_bias,
    conv_bc_weight,
    conv_bc_bias,
    dt_bias,
    a_log,
    skip,
    norm_weight,
    w_out,
    lengths,
    request_group,
):
    tp_count, seq_count = lax.axis_size("tp"), lax.axis_size("seq")
    t, s = lax.axis_index("tp"), lax.axis_index("seq")
    chips = seq_count // 2
    p, c = s // 2, s % 2
    tok_dev, width = tokens.shape
    rows = w_zx.shape[0]
    inner_all = w_zx.shape[1] // 2
    pair = conv_x_weight.shape[1]
    inner = pair // 2
    heads = dt_bias.shape[0] // 2
    head_width = inner // heads
    bc_width = w_bc.shape[1]
    state = bc_width // 2
    tok = 2 * tok_dev
    groups = tok // GROUP
    half = groups // 2
    conv = inner + bc_width
    prompts = lengths.shape[0]
    x_width = 2 * inner + bc_width + LANES
    depth = tp_count * rows

    ints = jnp.concatenate([jnp.stack([t, p, c]).astype(jnp.int32), lengths, request_group])
    floats = jnp.concatenate([dt_bias, a_log, skip])
    vecs = jnp.concatenate(
        [
            conv_x_weight,
            conv_x_bias[None, :],
            norm_weight[None, :],
            jnp.zeros((2, pair), F32),
            jnp.pad(conv_bc_weight, ((0, 0), (0, pair - bc_width))),
            jnp.pad(conv_bc_bias[None, :], ((0, 3), (0, pair - bc_width))),
        ],
        axis=0,
    )

    def packed(kernel, operands, specs, wide, name):
        return pl.pallas_call(
            functools.partial(kernel, tp_count),
            grid=(1,),
            out_shape=[sds((rows, wide), MM)] * tp_count,
            in_specs=specs,
            out_specs=[pl.BlockSpec((rows, wide), lambda i: (0, 0))] * tp_count,
            compiler_params=pltpu.CompilerParams(vmem_limit_bytes=VMEM_BYTES),
            name=name,
        )(*operands)

    def whole(x):
        return pl.BlockSpec(x.shape, lambda i: (0, 0))

    def sent_over_tp(pieces):
        return [pieces[0]] + [shift(x, j) for j, x in enumerate(pieces) if j]

    def assembled(kernel, outs, pieces, name):
        return call(
            functools.partial(kernel, tp_count), outs, [SMEM] + [VMEM] * tp_count, name=name
        )(ints, *pieces)

    def together(*lists):
        joined = lax.optimization_barrier(tuple(tuple(one) for one in lists))
        return [list(one) for one in joined]

    x_sent = packed(
        pack_x_kernel,
        (ints, w_zx, w_bc, w_dt),
        [SMEM, pl.BlockSpec((rows, inner_all), lambda i: (0, 1)), whole(w_bc), whole(w_dt)],
        x_width,
        "pack_x",
    )
    x_sent, (w_out,) = together(x_sent, [w_out])
    (x_block,) = assembled(
        assemble_x_kernel, [sds((depth, x_width), MM)], sent_over_tp(x_sent), "assemble_x"
    )

    other = flip(tokens, 1)
    first_tok = jnp.where(c == 0, tokens, other)
    second_tok = jnp.where(c == 0, other, tokens)
    before = lax.ppermute(
        second_tok[tok_dev - HALO :], "seq", [(i, i + 2) for i in range(seq_count - 2)]
    )
    all_tok = jnp.concatenate([before, first_tok, second_tok], axis=0)

    out_blocks = plane_far(plane_near(w_out.astype(MM)))
    out_own = [piece for k in out_blocks for piece in out_blocks[k]]
    out_where = [
        (k, 0, i * (w_out.shape[0] // 2)) for k in out_blocks for i in range(len(out_blocks[k]))
    ]

    (x_block, all_tok, ints, floats, vecs), out_own = together(
        [x_block, all_tok, ints, floats, vecs], out_own
    )
    near = plane_near(x_block)
    z_sent = packed(
        pack_z_kernel,
        (ints, w_zx),
        [SMEM, pl.BlockSpec((rows, inner_all), lambda i: (0, 0))],
        2 * inner,
        "pack_z",
    )
    z_got = sent_over_tp(z_sent)
    blocks, z_got = together([near[k][0] for k in near], z_got)
    far = plane_far({k: (block,) for k, block in zip(near, blocks)})
    where = [(k, 0, i * depth // 2) for k in far for i in range(len(far[k]))]
    x_pieces = [piece for k in far for piece in far[k]]
    x_pieces += [flip(piece, 1) for piece in x_pieces]
    where = tuple(where + [(k, 1, first) for k, _, first in where])
    z_mine, z_theirs = assembled(
        assemble_z_kernel, [sds((depth, inner), MM)] * 2, z_got, "assemble_z"
    )
    (z_block,) = call(
        merge_kernel, [sds((2 * depth, inner), MM)], [SMEM, VMEM, VMEM], name="merge_z"
    )(ints, z_mine, flip(z_theirs, 1))
    x_pieces, (z_block,) = together(x_pieces, [z_block])

    def front(side, where, operands):
        outs = [
            sds((tok_dev, inner), MM),
            sds((tok_dev, bc_width), MM),
            sds((tok_dev, LANES), F32),
            sds((tok_dev, LANES), F32),
            sds((half, inner + TERMS, state), MM),
        ]
        scratch = [pltpu.VMEM((2, HALO + GROUP, conv + LANES), F32)]
        if where:
            outs.append(sds((width, conv + LANES), MM))
            scratch.append(pltpu.SemaphoreType.DMA((2 * len(where),)))
        return call(
            functools.partial(
                front_kernel, (inner, bc_width, heads, prompts, where, depth, groups, side)
            ),
            outs,
            [SMEM, SMEM, VMEM, VMEM] + ([ANY] * len(where) if where else [VMEM]),
            scratch,
            flops=2 * (tok_dev + HALO) * width * (conv + LANES),
            moved=8_000_000,
            name="front_%d" % side,
        )(ints, floats, vecs, all_tok, *operands)

    z_near = plane_near(z_block)
    *first, weights = front(0, where, x_pieces)
    (*first, weights), z_blocks = together([*first, weights], [z_near[k][0] for k in z_near])

    z_far = plane_far({k: (block,) for k, block in zip(z_near, z_blocks)})
    z_where = tuple((k, i * depth) for k in z_far for i in range(len(z_far[k])))
    z_pieces = [piece for k in z_far for piece in z_far[k]]
    low_near = plane_near(first[4])
    second = front(1, (), [weights])
    second, lows, z_pieces = together(second, [low_near[k][0] for k in low_near], z_pieces)

    parts = {k: (block, None) for k, block in zip(low_near, lows)}
    high_near = plane_near(second[4])
    parts = {k: (parts[k][0], high_near[k][0]) for k in parts}
    for k in range(1, chips):
        if k not in parts:
            low, high = k & -k, 1 << (k.bit_length() - 1)
            parts[k] = (flip(parts[k ^ low][0], 2 * low), flip(parts[k ^ high][1], 2 * high))
    parts = [piece for k in range(chips) for piece in parts[k]]

    def mid(side, xs, bc, cum, step, message):
        return call(
            functools.partial(mid_kernel, (inner, heads, prompts, groups, side)),
            [sds((tok_dev, inner), F32)] * 2,
            [SMEM, SMEM] + [VMEM] * 4,
            flops=2 * tok_dev * GROUP * inner * 8,
            moved=6_000_000,
            name="mid_%d" % side,
        )(ints, floats, xs, bc, cum, step)

    y = [mid(0, *first), mid(1, *second)]
    gate = call(
        functools.partial(gate_kernel, (inner, z_where, 2 * depth)),
        [sds((tok_dev, inner), F32)] * 2,
        [SMEM, VMEM] + [ANY] * len(z_where),
        [pltpu.VMEM((width, inner), MM), pltpu.SemaphoreType.DMA((len(z_where),))],
        flops=2 * tok * width * inner,
        moved=8_000_000,
        name="gate",
    )(ints, all_tok, *z_pieces)
    out_other = [flip(piece, 1) for piece in out_own]
    out_where = tuple(out_where + [(k, 1, first_row) for k, _, first_row in out_where])
    sides = [*y[0], gate[0], first[1], *y[1], gate[1], second[1]]
    parts, sides, out_other = together(parts, sides, out_other)
    out_pieces = out_own + out_other

    per = request_group.shape[0] // seq_count
    sent = sds((tok_dev, inner + LANES), MM)
    theirs, low_states, asked, own_asked = call(
        functools.partial(back_kernel, (inner, heads, prompts, groups, len(parts), per)),
        [
            sent,
            sds((groups, inner, state), MM),
            sds((per, inner, state), MM),
            sds((per, inner, state), F32),
        ],
        [SMEM, VMEM] + [ANY] * len(parts) + [VMEM] * 8,
        [
            pltpu.VMEM((chips * groups, inner + TERMS, state), MM),
            pltpu.VMEM((chips * groups + 1, inner, state), F32),
            pltpu.SemaphoreType.DMA((len(parts),)),
        ],
        flops=2 * tok * state * inner,
        moved=8_000_000,
        name="back",
    )(ints, vecs, *parts, *sides)
    theirs = flip(theirs, 1)
    (mine,) = call(
        functools.partial(back_own_kernel, (inner, heads, groups)),
        [sent],
        [SMEM] + [VMEM] * 10,
        flops=2 * tok_dev * state * inner,
        moved=4_000_000,
        name="back_own",
    )(ints, vecs, low_states, *sides)

    out_width = seq_count * w_out.shape[1]
    piece = tok_dev // tp_count
    block = sds((piece, out_width + LANES), MM)
    ahead = tp_count - 2

    def project_out(chosen, outs, where, operands):
        scratch, extra = [], []
        if where:
            extra = [sds((2 * inner, out_width), MM)]
            scratch = [pltpu.SemaphoreType.DMA((len(where),))]
        return call(
            functools.partial(out_kernel, (inner, tp_count, chosen, where)),
            outs + extra,
            [SMEM, VMEM, VMEM] + ([ANY] * len(where) if where else [VMEM]),
            scratch,
            flops=4 * len(outs) * piece * inner * out_width,
            moved=8_000_000,
            name="out_%d" % len(chosen),
        )(ints, mine, theirs, *operands)

    *sent_first, out_weights = project_out(
        tuple(range(ahead)), [block] * ahead, out_where, out_pieces
    )
    near_block, own = project_out(
        (ahead, ahead + 1), [block, sds(block.shape, F32)], (), [out_weights]
    )
    received = sum_over_tp([*sent_first, near_block], own)
    (mixed,) = call(
        functools.partial(final_kernel, float(inner_all)),
        [sds((piece, out_width), MM)],
        [VMEM] * (1 + len(received)),
        name="final",
    )(own, *received)

    other_asked = flip(asked, 1).astype(F32)
    states = jnp.where(
        c == 0,
        jnp.concatenate([own_asked, other_asked], axis=1),
        jnp.concatenate([other_asked, own_asked], axis=1),
    )
    return (mixed, states.reshape(per, 2 * heads, head_width, state))


def solution(mesh):
    return jax.shard_map(
        on_device,
        mesh=mesh,
        in_specs=(
            P("seq", None),
            P(("seq", "tp"), None),
            P(("seq", "tp"), None),
            P(("seq", "tp"), None),
            P(None, "tp"),
            P("tp"),
            P(),
            P(),
            P("tp"),
            P("tp"),
            P("tp"),
            P("tp"),
            P("tp", "seq"),
            P(),
            P(),
        ),
        out_specs=(P(("seq", "tp"), None), P("seq", "tp", None, None)),
        check_vma=False,
    )
```

```python
import functools

import jax
import jax.numpy as jnp
from jax import lax
from jax.experimental import pallas as pl
from jax.experimental.pallas import tpu as pltpu
from jax.sharding import PartitionSpec as P

GROUP = 256
HALO = 16
LANES = 128
TERMS = 32
MM = jnp.bfloat16
F32 = jnp.float32
NEGATIVE = -1e30
sds = jax.ShapeDtypeStruct
VMEM_BYTES = 20 * 1024 * 1024

epsilon = 1e-05

ANY = pl.BlockSpec(memory_space=pl.ANY)
SMEM = pl.BlockSpec(memory_space=pltpu.SMEM)
VMEM = pl.BlockSpec(memory_space=pltpu.VMEM)


def flip(x, bits):
    count = lax.axis_size("seq")
    return lax.ppermute(x, "seq", [(i, i ^ bits) for i in range(count)])


def shift(x, by):
    count = lax.axis_size("tp")
    return lax.ppermute(x, "tp", [(i, (i + by) % count) for i in range(count)])


def plane_near(block):
    chips = lax.axis_size("seq") // 2
    return {k: (block if k == 0 else flip(block, 2 * k),) for k in range(chips) if k & (k - 1) == 0}


def plane_far(blocks):
    chips = lax.axis_size("seq") // 2
    blocks = dict(blocks)

    def half(k, side):
        if len(blocks[k]) == 2:
            return blocks[k][side]
        size = blocks[k][0].shape[0] // 2
        return blocks[k][0][side * size : (side + 1) * size]

    for k in range(1, chips):
        if k not in blocks:
            low = k & -k
            high = 1 << (k.bit_length() - 1)
            first = flip(half(k ^ low, 0), 2 * low)
            second = flip(half(k ^ high, 1), 2 * high)
            blocks[k] = (first, second)
    return blocks


def call(kernel, outs, in_specs, scratch=(), flops=0, moved=0, out_specs=None, name=None):
    return pl.pallas_call(
        kernel,
        out_shape=outs,
        in_specs=in_specs,
        out_specs=[VMEM] * len(outs) if out_specs is None else out_specs,
        scratch_shapes=list(scratch),
        compiler_params=pltpu.CompilerParams(vmem_limit_bytes=VMEM_BYTES),
        cost_estimate=pl.CostEstimate(flops=flops, bytes_accessed=moved, transcendentals=0),
        name=name,
    )


def split_terms(x):
    high = x.astype(MM).astype(F32)
    rest = x - high
    mid = rest.astype(MM).astype(F32)
    return high, mid, (rest - mid).astype(MM).astype(F32)


def silu(x):
    half = 0.5 * x
    return half + half * jnp.tanh(half)


def run_all(copies):
    for copy in copies:
        copy.start()
    for copy in copies:
        copy.wait()


def starts_of(position, ints):
    start, end = jnp.zeros_like(position), 0
    for i in range(ints.prompts):
        end = end + ints.ref[3 + i]
        start = jnp.where(position >= end, end, start)
    return start


class Ints:
    def __init__(self, ref, prompts):
        self.ref, self.prompts = ref, prompts
        self.t, self.p, self.c = ref[0], ref[1], ref[2]

    def wanted(self, i):
        return self.ref[3 + self.prompts + i]


def rows_at(first, size):
    return pl.ds(pl.multiple_of(first, 16), size)


def pack_x_kernel(tp_count, ints, w_ref, bc_ref, dt_ref, *outs):
    t = ints[0]
    pair = w_ref.shape[1] // tp_count
    inner = pair // 2
    bc_width = bc_ref.shape[1]
    heads = dt_ref.shape[1] // tp_count
    low_bc = bc_ref[...].astype(MM)
    for j, out in enumerate(outs):
        owner = lax.rem(t + j, tp_count)
        at = pl.multiple_of(owner * pair, LANES)
        out[:, :inner] = w_ref[:, pl.ds(at, inner)].astype(MM)
        out[:, inner : inner + bc_width] = low_bc
        steps = jnp.zeros((dt_ref.shape[0], heads), F32)
        for u in range(tp_count):
            steps = jnp.where(owner == u, dt_ref[:, u * heads : (u + 1) * heads], steps)
        steps = jnp.concatenate(
            [steps, jnp.zeros((dt_ref.shape[0], LANES - heads), F32)], axis=1
        )
        out[:, inner + bc_width : inner + bc_width + LANES] = steps.astype(MM)
        at = pl.multiple_of(owner * pair + inner, LANES)
        out[:, inner + bc_width + LANES :] = w_ref[:, pl.ds(at, inner)].astype(MM)


def pack_z_kernel(tp_count, ints, w_ref, *outs):
    pair = w_ref.shape[1] // tp_count
    for j, out in enumerate(outs):
        at = pl.multiple_of(lax.rem(ints[0] + j, tp_count) * pair, LANES)
        out[...] = w_ref[:, pl.ds(at, pair)].astype(MM)


def assemble_x_kernel(tp_count, ints, *refs):
    pieces, out = refs[:tp_count], refs[tp_count]
    rows = pieces[0].shape[0]
    for j, piece in enumerate(pieces):
        source = lax.rem(ints[0] + tp_count - j, tp_count)
        out[rows_at(source * rows, rows), :] = piece[...]


def assemble_z_kernel(tp_count, ints, *refs):
    pieces, (mine, theirs) = refs[:tp_count], refs[tp_count:]
    rows, inner = pieces[0].shape[0], mine.shape[1]
    c = ints[2]
    for j, piece in enumerate(pieces):
        at = rows_at(lax.rem(ints[0] + tp_count - j, tp_count) * rows, rows)
        mine[at, :] = piece[:, pl.ds(pl.multiple_of(c * inner, LANES), inner)]
        theirs[at, :] = piece[:, pl.ds(pl.multiple_of((1 - c) * inner, LANES), inner)]


def merge_kernel(ints, mine, theirs, out):
    rows = mine.shape[0]
    out[rows_at(ints[2] * rows, rows), :] = mine[...]
    out[rows_at((1 - ints[2]) * rows, rows), :] = theirs[...]


def lane_row(ref, first, count):
    lane = lax.broadcasted_iota(jnp.int32, (1, LANES), 1)
    row = jnp.zeros((1, LANES), F32)
    for i in range(count):
        row = jnp.where(lane == i, ref[first + i], row)
    return row


def front_kernel(sizes, ints_ref, floats, vecs, tok_ref, *refs):
    inner, bc_width, heads, prompts, where, depth, groups, side = sizes
    ints = Ints(ints_ref, prompts)
    c = ints.c
    conv = inner + bc_width
    state = bc_width // 2
    head_width = inner // heads
    half = groups // 2
    if where:
        pieces = refs[: len(where)]
        xs_ref, bc_ref, cum_ref, step_ref, message, weights, raw, sems = refs[len(where) :]
        start_x = pl.multiple_of(c * (conv + LANES), LANES)
        copies = []
        for piece, (k, other, first) in zip(pieces, where):
            core = 1 - c if other else c
            rows = rows_at(((ints.p ^ k) * 2 + core) * depth + first, piece.shape[0])
            for source, goal, size in ((start_x, 0, inner), (inner, inner, bc_width + LANES)):
                copies.append(
                    pltpu.make_async_copy(
                        piece.at[:, pl.ds(source, size)],
                        weights.at[rows, pl.ds(goal, size)],
                        sems.at[len(copies)],
                    )
                )
        run_all(copies)
    else:
        weights, xs_ref, bc_ref, cum_ref, step_ref, message, raw = refs
    taps = 4
    lower = (
        lax.broadcasted_iota(jnp.int32, (GROUP, GROUP), 0)
        >= lax.broadcasted_iota(jnp.int32, (GROUP, GROUP), 1)
    ).astype(F32)
    within = lax.broadcasted_iota(jnp.int32, (GROUP, LANES), 0)
    base = ints.p * (groups * GROUP) + side * half * GROUP
    all_heads = 2 * heads
    bias = lane_row(floats, c * heads, heads)
    rate = -jnp.exp(lane_row(floats, all_heads + c * heads, heads))

    def project(g):
        at = (side * half + g) * GROUP
        value = jnp.dot(
            tok_ref[at : at + GROUP + HALO, :], weights[...], preferred_element_type=F32
        )
        raw[g % 2, :, :conv] = value[:, :conv].astype(MM).astype(F32)
        raw[g % 2, :, conv:] = value[:, conv:]

    def one(g):
        rows = slice(g * GROUP, (g + 1) * GROUP)
        slot = g % 2
        first = base + g * GROUP
        position = first + within
        behind = position - starts_of(position, ints)
        keeps = [(behind >= lag).astype(F32) for lag in range(1, taps)]
        dt = raw[slot, HALO : HALO + GROUP, conv:]
        dt = jnp.where(c == 0, dt, pltpu.roll(dt, LANES - heads, 1)) + bias
        step = jnp.maximum(dt, 0.0) + jnp.log1p(jnp.exp(-jnp.abs(dt)))
        cum = jnp.dot(
            lower, step * rate, precision=lax.Precision.HIGHEST, preferred_element_type=F32
        )
        cum_ref[rows, :] = cum
        step_ref[rows, :] = step
        last = cum[GROUP - 1 : GROUP, :]
        start_last = starts_of(first + (GROUP - 1), ints)
        tail = jnp.where(position >= start_last, jnp.exp(last - cum), 0.0) * step
        for block in range(0, conv, LANES):
            lanes = slice(block, block + LANES)
            if block < inner:
                here = pl.ds(pl.multiple_of(c * inner + block, LANES), LANES)
                weight, offset = vecs[0:taps, here], vecs[taps : taps + 1, here]
            else:
                here = slice(block - inner, block - inner + LANES)
                weight, offset = vecs[8 : 8 + taps, here], vecs[8 + taps : 9 + taps, here]
            total = offset + raw[slot, HALO : HALO + GROUP, lanes] * weight[taps - 1 : taps]
            for lag in range(1, taps):
                term = raw[slot, HALO - lag : HALO - lag + GROUP, lanes] * keeps[lag - 1]
                total = total + term * weight[taps - 1 - lag : taps - lag]
            value = silu(total).astype(MM)
            if block < inner:
                xs_ref[rows, lanes] = value
            else:
                bc_ref[rows, here] = value
        b_wide = bc_ref[rows, :state].astype(F32)
        for h in range(0, heads, 2):
            weighted = jnp.concatenate(
                [(b_wide * tail[:, h + i : h + i + 1]).astype(MM) for i in range(2)], axis=1
            )
            both = lax.dot_general(
                xs_ref[rows, h * head_width : (h + 2) * head_width],
                weighted,
                (((0,), (0,)), ((), ())),
                preferred_element_type=F32,
            )
            at = h * head_width
            message[g, at : at + head_width, :] = both[:head_width, :state].astype(MM)
            at = at + head_width
            message[g, at : at + head_width, :] = both[head_width:, state:].astype(MM)
        spread = jnp.broadcast_to(jnp.exp(last), (8, LANES))
        diagonal = lax.broadcasted_iota(jnp.int32, (8, LANES), 0) == lax.broadcasted_iota(
            jnp.int32, (8, LANES), 1
        )
        gates = jnp.sum(jnp.where(diagonal, spread, 0.0), axis=1, keepdims=True)
        gates = jnp.where(start_last < first, jnp.broadcast_to(gates, (8, LANES)), 0.0)
        terms = jnp.concatenate(list(split_terms(gates)) + [jnp.zeros_like(gates)], axis=0)
        message[g, inner : inner + TERMS, :] = terms.astype(MM)

    project(0)
    for g in range(half):
        if g + 1 < half:
            project(g + 1)
        one(g)


def mid_kernel(sizes, ints_ref, floats, xs_ref, bc_ref, cum_ref, step_ref, y_ref, keep_ref):
    inner, heads, prompts, groups, side = sizes
    ints = Ints(ints_ref, prompts)
    state = bc_ref.shape[1] // 2
    head_width = inner // heads
    half = groups // 2
    base = ints.p * (groups * GROUP) + side * half * GROUP
    within_i = lax.broadcasted_iota(jnp.int32, (GROUP, GROUP), 0)
    within_j = lax.broadcasted_iota(jnp.int32, (GROUP, GROUP), 1)
    lane = lax.broadcasted_iota(jnp.int32, (GROUP, LANES), 1)
    skip_at = 4 * heads + ints.c * heads

    @pl.loop(0, half)
    def _(g):
        rows = rows_at(g * GROUP, GROUP)
        first = base + g * GROUP
        start = starts_of(first + within_i, ints)
        seen = (within_j <= within_i) & (first + within_j >= start)
        scores = lax.dot_general(
            bc_ref[rows, state:],
            bc_ref[rows, :state],
            (((1,), (1,)), ((), ())),
            preferred_element_type=F32,
        )
        cum = cum_ref[rows, :]
        cum_t = cum.T
        step_t = step_ref[rows, :].T
        keep = jnp.where(start[:, :LANES] < first, jnp.exp(cum), 0.0)
        for h in range(0, heads, 2):
            lanes = slice(h * head_width, (h + 2) * head_width)
            pair = xs_ref[rows, lanes]
            first_skip, second_skip = (floats[skip_at + h + i] for i in range(2))
            total = jnp.where(lane < head_width, first_skip, second_skip) * pair.astype(F32)
            for i in range(2):
                log_decay = cum[:, h + i : h + i + 1] - cum_t[h + i : h + i + 1, :]
                decay = jnp.exp(jnp.where(seen, log_decay, NEGATIVE))
                mix = (decay * scores * step_t[h + i : h + i + 1, :]).astype(MM)
                own = jnp.where((lane < head_width) == (i == 0), pair, jnp.zeros_like(pair))
                total = total + jnp.dot(mix, own, preferred_element_type=F32)
            y_ref[rows, lanes] = total
            keep_ref[rows, lanes] = jnp.where(
                lane < head_width, keep[:, h : h + 1], keep[:, h + 1 : h + 2]
            )


def gate_kernel(sizes, ints, tok_ref, *refs):
    inner, where, depth = sizes
    pieces = refs[: len(where)]
    low, high, weights, sems = refs[len(where) :]
    copies = []
    for i, (piece, (k, first)) in enumerate(zip(pieces, where)):
        rows = rows_at((ints[1] ^ k) * depth + first, piece.shape[0])
        copies.append(pltpu.make_async_copy(piece, weights.at[rows, :], sems.at[i]))
    run_all(copies)
    count = low.shape[0] // GROUP
    for side, out in enumerate((low, high)):

        @pl.loop(0, count)
        def _(g):
            row = (side * count + g) * GROUP + HALO
            value = jnp.dot(
                tok_ref[rows_at(row, GROUP), :], weights[...], preferred_element_type=F32
            )
            out[rows_at(g * GROUP, GROUP), :] = silu(value.astype(MM).astype(F32))


def gating(sizes, ints, low_states, vecs, side, y_ref, keep_ref, gate_ref, bc_ref, out):
    inner, heads, groups = sizes
    half = groups // 2
    state = bc_ref.shape[1] // 2
    lane = lax.broadcasted_iota(jnp.int32, (GROUP, LANES), 1)
    for g in range(half):
        rows = slice(g * GROUP, (g + 1) * GROUP)
        carried = lax.dot_general(
            bc_ref[rows, state:],
            low_states[side * half + g],
            (((1,), (1,)), ((), ())),
            preferred_element_type=F32,
        )
        squares = jnp.zeros((GROUP, LANES), F32)
        for at in range(0, inner, LANES):
            lanes = slice(at, at + LANES)
            y = y_ref[rows, lanes] + carried[:, lanes] * keep_ref[rows, lanes]
            gated = y * gate_ref[rows, lanes]
            squares = squares + gated * gated
            here = pl.ds(pl.multiple_of(ints[2] * inner + at, LANES), LANES)
            out[rows, lanes] = (gated * vecs[5:6, here]).astype(MM)
        total = jnp.broadcast_to(jnp.sum(squares, axis=1, keepdims=True), (GROUP, LANES))
        out[rows, inner:] = spread_terms(total).astype(MM)


def spread_terms(total):
    lane = lax.broadcasted_iota(jnp.int32, total.shape, 1)
    high, mid, low = split_terms(total)
    return jnp.where(lane == 0, high, jnp.where(lane == 1, mid, jnp.where(lane == 2, low, 0.0)))


def added_terms(ref, at):
    value = ref[:, at:].astype(F32)
    return jnp.broadcast_to(jnp.sum(value, axis=1, keepdims=True), value.shape)


def back_kernel(sizes, ints_ref, vecs, *refs):
    inner, heads, prompts, groups, n_pieces, per = sizes
    pieces = refs[:n_pieces]
    sides = (refs[n_pieces : n_pieces + 4], refs[n_pieces + 4 : n_pieces + 8])
    theirs, low_states, asked, own_asked, parts, states, sems = refs[n_pieces + 8 :]
    ints = Ints(ints_ref, prompts)
    p, c = ints.p, ints.c
    head_width = inner // heads
    half = groups // 2
    copies = []
    for i, piece in enumerate(pieces):
        k, side = i // 2, i % 2
        at = (p ^ k) * groups + side * half
        copies.append(pltpu.make_async_copy(piece, parts.at[pl.ds(at, half)], sems.at[i]))
    run_all(copies)
    blocks = parts.shape[0]
    states[0] = jnp.zeros(states.shape[1:], F32)

    @pl.loop(0, blocks)
    def _(b):
        terms = parts[b, inner : inner + TERMS, :].astype(F32)
        gates = terms[0:8] + terms[8:16] + terms[16:24]
        for h in range(heads):
            rows = slice(h * head_width, (h + 1) * head_width)
            states[b + 1, rows, :] = gates[h : h + 1, :] * states[b, rows, :] + parts[
                b, rows, :
            ].astype(F32)

    for g in range(groups):
        low_states[g] = states[p * groups + g].astype(MM)
    for side in range(2):

        @pl.when(c != side)
        def _():
            gating((inner, heads, groups), ints_ref, low_states, vecs, side, *sides[side], theirs)

    for i in range(per):
        own_asked[i] = states[ints.wanted((p * 2 + c) * per + i) + 1]
        asked[i] = states[ints.wanted((p * 2 + 1 - c) * per + i) + 1].astype(MM)


def back_own_kernel(sizes, ints_ref, vecs, low_states, *refs):
    sides = (refs[:4], refs[4:8])
    mine = refs[8]
    for side in range(2):

        @pl.when(ints_ref[2] == side)
        def _():
            gating(sizes, ints_ref, low_states, vecs, side, *sides[side], mine)


def block_places(t, tp_count):
    if tp_count == 4:
        return [jnp.where(t < 2, 3, 0), jnp.where(t < 2, 2, 1), t ^ 1, t]
    return [lax.rem(t + j, tp_count) for j in range(1, tp_count)] + [t]


def out_kernel(sizes, ints, mine, theirs, *refs):
    inner, tp_count, chosen, where = sizes
    t, p, c = ints[0], ints[1], ints[2]
    if where:
        pieces = refs[: len(where)]
        outs = refs[len(where) : len(where) + len(chosen)]
        weights, sems = refs[len(where) + len(chosen) :]
        copies = []
        for i, (piece, (k, other, first)) in enumerate(zip(pieces, where)):
            rows, columns = piece.shape
            core = 1 - c if other else c
            at = pl.multiple_of(((p ^ k) * 2 + core) * columns, LANES)
            copies.append(
                pltpu.make_async_copy(
                    piece, weights.at[pl.ds(first, rows), pl.ds(at, columns)], sems.at[i]
                )
            )
        run_all(copies)
    else:
        weights, outs = refs[0], refs[1:]
    width = weights.shape[1]
    piece_rows = mine.shape[0] // tp_count
    own_rows = rows_at(c * inner, inner)
    other_rows = rows_at((1 - c) * inner, inner)
    for i, out in zip(chosen, outs):
        rows = rows_at(block_places(t, tp_count)[i] * piece_rows, piece_rows)
        sums = jnp.sum(
            mine[rows, inner:].astype(F32) + theirs[rows, inner:].astype(F32), axis=1, keepdims=True
        )
        out[:, width:] = spread_terms(jnp.broadcast_to(sums, (piece_rows, LANES))).astype(out.dtype)
        for at in range(0, width, 512):
            lanes = slice(at, at + 512)
            value = jnp.dot(mine[rows, :inner], weights[own_rows, lanes], preferred_element_type=F32)
            value = value + jnp.dot(
                theirs[rows, :inner], weights[other_rows, lanes], preferred_element_type=F32
            )
            out[:, lanes] = value.astype(out.dtype)


def add_kernel(got, own, out):
    width = out.shape[1] - LANES
    for at in range(0, width, 512):
        lanes = slice(at, at + 512)
        out[:, lanes] = (got[:, lanes].astype(F32) + own[:, lanes].astype(F32)).astype(MM)
    out[:, width:] = spread_terms(added_terms(got, width) + added_terms(own, width)).astype(MM)


def final_kernel(channels, own, *refs):
    received, out = refs[:-1], refs[-1]
    width = out.shape[1]
    squares = added_terms(own, width)
    for got in received:
        squares = squares + added_terms(got, width)
    factor = lax.rsqrt(squares[:, :1] / channels + epsilon)
    for at in range(0, width, 512):
        lanes = slice(at, at + 512)
        total = own[:, lanes]
        for got in received:
            total = total + got[:, lanes].astype(F32)
        out[:, lanes] = (total * factor).astype(out.dtype)


def sum_over_tp(blocks, own):
    tp_count = lax.axis_size("tp")
    if tp_count != 4:
        return own, [shift(x, j + 1) for j, x in enumerate(blocks)]

    def send(x, pairs):
        return lax.ppermute(x, "tp", pairs)

    def add(got, x, name):
        return call(add_kernel, [sds(x.shape, MM)], [VMEM] * 2, moved=1_700_000, name=name)(got, x)[0]

    far, mid, near = blocks
    far_got = send(far, [(0, 1), (3, 2)])
    to_end = send(near, [(1, 0), (2, 3)])
    far_got, mid, near, own = lax.optimization_barrier((far_got, mid, near, own))
    mid_got = send(mid, [(0, 1), (3, 2)])
    far_sum = send(add(far_got, far, "add_far"), [(1, 3), (2, 0)])
    mid_got, near = lax.optimization_barrier((mid_got, near))
    to_inner = send(near, [(0, 1), (3, 2)])
    mid_sum = send(add(mid_got, mid, "add_mid"), [(1, 2), (2, 1)])
    return own, [to_end, to_inner, far_sum, mid_sum]


def on_device(
    tokens,
    w_zx,
    w_dt,
    w_bc,
    conv_x_weight,
    conv_x_bias,
    conv_bc_weight,
    conv_bc_bias,
    dt_bias,
    a_log,
    skip,
    norm_weight,
    w_out,
    lengths,
    request_group,
):
    tp_count, seq_count = lax.axis_size("tp"), lax.axis_size("seq")
    t, s = lax.axis_index("tp"), lax.axis_index("seq")
    chips = seq_count // 2
    p, c = s // 2, s % 2
    tok_dev, width = tokens.shape
    rows = w_zx.shape[0]
    inner_all = w_zx.shape[1] // 2
    pair = conv_x_weight.shape[1]
    inner = pair // 2
    heads = dt_bias.shape[0] // 2
    head_width = inner // heads
    bc_width = w_bc.shape[1]
    state = bc_width // 2
    tok = 2 * tok_dev
    groups = tok // GROUP
    half = groups // 2
    conv = inner + bc_width
    prompts = lengths.shape[0]
    x_width = 2 * inner + bc_width + LANES
    depth = tp_count * rows

    ints = jnp.concatenate([jnp.stack([t, p, c]).astype(jnp.int32), lengths, request_group])
    floats = jnp.concatenate([dt_bias, a_log, skip])
    vecs = jnp.concatenate(
        [
            conv_x_weight,
            conv_x_bias[None, :],
            norm_weight[None, :],
            jnp.zeros((2, pair), F32),
            jnp.pad(conv_bc_weight, ((0, 0), (0, pair - bc_width))),
            jnp.pad(conv_bc_bias[None, :], ((0, 3), (0, pair - bc_width))),
        ],
        axis=0,
    )

    def packed(kernel, operands, specs, wide, name):
        return pl.pallas_call(
            functools.partial(kernel, tp_count),
            grid=(1,),
            out_shape=[sds((rows, wide), MM)] * tp_count,
            in_specs=specs,
            out_specs=[pl.BlockSpec((rows, wide), lambda i: (0, 0))] * tp_count,
            compiler_params=pltpu.CompilerParams(vmem_limit_bytes=VMEM_BYTES),
            name=name,
        )(*operands)

    def whole(x):
        return pl.BlockSpec(x.shape, lambda i: (0, 0))

    def sent_over_tp(pieces):
        return [pieces[0]] + [shift(x, j) for j, x in enumerate(pieces) if j]

    def assembled(kernel, outs, pieces, name):
        return call(
            functools.partial(kernel, tp_count), outs, [SMEM] + [VMEM] * tp_count, name=name
        )(ints, *pieces)

    def together(*lists):
        joined = lax.optimization_barrier(tuple(tuple(one) for one in lists))
        return [list(one) for one in joined]

    x_sent = packed(
        pack_x_kernel,
        (ints, w_zx, w_bc, w_dt),
        [SMEM, pl.BlockSpec((rows, inner_all), lambda i: (0, 1)), whole(w_bc), whole(w_dt)],
        x_width,
        "pack_x",
    )
    x_got = sent_over_tp(x_sent)

    out_near = plane_near(w_out.astype(MM))
    keys = list(out_near)
    x_got[1:2], out_got = together(x_got[1:2], [out_near[k][0] for k in keys])
    out_blocks = plane_far({k: (piece,) for k, piece in zip(keys, out_got)})
    out_own = [piece for k in out_blocks for piece in out_blocks[k]]
    out_where = [
        (k, 0, i * (w_out.shape[0] // 2)) for k in out_blocks for i in range(len(out_blocks[k]))
    ]
    (x_block,) = assembled(assemble_x_kernel, [sds((depth, x_width), MM)], x_got, "assemble_x")

    other = flip(tokens, 1)
    first_tok = jnp.where(c == 0, tokens, other)
    second_tok = jnp.where(c == 0, other, tokens)
    before = lax.ppermute(
        second_tok[tok_dev - HALO :], "seq", [(i, i + 2) for i in range(seq_count - 2)]
    )
    all_tok = jnp.concatenate([before, first_tok, second_tok], axis=0)

    (x_block, all_tok, ints, floats, vecs), out_own = together(
        [x_block, all_tok, ints, floats, vecs], out_own
    )
    near = plane_near(x_block)
    z_sent = packed(
        pack_z_kernel,
        (ints, w_zx),
        [SMEM, pl.BlockSpec((rows, inner_all), lambda i: (0, 0))],
        2 * inner,
        "pack_z",
    )
    z_got = sent_over_tp(z_sent)
    own_other = flip(x_block, 1)
    blocks, z_got = together([near[k][0] for k in near if k], z_got)
    far = plane_far({k: (block,) for k, block in zip(near, [x_block] + blocks)})
    where = [(k, 0, i * depth // 2) for k in far for i in range(len(far[k]))]
    x_pieces = [piece for k in far for piece in far[k]]
    x_pieces += [own_other] + [flip(piece, 1) for piece in x_pieces[1:]]
    where = tuple(where + [(k, 1, first) for k, _, first in where])
    z_mine, z_theirs = assembled(
        assemble_z_kernel, [sds((depth, inner), MM)] * 2, z_got, "assemble_z"
    )
    (z_block,) = call(
        merge_kernel, [sds((2 * depth, inner), MM)], [SMEM, VMEM, VMEM], name="merge_z"
    )(ints, z_mine, flip(z_theirs, 1))
    x_pieces, (z_block,) = together(x_pieces, [z_block])

    def front(side, where, operands):
        outs = [
            sds((tok_dev, inner), MM),
            sds((tok_dev, bc_width), MM),
            sds((tok_dev, LANES), F32),
            sds((tok_dev, LANES), F32),
            sds((half, inner + TERMS, state), MM),
        ]
        scratch = [pltpu.VMEM((2, HALO + GROUP, conv + LANES), F32)]
        if where:
            outs.append(sds((width, conv + LANES), MM))
            scratch.append(pltpu.SemaphoreType.DMA((2 * len(where),)))
        return call(
            functools.partial(
                front_kernel, (inner, bc_width, heads, prompts, where, depth, groups, side)
            ),
            outs,
            [SMEM, SMEM, VMEM, VMEM] + ([ANY] * len(where) if where else [VMEM]),
            scratch,
            flops=2 * (tok_dev + HALO) * width * (conv + LANES),
            moved=8_000_000,
            name="front_%d" % side,
        )(ints, floats, vecs, all_tok, *operands)

    z_near = plane_near(z_block)
    *first, weights = front(0, where, x_pieces)
    *first, weights = together([*first, weights])[0]

    low_near = plane_near(first[4])
    out_other = [flip(piece, 1) for piece in out_own]
    out_where = tuple(out_where + [(k, 1, first_row) for k, _, first_row in out_where])
    second = front(1, (), [weights])
    second, lows, z_blocks, out_other = together(
        second,
        [low_near[k][0] for k in low_near],
        [z_near[k][0] for k in z_near],
        out_other,
    )
    out_pieces = out_own + out_other
    z_far = plane_far({k: (block,) for k, block in zip(z_near, z_blocks)})
    z_where = tuple((k, i * depth) for k in z_far for i in range(len(z_far[k])))
    z_pieces = [piece for k in z_far for piece in z_far[k]]

    def mid(side, xs, bc, cum, step, message):
        return call(
            functools.partial(mid_kernel, (inner, heads, prompts, groups, side)),
            [sds((tok_dev, inner), F32)] * 2,
            [SMEM, SMEM] + [VMEM] * 4,
            flops=2 * tok_dev * GROUP * inner,
            moved=1_000_000,
            name="mid_%d" % side,
        )(ints, floats, xs, bc, cum, step)

    parts = {k: (block, None) for k, block in zip(low_near, lows)}
    high_near = plane_near(second[4])
    first_y = mid(0, *first)
    highs, first_y = together([high_near[k][0] for k in parts], first_y)
    parts = {k: (parts[k][0], high) for k, high in zip(parts, highs)}
    for k in range(1, chips):
        if k not in parts:
            low, high = k & -k, 1 << (k.bit_length() - 1)
            parts[k] = (flip(parts[k ^ low][0], 2 * low), flip(parts[k ^ high][1], 2 * high))
    parts = [piece for k in range(chips) for piece in parts[k]]

    y = [first_y, mid(1, *second)]
    gate = call(
        functools.partial(gate_kernel, (inner, z_where, 2 * depth)),
        [sds((tok_dev, inner), F32)] * 2,
        [SMEM, VMEM] + [ANY] * len(z_where),
        [pltpu.VMEM((width, inner), MM), pltpu.SemaphoreType.DMA((len(z_where),))],
        flops=tok * width * inner // 4,
        moved=1_000_000,
        name="gate",
    )(ints, all_tok, *z_pieces)
    sides = [*y[0], gate[0], first[1], *y[1], gate[1], second[1]]
    parts, sides = together(parts, sides)

    per = request_group.shape[0] // seq_count
    sent = sds((tok_dev, inner + LANES), MM)
    theirs, low_states, asked, own_asked = call(
        functools.partial(back_kernel, (inner, heads, prompts, groups, len(parts), per)),
        [
            sent,
            sds((groups, inner, state), MM),
            sds((per, inner, state), MM),
            sds((per, inner, state), F32),
        ],
        [SMEM, VMEM] + [ANY] * len(parts) + [VMEM] * 8,
        [
            pltpu.VMEM((chips * groups, inner + TERMS, state), MM),
            pltpu.VMEM((chips * groups + 1, inner, state), F32),
            pltpu.SemaphoreType.DMA((len(parts),)),
        ],
        flops=2 * tok * state * inner,
        moved=8_000_000,
        name="back",
    )(ints, vecs, *parts, *sides)
    theirs = flip(theirs, 1)
    (mine,) = call(
        functools.partial(back_own_kernel, (inner, heads, groups)),
        [sent],
        [SMEM] + [VMEM] * 10,
        flops=2 * tok_dev * state * inner,
        moved=4_000_000,
        name="back_own",
    )(ints, vecs, low_states, *sides)

    out_width = seq_count * w_out.shape[1]
    piece = tok_dev // tp_count
    block = sds((piece, out_width + LANES), MM)
    ahead = tp_count - 2

    def project_out(chosen, outs, where, operands):
        scratch, extra = [], []
        if where:
            extra = [sds((2 * inner, out_width), MM)]
            scratch = [pltpu.SemaphoreType.DMA((len(where),))]
        return call(
            functools.partial(out_kernel, (inner, tp_count, chosen, where)),
            outs + extra,
            [SMEM, VMEM, VMEM] + ([ANY] * len(where) if where else [VMEM]),
            scratch,
            flops=4 * len(outs) * piece * inner * out_width,
            moved=8_000_000,
            name="out_%d" % len(chosen),
        )(ints, mine, theirs, *operands)

    *sent_first, out_weights = project_out(
        tuple(range(ahead)), [block] * ahead, out_where, out_pieces
    )
    near_block, own = project_out(
        (ahead, ahead + 1), [block, sds(block.shape, F32)], (), [out_weights]
    )
    own, received = sum_over_tp([*sent_first, near_block], own)
    (mixed,) = call(
        functools.partial(final_kernel, float(inner_all)),
        [sds((piece, out_width), MM)],
        [VMEM] * (1 + len(received)),
        name="final",
    )(own, *received)

    other_asked = flip(asked, 1).astype(F32)
    states = jnp.where(
        c == 0,
        jnp.concatenate([own_asked, other_asked], axis=1),
        jnp.concatenate([other_asked, own_asked], axis=1),
    )
    return (mixed, states.reshape(per, 2 * heads, head_width, state))


def solution(mesh):
    return jax.shard_map(
        on_device,
        mesh=mesh,
        in_specs=(
            P("seq", None),
            P(("seq", "tp"), None),
            P(("seq", "tp"), None),
            P(("seq", "tp"), None),
            P(None, "tp"),
            P("tp"),
            P(),
            P(),
            P("tp"),
            P("tp"),
            P("tp"),
            P("tp"),
            P("tp", "seq"),
            P(),
            P(),
        ),
        out_specs=(P(("seq", "tp"), None), P("seq", "tp", None, None)),
        check_vma=False,
    )
```

```python
import functools

import jax
import jax.numpy as jnp
from jax import lax
from jax.experimental import pallas as pl
from jax.experimental.pallas import tpu as pltpu
from jax.sharding import PartitionSpec as P

GROUP = 256
HALO = 16
LANES = 128
TERMS = 32
MM = jnp.bfloat16
F32 = jnp.float32
NEGATIVE = -1e30
sds = jax.ShapeDtypeStruct
VMEM_BYTES = 20 * 1024 * 1024

epsilon = 1e-05

ANY = pl.BlockSpec(memory_space=pl.ANY)
SMEM = pl.BlockSpec(memory_space=pltpu.SMEM)
VMEM = pl.BlockSpec(memory_space=pltpu.VMEM)


def flip(x, bits):
    count = lax.axis_size("seq")
    return lax.ppermute(x, "seq", [(i, i ^ bits) for i in range(count)])


def shift(x, by):
    count = lax.axis_size("tp")
    return lax.ppermute(x, "tp", [(i, (i + by) % count) for i in range(count)])


def plane_near(block):
    chips = lax.axis_size("seq") // 2
    return {k: (block if k == 0 else flip(block, 2 * k),) for k in range(chips) if k & (k - 1) == 0}


def plane_far(blocks):
    chips = lax.axis_size("seq") // 2
    blocks = dict(blocks)

    def half(k, side):
        if len(blocks[k]) == 2:
            return blocks[k][side]
        size = blocks[k][0].shape[0] // 2
        return blocks[k][0][side * size : (side + 1) * size]

    for k in range(1, chips):
        if k not in blocks:
            low = k & -k
            high = 1 << (k.bit_length() - 1)
            first = flip(half(k ^ low, 0), 2 * low)
            second = flip(half(k ^ high, 1), 2 * high)
            blocks[k] = (first, second)
    return blocks


def call(kernel, outs, in_specs, scratch=(), flops=0, moved=0, out_specs=None, name=None):
    return pl.pallas_call(
        kernel,
        out_shape=outs,
        in_specs=in_specs,
        out_specs=[VMEM] * len(outs) if out_specs is None else out_specs,
        scratch_shapes=list(scratch),
        compiler_params=pltpu.CompilerParams(vmem_limit_bytes=VMEM_BYTES),
        cost_estimate=pl.CostEstimate(flops=flops, bytes_accessed=moved, transcendentals=0),
        name=name,
    )


def split_terms(x):
    high = x.astype(MM).astype(F32)
    rest = x - high
    mid = rest.astype(MM).astype(F32)
    return high, mid, (rest - mid).astype(MM).astype(F32)


def silu(x):
    half = 0.5 * x
    return half + half * jnp.tanh(half)


def run_all(copies):
    for copy in copies:
        copy.start()
    for copy in copies:
        copy.wait()


def starts_of(position, ints):
    start, end = jnp.zeros_like(position), 0
    for i in range(ints.prompts):
        end = end + ints.ref[3 + i]
        start = jnp.where(position >= end, end, start)
    return start


class Ints:
    def __init__(self, ref, prompts):
        self.ref, self.prompts = ref, prompts
        self.t, self.p, self.c = ref[0], ref[1], ref[2]

    def wanted(self, i):
        return self.ref[3 + self.prompts + i]


def rows_at(first, size):
    return pl.ds(pl.multiple_of(first, 16), size)


def pack_x_kernel(tp_count, ints, w_ref, bc_ref, dt_ref, *outs):
    t = ints[0]
    pair = w_ref.shape[1] // tp_count
    inner = pair // 2
    bc_width = bc_ref.shape[1]
    heads = dt_ref.shape[1] // tp_count
    low_bc = bc_ref[...].astype(MM)
    for j, out in enumerate(outs):
        owner = lax.rem(t + j, tp_count)
        at = pl.multiple_of(owner * pair, LANES)
        out[:, :inner] = w_ref[:, pl.ds(at, inner)].astype(MM)
        out[:, inner : inner + bc_width] = low_bc
        steps = jnp.zeros((dt_ref.shape[0], heads), F32)
        for u in range(tp_count):
            steps = jnp.where(owner == u, dt_ref[:, u * heads : (u + 1) * heads], steps)
        steps = jnp.concatenate(
            [steps, jnp.zeros((dt_ref.shape[0], LANES - heads), F32)], axis=1
        )
        out[:, inner + bc_width : inner + bc_width + LANES] = steps.astype(MM)
        at = pl.multiple_of(owner * pair + inner, LANES)
        out[:, inner + bc_width + LANES :] = w_ref[:, pl.ds(at, inner)].astype(MM)


def pack_z_kernel(tp_count, ints, w_ref, *outs):
    pair = w_ref.shape[1] // tp_count
    for j, out in enumerate(outs):
        at = pl.multiple_of(lax.rem(ints[0] + j, tp_count) * pair, LANES)
        out[...] = w_ref[:, pl.ds(at, pair)].astype(MM)


def assemble_x_kernel(tp_count, ints, *refs):
    pieces, out = refs[:tp_count], refs[tp_count]
    rows = pieces[0].shape[0]
    for j, piece in enumerate(pieces):
        source = lax.rem(ints[0] + tp_count - j, tp_count)
        out[rows_at(source * rows, rows), :] = piece[...]


def assemble_z_kernel(tp_count, ints, *refs):
    pieces, (mine, theirs) = refs[:tp_count], refs[tp_count:]
    rows, inner = pieces[0].shape[0], mine.shape[1]
    c = ints[2]
    for j, piece in enumerate(pieces):
        at = rows_at(lax.rem(ints[0] + tp_count - j, tp_count) * rows, rows)
        mine[at, :] = piece[:, pl.ds(pl.multiple_of(c * inner, LANES), inner)]
        theirs[at, :] = piece[:, pl.ds(pl.multiple_of((1 - c) * inner, LANES), inner)]


def merge_kernel(ints, mine, theirs, out):
    rows = mine.shape[0]
    out[rows_at(ints[2] * rows, rows), :] = mine[...]
    out[rows_at((1 - ints[2]) * rows, rows), :] = theirs[...]


def lane_row(ref, first, count):
    lane = lax.broadcasted_iota(jnp.int32, (1, LANES), 1)
    row = jnp.zeros((1, LANES), F32)
    for i in range(count):
        row = jnp.where(lane == i, ref[first + i], row)
    return row


def front_kernel(sizes, ints_ref, floats, vecs, tok_ref, *refs):
    inner, bc_width, heads, prompts, where, depth, groups, side = sizes
    ints = Ints(ints_ref, prompts)
    c = ints.c
    conv = inner + bc_width
    state = bc_width // 2
    head_width = inner // heads
    half = groups // 2
    if where:
        pieces = refs[: len(where)]
        xs_ref, bc_ref, cum_ref, step_ref, message, weights, raw, sems = refs[len(where) :]
        start_x = pl.multiple_of(c * (conv + LANES), LANES)
        copies = []
        for piece, (k, other, first) in zip(pieces, where):
            core = 1 - c if other else c
            rows = rows_at(((ints.p ^ k) * 2 + core) * depth + first, piece.shape[0])
            for source, goal, size in ((start_x, 0, inner), (inner, inner, bc_width + LANES)):
                copies.append(
                    pltpu.make_async_copy(
                        piece.at[:, pl.ds(source, size)],
                        weights.at[rows, pl.ds(goal, size)],
                        sems.at[len(copies)],
                    )
                )
        run_all(copies)
    else:
        weights, xs_ref, bc_ref, cum_ref, step_ref, message, raw = refs
    taps = 4
    lower = (
        lax.broadcasted_iota(jnp.int32, (GROUP, GROUP), 0)
        >= lax.broadcasted_iota(jnp.int32, (GROUP, GROUP), 1)
    ).astype(F32)
    within = lax.broadcasted_iota(jnp.int32, (GROUP, LANES), 0)
    base = ints.p * (groups * GROUP) + side * half * GROUP
    all_heads = 2 * heads
    bias = lane_row(floats, c * heads, heads)
    rate = -jnp.exp(lane_row(floats, all_heads + c * heads, heads))

    def project(g):
        at = (side * half + g) * GROUP
        value = jnp.dot(
            tok_ref[at : at + GROUP + HALO, :], weights[...], preferred_element_type=F32
        )
        raw[g % 2, :, :conv] = value[:, :conv].astype(MM).astype(F32)
        raw[g % 2, :, conv:] = value[:, conv:]

    def one(g):
        rows = slice(g * GROUP, (g + 1) * GROUP)
        slot = g % 2
        first = base + g * GROUP
        position = first + within
        behind = position - starts_of(position, ints)
        keeps = [(behind >= lag).astype(F32) for lag in range(1, taps)]
        dt = raw[slot, HALO : HALO + GROUP, conv:]
        dt = jnp.where(c == 0, dt, pltpu.roll(dt, LANES - heads, 1)) + bias
        step = jnp.maximum(dt, 0.0) + jnp.log1p(jnp.exp(-jnp.abs(dt)))
        cum = jnp.dot(
            lower, step * rate, precision=lax.Precision.HIGHEST, preferred_element_type=F32
        )
        cum_ref[rows, :] = cum
        step_ref[rows, :] = step
        last = cum[GROUP - 1 : GROUP, :]
        start_last = starts_of(first + (GROUP - 1), ints)
        tail = jnp.where(position >= start_last, jnp.exp(last - cum), 0.0) * step
        for block in range(0, conv, LANES):
            lanes = slice(block, block + LANES)
            if block < inner:
                here = pl.ds(pl.multiple_of(c * inner + block, LANES), LANES)
                weight, offset = vecs[0:taps, here], vecs[taps : taps + 1, here]
            else:
                here = slice(block - inner, block - inner + LANES)
                weight, offset = vecs[8 : 8 + taps, here], vecs[8 + taps : 9 + taps, here]
            total = offset + raw[slot, HALO : HALO + GROUP, lanes] * weight[taps - 1 : taps]
            for lag in range(1, taps):
                term = raw[slot, HALO - lag : HALO - lag + GROUP, lanes] * keeps[lag - 1]
                total = total + term * weight[taps - 1 - lag : taps - lag]
            value = silu(total).astype(MM)
            if block < inner:
                xs_ref[rows, lanes] = value
            else:
                bc_ref[rows, here] = value
        b_wide = bc_ref[rows, :state].astype(F32)
        for h in range(0, heads, 2):
            weighted = jnp.concatenate(
                [(b_wide * tail[:, h + i : h + i + 1]).astype(MM) for i in range(2)], axis=1
            )
            both = lax.dot_general(
                xs_ref[rows, h * head_width : (h + 2) * head_width],
                weighted,
                (((0,), (0,)), ((), ())),
                preferred_element_type=F32,
            )
            at = h * head_width
            message[g, at : at + head_width, :] = both[:head_width, :state].astype(MM)
            at = at + head_width
            message[g, at : at + head_width, :] = both[head_width:, state:].astype(MM)
        spread = jnp.broadcast_to(jnp.exp(last), (8, LANES))
        diagonal = lax.broadcasted_iota(jnp.int32, (8, LANES), 0) == lax.broadcasted_iota(
            jnp.int32, (8, LANES), 1
        )
        gates = jnp.sum(jnp.where(diagonal, spread, 0.0), axis=1, keepdims=True)
        gates = jnp.where(start_last < first, jnp.broadcast_to(gates, (8, LANES)), 0.0)
        terms = jnp.concatenate(list(split_terms(gates)) + [jnp.zeros_like(gates)], axis=0)
        message[g, inner : inner + TERMS, :] = terms.astype(MM)

    project(0)
    for g in range(half):
        if g + 1 < half:
            project(g + 1)
        one(g)


def mid_kernel(sizes, ints_ref, floats, xs_ref, bc_ref, cum_ref, step_ref, y_ref, keep_ref):
    inner, heads, prompts, groups, side = sizes
    ints = Ints(ints_ref, prompts)
    state = bc_ref.shape[1] // 2
    head_width = inner // heads
    half = groups // 2
    base = ints.p * (groups * GROUP) + side * half * GROUP
    within_i = lax.broadcasted_iota(jnp.int32, (GROUP, GROUP), 0)
    within_j = lax.broadcasted_iota(jnp.int32, (GROUP, GROUP), 1)
    lane = lax.broadcasted_iota(jnp.int32, (GROUP, LANES), 1)
    skip_at = 4 * heads + ints.c * heads

    @pl.loop(0, half)
    def _(g):
        rows = rows_at(g * GROUP, GROUP)
        first = base + g * GROUP
        start = starts_of(first + within_i, ints)
        seen = (within_j <= within_i) & (first + within_j >= start)
        scores = lax.dot_general(
            bc_ref[rows, state:],
            bc_ref[rows, :state],
            (((1,), (1,)), ((), ())),
            preferred_element_type=F32,
        )
        cum = cum_ref[rows, :]
        cum_t = cum.T
        step_t = step_ref[rows, :].T
        keep = jnp.where(start[:, :LANES] < first, jnp.exp(cum), 0.0)
        for h in range(0, heads, 2):
            lanes = slice(h * head_width, (h + 2) * head_width)
            pair = xs_ref[rows, lanes]
            first_skip, second_skip = (floats[skip_at + h + i] for i in range(2))
            total = jnp.where(lane < head_width, first_skip, second_skip) * pair.astype(F32)
            for i in range(2):
                log_decay = cum[:, h + i : h + i + 1] - cum_t[h + i : h + i + 1, :]
                decay = jnp.exp(jnp.where(seen, log_decay, NEGATIVE))
                mix = (decay * scores * step_t[h + i : h + i + 1, :]).astype(MM)
                own = jnp.where((lane < head_width) == (i == 0), pair, jnp.zeros_like(pair))
                total = total + jnp.dot(mix, own, preferred_element_type=F32)
            y_ref[rows, lanes] = total
            keep_ref[rows, lanes] = jnp.where(
                lane < head_width, keep[:, h : h + 1], keep[:, h + 1 : h + 2]
            )


def gate_kernel(sizes, ints, tok_ref, *refs):
    inner, where, depth = sizes
    pieces = refs[: len(where)]
    low, high, weights, sems = refs[len(where) :]
    copies = []
    for i, (piece, (k, first)) in enumerate(zip(pieces, where)):
        rows = rows_at((ints[1] ^ k) * depth + first, piece.shape[0])
        copies.append(pltpu.make_async_copy(piece, weights.at[rows, :], sems.at[i]))
    run_all(copies)
    count = low.shape[0] // GROUP
    for side, out in enumerate((low, high)):

        @pl.loop(0, count)
        def _(g):
            row = (side * count + g) * GROUP + HALO
            value = jnp.dot(
                tok_ref[rows_at(row, GROUP), :], weights[...], preferred_element_type=F32
            )
            out[rows_at(g * GROUP, GROUP), :] = silu(value.astype(MM).astype(F32))


def gating(sizes, ints, low_states, vecs, side, y_ref, keep_ref, gate_ref, bc_ref, out):
    inner, heads, groups = sizes
    half = groups // 2
    state = bc_ref.shape[1] // 2
    lane = lax.broadcasted_iota(jnp.int32, (GROUP, LANES), 1)
    for g in range(half):
        rows = slice(g * GROUP, (g + 1) * GROUP)
        carried = lax.dot_general(
            bc_ref[rows, state:],
            low_states[side * half + g],
            (((1,), (1,)), ((), ())),
            preferred_element_type=F32,
        )
        squares = jnp.zeros((GROUP, LANES), F32)
        for at in range(0, inner, LANES):
            lanes = slice(at, at + LANES)
            y = y_ref[rows, lanes] + carried[:, lanes] * keep_ref[rows, lanes]
            gated = y * gate_ref[rows, lanes]
            squares = squares + gated * gated
            here = pl.ds(pl.multiple_of(ints[2] * inner + at, LANES), LANES)
            out[rows, lanes] = (gated * vecs[5:6, here]).astype(MM)
        total = jnp.broadcast_to(jnp.sum(squares, axis=1, keepdims=True), (GROUP, LANES))
        out[rows, inner:] = spread_terms(total).astype(MM)


def spread_terms(total):
    lane = lax.broadcasted_iota(jnp.int32, total.shape, 1)
    high, mid, low = split_terms(total)
    return jnp.where(lane == 0, high, jnp.where(lane == 1, mid, jnp.where(lane == 2, low, 0.0)))


def added_terms(ref, at):
    value = ref[:, at:].astype(F32)
    return jnp.broadcast_to(jnp.sum(value, axis=1, keepdims=True), value.shape)


def back_kernel(sizes, ints_ref, vecs, *refs):
    inner, heads, prompts, groups, n_pieces, per = sizes
    pieces = refs[:n_pieces]
    sides = (refs[n_pieces : n_pieces + 4], refs[n_pieces + 4 : n_pieces + 8])
    theirs, low_states, asked, own_asked, parts, states, sems = refs[n_pieces + 8 :]
    ints = Ints(ints_ref, prompts)
    p, c = ints.p, ints.c
    head_width = inner // heads
    half = groups // 2
    copies = []
    for i, piece in enumerate(pieces):
        k, side = i // 2, i % 2
        at = (p ^ k) * groups + side * half
        copies.append(pltpu.make_async_copy(piece, parts.at[pl.ds(at, half)], sems.at[i]))
    run_all(copies)
    blocks = parts.shape[0]
    states[0] = jnp.zeros(states.shape[1:], F32)

    @pl.loop(0, blocks)
    def _(b):
        terms = parts[b, inner : inner + TERMS, :].astype(F32)
        gates = terms[0:8] + terms[8:16] + terms[16:24]
        for h in range(heads):
            rows = slice(h * head_width, (h + 1) * head_width)
            states[b + 1, rows, :] = gates[h : h + 1, :] * states[b, rows, :] + parts[
                b, rows, :
            ].astype(F32)

    for g in range(groups):
        low_states[g] = states[p * groups + g].astype(MM)
    for side in range(2):

        @pl.when(c != side)
        def _():
            gating((inner, heads, groups), ints_ref, low_states, vecs, side, *sides[side], theirs)

    for i in range(per):
        own_asked[i] = states[ints.wanted((p * 2 + c) * per + i) + 1]
        asked[i] = states[ints.wanted((p * 2 + 1 - c) * per + i) + 1].astype(MM)


def back_own_kernel(sizes, ints_ref, vecs, low_states, *refs):
    sides = (refs[:4], refs[4:8])
    mine = refs[8]
    for side in range(2):

        @pl.when(ints_ref[2] == side)
        def _():
            gating(sizes, ints_ref, low_states, vecs, side, *sides[side], mine)


def block_places(t, tp_count):
    if tp_count == 4:
        inside = is_inner(t)
        far, mid, near = jnp.where(t < 2, 3, 0), jnp.where(t < 2, 2, 1), t ^ 1
        return [
            jnp.where(inside, near, far),
            jnp.where(inside, far, mid),
            jnp.where(inside, mid, near),
            t,
        ]
    return [lax.rem(t + j, tp_count) for j in range(1, tp_count)] + [t]


def is_inner(t):
    return (t == 1) | (t == 2)


def out_kernel(sizes, ints, mine, theirs, *refs):
    inner, tp_count, chosen, where = sizes
    t, p, c = ints[0], ints[1], ints[2]
    if where:
        pieces = refs[: len(where)]
        outs = refs[len(where) : len(where) + len(chosen)]
        weights, sems = refs[len(where) + len(chosen) :]
        copies = []
        for i, (piece, (k, other, first)) in enumerate(zip(pieces, where)):
            rows, columns = piece.shape
            core = 1 - c if other else c
            at = pl.multiple_of(((p ^ k) * 2 + core) * columns, LANES)
            copies.append(
                pltpu.make_async_copy(
                    piece, weights.at[pl.ds(first, rows), pl.ds(at, columns)], sems.at[i]
                )
            )
        run_all(copies)
    else:
        weights, outs = refs[0], refs[1:]
    width = weights.shape[1]
    piece_rows = mine.shape[0] // tp_count
    own_rows = rows_at(c * inner, inner)
    other_rows = rows_at((1 - c) * inner, inner)
    for i, out in zip(chosen, outs):
        rows = rows_at(block_places(t, tp_count)[i] * piece_rows, piece_rows)
        sums = jnp.sum(
            mine[rows, inner:].astype(F32) + theirs[rows, inner:].astype(F32), axis=1, keepdims=True
        )
        out[:, width:] = spread_terms(jnp.broadcast_to(sums, (piece_rows, LANES))).astype(out.dtype)
        for at in range(0, width, 512):
            lanes = slice(at, at + 512)
            value = jnp.dot(mine[rows, :inner], weights[own_rows, lanes], preferred_element_type=F32)
            value = value + jnp.dot(
                theirs[rows, :inner], weights[other_rows, lanes], preferred_element_type=F32
            )
            out[:, lanes] = value.astype(out.dtype)


def add_kernel(ints, got, own, out):
    width = out.shape[1] - LANES
    inside = is_inner(ints[0])
    for at in range(0, width, 512):
        lanes = slice(at, at + 512)
        came = jnp.where(inside, got[:, lanes].astype(F32), 0.0)
        out[:, lanes] = (came + own[:, lanes].astype(F32)).astype(MM)
    came = jnp.where(inside, added_terms(got, width), 0.0)
    out[:, width:] = spread_terms(came + added_terms(own, width)).astype(MM)


def final_kernel(channels, at_ends, ints, own, *refs):
    received, out = refs[:-1], refs[-1]
    width = out.shape[1]
    inside = is_inner(ints[0])

    def taken(value, where):
        if where is None:
            return value
        return jnp.where(inside, 0.0, value) if where else jnp.where(inside, value, 0.0)

    squares = added_terms(own, width)
    for got, where in zip(received, at_ends):
        squares = squares + taken(added_terms(got, width), where)
    factor = lax.rsqrt(squares[:, :1] / channels + epsilon)
    for at in range(0, width, 512):
        lanes = slice(at, at + 512)
        total = own[:, lanes]
        for got, where in zip(received, at_ends):
            total = total + taken(got[:, lanes].astype(F32), where)
        out[:, lanes] = (total * factor).astype(out.dtype)


def sum_over_tp(ints, blocks, own):
    tp_count = lax.axis_size("tp")
    if tp_count != 4:
        return own, [shift(x, j + 1) for j, x in enumerate(blocks)], (None,) * (tp_count - 1)

    def send(x, pairs):
        return lax.ppermute(x, "tp", pairs)

    def add(got, x, name):
        specs = [SMEM, VMEM, VMEM]
        return call(add_kernel, [sds(x.shape, MM)], specs, moved=1_700_000, name=name)(ints, got, x)[0]

    first, second, third = blocks
    from_near = send(first, [(0, 1), (1, 0), (2, 3), (3, 2)])
    from_near, third, own = lax.optimization_barrier((from_near, third, own))
    second = add(from_near, second, "add_far")
    second, third = lax.optimization_barrier((second, third))
    from_second = send(second, [(0, 1), (3, 2), (1, 3), (2, 0)])
    from_end = send(third, [(0, 1), (3, 2)])
    third = add(from_second, third, "add_mid")
    from_middle = send(third, [(1, 2), (2, 1), (0, 0), (3, 3)])
    return own, [from_near, from_second, from_end, from_middle], (True, True, False, False)


def on_device(
    tokens,
    w_zx,
    w_dt,
    w_bc,
    conv_x_weight,
    conv_x_bias,
    conv_bc_weight,
    conv_bc_bias,
    dt_bias,
    a_log,
    skip,
    norm_weight,
    w_out,
    lengths,
    request_group,
):
    tp_count, seq_count = lax.axis_size("tp"), lax.axis_size("seq")
    t, s = lax.axis_index("tp"), lax.axis_index("seq")
    chips = seq_count // 2
    p, c = s // 2, s % 2
    tok_dev, width = tokens.shape
    rows = w_zx.shape[0]
    inner_all = w_zx.shape[1] // 2
    pair = conv_x_weight.shape[1]
    inner = pair // 2
    heads = dt_bias.shape[0] // 2
    head_width = inner // heads
    bc_width = w_bc.shape[1]
    state = bc_width // 2
    tok = 2 * tok_dev
    groups = tok // GROUP
    half = groups // 2
    conv = inner + bc_width
    prompts = lengths.shape[0]
    x_width = 2 * inner + bc_width + LANES
    depth = tp_count * rows

    ints = jnp.concatenate([jnp.stack([t, p, c]).astype(jnp.int32), lengths, request_group])
    floats = jnp.concatenate([dt_bias, a_log, skip])
    vecs = jnp.concatenate(
        [
            conv_x_weight,
            conv_x_bias[None, :],
            norm_weight[None, :],
            jnp.zeros((2, pair), F32),
            jnp.pad(conv_bc_weight, ((0, 0), (0, pair - bc_width))),
            jnp.pad(conv_bc_bias[None, :], ((0, 3), (0, pair - bc_width))),
        ],
        axis=0,
    )

    def packed(kernel, operands, specs, wide, name):
        return pl.pallas_call(
            functools.partial(kernel, tp_count),
            grid=(1,),
            out_shape=[sds((rows, wide), MM)] * tp_count,
            in_specs=specs,
            out_specs=[pl.BlockSpec((rows, wide), lambda i: (0, 0))] * tp_count,
            compiler_params=pltpu.CompilerParams(vmem_limit_bytes=VMEM_BYTES),
            name=name,
        )(*operands)

    def whole(x):
        return pl.BlockSpec(x.shape, lambda i: (0, 0))

    def sent_over_tp(pieces):
        return [pieces[0]] + [shift(x, j) for j, x in enumerate(pieces) if j]

    def assembled(kernel, outs, pieces, name):
        return call(
            functools.partial(kernel, tp_count), outs, [SMEM] + [VMEM] * tp_count, name=name
        )(ints, *pieces)

    def together(*lists):
        joined = lax.optimization_barrier(tuple(tuple(one) for one in lists))
        return [list(one) for one in joined]

    x_sent = packed(
        pack_x_kernel,
        (ints, w_zx, w_bc, w_dt),
        [SMEM, pl.BlockSpec((rows, inner_all), lambda i: (0, 1)), whole(w_bc), whole(w_dt)],
        x_width,
        "pack_x",
    )
    x_got = sent_over_tp(x_sent)

    out_near = plane_near(w_out.astype(MM))
    keys = list(out_near)
    other = flip(tokens, 1)
    first_tok = jnp.where(c == 0, tokens, other)
    second_tok = jnp.where(c == 0, other, tokens)
    out_got, (first_tok, second_tok) = together(
        [out_near[k][0] for k in keys], [first_tok, second_tok]
    )
    out_blocks = plane_far({k: (piece,) for k, piece in zip(keys, out_got)})
    out_own = [piece for k in out_blocks for piece in out_blocks[k]]
    out_where = [
        (k, 0, i * (w_out.shape[0] // 2)) for k in out_blocks for i in range(len(out_blocks[k]))
    ]
    x_got, out_own = together(x_got, out_own)
    (x_block,) = assembled(assemble_x_kernel, [sds((depth, x_width), MM)], x_got, "assemble_x")

    before = lax.ppermute(
        second_tok[tok_dev - HALO :], "seq", [(i, i + 2) for i in range(seq_count - 2)]
    )
    all_tok = jnp.concatenate([before, first_tok, second_tok], axis=0)

    ((x_block, all_tok, ints, floats, vecs),) = together([x_block, all_tok, ints, floats, vecs])
    near = plane_near(x_block)
    z_sent = packed(
        pack_z_kernel,
        (ints, w_zx),
        [SMEM, pl.BlockSpec((rows, inner_all), lambda i: (0, 0))],
        2 * inner,
        "pack_z",
    )
    z_got = sent_over_tp(z_sent)
    own_other = flip(x_block, 1)
    blocks, z_got = together([near[k][0] for k in near if k], z_got)
    far = plane_far({k: (block,) for k, block in zip(near, [x_block] + blocks)})
    where = [(k, 0, i * depth // 2) for k in far for i in range(len(far[k]))]
    x_pieces = [piece for k in far for piece in far[k]]
    x_pieces += [own_other] + [flip(piece, 1) for piece in x_pieces[1:]]
    where = tuple(where + [(k, 1, first) for k, _, first in where])
    z_mine, z_theirs = assembled(
        assemble_z_kernel, [sds((depth, inner), MM)] * 2, z_got, "assemble_z"
    )
    (z_block,) = call(
        merge_kernel, [sds((2 * depth, inner), MM)], [SMEM, VMEM, VMEM], name="merge_z"
    )(ints, z_mine, flip(z_theirs, 1))
    x_pieces, (z_block,) = together(x_pieces, [z_block])

    def front(side, where, operands):
        outs = [
            sds((tok_dev, inner), MM),
            sds((tok_dev, bc_width), MM),
            sds((tok_dev, LANES), F32),
            sds((tok_dev, LANES), F32),
            sds((half, inner + TERMS, state), MM),
        ]
        scratch = [pltpu.VMEM((2, HALO + GROUP, conv + LANES), F32)]
        if where:
            outs.append(sds((width, conv + LANES), MM))
            scratch.append(pltpu.SemaphoreType.DMA((2 * len(where),)))
        return call(
            functools.partial(
                front_kernel, (inner, bc_width, heads, prompts, where, depth, groups, side)
            ),
            outs,
            [SMEM, SMEM, VMEM, VMEM] + ([ANY] * len(where) if where else [VMEM]),
            scratch,
            flops=2 * (tok_dev + HALO) * width * (conv + LANES),
            moved=8_000_000,
            name="front_%d" % side,
        )(ints, floats, vecs, all_tok, *operands)

    z_near = plane_near(z_block)
    *first, weights = front(0, where, x_pieces)
    *first, weights = together([*first, weights])[0]

    low_near = plane_near(first[4])
    out_other = [flip(piece, 1) for piece in out_own]
    out_where = tuple(out_where + [(k, 1, first_row) for k, _, first_row in out_where])
    second = front(1, (), [weights])
    second, lows, z_blocks, out_other = together(
        second,
        [low_near[k][0] for k in low_near],
        [z_near[k][0] for k in z_near],
        out_other,
    )
    out_pieces = out_own + out_other
    z_far = plane_far({k: (block,) for k, block in zip(z_near, z_blocks)})
    z_where = tuple((k, i * depth) for k in z_far for i in range(len(z_far[k])))
    z_pieces = [piece for k in z_far for piece in z_far[k]]

    def mid(side, xs, bc, cum, step, message):
        return call(
            functools.partial(mid_kernel, (inner, heads, prompts, groups, side)),
            [sds((tok_dev, inner), F32)] * 2,
            [SMEM, SMEM] + [VMEM] * 4,
            flops=2 * tok_dev * GROUP * inner,
            moved=1_000_000,
            name="mid_%d" % side,
        )(ints, floats, xs, bc, cum, step)

    parts = {k: (block, None) for k, block in zip(low_near, lows)}
    high_near = plane_near(second[4])
    first_y = mid(0, *first)
    highs, first_y = together([high_near[k][0] for k in parts], first_y)
    parts = {k: (parts[k][0], high) for k, high in zip(parts, highs)}
    for k in range(1, chips):
        if k not in parts:
            low, high = k & -k, 1 << (k.bit_length() - 1)
            parts[k] = (flip(parts[k ^ low][0], 2 * low), flip(parts[k ^ high][1], 2 * high))
    parts = [piece for k in range(chips) for piece in parts[k]]

    y = [first_y, mid(1, *second)]
    gate = call(
        functools.partial(gate_kernel, (inner, z_where, 2 * depth)),
        [sds((tok_dev, inner), F32)] * 2,
        [SMEM, VMEM] + [ANY] * len(z_where),
        [pltpu.VMEM((width, inner), MM), pltpu.SemaphoreType.DMA((len(z_where),))],
        flops=tok * width * inner // 4,
        moved=1_000_000,
        name="gate",
    )(ints, all_tok, *z_pieces)
    sides = [*y[0], gate[0], first[1], *y[1], gate[1], second[1]]
    parts, sides = together(parts, sides)

    per = request_group.shape[0] // seq_count
    sent = sds((tok_dev, inner + LANES), MM)
    theirs, low_states, asked, own_asked = call(
        functools.partial(back_kernel, (inner, heads, prompts, groups, len(parts), per)),
        [
            sent,
            sds((groups, inner, state), MM),
            sds((per, inner, state), MM),
            sds((per, inner, state), F32),
        ],
        [SMEM, VMEM] + [ANY] * len(parts) + [VMEM] * 8,
        [
            pltpu.VMEM((chips * groups, inner + TERMS, state), MM),
            pltpu.VMEM((chips * groups + 1, inner, state), F32),
            pltpu.SemaphoreType.DMA((len(parts),)),
        ],
        flops=2 * tok * state * inner,
        moved=8_000_000,
        name="back",
    )(ints, vecs, *parts, *sides)
    theirs = flip(theirs, 1)
    (mine,) = call(
        functools.partial(back_own_kernel, (inner, heads, groups)),
        [sent],
        [SMEM] + [VMEM] * 10,
        flops=2 * tok_dev * state * inner,
        moved=4_000_000,
        name="back_own",
    )(ints, vecs, low_states, *sides)

    out_width = seq_count * w_out.shape[1]
    piece = tok_dev // tp_count
    block = sds((piece, out_width + LANES), MM)
    ahead = tp_count - 2

    def project_out(chosen, outs, where, operands):
        scratch, extra = [], []
        if where:
            extra = [sds((2 * inner, out_width), MM)]
            scratch = [pltpu.SemaphoreType.DMA((len(where),))]
        return call(
            functools.partial(out_kernel, (inner, tp_count, chosen, where)),
            outs + extra,
            [SMEM, VMEM, VMEM] + ([ANY] * len(where) if where else [VMEM]),
            scratch,
            flops=4 * len(outs) * piece * inner * out_width,
            moved=8_000_000,
            name="out_%d" % len(chosen),
        )(ints, mine, theirs, *operands)

    *sent_first, out_weights = project_out(
        tuple(range(ahead)), [block] * ahead, out_where, out_pieces
    )
    near_block, own = project_out(
        (ahead, ahead + 1), [block, sds(block.shape, F32)], (), [out_weights]
    )
    own, received, at_ends = sum_over_tp(ints, [*sent_first, near_block], own)
    (mixed,) = call(
        functools.partial(final_kernel, float(inner_all), at_ends),
        [sds((piece, out_width), MM)],
        [SMEM] + [VMEM] * (1 + len(received)),
        name="final",
    )(ints, own, *received)

    other_asked = flip(asked, 1).astype(F32)
    states = jnp.where(
        c == 0,
        jnp.concatenate([own_asked, other_asked], axis=1),
        jnp.concatenate([other_asked, own_asked], axis=1),
    )
    return (mixed, states.reshape(per, 2 * heads, head_width, state))


def solution(mesh):
    return jax.shard_map(
        on_device,
        mesh=mesh,
        in_specs=(
            P("seq", None),
            P(("seq", "tp"), None),
            P(("seq", "tp"), None),
            P(("seq", "tp"), None),
            P(None, "tp"),
            P("tp"),
            P(),
            P(),
            P("tp"),
            P("tp"),
            P("tp"),
            P("tp"),
            P("tp", "seq"),
            P(),
            P(),
        ),
        out_specs=(P(("seq", "tp"), None), P("seq", "tp", None, None)),
        check_vma=False,
    )
```

```python
import functools

import jax
import jax.numpy as jnp
from jax import lax
from jax.experimental import pallas as pl
from jax.experimental.pallas import tpu as pltpu
from jax.sharding import PartitionSpec as P

GROUP = 256
HALO = 16
LANES = 128
TERMS = 32
MM = jnp.bfloat16
F32 = jnp.float32
NEGATIVE = -1e30
sds = jax.ShapeDtypeStruct
VMEM_BYTES = 20 * 1024 * 1024

epsilon = 1e-05

ANY = pl.BlockSpec(memory_space=pl.ANY)
SMEM = pl.BlockSpec(memory_space=pltpu.SMEM)
VMEM = pl.BlockSpec(memory_space=pltpu.VMEM)


def flip(x, bits):
    count = lax.axis_size("seq")
    return lax.ppermute(x, "seq", [(i, i ^ bits) for i in range(count)])


def shift(x, by):
    count = lax.axis_size("tp")
    return lax.ppermute(x, "tp", [(i, (i + by) % count) for i in range(count)])


def plane_near(block):
    chips = lax.axis_size("seq") // 2
    return {k: (block if k == 0 else flip(block, 2 * k),) for k in range(chips) if k & (k - 1) == 0}


def plane_far(blocks):
    chips = lax.axis_size("seq") // 2
    blocks = dict(blocks)

    def half(k, side):
        if len(blocks[k]) == 2:
            return blocks[k][side]
        size = blocks[k][0].shape[0] // 2
        return blocks[k][0][side * size : (side + 1) * size]

    for k in range(1, chips):
        if k not in blocks:
            low = k & -k
            high = 1 << (k.bit_length() - 1)
            first = flip(half(k ^ low, 0), 2 * low)
            second = flip(half(k ^ high, 1), 2 * high)
            blocks[k] = (first, second)
    return blocks


def call(kernel, outs, in_specs, scratch=(), flops=0, moved=0, out_specs=None, name=None):
    return pl.pallas_call(
        kernel,
        out_shape=outs,
        in_specs=in_specs,
        out_specs=[VMEM] * len(outs) if out_specs is None else out_specs,
        scratch_shapes=list(scratch),
        compiler_params=pltpu.CompilerParams(vmem_limit_bytes=VMEM_BYTES),
        cost_estimate=pl.CostEstimate(flops=flops, bytes_accessed=moved, transcendentals=0),
        name=name,
    )


def split_terms(x):
    high = x.astype(MM).astype(F32)
    rest = x - high
    mid = rest.astype(MM).astype(F32)
    return high, mid, (rest - mid).astype(MM).astype(F32)


def silu(x):
    half = 0.5 * x
    return half + half * jnp.tanh(half)


def run_all(copies):
    for copy in copies:
        copy.start()
    for copy in copies:
        copy.wait()


def starts_of(position, ints):
    start, end = jnp.zeros_like(position), 0
    for i in range(ints.prompts):
        end = end + ints.ref[3 + i]
        start = jnp.where(position >= end, end, start)
    return start


class Ints:
    def __init__(self, ref, prompts):
        self.ref, self.prompts = ref, prompts
        self.t, self.p, self.c = ref[0], ref[1], ref[2]

    def wanted(self, i):
        return self.ref[3 + self.prompts + i]


def rows_at(first, size):
    return pl.ds(pl.multiple_of(first, 16), size)


def pack_x_kernel(tp_count, ints, w_ref, bc_ref, dt_ref, *outs):
    t = ints[0]
    pair = w_ref.shape[1] // tp_count
    inner = pair // 2
    bc_width = bc_ref.shape[1]
    heads = dt_ref.shape[1] // tp_count
    low_bc = bc_ref[...].astype(MM)
    for j, out in enumerate(outs):
        owner = lax.rem(t + j, tp_count)
        at = pl.multiple_of(owner * pair, LANES)
        out[:, :inner] = w_ref[:, pl.ds(at, inner)].astype(MM)
        out[:, inner : inner + bc_width] = low_bc
        steps = jnp.zeros((dt_ref.shape[0], heads), F32)
        for u in range(tp_count):
            steps = jnp.where(owner == u, dt_ref[:, u * heads : (u + 1) * heads], steps)
        steps = jnp.concatenate(
            [steps, jnp.zeros((dt_ref.shape[0], LANES - heads), F32)], axis=1
        )
        out[:, inner + bc_width : inner + bc_width + LANES] = steps.astype(MM)
        at = pl.multiple_of(owner * pair + inner, LANES)
        out[:, inner + bc_width + LANES :] = w_ref[:, pl.ds(at, inner)].astype(MM)


def pack_z_kernel(tp_count, ints, w_ref, *outs):
    pair = w_ref.shape[1] // tp_count
    for j, out in enumerate(outs):
        at = pl.multiple_of(lax.rem(ints[0] + j, tp_count) * pair, LANES)
        out[...] = w_ref[:, pl.ds(at, pair)].astype(MM)


def assemble_x_kernel(tp_count, ints, *refs):
    pieces, out = refs[:tp_count], refs[tp_count]
    rows = pieces[0].shape[0]
    for j, piece in enumerate(pieces):
        source = lax.rem(ints[0] + tp_count - j, tp_count)
        out[rows_at(source * rows, rows), :] = piece[...]


def assemble_z_kernel(tp_count, ints, *refs):
    pieces, (mine, theirs) = refs[:tp_count], refs[tp_count:]
    rows, inner = pieces[0].shape[0], mine.shape[1]
    c = ints[2]
    for j, piece in enumerate(pieces):
        at = rows_at(lax.rem(ints[0] + tp_count - j, tp_count) * rows, rows)
        mine[at, :] = piece[:, pl.ds(pl.multiple_of(c * inner, LANES), inner)]
        theirs[at, :] = piece[:, pl.ds(pl.multiple_of((1 - c) * inner, LANES), inner)]


def join_kernel(*refs):
    pieces, out = refs[:-1], refs[-1]
    at = 0
    for piece in pieces:
        out[at : at + piece.shape[0], :] = piece[...]
        at = at + piece.shape[0]


def merge_kernel(ints, mine, theirs, out):
    rows = mine.shape[0]
    out[rows_at(ints[2] * rows, rows), :] = mine[...]
    out[rows_at((1 - ints[2]) * rows, rows), :] = theirs[...]


def lane_row(ref, first, count):
    lane = lax.broadcasted_iota(jnp.int32, (1, LANES), 1)
    row = jnp.zeros((1, LANES), F32)
    for i in range(count):
        row = jnp.where(lane == i, ref[first + i], row)
    return row


def front_kernel(sizes, ints_ref, floats, vecs, tok_ref, *refs):
    inner, bc_width, heads, prompts, where, depth, groups, side = sizes
    ints = Ints(ints_ref, prompts)
    c = ints.c
    conv = inner + bc_width
    state = bc_width // 2
    head_width = inner // heads
    half = groups // 2
    if where:
        pieces = refs[: len(where)]
        xs_ref, bc_ref, cum_ref, step_ref, message, weights, raw, sems = refs[len(where) :]
        start_x = pl.multiple_of(c * (conv + LANES), LANES)
        copies = []
        for piece, (k, other, first) in zip(pieces, where):
            core = 1 - c if other else c
            rows = rows_at(((ints.p ^ k) * 2 + core) * depth + first, piece.shape[0])
            for source, goal, size in ((start_x, 0, inner), (inner, inner, bc_width + LANES)):
                copies.append(
                    pltpu.make_async_copy(
                        piece.at[:, pl.ds(source, size)],
                        weights.at[rows, pl.ds(goal, size)],
                        sems.at[len(copies)],
                    )
                )
        run_all(copies)
    else:
        weights, xs_ref, bc_ref, cum_ref, step_ref, message, raw = refs
    taps = 4
    lower = (
        lax.broadcasted_iota(jnp.int32, (GROUP, GROUP), 0)
        >= lax.broadcasted_iota(jnp.int32, (GROUP, GROUP), 1)
    ).astype(F32)
    within = lax.broadcasted_iota(jnp.int32, (GROUP, LANES), 0)
    base = ints.p * (groups * GROUP) + side * half * GROUP
    all_heads = 2 * heads
    bias = lane_row(floats, c * heads, heads)
    rate = -jnp.exp(lane_row(floats, all_heads + c * heads, heads))

    def project(g):
        at = (side * half + g) * GROUP
        value = jnp.dot(
            tok_ref[at : at + GROUP + HALO, :], weights[...], preferred_element_type=F32
        )
        raw[g % 2, :, :conv] = value[:, :conv].astype(MM).astype(F32)
        raw[g % 2, :, conv:] = value[:, conv:]

    def one(g):
        rows = slice(g * GROUP, (g + 1) * GROUP)
        slot = g % 2
        first = base + g * GROUP
        position = first + within
        behind = position - starts_of(position, ints)
        keeps = [(behind >= lag).astype(F32) for lag in range(1, taps)]
        dt = raw[slot, HALO : HALO + GROUP, conv:]
        dt = jnp.where(c == 0, dt, pltpu.roll(dt, LANES - heads, 1)) + bias
        step = jnp.maximum(dt, 0.0) + jnp.log1p(jnp.exp(-jnp.abs(dt)))
        cum = jnp.dot(
            lower, step * rate, precision=lax.Precision.HIGHEST, preferred_element_type=F32
        )
        cum_ref[rows, :] = cum
        step_ref[rows, :] = step
        last = cum[GROUP - 1 : GROUP, :]
        start_last = starts_of(first + (GROUP - 1), ints)
        tail = jnp.where(position >= start_last, jnp.exp(last - cum), 0.0) * step
        for block in range(0, conv, LANES):
            lanes = slice(block, block + LANES)
            if block < inner:
                here = pl.ds(pl.multiple_of(c * inner + block, LANES), LANES)
                weight, offset = vecs[0:taps, here], vecs[taps : taps + 1, here]
            else:
                here = slice(block - inner, block - inner + LANES)
                weight, offset = vecs[8 : 8 + taps, here], vecs[8 + taps : 9 + taps, here]
            total = offset + raw[slot, HALO : HALO + GROUP, lanes] * weight[taps - 1 : taps]
            for lag in range(1, taps):
                term = raw[slot, HALO - lag : HALO - lag + GROUP, lanes] * keeps[lag - 1]
                total = total + term * weight[taps - 1 - lag : taps - lag]
            value = silu(total).astype(MM)
            if block < inner:
                xs_ref[rows, lanes] = value
            else:
                bc_ref[rows, here] = value
        b_wide = bc_ref[rows, :state].astype(F32)
        for h in range(0, heads, 2):
            weighted = jnp.concatenate(
                [(b_wide * tail[:, h + i : h + i + 1]).astype(MM) for i in range(2)], axis=1
            )
            both = lax.dot_general(
                xs_ref[rows, h * head_width : (h + 2) * head_width],
                weighted,
                (((0,), (0,)), ((), ())),
                preferred_element_type=F32,
            )
            at = h * head_width
            message[g, at : at + head_width, :] = both[:head_width, :state].astype(MM)
            at = at + head_width
            message[g, at : at + head_width, :] = both[head_width:, state:].astype(MM)
        spread = jnp.broadcast_to(jnp.exp(last), (8, LANES))
        diagonal = lax.broadcasted_iota(jnp.int32, (8, LANES), 0) == lax.broadcasted_iota(
            jnp.int32, (8, LANES), 1
        )
        gates = jnp.sum(jnp.where(diagonal, spread, 0.0), axis=1, keepdims=True)
        gates = jnp.where(start_last < first, jnp.broadcast_to(gates, (8, LANES)), 0.0)
        terms = jnp.concatenate(list(split_terms(gates)) + [jnp.zeros_like(gates)], axis=0)
        message[g, inner : inner + TERMS, :] = terms.astype(MM)

    project(0)
    for g in range(half):
        if g + 1 < half:
            project(g + 1)
        one(g)


def mid_kernel(sizes, ints_ref, floats, xs_ref, bc_ref, cum_ref, step_ref, y_ref, keep_ref):
    inner, heads, prompts, groups, side = sizes
    ints = Ints(ints_ref, prompts)
    state = bc_ref.shape[1] // 2
    head_width = inner // heads
    half = groups // 2
    base = ints.p * (groups * GROUP) + side * half * GROUP
    within_i = lax.broadcasted_iota(jnp.int32, (GROUP, GROUP), 0)
    within_j = lax.broadcasted_iota(jnp.int32, (GROUP, GROUP), 1)
    lane = lax.broadcasted_iota(jnp.int32, (GROUP, LANES), 1)
    skip_at = 4 * heads + ints.c * heads

    @pl.loop(0, half)
    def _(g):
        rows = rows_at(g * GROUP, GROUP)
        first = base + g * GROUP
        start = starts_of(first + within_i, ints)
        seen = (within_j <= within_i) & (first + within_j >= start)
        scores = lax.dot_general(
            bc_ref[rows, state:],
            bc_ref[rows, :state],
            (((1,), (1,)), ((), ())),
            preferred_element_type=F32,
        )
        cum = cum_ref[rows, :]
        cum_t = cum.T
        step_t = step_ref[rows, :].T
        keep = jnp.where(start[:, :LANES] < first, jnp.exp(cum), 0.0)
        for h in range(0, heads, 2):
            lanes = slice(h * head_width, (h + 2) * head_width)
            pair = xs_ref[rows, lanes]
            first_skip, second_skip = (floats[skip_at + h + i] for i in range(2))
            total = jnp.where(lane < head_width, first_skip, second_skip) * pair.astype(F32)
            for i in range(2):
                log_decay = cum[:, h + i : h + i + 1] - cum_t[h + i : h + i + 1, :]
                decay = jnp.exp(jnp.where(seen, log_decay, NEGATIVE))
                mix = (decay * scores * step_t[h + i : h + i + 1, :]).astype(MM)
                own = jnp.where((lane < head_width) == (i == 0), pair, jnp.zeros_like(pair))
                total = total + jnp.dot(mix, own, preferred_element_type=F32)
            y_ref[rows, lanes] = total
            keep_ref[rows, lanes] = jnp.where(
                lane < head_width, keep[:, h : h + 1], keep[:, h + 1 : h + 2]
            )


def gate_kernel(sizes, ints, tok_ref, *refs):
    inner, where, depth = sizes
    pieces = refs[: len(where)]
    low, high, weights, sems = refs[len(where) :]
    copies = []
    for i, (piece, (k, first)) in enumerate(zip(pieces, where)):
        rows = rows_at((ints[1] ^ k) * depth + first, piece.shape[0])
        copies.append(pltpu.make_async_copy(piece, weights.at[rows, :], sems.at[i]))
    run_all(copies)
    count = low.shape[0] // GROUP
    for side, out in enumerate((low, high)):

        @pl.loop(0, count)
        def _(g):
            row = (side * count + g) * GROUP + HALO
            value = jnp.dot(
                tok_ref[rows_at(row, GROUP), :], weights[...], preferred_element_type=F32
            )
            out[rows_at(g * GROUP, GROUP), :] = silu(value.astype(MM).astype(F32))


def gating(sizes, ints, low_states, vecs, side, y_ref, keep_ref, gate_ref, bc_ref, out):
    inner, heads, groups = sizes
    half = groups // 2
    state = bc_ref.shape[1] // 2
    lane = lax.broadcasted_iota(jnp.int32, (GROUP, LANES), 1)
    for g in range(half):
        rows = slice(g * GROUP, (g + 1) * GROUP)
        carried = lax.dot_general(
            bc_ref[rows, state:],
            low_states[side * half + g],
            (((1,), (1,)), ((), ())),
            preferred_element_type=F32,
        )
        squares = jnp.zeros((GROUP, LANES), F32)
        for at in range(0, inner, LANES):
            lanes = slice(at, at + LANES)
            y = y_ref[rows, lanes] + carried[:, lanes] * keep_ref[rows, lanes]
            gated = y * gate_ref[rows, lanes]
            squares = squares + gated * gated
            here = pl.ds(pl.multiple_of(ints[2] * inner + at, LANES), LANES)
            out[rows, lanes] = (gated * vecs[5:6, here]).astype(MM)
        total = jnp.broadcast_to(jnp.sum(squares, axis=1, keepdims=True), (GROUP, LANES))
        out[rows, inner:] = spread_terms(total).astype(MM)


def spread_terms(total):
    lane = lax.broadcasted_iota(jnp.int32, total.shape, 1)
    high, mid, low = split_terms(total)
    return jnp.where(lane == 0, high, jnp.where(lane == 1, mid, jnp.where(lane == 2, low, 0.0)))


def added_terms(ref, at):
    value = ref[:, at:].astype(F32)
    return jnp.broadcast_to(jnp.sum(value, axis=1, keepdims=True), value.shape)


def back_kernel(sizes, ints_ref, vecs, *refs):
    inner, heads, prompts, groups, n_pieces, per = sizes
    pieces = refs[:n_pieces]
    sides = (refs[n_pieces : n_pieces + 4], refs[n_pieces + 4 : n_pieces + 8])
    theirs, low_states, asked, own_asked, parts, states, sems = refs[n_pieces + 8 :]
    ints = Ints(ints_ref, prompts)
    p, c = ints.p, ints.c
    head_width = inner // heads
    half = groups // 2
    copies = []
    for i, piece in enumerate(pieces):
        k, side = i // 2, i % 2
        at = (p ^ k) * groups + side * half
        copies.append(pltpu.make_async_copy(piece, parts.at[pl.ds(at, half)], sems.at[i]))
    run_all(copies)
    blocks = parts.shape[0]
    states[0] = jnp.zeros(states.shape[1:], F32)

    @pl.loop(0, blocks)
    def _(b):
        terms = parts[b, inner : inner + TERMS, :].astype(F32)
        gates = terms[0:8] + terms[8:16] + terms[16:24]
        for h in range(heads):
            rows = slice(h * head_width, (h + 1) * head_width)
            states[b + 1, rows, :] = gates[h : h + 1, :] * states[b, rows, :] + parts[
                b, rows, :
            ].astype(F32)

    for g in range(groups):
        low_states[g] = states[p * groups + g].astype(MM)
    for side in range(2):

        @pl.when(c != side)
        def _():
            gating((inner, heads, groups), ints_ref, low_states, vecs, side, *sides[side], theirs)

    for i in range(per):
        own_asked[i] = states[ints.wanted((p * 2 + c) * per + i) + 1]
        asked[i] = states[ints.wanted((p * 2 + 1 - c) * per + i) + 1].astype(MM)


def back_own_kernel(sizes, ints_ref, vecs, low_states, *refs):
    sides = (refs[:4], refs[4:8])
    mine = refs[8]
    for side in range(2):

        @pl.when(ints_ref[2] == side)
        def _():
            gating(sizes, ints_ref, low_states, vecs, side, *sides[side], mine)


def block_places(t, tp_count):
    if tp_count == 4:
        inside = is_inner(t)
        far, mid, near = jnp.where(t < 2, 3, 0), jnp.where(t < 2, 2, 1), t ^ 1
        return [
            jnp.where(inside, near, far),
            jnp.where(inside, far, mid),
            jnp.where(inside, mid, near),
            t,
        ]
    return [lax.rem(t + j, tp_count) for j in range(1, tp_count)] + [t]


def is_inner(t):
    return (t == 1) | (t == 2)


def out_kernel(sizes, ints, mine, theirs, *refs):
    inner, tp_count, chosen, where = sizes
    t, p, c = ints[0], ints[1], ints[2]
    if where:
        both, outs = refs[0], refs[1 : 1 + 2 * len(chosen)]
        weights, sems = refs[1 + 2 * len(chosen) :]
        columns = both.shape[2]
        copies = []
        for core in range(2):
            source = 0
            for k, first, size in where:
                at = pl.multiple_of(((p ^ k) * 2 + core) * columns, LANES)
                copies.append(
                    pltpu.make_async_copy(
                        both.at[core, pl.ds(source, size)],
                        weights.at[pl.ds(first, size), pl.ds(at, columns)],
                        sems.at[len(copies)],
                    )
                )
                source = source + size
        run_all(copies)
    else:
        weights, outs = refs[0], refs[1:]
    width = weights.shape[1]
    piece_rows = mine.shape[0] // tp_count
    own_rows = rows_at(c * inner, inner)
    other_rows = rows_at((1 - c) * inner, inner)
    for i, low, high in zip(chosen, outs[::2], outs[1::2]):
        rows = rows_at(block_places(t, tp_count)[i] * piece_rows, piece_rows)
        sums = jnp.sum(
            mine[rows, inner:].astype(F32) + theirs[rows, inner:].astype(F32), axis=1, keepdims=True
        )
        sums = spread_terms(jnp.broadcast_to(sums, (piece_rows, LANES)))
        high[:, width // 2 :] = sums.astype(high.dtype)
        for at in range(0, width, width // 4):
            lanes = slice(at, at + width // 4)
            value = jnp.dot(mine[rows, :inner], weights[own_rows, lanes], preferred_element_type=F32)
            value = value + jnp.dot(
                theirs[rows, :inner], weights[other_rows, lanes], preferred_element_type=F32
            )
            out, first = (low, at) if at < width // 2 else (high, at - width // 2)
            out[:, first : first + width // 4] = value.astype(out.dtype)


def add_kernel(width, ints, got, own, out):
    inside = is_inner(ints[0])
    came = jnp.where(inside, got[:, :width].astype(F32), 0.0)
    out[:, :width] = (came + own[:, :width].astype(F32)).astype(MM)
    if out.shape[1] > width:
        came = jnp.where(inside, added_terms(got, width), 0.0)
        out[:, width:] = spread_terms(came + added_terms(own, width)).astype(MM)


def final_kernel(channels, at_ends, ints, *refs):
    own, received, out = refs[:2], refs[2:-1], refs[-1]
    half = out.shape[1] // 2
    inside = is_inner(ints[0])

    def taken(value, where):
        if where is None:
            return value
        return jnp.where(inside, 0.0, value) if where else jnp.where(inside, value, 0.0)

    squares = added_terms(own[1], half)
    for got, where in zip(received[1::2], at_ends):
        squares = squares + taken(added_terms(got, half), where)
    factor = lax.rsqrt(squares[:, :1] / channels + epsilon)
    for side in range(2):
        total = own[side][:, :half]
        for got, where in zip(received[side::2], at_ends):
            total = total + taken(got[:, :half].astype(F32), where)
        out[:, side * half : (side + 1) * half] = (total * factor).astype(out.dtype)


def sum_over_tp(ints, blocks, own):
    tp_count = lax.axis_size("tp")
    if tp_count != 4:
        received = [[shift(x, j + 1) for x in block] for j, block in enumerate(blocks)]
        return own, received, (None,) * (tp_count - 1)

    def send(x, pairs):
        return lax.ppermute(x, "tp", pairs)

    def add(got, x, name):
        kernel = functools.partial(add_kernel, blocks[0][0].shape[1])
        specs = [SMEM, VMEM, VMEM]
        return call(kernel, [sds(x.shape, MM)], specs, moved=100_000, name=name)(ints, got, x)[0]

    first, second, third = blocks
    from_near = [send(x, [(0, 1), (1, 0), (2, 3), (3, 2)]) for x in first]
    from_near[0], *third, own_low, own_high = lax.optimization_barrier((from_near[0], *third, *own))
    second = [add(got, x, "add_far") for got, x in zip(from_near, second)]
    from_second = [send(x, [(0, 1), (3, 2), (1, 3), (2, 0)]) for x in second]
    second[1], *third = lax.optimization_barrier((second[1], *third))
    from_end = [send(x, [(0, 1), (3, 2)]) for x in third]
    third = [add(got, x, "add_mid") for got, x in zip(from_second, third)]
    from_middle = [send(x, [(1, 2), (2, 1), (0, 0), (3, 3)]) for x in third]
    received = [from_near, from_second, from_end, from_middle]
    return [own_low, own_high], received, (True, True, False, False)


def on_device(
    tokens,
    w_zx,
    w_dt,
    w_bc,
    conv_x_weight,
    conv_x_bias,
    conv_bc_weight,
    conv_bc_bias,
    dt_bias,
    a_log,
    skip,
    norm_weight,
    w_out,
    lengths,
    request_group,
):
    tp_count, seq_count = lax.axis_size("tp"), lax.axis_size("seq")
    t, s = lax.axis_index("tp"), lax.axis_index("seq")
    chips = seq_count // 2
    p, c = s // 2, s % 2
    tok_dev, width = tokens.shape
    rows = w_zx.shape[0]
    inner_all = w_zx.shape[1] // 2
    pair = conv_x_weight.shape[1]
    inner = pair // 2
    heads = dt_bias.shape[0] // 2
    head_width = inner // heads
    bc_width = w_bc.shape[1]
    state = bc_width // 2
    tok = 2 * tok_dev
    groups = tok // GROUP
    half = groups // 2
    conv = inner + bc_width
    prompts = lengths.shape[0]
    x_width = 2 * inner + bc_width + LANES
    depth = tp_count * rows

    ints = jnp.concatenate([jnp.stack([t, p, c]).astype(jnp.int32), lengths, request_group])
    floats = jnp.concatenate([dt_bias, a_log, skip])
    vecs = jnp.concatenate(
        [
            conv_x_weight,
            conv_x_bias[None, :],
            norm_weight[None, :],
            jnp.zeros((2, pair), F32),
            jnp.pad(conv_bc_weight, ((0, 0), (0, pair - bc_width))),
            jnp.pad(conv_bc_bias[None, :], ((0, 3), (0, pair - bc_width))),
        ],
        axis=0,
    )

    def packed(kernel, operands, specs, wide, name):
        return pl.pallas_call(
            functools.partial(kernel, tp_count),
            grid=(1,),
            out_shape=[sds((rows, wide), MM)] * tp_count,
            in_specs=specs,
            out_specs=[pl.BlockSpec((rows, wide), lambda i: (0, 0))] * tp_count,
            compiler_params=pltpu.CompilerParams(vmem_limit_bytes=VMEM_BYTES),
            name=name,
        )(*operands)

    def whole(x):
        return pl.BlockSpec(x.shape, lambda i: (0, 0))

    def sent_over_tp(pieces):
        return [pieces[0]] + [shift(x, j) for j, x in enumerate(pieces) if j]

    def assembled(kernel, outs, pieces, name):
        return call(
            functools.partial(kernel, tp_count), outs, [SMEM] + [VMEM] * tp_count, name=name
        )(ints, *pieces)

    def together(*lists):
        joined = lax.optimization_barrier(tuple(tuple(one) for one in lists))
        return [list(one) for one in joined]

    x_sent = packed(
        pack_x_kernel,
        (ints, w_zx, w_bc, w_dt),
        [SMEM, pl.BlockSpec((rows, inner_all), lambda i: (0, 1)), whole(w_bc), whole(w_dt)],
        x_width,
        "pack_x",
    )
    x_got = sent_over_tp(x_sent)

    out_near = plane_near(w_out.astype(MM))
    keys = list(out_near)
    other = flip(tokens, 1)
    first_tok = jnp.where(c == 0, tokens, other)
    second_tok = jnp.where(c == 0, other, tokens)
    out_got, (first_tok, second_tok) = together(
        [out_near[k][0] for k in keys], [first_tok, second_tok]
    )
    out_blocks = plane_far({k: (piece,) for k, piece in zip(keys, out_got)})
    out_own = [piece for k in out_blocks for piece in out_blocks[k]]
    out_where = tuple(
        (k, i * (w_out.shape[0] // 2), out_blocks[k][i].shape[0])
        for k in out_blocks
        for i in range(len(out_blocks[k]))
    )
    x_got, out_own = together(x_got, out_own)
    (x_block,) = assembled(assemble_x_kernel, [sds((depth, x_width), MM)], x_got, "assemble_x")

    before = lax.ppermute(
        second_tok[tok_dev - HALO :], "seq", [(i, i + 2) for i in range(seq_count - 2)]
    )
    all_tok = jnp.concatenate([before, first_tok, second_tok], axis=0)

    ((x_block, all_tok, ints, floats, vecs),) = together([x_block, all_tok, ints, floats, vecs])
    near = plane_near(x_block)
    z_sent = packed(
        pack_z_kernel,
        (ints, w_zx),
        [SMEM, pl.BlockSpec((rows, inner_all), lambda i: (0, 0))],
        2 * inner,
        "pack_z",
    )
    z_got = sent_over_tp(z_sent)
    own_other = flip(x_block, 1)
    joined_rows = sum(size for _, _, size in out_where)
    (out_joined,) = call(
        join_kernel,
        [sds((joined_rows, w_out.shape[1]), MM)],
        [VMEM] * len(out_own),
        name="join_out",
    )(*out_own)
    blocks, z_got, (own_other, out_joined) = together(
        [near[k][0] for k in near if k], z_got, [own_other, out_joined]
    )

    out_all = lax.all_gather(
        out_joined, "seq", axis_index_groups=[[i, i + 1] for i in range(0, seq_count, 2)]
    )
    far = plane_far({k: (block,) for k, block in zip(near, [x_block] + blocks)})
    z_mine, z_theirs = assembled(
        assemble_z_kernel, [sds((depth, inner), MM)] * 2, z_got, "assemble_z"
    )
    (z_block,) = call(
        merge_kernel, [sds((2 * depth, inner), MM)], [SMEM, VMEM, VMEM], name="merge_z"
    )(ints, z_mine, flip(z_theirs, 1))
    near_other = [flip(far[k][0], 1) for k in near if k]
    order = [k for k in far if k not in near]
    x_far, near_other, (z_block,) = together(
        [piece for k in order for piece in far[k]], near_other, [z_block]
    )
    far_other = [flip(piece, 1) for piece in x_far]
    far_other, (z_block,) = together(far_other, [z_block])
    where = [(k, 0) for k in near] + [(k, i * depth // 2) for k in order for i in range(2)]
    where = tuple((k, other, first) for other in range(2) for k, first in where)
    x_pieces = [far[k][0] for k in near] + x_far + [own_other] + near_other + far_other

    def front(side, where, operands):
        outs = [
            sds((tok_dev, inner), MM),
            sds((tok_dev, bc_width), MM),
            sds((tok_dev, LANES), F32),
            sds((tok_dev, LANES), F32),
            sds((half, inner + TERMS, state), MM),
        ]
        scratch = [pltpu.VMEM((2, HALO + GROUP, conv + LANES), F32)]
        if where:
            outs.append(sds((width, conv + LANES), MM))
            scratch.append(pltpu.SemaphoreType.DMA((2 * len(where),)))
        return call(
            functools.partial(
                front_kernel, (inner, bc_width, heads, prompts, where, depth, groups, side)
            ),
            outs,
            [SMEM, SMEM, VMEM, VMEM] + ([ANY] * len(where) if where else [VMEM]),
            scratch,
            flops=0,
            moved=1_000_000,
            name="front_%d" % side,
        )(ints, floats, vecs, all_tok, *operands)

    z_near = plane_near(z_block)
    *first, weights = front(0, where, x_pieces)
    ((*first, weights),) = together([*first, weights])

    low_near = plane_near(first[4])
    second = front(1, (), [weights])
    second, lows, z_blocks = together(
        second, [low_near[k][0] for k in low_near], [z_near[k][0] for k in z_near]
    )
    z_far = plane_far({k: (block,) for k, block in zip(z_near, z_blocks)})
    z_where = tuple((k, i * depth) for k in z_far for i in range(len(z_far[k])))
    z_pieces = [piece for k in z_far for piece in z_far[k]]

    def mid(side, xs, bc, cum, step, message):
        return call(
            functools.partial(mid_kernel, (inner, heads, prompts, groups, side)),
            [sds((tok_dev, inner), F32)] * 2,
            [SMEM, SMEM] + [VMEM] * 4,
            flops=2 * tok_dev * GROUP * inner,
            moved=1_000_000,
            name="mid_%d" % side,
        )(ints, floats, xs, bc, cum, step)

    parts = {k: (block, None) for k, block in zip(low_near, lows)}
    high_near = plane_near(second[4])
    first_y = mid(0, *first)
    highs, first_y = together([high_near[k][0] for k in parts], first_y)
    parts = {k: (parts[k][0], high) for k, high in zip(parts, highs)}
    for k in range(1, chips):
        if k not in parts:
            low, high = k & -k, 1 << (k.bit_length() - 1)
            parts[k] = (flip(parts[k ^ low][0], 2 * low), flip(parts[k ^ high][1], 2 * high))
    parts = [piece for k in range(chips) for piece in parts[k]]

    y = [first_y, mid(1, *second)]
    gate = call(
        functools.partial(gate_kernel, (inner, z_where, 2 * depth)),
        [sds((tok_dev, inner), F32)] * 2,
        [SMEM, VMEM] + [ANY] * len(z_where),
        [pltpu.VMEM((width, inner), MM), pltpu.SemaphoreType.DMA((len(z_where),))],
        flops=tok * width * inner // 4,
        moved=1_000_000,
        name="gate",
    )(ints, all_tok, *z_pieces)
    sides = [*y[0], gate[0], first[1], *y[1], gate[1], second[1]]
    parts, sides = together(parts, sides)

    per = request_group.shape[0] // seq_count
    sent = sds((tok_dev, inner + LANES), MM)
    theirs, low_states, asked, own_asked = call(
        functools.partial(back_kernel, (inner, heads, prompts, groups, len(parts), per)),
        [
            sent,
            sds((groups, inner, state), MM),
            sds((per, inner, state), MM),
            sds((per, inner, state), F32),
        ],
        [SMEM, VMEM] + [ANY] * len(parts) + [VMEM] * 8,
        [
            pltpu.VMEM((chips * groups, inner + TERMS, state), MM),
            pltpu.VMEM((chips * groups + 1, inner, state), F32),
            pltpu.SemaphoreType.DMA((len(parts),)),
        ],
        flops=2 * tok * state * inner,
        moved=8_000_000,
        name="back",
    )(ints, vecs, *parts, *sides)
    theirs = flip(theirs, 1)
    (mine,) = call(
        functools.partial(back_own_kernel, (inner, heads, groups)),
        [sent],
        [SMEM] + [VMEM] * 10,
        flops=2 * tok_dev * state * inner,
        moved=4_000_000,
        name="back_own",
    )(ints, vecs, low_states, *sides)

    out_width = seq_count * w_out.shape[1]
    piece = tok_dev // tp_count
    ahead = tp_count - 2

    def project_out(chosen, outs, where, operands):
        scratch, extra = [], []
        outs = [
            sds((piece, out_width // 2 + side * LANES), kind) for kind in outs for side in range(2)
        ]
        if where:
            extra = [sds((2 * inner, out_width), MM)]
            scratch = [pltpu.SemaphoreType.DMA((2 * len(where),))]
        return call(
            functools.partial(out_kernel, (inner, tp_count, chosen, where)),
            outs + extra,
            [SMEM, VMEM, VMEM, ANY if where else VMEM],
            scratch,
            flops=len(outs) * piece * inner * out_width,
            moved=1_000_000,
            name="out_%d" % len(chosen),
        )(ints, mine, theirs, *operands)

    *sent_first, out_weights = project_out(tuple(range(ahead)), [MM] * ahead, out_where, [out_all])
    *near_block, own_low, own_high = project_out((ahead, ahead + 1), [MM, F32], (), [out_weights])
    halves = [*sent_first, *near_block]
    own, received, at_ends = sum_over_tp(
        ints, [halves[i : i + 2] for i in range(0, len(halves), 2)], [own_low, own_high]
    )
    received = [half for block in received for half in block]
    (mixed,) = call(
        functools.partial(final_kernel, float(inner_all), at_ends),
        [sds((piece, out_width), MM)],
        [SMEM] + [VMEM] * (2 + len(received)),
        name="final",
    )(ints, *own, *received)

    other_asked = flip(asked, 1).astype(F32)
    states = jnp.where(
        c == 0,
        jnp.concatenate([own_asked, other_asked], axis=1),
        jnp.concatenate([other_asked, own_asked], axis=1),
    )
    return (mixed, states.reshape(per, 2 * heads, head_width, state))


def solution(mesh):
    return jax.shard_map(
        on_device,
        mesh=mesh,
        in_specs=(
            P("seq", None),
            P(("seq", "tp"), None),
            P(("seq", "tp"), None),
            P(("seq", "tp"), None),
            P(None, "tp"),
            P("tp"),
            P(),
            P(),
            P("tp"),
            P("tp"),
            P("tp"),
            P("tp"),
            P("tp", "seq"),
            P(),
            P(),
        ),
        out_specs=(P(("seq", "tp"), None), P("seq", "tp", None, None)),
        check_vma=False,
    )
```

```python
import functools

import jax
import jax.numpy as jnp
from jax import lax
from jax.experimental import pallas as pl
from jax.experimental.pallas import tpu as pltpu
from jax.sharding import PartitionSpec as P

GROUP = 256
HALO = 16
LANES = 128
TERMS = 32
MM = jnp.bfloat16
F32 = jnp.float32
NEGATIVE = -1e30
sds = jax.ShapeDtypeStruct
VMEM_BYTES = 20 * 1024 * 1024

epsilon = 1e-05

ANY = pl.BlockSpec(memory_space=pl.ANY)
SMEM = pl.BlockSpec(memory_space=pltpu.SMEM)
VMEM = pl.BlockSpec(memory_space=pltpu.VMEM)


def flip(x, bits):
    count = lax.axis_size("seq")
    return lax.ppermute(x, "seq", [(i, i ^ bits) for i in range(count)])


def shift(x, by):
    count = lax.axis_size("tp")
    return lax.ppermute(x, "tp", [(i, (i + by) % count) for i in range(count)])


def plane_near(block):
    chips = lax.axis_size("seq") // 2
    return {k: (block if k == 0 else flip(block, 2 * k),) for k in range(chips) if k & (k - 1) == 0}


def plane_far(blocks):
    chips = lax.axis_size("seq") // 2
    blocks = dict(blocks)

    def half(k, side):
        if len(blocks[k]) == 2:
            return blocks[k][side]
        size = blocks[k][0].shape[0] // 2
        return blocks[k][0][side * size : (side + 1) * size]

    for k in range(1, chips):
        if k not in blocks:
            low = k & -k
            high = 1 << (k.bit_length() - 1)
            first = flip(half(k ^ low, 0), 2 * low)
            second = flip(half(k ^ high, 1), 2 * high)
            blocks[k] = (first, second)
    return blocks


def call(kernel, outs, in_specs, scratch=(), flops=0, moved=0, out_specs=None, name=None):
    return pl.pallas_call(
        kernel,
        out_shape=outs,
        in_specs=in_specs,
        out_specs=[VMEM] * len(outs) if out_specs is None else out_specs,
        scratch_shapes=list(scratch),
        compiler_params=pltpu.CompilerParams(vmem_limit_bytes=VMEM_BYTES),
        cost_estimate=pl.CostEstimate(flops=flops, bytes_accessed=moved, transcendentals=0),
        name=name,
    )


def split_terms(x):
    high = x.astype(MM).astype(F32)
    rest = x - high
    mid = rest.astype(MM).astype(F32)
    return high, mid, (rest - mid).astype(MM).astype(F32)


def silu(x):
    half = 0.5 * x
    return half + half * jnp.tanh(half)


def run_all(copies):
    for copy in copies:
        copy.start()
    for copy in copies:
        copy.wait()


def starts_of(position, ints):
    start, end = jnp.zeros_like(position), 0
    for i in range(ints.prompts):
        end = end + ints.ref[3 + i]
        start = jnp.where(position >= end, end, start)
    return start


class Ints:
    def __init__(self, ref, prompts):
        self.ref, self.prompts = ref, prompts
        self.t, self.p, self.c = ref[0], ref[1], ref[2]

    def wanted(self, i):
        return self.ref[3 + self.prompts + i]


def rows_at(first, size):
    return pl.ds(pl.multiple_of(first, 16), size)


def pack_x_kernel(tp_count, ints, w_ref, bc_ref, dt_ref, *outs):
    t = ints[0]
    pair = w_ref.shape[1] // tp_count
    inner = pair // 2
    bc_width = bc_ref.shape[1]
    heads = dt_ref.shape[1] // tp_count
    low_bc = bc_ref[...].astype(MM)
    for j, out in enumerate(outs):
        owner = lax.rem(t + j, tp_count)
        at = pl.multiple_of(owner * pair, LANES)
        out[:, :inner] = w_ref[:, pl.ds(at, inner)].astype(MM)
        out[:, inner : inner + bc_width] = low_bc
        steps = jnp.zeros((dt_ref.shape[0], heads), F32)
        for u in range(tp_count):
            steps = jnp.where(owner == u, dt_ref[:, u * heads : (u + 1) * heads], steps)
        steps = jnp.concatenate(
            [steps, jnp.zeros((dt_ref.shape[0], LANES - heads), F32)], axis=1
        )
        out[:, inner + bc_width : inner + bc_width + LANES] = steps.astype(MM)
        at = pl.multiple_of(owner * pair + inner, LANES)
        out[:, inner + bc_width + LANES :] = w_ref[:, pl.ds(at, inner)].astype(MM)


def pack_z_kernel(tp_count, ints, w_ref, *outs):
    pair = w_ref.shape[1] // tp_count
    for j, out in enumerate(outs):
        at = pl.multiple_of(lax.rem(ints[0] + j, tp_count) * pair, LANES)
        out[...] = w_ref[:, pl.ds(at, pair)].astype(MM)


def assemble_x_kernel(tp_count, ints, *refs):
    pieces, out = refs[:tp_count], refs[tp_count]
    rows = pieces[0].shape[0]
    for j, piece in enumerate(pieces):
        source = lax.rem(ints[0] + tp_count - j, tp_count)
        out[rows_at(source * rows, rows), :] = piece[...]


def assemble_z_kernel(tp_count, ints, *refs):
    pieces, (mine, theirs) = refs[:tp_count], refs[tp_count:]
    rows, inner = pieces[0].shape[0], mine.shape[1]
    c = ints[2]
    for j, piece in enumerate(pieces):
        at = rows_at(lax.rem(ints[0] + tp_count - j, tp_count) * rows, rows)
        mine[at, :] = piece[:, pl.ds(pl.multiple_of(c * inner, LANES), inner)]
        theirs[at, :] = piece[:, pl.ds(pl.multiple_of((1 - c) * inner, LANES), inner)]


def merge_kernel(ints, mine, theirs, out):
    rows = mine.shape[0]
    out[rows_at(ints[2] * rows, rows), :] = mine[...]
    out[rows_at((1 - ints[2]) * rows, rows), :] = theirs[...]


def lane_row(ref, first, count):
    lane = lax.broadcasted_iota(jnp.int32, (1, LANES), 1)
    row = jnp.zeros((1, LANES), F32)
    for i in range(count):
        row = jnp.where(lane == i, ref[first + i], row)
    return row


def front_kernel(sizes, ints_ref, floats, vecs, tok_ref, *refs):
    inner, bc_width, heads, prompts, where, depth, groups, side = sizes
    ints = Ints(ints_ref, prompts)
    c = ints.c
    conv = inner + bc_width
    state = bc_width // 2
    head_width = inner // heads
    half = groups // 2
    if where:
        pieces = refs[: len(where)]
        xs_ref, bc_ref, cum_ref, step_ref, message, weights, raw, sems = refs[len(where) :]
        start_x = pl.multiple_of(c * (conv + LANES), LANES)
        copies = []
        for piece, (k, other, first) in zip(pieces, where):
            core = 1 - c if other else c
            rows = rows_at(((ints.p ^ k) * 2 + core) * depth + first, piece.shape[0])
            for source, goal, size in ((start_x, 0, inner), (inner, inner, bc_width + LANES)):
                copies.append(
                    pltpu.make_async_copy(
                        piece.at[:, pl.ds(source, size)],
                        weights.at[rows, pl.ds(goal, size)],
                        sems.at[len(copies)],
                    )
                )
        run_all(copies)
    else:
        weights, xs_ref, bc_ref, cum_ref, step_ref, message, raw = refs
    taps = 4
    lower = (
        lax.broadcasted_iota(jnp.int32, (GROUP, GROUP), 0)
        >= lax.broadcasted_iota(jnp.int32, (GROUP, GROUP), 1)
    ).astype(F32)
    within = lax.broadcasted_iota(jnp.int32, (GROUP, LANES), 0)
    base = ints.p * (groups * GROUP) + side * half * GROUP
    all_heads = 2 * heads
    bias = lane_row(floats, c * heads, heads)
    rate = -jnp.exp(lane_row(floats, all_heads + c * heads, heads))

    def project(g):
        at = (side * half + g) * GROUP
        value = jnp.dot(
            tok_ref[at : at + GROUP + HALO, :], weights[...], preferred_element_type=F32
        )
        raw[g % 2, :, :conv] = value[:, :conv].astype(MM).astype(F32)
        raw[g % 2, :, conv:] = value[:, conv:]

    def one(g):
        rows = slice(g * GROUP, (g + 1) * GROUP)
        slot = g % 2
        first = base + g * GROUP
        position = first + within
        behind = position - starts_of(position, ints)
        keeps = [(behind >= lag).astype(F32) for lag in range(1, taps)]
        dt = raw[slot, HALO : HALO + GROUP, conv:]
        dt = jnp.where(c == 0, dt, pltpu.roll(dt, LANES - heads, 1)) + bias
        step = jnp.maximum(dt, 0.0) + jnp.log1p(jnp.exp(-jnp.abs(dt)))
        cum = jnp.dot(
            lower, step * rate, precision=lax.Precision.HIGHEST, preferred_element_type=F32
        )
        cum_ref[rows, :] = cum
        step_ref[rows, :] = step
        last = cum[GROUP - 1 : GROUP, :]
        start_last = starts_of(first + (GROUP - 1), ints)
        tail = jnp.where(position >= start_last, jnp.exp(last - cum), 0.0) * step
        for block in range(0, conv, LANES):
            lanes = slice(block, block + LANES)
            if block < inner:
                here = pl.ds(pl.multiple_of(c * inner + block, LANES), LANES)
                weight, offset = vecs[0:taps, here], vecs[taps : taps + 1, here]
            else:
                here = slice(block - inner, block - inner + LANES)
                weight, offset = vecs[8 : 8 + taps, here], vecs[8 + taps : 9 + taps, here]
            total = offset + raw[slot, HALO : HALO + GROUP, lanes] * weight[taps - 1 : taps]
            for lag in range(1, taps):
                term = raw[slot, HALO - lag : HALO - lag + GROUP, lanes] * keeps[lag - 1]
                total = total + term * weight[taps - 1 - lag : taps - lag]
            value = silu(total).astype(MM)
            if block < inner:
                xs_ref[rows, lanes] = value
            else:
                bc_ref[rows, here] = value
        b_wide = bc_ref[rows, :state].astype(F32)
        for h in range(0, heads, 2):
            weighted = jnp.concatenate(
                [(b_wide * tail[:, h + i : h + i + 1]).astype(MM) for i in range(2)], axis=1
            )
            both = lax.dot_general(
                xs_ref[rows, h * head_width : (h + 2) * head_width],
                weighted,
                (((0,), (0,)), ((), ())),
                preferred_element_type=F32,
            )
            at = h * head_width
            message[g, at : at + head_width, :] = both[:head_width, :state].astype(MM)
            at = at + head_width
            message[g, at : at + head_width, :] = both[head_width:, state:].astype(MM)
        spread = jnp.broadcast_to(jnp.exp(last), (8, LANES))
        diagonal = lax.broadcasted_iota(jnp.int32, (8, LANES), 0) == lax.broadcasted_iota(
            jnp.int32, (8, LANES), 1
        )
        gates = jnp.sum(jnp.where(diagonal, spread, 0.0), axis=1, keepdims=True)
        gates = jnp.where(start_last < first, jnp.broadcast_to(gates, (8, LANES)), 0.0)
        terms = jnp.concatenate(list(split_terms(gates)) + [jnp.zeros_like(gates)], axis=0)
        message[g, inner : inner + TERMS, :] = terms.astype(MM)

    project(0)
    for g in range(half):
        if g + 1 < half:
            project(g + 1)
        one(g)


def mid_kernel(sizes, ints_ref, floats, xs_ref, bc_ref, cum_ref, step_ref, y_ref, keep_ref):
    inner, heads, prompts, groups, side = sizes
    ints = Ints(ints_ref, prompts)
    state = bc_ref.shape[1] // 2
    head_width = inner // heads
    half = groups // 2
    base = ints.p * (groups * GROUP) + side * half * GROUP
    within_i = lax.broadcasted_iota(jnp.int32, (GROUP, GROUP), 0)
    within_j = lax.broadcasted_iota(jnp.int32, (GROUP, GROUP), 1)
    lane = lax.broadcasted_iota(jnp.int32, (GROUP, LANES), 1)
    skip_at = 4 * heads + ints.c * heads

    @pl.loop(0, half)
    def _(g):
        rows = rows_at(g * GROUP, GROUP)
        first = base + g * GROUP
        start = starts_of(first + within_i, ints)
        seen = (within_j <= within_i) & (first + within_j >= start)
        scores = lax.dot_general(
            bc_ref[rows, state:],
            bc_ref[rows, :state],
            (((1,), (1,)), ((), ())),
            preferred_element_type=F32,
        )
        cum = cum_ref[rows, :]
        cum_t = cum.T
        step_t = step_ref[rows, :].T
        keep = jnp.where(start[:, :LANES] < first, jnp.exp(cum), 0.0)
        for h in range(0, heads, 2):
            lanes = slice(h * head_width, (h + 2) * head_width)
            pair = xs_ref[rows, lanes]
            first_skip, second_skip = (floats[skip_at + h + i] for i in range(2))
            total = jnp.where(lane < head_width, first_skip, second_skip) * pair.astype(F32)
            for i in range(2):
                log_decay = cum[:, h + i : h + i + 1] - cum_t[h + i : h + i + 1, :]
                decay = jnp.exp(jnp.where(seen, log_decay, NEGATIVE))
                mix = (decay * scores * step_t[h + i : h + i + 1, :]).astype(MM)
                own = jnp.where((lane < head_width) == (i == 0), pair, jnp.zeros_like(pair))
                total = total + jnp.dot(mix, own, preferred_element_type=F32)
            y_ref[rows, lanes] = total
            keep_ref[rows, lanes] = jnp.where(
                lane < head_width, keep[:, h : h + 1], keep[:, h + 1 : h + 2]
            )


def gate_kernel(sizes, ints, tok_ref, *refs):
    inner, where, depth = sizes
    pieces = refs[: len(where)]
    low, high, weights, sems = refs[len(where) :]
    copies = []
    for i, (piece, (k, first)) in enumerate(zip(pieces, where)):
        rows = rows_at((ints[1] ^ k) * depth + first, piece.shape[0])
        copies.append(pltpu.make_async_copy(piece, weights.at[rows, :], sems.at[i]))
    run_all(copies)
    count = low.shape[0] // GROUP
    for side, out in enumerate((low, high)):

        @pl.loop(0, count)
        def _(g):
            row = (side * count + g) * GROUP + HALO
            value = jnp.dot(
                tok_ref[rows_at(row, GROUP), :], weights[...], preferred_element_type=F32
            )
            out[rows_at(g * GROUP, GROUP), :] = silu(value.astype(MM).astype(F32))


def gating(sizes, ints, low_states, vecs, side, y_ref, keep_ref, gate_ref, bc_ref, out):
    inner, heads, groups = sizes
    half = groups // 2
    state = bc_ref.shape[1] // 2
    lane = lax.broadcasted_iota(jnp.int32, (GROUP, LANES), 1)
    for g in range(half):
        rows = slice(g * GROUP, (g + 1) * GROUP)
        carried = lax.dot_general(
            bc_ref[rows, state:],
            low_states[side * half + g],
            (((1,), (1,)), ((), ())),
            preferred_element_type=F32,
        )
        squares = jnp.zeros((GROUP, LANES), F32)
        for at in range(0, inner, LANES):
            lanes = slice(at, at + LANES)
            y = y_ref[rows, lanes] + carried[:, lanes] * keep_ref[rows, lanes]
            gated = y * gate_ref[rows, lanes]
            squares = squares + gated * gated
            here = pl.ds(pl.multiple_of(ints[2] * inner + at, LANES), LANES)
            out[rows, lanes] = (gated * vecs[5:6, here]).astype(MM)
        total = jnp.broadcast_to(jnp.sum(squares, axis=1, keepdims=True), (GROUP, LANES))
        out[rows, inner:] = spread_terms(total).astype(MM)


def spread_terms(total):
    lane = lax.broadcasted_iota(jnp.int32, total.shape, 1)
    high, mid, low = split_terms(total)
    return jnp.where(lane == 0, high, jnp.where(lane == 1, mid, jnp.where(lane == 2, low, 0.0)))


def added_terms(ref, at):
    value = ref[:, at:].astype(F32)
    return jnp.broadcast_to(jnp.sum(value, axis=1, keepdims=True), value.shape)


def back_kernel(sizes, ints_ref, vecs, *refs):
    inner, heads, prompts, groups, n_pieces, per = sizes
    pieces = refs[:n_pieces]
    sides = (refs[n_pieces : n_pieces + 4], refs[n_pieces + 4 : n_pieces + 8])
    theirs, low_states, asked, own_asked, parts, states, sems = refs[n_pieces + 8 :]
    ints = Ints(ints_ref, prompts)
    p, c = ints.p, ints.c
    head_width = inner // heads
    half = groups // 2
    copies = []
    for i, piece in enumerate(pieces):
        k, side = i // 2, i % 2
        at = (p ^ k) * groups + side * half
        copies.append(pltpu.make_async_copy(piece, parts.at[pl.ds(at, half)], sems.at[i]))
    run_all(copies)
    blocks = parts.shape[0]
    states[0] = jnp.zeros(states.shape[1:], F32)

    @pl.loop(0, blocks)
    def _(b):
        terms = parts[b, inner : inner + TERMS, :].astype(F32)
        gates = terms[0:8] + terms[8:16] + terms[16:24]
        for h in range(heads):
            rows = slice(h * head_width, (h + 1) * head_width)
            states[b + 1, rows, :] = gates[h : h + 1, :] * states[b, rows, :] + parts[
                b, rows, :
            ].astype(F32)

    for g in range(groups):
        low_states[g] = states[p * groups + g].astype(MM)
    for side in range(2):

        @pl.when(c != side)
        def _():
            gating((inner, heads, groups), ints_ref, low_states, vecs, side, *sides[side], theirs)

    for i in range(per):
        own_asked[i] = states[ints.wanted((p * 2 + c) * per + i) + 1]
        asked[i] = states[ints.wanted((p * 2 + 1 - c) * per + i) + 1].astype(MM)


def back_own_kernel(sizes, ints_ref, vecs, low_states, *refs):
    sides = (refs[:4], refs[4:8])
    mine = refs[8]
    for side in range(2):

        @pl.when(ints_ref[2] == side)
        def _():
            gating(sizes, ints_ref, low_states, vecs, side, *sides[side], mine)


def block_order(tp_count):
    return [2, 1, 3, 0] if tp_count == 4 else list(range(1, tp_count)) + [0]


def out_kernel(sizes, ints, mine, theirs, *refs):
    inner, tp_count, chosen, where = sizes
    t, p, c = ints[0], ints[1], ints[2]
    if where:
        pieces = refs[: len(where)]
        outs = refs[len(where) : len(where) + 2 * len(chosen)]
        weights, sems = refs[len(where) + 2 * len(chosen) :]
        copies = []
        for i, (piece, (k, other, first)) in enumerate(zip(pieces, where)):
            rows, columns = piece.shape
            core = 1 - c if other else c
            at = pl.multiple_of(((p ^ k) * 2 + core) * columns, LANES)
            copies.append(
                pltpu.make_async_copy(
                    piece, weights.at[pl.ds(first, rows), pl.ds(at, columns)], sems.at[i]
                )
            )
        run_all(copies)
    else:
        weights, outs = refs[0], refs[1:]
    width = weights.shape[1]
    piece_rows = mine.shape[0] // tp_count
    own_rows = rows_at(c * inner, inner)
    other_rows = rows_at((1 - c) * inner, inner)
    for i, low, high in zip(chosen, outs[::2], outs[1::2]):
        rows = rows_at(lax.rem(t + block_order(tp_count)[i], tp_count) * piece_rows, piece_rows)
        sums = jnp.sum(
            mine[rows, inner:].astype(F32) + theirs[rows, inner:].astype(F32), axis=1, keepdims=True
        )
        sums = spread_terms(jnp.broadcast_to(sums, (piece_rows, LANES)))
        high[:, width // 2 :] = sums.astype(high.dtype)
        for at in range(0, width, width // 4):
            lanes = slice(at, at + width // 4)
            value = jnp.dot(mine[rows, :inner], weights[own_rows, lanes], preferred_element_type=F32)
            value = value + jnp.dot(
                theirs[rows, :inner], weights[other_rows, lanes], preferred_element_type=F32
            )
            out, first = (low, at) if at < width // 2 else (high, at - width // 2)
            out[:, first : first + width // 4] = value.astype(out.dtype)


def add_kernel(width, got, own, out):
    out[:, :width] = (got[:, :width].astype(F32) + own[:, :width].astype(F32)).astype(MM)
    if out.shape[1] > width:
        out[:, width:] = spread_terms(added_terms(got, width) + added_terms(own, width)).astype(MM)


def final_kernel(channels, *refs):
    own, received, out = refs[:2], refs[2:-1], refs[-1]
    half = out.shape[1] // 2
    squares = added_terms(own[1], half)
    for got in received[1::2]:
        squares = squares + added_terms(got, half)
    factor = lax.rsqrt(squares[:, :1] / channels + epsilon)
    for side in range(2):
        total = own[side][:, :half]
        for got in received[side::2]:
            total = total + got[:, :half].astype(F32)
        out[:, side * half : (side + 1) * half] = (total * factor).astype(out.dtype)


def sum_over_tp(blocks, own):
    tp_count = lax.axis_size("tp")
    if tp_count != 4:
        return own, [[shift(x, j + 1) for x in block] for j, block in enumerate(blocks)]

    def add(got, x, name):
        kernel = functools.partial(add_kernel, own[0].shape[1])
        return call(kernel, [sds(x.shape, MM)], [VMEM] * 2, moved=100_000, name=name)(got, x)[0]

    (far_low, far_high), (next_low, next_high), (last_low, last_high) = blocks
    came_low, came_high = shift(far_low, 1), shift(far_high, 3)
    from_last_high, from_next_low = shift(next_high, 1), shift(last_low, 3)
    came_low, came_high, next_low, last_high, *own = lax.optimization_barrier(
        (came_low, came_high, next_low, last_high, *own)
    )
    from_last_low = shift(add(came_low, next_low, "add_low"), 1)
    from_next_high = shift(add(came_high, last_high, "add_high"), 3)
    return own, [[from_last_low, from_last_high], [from_next_low, from_next_high]]


def on_device(
    tokens,
    w_zx,
    w_dt,
    w_bc,
    conv_x_weight,
    conv_x_bias,
    conv_bc_weight,
    conv_bc_bias,
    dt_bias,
    a_log,
    skip,
    norm_weight,
    w_out,
    lengths,
    request_group,
):
    tp_count, seq_count = lax.axis_size("tp"), lax.axis_size("seq")
    t, s = lax.axis_index("tp"), lax.axis_index("seq")
    chips = seq_count // 2
    p, c = s // 2, s % 2
    tok_dev, width = tokens.shape
    rows = w_zx.shape[0]
    inner_all = w_zx.shape[1] // 2
    pair = conv_x_weight.shape[1]
    inner = pair // 2
    heads = dt_bias.shape[0] // 2
    head_width = inner // heads
    bc_width = w_bc.shape[1]
    state = bc_width // 2
    tok = 2 * tok_dev
    groups = tok // GROUP
    half = groups // 2
    conv = inner + bc_width
    prompts = lengths.shape[0]
    x_width = 2 * inner + bc_width + LANES
    depth = tp_count * rows

    ints = jnp.concatenate([jnp.stack([t, p, c]).astype(jnp.int32), lengths, request_group])
    floats = jnp.concatenate([dt_bias, a_log, skip])
    vecs = jnp.concatenate(
        [
            conv_x_weight,
            conv_x_bias[None, :],
            norm_weight[None, :],
            jnp.zeros((2, pair), F32),
            jnp.pad(conv_bc_weight, ((0, 0), (0, pair - bc_width))),
            jnp.pad(conv_bc_bias[None, :], ((0, 3), (0, pair - bc_width))),
        ],
        axis=0,
    )

    def packed(kernel, operands, specs, wide, name):
        return pl.pallas_call(
            functools.partial(kernel, tp_count),
            grid=(1,),
            out_shape=[sds((rows, wide), MM)] * tp_count,
            in_specs=specs,
            out_specs=[pl.BlockSpec((rows, wide), lambda i: (0, 0))] * tp_count,
            compiler_params=pltpu.CompilerParams(vmem_limit_bytes=VMEM_BYTES),
            name=name,
        )(*operands)

    def whole(x):
        return pl.BlockSpec(x.shape, lambda i: (0, 0))

    def sent_over_tp(pieces):
        return [pieces[0]] + [shift(x, j) for j, x in enumerate(pieces) if j]

    def assembled(kernel, outs, pieces, name):
        return call(
            functools.partial(kernel, tp_count), outs, [SMEM] + [VMEM] * tp_count, name=name
        )(ints, *pieces)

    def together(*lists):
        joined = lax.optimization_barrier(tuple(tuple(one) for one in lists))
        return [list(one) for one in joined]

    x_sent = packed(
        pack_x_kernel,
        (ints, w_zx, w_bc, w_dt),
        [SMEM, pl.BlockSpec((rows, inner_all), lambda i: (0, 1)), whole(w_bc), whole(w_dt)],
        x_width,
        "pack_x",
    )
    x_got = sent_over_tp(x_sent)

    out_near = plane_near(w_out.astype(MM))
    keys = list(out_near)
    other = flip(tokens, 1)
    first_tok = jnp.where(c == 0, tokens, other)
    second_tok = jnp.where(c == 0, other, tokens)
    out_got, (first_tok, second_tok) = together(
        [out_near[k][0] for k in keys], [first_tok, second_tok]
    )
    out_blocks = plane_far({k: (piece,) for k, piece in zip(keys, out_got)})
    out_own = [piece for k in out_blocks for piece in out_blocks[k]]
    out_where = [
        (k, 0, i * (w_out.shape[0] // 2)) for k in out_blocks for i in range(len(out_blocks[k]))
    ]
    x_got, out_own = together(x_got, out_own)
    (x_block,) = assembled(assemble_x_kernel, [sds((depth, x_width), MM)], x_got, "assemble_x")

    before = lax.ppermute(
        second_tok[tok_dev - HALO :], "seq", [(i, i + 2) for i in range(seq_count - 2)]
    )
    all_tok = jnp.concatenate([before, first_tok, second_tok], axis=0)

    ((x_block, all_tok, ints, floats, vecs),) = together([x_block, all_tok, ints, floats, vecs])
    near = plane_near(x_block)
    z_sent = packed(
        pack_z_kernel,
        (ints, w_zx),
        [SMEM, pl.BlockSpec((rows, inner_all), lambda i: (0, 0))],
        2 * inner,
        "pack_z",
    )
    z_got = sent_over_tp(z_sent)
    own_other = flip(x_block, 1)
    blocks, z_got, (own_other,) = together(
        [near[k][0] for k in near if k], z_got, [own_other]
    )
    far = plane_far({k: (block,) for k, block in zip(near, [x_block] + blocks)})
    z_mine, z_theirs = assembled(
        assemble_z_kernel, [sds((depth, inner), MM)] * 2, z_got, "assemble_z"
    )
    (z_block,) = call(
        merge_kernel, [sds((2 * depth, inner), MM)], [SMEM, VMEM, VMEM], name="merge_z"
    )(ints, z_mine, flip(z_theirs, 1))
    near_other = [flip(far[k][0], 1) for k in near if k]
    order = [k for k in far if k not in near]
    x_far, near_other, (z_block,) = together(
        [piece for k in order for piece in far[k]], near_other, [z_block]
    )
    far_other = [flip(piece, 1) for piece in x_far]
    far_other, (z_block,) = together(far_other, [z_block])
    where = [(k, 0) for k in near] + [(k, i * depth // 2) for k in order for i in range(2)]
    where = tuple((k, other, first) for other in range(2) for k, first in where)
    x_pieces = [far[k][0] for k in near] + x_far + [own_other] + near_other + far_other

    def front(side, where, operands):
        outs = [
            sds((tok_dev, inner), MM),
            sds((tok_dev, bc_width), MM),
            sds((tok_dev, LANES), F32),
            sds((tok_dev, LANES), F32),
            sds((half, inner + TERMS, state), MM),
        ]
        scratch = [pltpu.VMEM((2, HALO + GROUP, conv + LANES), F32)]
        if where:
            outs.append(sds((width, conv + LANES), MM))
            scratch.append(pltpu.SemaphoreType.DMA((2 * len(where),)))
        return call(
            functools.partial(
                front_kernel, (inner, bc_width, heads, prompts, where, depth, groups, side)
            ),
            outs,
            [SMEM, SMEM, VMEM, VMEM] + ([ANY] * len(where) if where else [VMEM]),
            scratch,
            flops=0,
            moved=1_000_000,
            name="front_%d" % side,
        )(ints, floats, vecs, all_tok, *operands)

    z_near = plane_near(z_block)
    *first, weights = front(0, where, x_pieces)
    ((*first, weights),) = together([*first, weights])

    low_near = plane_near(first[4])
    second = front(1, (), [weights])
    out_other = [flip(piece, 1) for piece in out_own]
    second, lows, z_blocks, out_other = together(
        second,
        [low_near[k][0] for k in low_near],
        [z_near[k][0] for k in z_near],
        out_other,
    )
    out_pieces = out_own + out_other
    out_where = tuple(out_where + [(k, 1, first_row) for k, _, first_row in out_where])
    z_far = plane_far({k: (block,) for k, block in zip(z_near, z_blocks)})
    z_where = tuple((k, i * depth) for k in z_far for i in range(len(z_far[k])))
    z_pieces = [piece for k in z_far for piece in z_far[k]]

    def mid(side, xs, bc, cum, step, message):
        return call(
            functools.partial(mid_kernel, (inner, heads, prompts, groups, side)),
            [sds((tok_dev, inner), F32)] * 2,
            [SMEM, SMEM] + [VMEM] * 4,
            flops=2 * tok_dev * GROUP * inner,
            moved=1_000_000,
            name="mid_%d" % side,
        )(ints, floats, xs, bc, cum, step)

    parts = {k: (block, None) for k, block in zip(low_near, lows)}
    high_near = plane_near(second[4])
    first_y = mid(0, *first)
    highs, first_y = together([high_near[k][0] for k in parts], first_y)
    parts = {k: (parts[k][0], high) for k, high in zip(parts, highs)}
    for k in range(1, chips):
        if k not in parts:
            low, high = k & -k, 1 << (k.bit_length() - 1)
            parts[k] = (flip(parts[k ^ low][0], 2 * low), flip(parts[k ^ high][1], 2 * high))
    parts = [piece for k in range(chips) for piece in parts[k]]

    y = [first_y, mid(1, *second)]
    gate = call(
        functools.partial(gate_kernel, (inner, z_where, 2 * depth)),
        [sds((tok_dev, inner), F32)] * 2,
        [SMEM, VMEM] + [ANY] * len(z_where),
        [pltpu.VMEM((width, inner), MM), pltpu.SemaphoreType.DMA((len(z_where),))],
        flops=tok * width * inner // 4,
        moved=1_000_000,
        name="gate",
    )(ints, all_tok, *z_pieces)
    sides = [*y[0], gate[0], first[1], *y[1], gate[1], second[1]]
    parts, sides = together(parts, sides)

    per = request_group.shape[0] // seq_count
    sent = sds((tok_dev, inner + LANES), MM)
    theirs, low_states, asked, own_asked = call(
        functools.partial(back_kernel, (inner, heads, prompts, groups, len(parts), per)),
        [
            sent,
            sds((groups, inner, state), MM),
            sds((per, inner, state), MM),
            sds((per, inner, state), F32),
        ],
        [SMEM, VMEM] + [ANY] * len(parts) + [VMEM] * 8,
        [
            pltpu.VMEM((chips * groups, inner + TERMS, state), MM),
            pltpu.VMEM((chips * groups + 1, inner, state), F32),
            pltpu.SemaphoreType.DMA((len(parts),)),
        ],
        flops=2 * tok * state * inner,
        moved=8_000_000,
        name="back",
    )(ints, vecs, *parts, *sides)
    theirs = flip(theirs, 1)
    (mine,) = call(
        functools.partial(back_own_kernel, (inner, heads, groups)),
        [sent],
        [SMEM] + [VMEM] * 10,
        flops=2 * tok_dev * state * inner,
        moved=4_000_000,
        name="back_own",
    )(ints, vecs, low_states, *sides)

    out_width = seq_count * w_out.shape[1]
    piece = tok_dev // tp_count
    ahead = 1 if tp_count == 4 else tp_count - 2

    def project_out(chosen, outs, where, operands):
        scratch, extra = [], []
        outs = [
            sds((piece, out_width // 2 + side * LANES), kind) for kind in outs for side in range(2)
        ]
        if where:
            extra = [sds((2 * inner, out_width), MM)]
            scratch = [pltpu.SemaphoreType.DMA((len(where),))]
        return call(
            functools.partial(out_kernel, (inner, tp_count, chosen, where)),
            outs + extra,
            [SMEM, VMEM, VMEM] + ([ANY] * len(where) if where else [VMEM]),
            scratch,
            flops=len(outs) * piece * inner * out_width,
            moved=1_000_000,
            name="out_%d" % len(chosen),
        )(ints, mine, theirs, *operands)

    *sent_first, out_weights = project_out(tuple(range(ahead)), [MM] * ahead, out_where, out_pieces)
    *sent_next, own_low, own_high = project_out(
        tuple(range(ahead, tp_count)), [MM] * (tp_count - 1 - ahead) + [F32], (), [out_weights]
    )
    halves = [*sent_first, *sent_next]
    own, received = sum_over_tp(
        [halves[i : i + 2] for i in range(0, len(halves), 2)], [own_low, own_high]
    )
    received = [half for block in received for half in block]
    (mixed,) = call(
        functools.partial(final_kernel, float(inner_all)),
        [sds((piece, out_width), MM)],
        [VMEM] * (2 + len(received)),
        name="final",
    )(*own, *received)

    other_asked = flip(asked, 1).astype(F32)
    states = jnp.where(
        c == 0,
        jnp.concatenate([own_asked, other_asked], axis=1),
        jnp.concatenate([other_asked, own_asked], axis=1),
    )
    return (mixed, states.reshape(per, 2 * heads, head_width, state))


def solution(mesh):
    return jax.shard_map(
        on_device,
        mesh=mesh,
        in_specs=(
            P("seq", None),
            P(("seq", "tp"), None),
            P(("seq", "tp"), None),
            P(("seq", "tp"), None),
            P(None, "tp"),
            P("tp"),
            P(),
            P(),
            P("tp"),
            P("tp"),
            P("tp"),
            P("tp"),
            P("tp", "seq"),
            P(),
            P(),
        ),
        out_specs=(P(("seq", "tp"), None), P("seq", "tp", None, None)),
        check_vma=False,
    )
```

```python
import functools

import jax
import jax.numpy as jnp
from jax import lax
from jax.experimental import pallas as pl
from jax.experimental.pallas import tpu as pltpu
from jax.sharding import PartitionSpec as P

GROUP = 256
HALO = 16
LANES = 128
TERMS = 32
MM = jnp.bfloat16
F32 = jnp.float32
NEGATIVE = -1e30
sds = jax.ShapeDtypeStruct
VMEM_BYTES = 20 * 1024 * 1024

epsilon = 1e-05

ANY = pl.BlockSpec(memory_space=pl.ANY)
SMEM = pl.BlockSpec(memory_space=pltpu.SMEM)
VMEM = pl.BlockSpec(memory_space=pltpu.VMEM)


def flip(x, bits):
    count = lax.axis_size("seq")
    return lax.ppermute(x, "seq", [(i, i ^ bits) for i in range(count)])


def shift(x, by):
    count = lax.axis_size("tp")
    return lax.ppermute(x, "tp", [(i, (i + by) % count) for i in range(count)])


def plane_near(block):
    chips = lax.axis_size("seq") // 2
    return {k: (block if k == 0 else flip(block, 2 * k),) for k in range(chips) if k & (k - 1) == 0}


def plane_far(blocks):
    chips = lax.axis_size("seq") // 2
    blocks = dict(blocks)

    def half(k, side):
        if len(blocks[k]) == 2:
            return blocks[k][side]
        size = blocks[k][0].shape[0] // 2
        return blocks[k][0][side * size : (side + 1) * size]

    for k in range(1, chips):
        if k not in blocks:
            low = k & -k
            high = 1 << (k.bit_length() - 1)
            first = flip(half(k ^ low, 0), 2 * low)
            second = flip(half(k ^ high, 1), 2 * high)
            blocks[k] = (first, second)
    return blocks


def call(kernel, outs, in_specs, scratch=(), flops=0, moved=0, out_specs=None, name=None):
    return pl.pallas_call(
        kernel,
        out_shape=outs,
        in_specs=in_specs,
        out_specs=[VMEM] * len(outs) if out_specs is None else out_specs,
        scratch_shapes=list(scratch),
        compiler_params=pltpu.CompilerParams(vmem_limit_bytes=VMEM_BYTES),
        cost_estimate=pl.CostEstimate(flops=flops, bytes_accessed=moved, transcendentals=0),
        name=name,
    )


def split_terms(x):
    high = x.astype(MM).astype(F32)
    rest = x - high
    mid = rest.astype(MM).astype(F32)
    return high, mid, (rest - mid).astype(MM).astype(F32)


def silu(x):
    half = 0.5 * x
    return half + half * jnp.tanh(half)


def run_all(copies):
    for copy in copies:
        copy.start()
    for copy in copies:
        copy.wait()


def starts_of(position, ints):
    start, end = jnp.zeros_like(position), 0
    for i in range(ints.prompts):
        end = end + ints.ref[3 + i]
        start = jnp.where(position >= end, end, start)
    return start


class Ints:
    def __init__(self, ref, prompts):
        self.ref, self.prompts = ref, prompts
        self.t, self.p, self.c = ref[0], ref[1], ref[2]

    def wanted(self, i):
        return self.ref[3 + self.prompts + i]


def rows_at(first, size):
    return pl.ds(pl.multiple_of(first, 16), size)


def pack_x_kernel(tp_count, ints, w_ref, bc_ref, dt_ref, *outs):
    t = ints[0]
    pair = w_ref.shape[1] // tp_count
    inner = pair // 2
    bc_width = bc_ref.shape[1]
    heads = dt_ref.shape[1] // tp_count
    low_bc = bc_ref[...].astype(MM)
    for j, out in enumerate(outs):
        owner = lax.rem(t + j, tp_count)
        at = pl.multiple_of(owner * pair, LANES)
        out[:, :inner] = w_ref[:, pl.ds(at, inner)].astype(MM)
        out[:, inner : inner + bc_width] = low_bc
        steps = jnp.zeros((dt_ref.shape[0], heads), F32)
        for u in range(tp_count):
            steps = jnp.where(owner == u, dt_ref[:, u * heads : (u + 1) * heads], steps)
        steps = jnp.concatenate(
            [steps, jnp.zeros((dt_ref.shape[0], LANES - heads), F32)], axis=1
        )
        out[:, inner + bc_width : inner + bc_width + LANES] = steps.astype(MM)
        at = pl.multiple_of(owner * pair + inner, LANES)
        out[:, inner + bc_width + LANES :] = w_ref[:, pl.ds(at, inner)].astype(MM)


def pack_z_kernel(tp_count, ints, w_ref, *outs):
    pair = w_ref.shape[1] // tp_count
    for j, out in enumerate(outs):
        at = pl.multiple_of(lax.rem(ints[0] + j, tp_count) * pair, LANES)
        out[...] = w_ref[:, pl.ds(at, pair)].astype(MM)


def assemble_x_kernel(tp_count, ints, *refs):
    pieces, out = refs[:tp_count], refs[tp_count]
    rows = pieces[0].shape[0]
    for j, piece in enumerate(pieces):
        source = lax.rem(ints[0] + tp_count - j, tp_count)
        out[rows_at(source * rows, rows), :] = piece[...]


def assemble_z_kernel(tp_count, ints, *refs):
    pieces, (mine, theirs) = refs[:tp_count], refs[tp_count:]
    rows, inner = pieces[0].shape[0], mine.shape[1]
    c = ints[2]
    for j, piece in enumerate(pieces):
        at = rows_at(lax.rem(ints[0] + tp_count - j, tp_count) * rows, rows)
        mine[at, :] = piece[:, pl.ds(pl.multiple_of(c * inner, LANES), inner)]
        theirs[at, :] = piece[:, pl.ds(pl.multiple_of((1 - c) * inner, LANES), inner)]


def merge_kernel(ints, mine, theirs, out):
    rows = mine.shape[0]
    out[rows_at(ints[2] * rows, rows), :] = mine[...]
    out[rows_at((1 - ints[2]) * rows, rows), :] = theirs[...]


def lane_row(ref, first, count):
    lane = lax.broadcasted_iota(jnp.int32, (1, LANES), 1)
    row = jnp.zeros((1, LANES), F32)
    for i in range(count):
        row = jnp.where(lane == i, ref[first + i], row)
    return row


def front_kernel(sizes, ints_ref, floats, vecs, tok_ref, *refs):
    inner, bc_width, heads, prompts, where, depth, groups, side = sizes
    ints = Ints(ints_ref, prompts)
    c = ints.c
    conv = inner + bc_width
    state = bc_width // 2
    head_width = inner // heads
    half = groups // 2
    if where:
        pieces = refs[: len(where)]
        xs_ref, bc_ref, cum_ref, step_ref, message, weights, raw, sems = refs[len(where) :]
        start_x = pl.multiple_of(c * (conv + LANES), LANES)
        copies = []
        for piece, (k, other, first) in zip(pieces, where):
            core = 1 - c if other else c
            rows = rows_at(((ints.p ^ k) * 2 + core) * depth + first, piece.shape[0])
            for source, goal, size in ((start_x, 0, inner), (inner, inner, bc_width + LANES)):
                copies.append(
                    pltpu.make_async_copy(
                        piece.at[:, pl.ds(source, size)],
                        weights.at[rows, pl.ds(goal, size)],
                        sems.at[len(copies)],
                    )
                )
        run_all(copies)
    else:
        weights, xs_ref, bc_ref, cum_ref, step_ref, message, raw = refs
    taps = 4
    lower = (
        lax.broadcasted_iota(jnp.int32, (GROUP, GROUP), 0)
        >= lax.broadcasted_iota(jnp.int32, (GROUP, GROUP), 1)
    ).astype(F32)
    within = lax.broadcasted_iota(jnp.int32, (GROUP, LANES), 0)
    base = ints.p * (groups * GROUP) + side * half * GROUP
    all_heads = 2 * heads
    bias = lane_row(floats, c * heads, heads)
    rate = -jnp.exp(lane_row(floats, all_heads + c * heads, heads))

    def project(g):
        at = (side * half + g) * GROUP
        value = jnp.dot(
            tok_ref[at : at + GROUP + HALO, :], weights[...], preferred_element_type=F32
        )
        raw[g % 2, :, :conv] = value[:, :conv].astype(MM).astype(F32)
        raw[g % 2, :, conv:] = value[:, conv:]

    def one(g):
        rows = slice(g * GROUP, (g + 1) * GROUP)
        slot = g % 2
        first = base + g * GROUP
        position = first + within
        behind = position - starts_of(position, ints)
        keeps = [(behind >= lag).astype(F32) for lag in range(1, taps)]
        dt = raw[slot, HALO : HALO + GROUP, conv:]
        dt = jnp.where(c == 0, dt, pltpu.roll(dt, LANES - heads, 1)) + bias
        step = jnp.maximum(dt, 0.0) + jnp.log1p(jnp.exp(-jnp.abs(dt)))
        cum = jnp.dot(
            lower, step * rate, precision=lax.Precision.HIGHEST, preferred_element_type=F32
        )
        cum_ref[rows, :] = cum
        step_ref[rows, :] = step
        last = cum[GROUP - 1 : GROUP, :]
        start_last = starts_of(first + (GROUP - 1), ints)
        tail = jnp.where(position >= start_last, jnp.exp(last - cum), 0.0) * step
        for block in range(0, conv, LANES):
            lanes = slice(block, block + LANES)
            if block < inner:
                here = pl.ds(pl.multiple_of(c * inner + block, LANES), LANES)
                weight, offset = vecs[0:taps, here], vecs[taps : taps + 1, here]
            else:
                here = slice(block - inner, block - inner + LANES)
                weight, offset = vecs[8 : 8 + taps, here], vecs[8 + taps : 9 + taps, here]
            total = offset + raw[slot, HALO : HALO + GROUP, lanes] * weight[taps - 1 : taps]
            for lag in range(1, taps):
                term = raw[slot, HALO - lag : HALO - lag + GROUP, lanes] * keeps[lag - 1]
                total = total + term * weight[taps - 1 - lag : taps - lag]
            value = silu(total).astype(MM)
            if block < inner:
                xs_ref[rows, lanes] = value
            else:
                bc_ref[rows, here] = value
        b_wide = bc_ref[rows, :state].astype(F32)
        for h in range(0, heads, 2):
            weighted = jnp.concatenate(
                [(b_wide * tail[:, h + i : h + i + 1]).astype(MM) for i in range(2)], axis=1
            )
            both = lax.dot_general(
                xs_ref[rows, h * head_width : (h + 2) * head_width],
                weighted,
                (((0,), (0,)), ((), ())),
                preferred_element_type=F32,
            )
            at = h * head_width
            message[g, at : at + head_width, :] = both[:head_width, :state].astype(MM)
            at = at + head_width
            message[g, at : at + head_width, :] = both[head_width:, state:].astype(MM)
        spread = jnp.broadcast_to(jnp.exp(last), (8, LANES))
        diagonal = lax.broadcasted_iota(jnp.int32, (8, LANES), 0) == lax.broadcasted_iota(
            jnp.int32, (8, LANES), 1
        )
        gates = jnp.sum(jnp.where(diagonal, spread, 0.0), axis=1, keepdims=True)
        gates = jnp.where(start_last < first, jnp.broadcast_to(gates, (8, LANES)), 0.0)
        terms = jnp.concatenate(list(split_terms(gates)) + [jnp.zeros_like(gates)], axis=0)
        message[g, inner : inner + TERMS, :] = terms.astype(MM)

    project(0)
    for g in range(half):
        if g + 1 < half:
            project(g + 1)
        one(g)


def mid_kernel(sizes, ints_ref, floats, xs_ref, bc_ref, cum_ref, step_ref, y_ref, keep_ref):
    inner, heads, prompts, groups, side = sizes
    ints = Ints(ints_ref, prompts)
    state = bc_ref.shape[1] // 2
    head_width = inner // heads
    half = groups // 2
    base = ints.p * (groups * GROUP) + side * half * GROUP
    within_i = lax.broadcasted_iota(jnp.int32, (GROUP, GROUP), 0)
    within_j = lax.broadcasted_iota(jnp.int32, (GROUP, GROUP), 1)
    lane = lax.broadcasted_iota(jnp.int32, (GROUP, LANES), 1)
    skip_at = 4 * heads + ints.c * heads

    @pl.loop(0, half)
    def _(g):
        rows = rows_at(g * GROUP, GROUP)
        first = base + g * GROUP
        start = starts_of(first + within_i, ints)
        seen = (within_j <= within_i) & (first + within_j >= start)
        scores = lax.dot_general(
            bc_ref[rows, state:],
            bc_ref[rows, :state],
            (((1,), (1,)), ((), ())),
            preferred_element_type=F32,
        )
        cum = cum_ref[rows, :]
        cum_t = cum.T
        step_t = step_ref[rows, :].T
        keep = jnp.where(start[:, :LANES] < first, jnp.exp(cum), 0.0)
        for h in range(0, heads, 2):
            lanes = slice(h * head_width, (h + 2) * head_width)
            pair = xs_ref[rows, lanes]
            first_skip, second_skip = (floats[skip_at + h + i] for i in range(2))
            total = jnp.where(lane < head_width, first_skip, second_skip) * pair.astype(F32)
            for i in range(2):
                log_decay = cum[:, h + i : h + i + 1] - cum_t[h + i : h + i + 1, :]
                decay = jnp.exp(jnp.where(seen, log_decay, NEGATIVE))
                mix = (decay * scores * step_t[h + i : h + i + 1, :]).astype(MM)
                own = jnp.where((lane < head_width) == (i == 0), pair, jnp.zeros_like(pair))
                total = total + jnp.dot(mix, own, preferred_element_type=F32)
            y_ref[rows, lanes] = total
            keep_ref[rows, lanes] = jnp.where(
                lane < head_width, keep[:, h : h + 1], keep[:, h + 1 : h + 2]
            )


def gate_kernel(where, depth, last, ints, tok_ref, *refs):
    pieces, refs = refs[: len(where)], refs[len(where) :]
    before, outs = (refs[:2], refs[2:]) if last else ((None, None), refs)
    count = outs[0].shape[0] // GROUP
    for side, (earlier, out) in enumerate(zip(before, outs)):

        @pl.loop(0, count)
        def _(g):
            rows = rows_at(g * GROUP, GROUP)
            total = earlier[rows, :] if last else 0.0
            for piece, (k, first) in zip(pieces, where):
                columns = pl.ds(
                    pl.multiple_of((ints[1] ^ k) * depth + first, LANES), piece.shape[0]
                )
                total = total + jnp.dot(
                    tok_ref[rows_at((side * count + g) * GROUP + HALO, GROUP), columns],
                    piece[...],
                    preferred_element_type=F32,
                )
            out[rows, :] = silu(total.astype(MM).astype(F32)) if last else total


def gating(sizes, ints, low_states, vecs, side, y_ref, keep_ref, gate_ref, bc_ref, out):
    inner, heads, groups = sizes
    half = groups // 2
    state = bc_ref.shape[1] // 2
    lane = lax.broadcasted_iota(jnp.int32, (GROUP, LANES), 1)
    for g in range(half):
        rows = slice(g * GROUP, (g + 1) * GROUP)
        carried = lax.dot_general(
            bc_ref[rows, state:],
            low_states[side * half + g],
            (((1,), (1,)), ((), ())),
            preferred_element_type=F32,
        )
        squares = jnp.zeros((GROUP, LANES), F32)
        for at in range(0, inner, LANES):
            lanes = slice(at, at + LANES)
            y = y_ref[rows, lanes] + carried[:, lanes] * keep_ref[rows, lanes]
            gated = y * gate_ref[rows, lanes]
            squares = squares + gated * gated
            here = pl.ds(pl.multiple_of(ints[2] * inner + at, LANES), LANES)
            out[rows, lanes] = (gated * vecs[5:6, here]).astype(MM)
        total = jnp.broadcast_to(jnp.sum(squares, axis=1, keepdims=True), (GROUP, LANES))
        out[rows, inner:] = spread_terms(total).astype(MM)


def spread_terms(total):
    lane = lax.broadcasted_iota(jnp.int32, total.shape, 1)
    high, mid, low = split_terms(total)
    return jnp.where(lane == 0, high, jnp.where(lane == 1, mid, jnp.where(lane == 2, low, 0.0)))


def added_terms(ref, at):
    value = ref[:, at:].astype(F32)
    return jnp.broadcast_to(jnp.sum(value, axis=1, keepdims=True), value.shape)


def back_kernel(sizes, ints_ref, vecs, *refs):
    inner, heads, prompts, groups, n_pieces, per = sizes
    pieces = refs[:n_pieces]
    sides = (refs[n_pieces : n_pieces + 4], refs[n_pieces + 4 : n_pieces + 8])
    theirs, low_states, asked, own_asked, parts, states, sems = refs[n_pieces + 8 :]
    ints = Ints(ints_ref, prompts)
    p, c = ints.p, ints.c
    head_width = inner // heads
    half = groups // 2
    copies = []
    for i, piece in enumerate(pieces):
        k, side = i // 2, i % 2
        at = (p ^ k) * groups + side * half
        copies.append(pltpu.make_async_copy(piece, parts.at[pl.ds(at, half)], sems.at[i]))
    run_all(copies)
    blocks = parts.shape[0]
    states[0] = jnp.zeros(states.shape[1:], F32)

    @pl.loop(0, blocks)
    def _(b):
        terms = parts[b, inner : inner + TERMS, :].astype(F32)
        gates = terms[0:8] + terms[8:16] + terms[16:24]
        for h in range(heads):
            rows = slice(h * head_width, (h + 1) * head_width)
            states[b + 1, rows, :] = gates[h : h + 1, :] * states[b, rows, :] + parts[
                b, rows, :
            ].astype(F32)

    for g in range(groups):
        low_states[g] = states[p * groups + g].astype(MM)
    for side in range(2):

        @pl.when(c != side)
        def _():
            gating((inner, heads, groups), ints_ref, low_states, vecs, side, *sides[side], theirs)

    for i in range(per):
        own_asked[i] = states[ints.wanted((p * 2 + c) * per + i) + 1]
        asked[i] = states[ints.wanted((p * 2 + 1 - c) * per + i) + 1].astype(MM)


def back_own_kernel(sizes, ints_ref, vecs, low_states, *refs):
    sides = (refs[:4], refs[4:8])
    mine = refs[8]
    for side in range(2):

        @pl.when(ints_ref[2] == side)
        def _():
            gating(sizes, ints_ref, low_states, vecs, side, *sides[side], mine)


def is_inner(t):
    return (t == 1) | (t == 2)


def block_places(t, tp_count):
    if tp_count == 4:
        inside = is_inner(t)
        first = jnp.where(inside, t ^ 1, 3 - t)
        return [first, lax.rem(t + 2, 4), jnp.where(inside, 3 - t, t ^ 1), t]
    return [lax.rem(t + j, tp_count) for j in range(1, tp_count)] + [t]


def out_kernel(sizes, ints, mine, theirs, *refs):
    inner, tp_count, chosen, where = sizes
    t, p, c = ints[0], ints[1], ints[2]
    if where:
        pieces = refs[: len(where)]
        outs = refs[len(where) : len(where) + 2 * len(chosen)]
        weights, sems = refs[len(where) + 2 * len(chosen) :]
        copies = []
        for i, (piece, (k, other, first)) in enumerate(zip(pieces, where)):
            rows, columns = piece.shape
            core = 1 - c if other else c
            at = pl.multiple_of(((p ^ k) * 2 + core) * columns, LANES)
            copies.append(
                pltpu.make_async_copy(
                    piece, weights.at[pl.ds(first, rows), pl.ds(at, columns)], sems.at[i]
                )
            )
        run_all(copies)
    else:
        weights, outs = refs[0], refs[1:]
    width = weights.shape[1]
    piece_rows = mine.shape[0] // tp_count
    own_rows = rows_at(c * inner, inner)
    other_rows = rows_at((1 - c) * inner, inner)
    for i, low, high in zip(chosen, outs[::2], outs[1::2]):
        rows = rows_at(block_places(t, tp_count)[i] * piece_rows, piece_rows)
        sums = jnp.sum(
            mine[rows, inner:].astype(F32) + theirs[rows, inner:].astype(F32), axis=1, keepdims=True
        )
        sums = spread_terms(jnp.broadcast_to(sums, (piece_rows, LANES)))
        high[:, width // 2 :] = sums.astype(high.dtype)
        for at in range(0, width, width // 4):
            lanes = slice(at, at + width // 4)
            value = jnp.dot(mine[rows, :inner], weights[own_rows, lanes], preferred_element_type=F32)
            value = value + jnp.dot(
                theirs[rows, :inner], weights[other_rows, lanes], preferred_element_type=F32
            )
            out, first = (low, at) if at < width // 2 else (high, at - width // 2)
            out[:, first : first + width // 4] = value.astype(out.dtype)


def add_kernel(width, ints, got, own, out):
    inside = is_inner(ints[0])
    came = jnp.where(inside, got[:, :width].astype(F32), 0.0)
    out[:, :width] = (came + own[:, :width].astype(F32)).astype(MM)
    if out.shape[1] > width:
        came = jnp.where(inside, added_terms(got, width), 0.0)
        out[:, width:] = spread_terms(came + added_terms(own, width)).astype(MM)


def final_kernel(channels, takers, ints, *refs):
    own, received, out = refs[:2], refs[2:-1], refs[-1]
    half = out.shape[1] // 2
    inside = is_inner(ints[0])

    def taken(value, inner):
        if inner is None:
            return value
        return jnp.where(inside, value, 0.0) if inner else jnp.where(inside, 0.0, value)

    squares = added_terms(own[1], half)
    for got, inner in zip(received[1::2], takers):
        squares = squares + taken(added_terms(got, half), inner)
    factor = lax.rsqrt(squares[:, :1] / channels + epsilon)
    for side in range(2):
        total = own[side][:, :half]
        for got, inner in zip(received[side::2], takers):
            total = total + taken(got[:, :half].astype(F32), inner)
        out[:, side * half : (side + 1) * half] = (total * factor).astype(out.dtype)


def sum_over_tp(ints, blocks, own):
    tp_count = lax.axis_size("tp")
    if tp_count != 4:
        received = [[shift(x, j + 1) for x in block] for j, block in enumerate(blocks)]
        return own, received, (None,) * (tp_count - 1)

    def send(block, pairs):
        return [lax.ppermute(x, "tp", pairs) for x in block]

    def add(got, x, name):
        kernel = functools.partial(add_kernel, own[0].shape[1])
        specs = [SMEM, VMEM, VMEM]
        return call(kernel, [sds(x.shape, MM)], specs, moved=100_000, name=name)(ints, got, x)[0]

    first, second, third = blocks
    beside = send(first, [(0, 1), (1, 0), (2, 3), (3, 2)])
    to_middle = send(third, [(1, 2), (2, 1), (0, 0), (3, 3)])
    to_inner = send(third, [(0, 1), (3, 2)])
    joined = lax.optimization_barrier((*beside, *second, *own))
    beside, second, own = list(joined[:2]), joined[2:4], list(joined[4:])
    second = [add(got, x, "add_far") for got, x in zip(beside, second)]
    across = [shift(x, 2) for x in second]
    return own, [beside, across, to_middle, to_inner], (False, None, True, True)


def on_device(
    tokens,
    w_zx,
    w_dt,
    w_bc,
    conv_x_weight,
    conv_x_bias,
    conv_bc_weight,
    conv_bc_bias,
    dt_bias,
    a_log,
    skip,
    norm_weight,
    w_out,
    lengths,
    request_group,
):
    tp_count, seq_count = lax.axis_size("tp"), lax.axis_size("seq")
    t, s = lax.axis_index("tp"), lax.axis_index("seq")
    chips = seq_count // 2
    p, c = s // 2, s % 2
    tok_dev, width = tokens.shape
    rows = w_zx.shape[0]
    inner_all = w_zx.shape[1] // 2
    pair = conv_x_weight.shape[1]
    inner = pair // 2
    heads = dt_bias.shape[0] // 2
    head_width = inner // heads
    bc_width = w_bc.shape[1]
    state = bc_width // 2
    tok = 2 * tok_dev
    groups = tok // GROUP
    half = groups // 2
    conv = inner + bc_width
    prompts = lengths.shape[0]
    x_width = 2 * inner + bc_width + LANES
    depth = tp_count * rows

    ints = jnp.concatenate([jnp.stack([t, p, c]).astype(jnp.int32), lengths, request_group])
    floats = jnp.concatenate([dt_bias, a_log, skip])
    vecs = jnp.concatenate(
        [
            conv_x_weight,
            conv_x_bias[None, :],
            norm_weight[None, :],
            jnp.zeros((2, pair), F32),
            jnp.pad(conv_bc_weight, ((0, 0), (0, pair - bc_width))),
            jnp.pad(conv_bc_bias[None, :], ((0, 3), (0, pair - bc_width))),
        ],
        axis=0,
    )

    def packed(kernel, operands, specs, wide, name):
        return pl.pallas_call(
            functools.partial(kernel, tp_count),
            grid=(1,),
            out_shape=[sds((rows, wide), MM)] * tp_count,
            in_specs=specs,
            out_specs=[pl.BlockSpec((rows, wide), lambda i: (0, 0))] * tp_count,
            compiler_params=pltpu.CompilerParams(vmem_limit_bytes=VMEM_BYTES),
            name=name,
        )(*operands)

    def whole(x):
        return pl.BlockSpec(x.shape, lambda i: (0, 0))

    def sent_over_tp(pieces):
        return [pieces[0]] + [shift(x, j) for j, x in enumerate(pieces) if j]

    def assembled(kernel, outs, pieces, name):
        return call(
            functools.partial(kernel, tp_count), outs, [SMEM] + [VMEM] * tp_count, name=name
        )(ints, *pieces)

    def together(*lists):
        joined = lax.optimization_barrier(tuple(tuple(one) for one in lists))
        return [list(one) for one in joined]

    x_sent = packed(
        pack_x_kernel,
        (ints, w_zx, w_bc, w_dt),
        [SMEM, pl.BlockSpec((rows, inner_all), lambda i: (0, 1)), whole(w_bc), whole(w_dt)],
        x_width,
        "pack_x",
    )
    x_got = sent_over_tp(x_sent)

    out_near = plane_near(w_out.astype(MM))
    keys = list(out_near)
    other = flip(tokens, 1)
    first_tok = jnp.where(c == 0, tokens, other)
    second_tok = jnp.where(c == 0, other, tokens)
    out_got, (first_tok, second_tok) = together(
        [out_near[k][0] for k in keys], [first_tok, second_tok]
    )
    out_blocks = plane_far({k: (piece,) for k, piece in zip(keys, out_got)})
    out_own = [piece for k in out_blocks for piece in out_blocks[k]]
    out_where = [
        (k, 0, i * (w_out.shape[0] // 2)) for k in out_blocks for i in range(len(out_blocks[k]))
    ]
    x_got, out_own = together(x_got, out_own)
    (x_block,) = assembled(assemble_x_kernel, [sds((depth, x_width), MM)], x_got, "assemble_x")

    before = lax.ppermute(
        second_tok[tok_dev - HALO :], "seq", [(i, i + 2) for i in range(seq_count - 2)]
    )
    all_tok = jnp.concatenate([before, first_tok, second_tok], axis=0)

    ((x_block, all_tok, ints, floats, vecs),) = together([x_block, all_tok, ints, floats, vecs])
    near = plane_near(x_block)
    z_sent = packed(
        pack_z_kernel,
        (ints, w_zx),
        [SMEM, pl.BlockSpec((rows, inner_all), lambda i: (0, 0))],
        2 * inner,
        "pack_z",
    )
    z_got = sent_over_tp(z_sent)
    blocks, z_got, (x_own,) = together([near[k][0] for k in near if k], z_got, [x_block])
    own_other = flip(x_own, 1)
    far = plane_far({k: (block,) for k, block in zip(near, [x_block] + blocks)})
    z_mine, z_theirs = assembled(
        assemble_z_kernel, [sds((depth, inner), MM)] * 2, z_got, "assemble_z"
    )
    (z_block,) = call(
        merge_kernel, [sds((2 * depth, inner), MM)], [SMEM, VMEM, VMEM], name="merge_z"
    )(ints, z_mine, flip(z_theirs, 1))
    near_other = [flip(far[k][0], 1) for k in near if k]
    order = [k for k in far if k not in near]
    near_other, (z_block,) = together(near_other, [z_block])
    x_far, near_other = together([piece for k in order for piece in far[k]], near_other)
    far_other = [flip(piece, 1) for piece in x_far]
    where = [(k, 0) for k in near] + [(k, i * depth // 2) for k in order for i in range(2)]
    where = tuple((k, other, first) for other in range(2) for k, first in where)
    x_pieces = [far[k][0] for k in near] + x_far + [own_other] + near_other + far_other

    def front(side, where, operands):
        outs = [
            sds((tok_dev, inner), MM),
            sds((tok_dev, bc_width), MM),
            sds((tok_dev, LANES), F32),
            sds((tok_dev, LANES), F32),
            sds((half, inner + TERMS, state), MM),
        ]
        scratch = [pltpu.VMEM((2, HALO + GROUP, conv + LANES), F32)]
        if where:
            outs.append(sds((width, conv + LANES), MM))
            scratch.append(pltpu.SemaphoreType.DMA((2 * len(where),)))
        return call(
            functools.partial(
                front_kernel, (inner, bc_width, heads, prompts, where, depth, groups, side)
            ),
            outs,
            [SMEM, SMEM, VMEM, VMEM] + ([ANY] * len(where) if where else [VMEM]),
            scratch,
            flops=0,
            moved=1_000_000,
            name="front_%d" % side,
        )(ints, floats, vecs, all_tok, *operands)

    z_near = plane_near(z_block)
    *first, weights = front(0, where, x_pieces)
    ((*first, weights),) = together([*first, weights])

    low_near = plane_near(first[4])
    second = front(1, (), [weights])
    out_other = [flip(piece, 1) for piece in out_own]
    second, lows, z_blocks, out_other = together(
        second,
        [low_near[k][0] for k in low_near],
        [z_near[k][0] for k in z_near],
        out_other,
    )
    out_pieces = out_own + out_other
    out_where = tuple(out_where + [(k, 1, first_row) for k, _, first_row in out_where])
    z_far = plane_far({k: (block,) for k, block in zip(z_near, z_blocks)})
    z_order = [k for k in z_far if k in z_near] + [k for k in z_far if k not in z_near]
    z_where = tuple((k, i * depth) for k in z_order for i in range(len(z_far[k])))
    z_pieces = [piece for k in z_order for piece in z_far[k]]

    def mid(side, xs, bc, cum, step, message):
        return call(
            functools.partial(mid_kernel, (inner, heads, prompts, groups, side)),
            [sds((tok_dev, inner), F32)] * 2,
            [SMEM, SMEM] + [VMEM] * 4,
            flops=2 * tok_dev * GROUP * inner,
            moved=1_000_000,
            name="mid_%d" % side,
        )(ints, floats, xs, bc, cum, step)

    parts = {k: (block, None) for k, block in zip(low_near, lows)}
    high_near = plane_near(second[4])
    first_y = mid(0, *first)
    highs, first_y = together([high_near[k][0] for k in parts], first_y)
    parts = {k: (parts[k][0], high) for k, high in zip(parts, highs)}
    for k in range(1, chips):
        if k not in parts:
            low, high = k & -k, 1 << (k.bit_length() - 1)
            parts[k] = (flip(parts[k ^ low][0], 2 * low), flip(parts[k ^ high][1], 2 * high))
    parts = [piece for k in range(chips) for piece in parts[k]]

    y = [first_y, mid(1, *second)]
    near_count = len(z_near)
    gate = []
    for part in (slice(0, near_count), slice(near_count, None)):
        chosen = z_where[part]
        gate = call(
            functools.partial(gate_kernel, chosen, 2 * depth, len(gate) > 0),
            [sds((tok_dev, inner), F32)] * 2,
            [SMEM, VMEM] + [VMEM] * (len(chosen) + len(gate)),
            flops=tok * width * inner // 4,
            moved=1_000_000,
            name="gate_%d" % (len(gate) > 0),
        )(ints, all_tok, *z_pieces[part], *gate)
    sides = [*y[0], gate[0], first[1], *y[1], gate[1], second[1]]
    parts, sides = together(parts, sides)

    per = request_group.shape[0] // seq_count
    sent = sds((tok_dev, inner + LANES), MM)
    theirs, low_states, asked, own_asked = call(
        functools.partial(back_kernel, (inner, heads, prompts, groups, len(parts), per)),
        [
            sent,
            sds((groups, inner, state), MM),
            sds((per, inner, state), MM),
            sds((per, inner, state), F32),
        ],
        [SMEM, VMEM] + [ANY] * len(parts) + [VMEM] * 8,
        [
            pltpu.VMEM((chips * groups, inner + TERMS, state), MM),
            pltpu.VMEM((chips * groups + 1, inner, state), F32),
            pltpu.SemaphoreType.DMA((len(parts),)),
        ],
        flops=2 * tok * state * inner,
        moved=8_000_000,
        name="back",
    )(ints, vecs, *parts, *sides)
    theirs = flip(theirs, 1)
    (mine,) = call(
        functools.partial(back_own_kernel, (inner, heads, groups)),
        [sent],
        [SMEM] + [VMEM] * 10,
        flops=2 * tok_dev * state * inner,
        moved=4_000_000,
        name="back_own",
    )(ints, vecs, low_states, *sides)

    out_width = seq_count * w_out.shape[1]
    piece = tok_dev // tp_count
    ahead = 1 if tp_count == 4 else tp_count - 2

    def project_out(chosen, outs, where, operands):
        scratch, extra = [], []
        outs = [
            sds((piece, out_width // 2 + side * LANES), kind) for kind in outs for side in range(2)
        ]
        if where:
            extra = [sds((2 * inner, out_width), MM)]
            scratch = [pltpu.SemaphoreType.DMA((len(where),))]
        return call(
            functools.partial(out_kernel, (inner, tp_count, chosen, where)),
            outs + extra,
            [SMEM, VMEM, VMEM] + ([ANY] * len(where) if where else [VMEM]),
            scratch,
            flops=len(outs) * piece * inner * out_width,
            moved=1_000_000,
            name="out_%d" % len(chosen),
        )(ints, mine, theirs, *operands)

    *sent_first, out_weights = project_out(tuple(range(ahead)), [MM] * ahead, out_where, out_pieces)
    *sent_next, own_low, own_high = project_out(
        tuple(range(ahead, tp_count)), [MM] * (tp_count - 1 - ahead) + [F32], (), [out_weights]
    )
    halves = [*sent_first, *sent_next]
    own, received, takers = sum_over_tp(
        ints, [halves[i : i + 2] for i in range(0, len(halves), 2)], [own_low, own_high]
    )
    received = [half for block in received for half in block]
    (mixed,) = call(
        functools.partial(final_kernel, float(inner_all), takers),
        [sds((piece, out_width), MM)],
        [SMEM] + [VMEM] * (2 + len(received)),
        name="final",
    )(ints, *own, *received)

    other_asked = flip(asked, 1).astype(F32)
    states = jnp.where(
        c == 0,
        jnp.concatenate([own_asked, other_asked], axis=1),
        jnp.concatenate([other_asked, own_asked], axis=1),
    )
    return (mixed, states.reshape(per, 2 * heads, head_width, state))


def solution(mesh):
    return jax.shard_map(
        on_device,
        mesh=mesh,
        in_specs=(
            P("seq", None),
            P(("seq", "tp"), None),
            P(("seq", "tp"), None),
            P(("seq", "tp"), None),
            P(None, "tp"),
            P("tp"),
            P(),
            P(),
            P("tp"),
            P("tp"),
            P("tp"),
            P("tp"),
            P("tp", "seq"),
            P(),
            P(),
        ),
        out_specs=(P(("seq", "tp"), None), P("seq", "tp", None, None)),
        check_vma=False,
    )
```

```python
import functools

import jax
import jax.numpy as jnp
from jax import lax
from jax.experimental import pallas as pl
from jax.experimental.pallas import tpu as pltpu
from jax.sharding import PartitionSpec as P

GROUP = 256
HALO = 16
LANES = 128
TERMS = 32
MM = jnp.bfloat16
F32 = jnp.float32
NEGATIVE = -1e30
sds = jax.ShapeDtypeStruct
VMEM_BYTES = 20 * 1024 * 1024

epsilon = 1e-05

ANY = pl.BlockSpec(memory_space=pl.ANY)
SMEM = pl.BlockSpec(memory_space=pltpu.SMEM)
VMEM = pl.BlockSpec(memory_space=pltpu.VMEM)


def flip(x, bits):
    count = lax.axis_size("seq")
    return lax.ppermute(x, "seq", [(i, i ^ bits) for i in range(count)])


def shift(x, by):
    count = lax.axis_size("tp")
    return lax.ppermute(x, "tp", [(i, (i + by) % count) for i in range(count)])


def plane_near(block):
    chips = lax.axis_size("seq") // 2
    return {k: (block if k == 0 else flip(block, 2 * k),) for k in range(chips) if k & (k - 1) == 0}


def plane_far(blocks):
    chips = lax.axis_size("seq") // 2
    blocks = dict(blocks)

    def half(k, side):
        if len(blocks[k]) == 2:
            return blocks[k][side]
        size = blocks[k][0].shape[0] // 2
        return blocks[k][0][side * size : (side + 1) * size]

    for k in range(1, chips):
        if k not in blocks:
            low = k & -k
            high = 1 << (k.bit_length() - 1)
            first = flip(half(k ^ low, 0), 2 * low)
            second = flip(half(k ^ high, 1), 2 * high)
            blocks[k] = (first, second)
    return blocks


def call(kernel, outs, in_specs, scratch=(), flops=0, moved=0, out_specs=None, name=None):
    return pl.pallas_call(
        kernel,
        out_shape=outs,
        in_specs=in_specs,
        out_specs=[VMEM] * len(outs) if out_specs is None else out_specs,
        scratch_shapes=list(scratch),
        compiler_params=pltpu.CompilerParams(vmem_limit_bytes=VMEM_BYTES),
        cost_estimate=pl.CostEstimate(flops=flops, bytes_accessed=moved, transcendentals=0),
        name=name,
    )


def split_terms(x):
    high = x.astype(MM).astype(F32)
    rest = x - high
    mid = rest.astype(MM).astype(F32)
    return high, mid, (rest - mid).astype(MM).astype(F32)


def silu(x):
    half = 0.5 * x
    return half + half * jnp.tanh(half)


def run_all(copies):
    for copy in copies:
        copy.start()
    for copy in copies:
        copy.wait()


def starts_of(position, ints):
    start, end = jnp.zeros_like(position), 0
    for i in range(ints.prompts):
        end = end + ints.ref[3 + i]
        start = jnp.where(position >= end, end, start)
    return start


class Ints:
    def __init__(self, ref, prompts):
        self.ref, self.prompts = ref, prompts
        self.t, self.p, self.c = ref[0], ref[1], ref[2]

    def wanted(self, i):
        return self.ref[3 + self.prompts + i]


def rows_at(first, size):
    return pl.ds(pl.multiple_of(first, 16), size)


def pack_x_kernel(tp_count, ints, w_ref, bc_ref, dt_ref, *outs):
    t = ints[0]
    pair = w_ref.shape[1] // tp_count
    inner = pair // 2
    bc_width = bc_ref.shape[1]
    heads = dt_ref.shape[1] // tp_count
    low_bc = bc_ref[...].astype(MM)
    for j, out in enumerate(outs):
        owner = lax.rem(t + j, tp_count)
        at = pl.multiple_of(owner * pair, LANES)
        out[:, :inner] = w_ref[:, pl.ds(at, inner)].astype(MM)
        out[:, inner : inner + bc_width] = low_bc
        steps = jnp.zeros((dt_ref.shape[0], heads), F32)
        for u in range(tp_count):
            steps = jnp.where(owner == u, dt_ref[:, u * heads : (u + 1) * heads], steps)
        steps = jnp.concatenate(
            [steps, jnp.zeros((dt_ref.shape[0], LANES - heads), F32)], axis=1
        )
        out[:, inner + bc_width : inner + bc_width + LANES] = steps.astype(MM)
        at = pl.multiple_of(owner * pair + inner, LANES)
        out[:, inner + bc_width + LANES :] = w_ref[:, pl.ds(at, inner)].astype(MM)


def pack_z_kernel(tp_count, ints, w_ref, *outs):
    pair = w_ref.shape[1] // tp_count
    for j, out in enumerate(outs):
        at = pl.multiple_of(lax.rem(ints[0] + j, tp_count) * pair, LANES)
        out[...] = w_ref[:, pl.ds(at, pair)].astype(MM)


def assemble_x_kernel(tp_count, ints, *refs):
    pieces, out = refs[:tp_count], refs[tp_count]
    rows = pieces[0].shape[0]
    for j, piece in enumerate(pieces):
        source = lax.rem(ints[0] + tp_count - j, tp_count)
        out[rows_at(source * rows, rows), :] = piece[...]


def assemble_z_kernel(tp_count, ints, *refs):
    pieces, (mine, theirs) = refs[:tp_count], refs[tp_count:]
    rows, inner = pieces[0].shape[0], mine.shape[1]
    c = ints[2]
    for j, piece in enumerate(pieces):
        at = rows_at(lax.rem(ints[0] + tp_count - j, tp_count) * rows, rows)
        mine[at, :] = piece[:, pl.ds(pl.multiple_of(c * inner, LANES), inner)]
        theirs[at, :] = piece[:, pl.ds(pl.multiple_of((1 - c) * inner, LANES), inner)]


def merge_kernel(ints, mine, theirs, out):
    rows = mine.shape[0]
    out[rows_at(ints[2] * rows, rows), :] = mine[...]
    out[rows_at((1 - ints[2]) * rows, rows), :] = theirs[...]


def lane_row(ref, first, count):
    lane = lax.broadcasted_iota(jnp.int32, (1, LANES), 1)
    row = jnp.zeros((1, LANES), F32)
    for i in range(count):
        row = jnp.where(lane == i, ref[first + i], row)
    return row


def front_kernel(sizes, ints_ref, floats, vecs, tok_ref, *refs):
    inner, bc_width, heads, prompts, where, depth, groups, side = sizes
    ints = Ints(ints_ref, prompts)
    c = ints.c
    conv = inner + bc_width
    state = bc_width // 2
    head_width = inner // heads
    half = groups // 2
    if where:
        pieces = refs[: len(where)]
        xs_ref, bc_ref, cum_ref, step_ref, message, weights, raw, sems = refs[len(where) :]
        start_x = pl.multiple_of(c * (conv + LANES), LANES)
        copies = []
        for piece, (k, other, first) in zip(pieces, where):
            core = 1 - c if other else c
            rows = rows_at(((ints.p ^ k) * 2 + core) * depth + first, piece.shape[0])
            for source, goal, size in ((start_x, 0, inner), (inner, inner, bc_width + LANES)):
                copies.append(
                    pltpu.make_async_copy(
                        piece.at[:, pl.ds(source, size)],
                        weights.at[rows, pl.ds(goal, size)],
                        sems.at[len(copies)],
                    )
                )
        run_all(copies)
    else:
        weights, xs_ref, bc_ref, cum_ref, step_ref, message, raw = refs
    taps = 4
    lower = (
        lax.broadcasted_iota(jnp.int32, (GROUP, GROUP), 0)
        >= lax.broadcasted_iota(jnp.int32, (GROUP, GROUP), 1)
    ).astype(F32)
    within = lax.broadcasted_iota(jnp.int32, (GROUP, LANES), 0)
    base = ints.p * (groups * GROUP) + side * half * GROUP
    all_heads = 2 * heads
    bias = lane_row(floats, c * heads, heads)
    rate = -jnp.exp(lane_row(floats, all_heads + c * heads, heads))

    def project(g):
        at = (side * half + g) * GROUP
        value = jnp.dot(
            tok_ref[at : at + GROUP + HALO, :], weights[...], preferred_element_type=F32
        )
        raw[g % 2, :, :conv] = value[:, :conv].astype(MM).astype(F32)
        raw[g % 2, :, conv:] = value[:, conv:]

    def one(g):
        rows = slice(g * GROUP, (g + 1) * GROUP)
        slot = g % 2
        first = base + g * GROUP
        position = first + within
        behind = position - starts_of(position, ints)
        keeps = [(behind >= lag).astype(F32) for lag in range(1, taps)]
        dt = raw[slot, HALO : HALO + GROUP, conv:]
        dt = jnp.where(c == 0, dt, pltpu.roll(dt, LANES - heads, 1)) + bias
        step = jnp.maximum(dt, 0.0) + jnp.log1p(jnp.exp(-jnp.abs(dt)))
        cum = jnp.dot(
            lower, step * rate, precision=lax.Precision.HIGHEST, preferred_element_type=F32
        )
        cum_ref[rows, :] = cum
        step_ref[rows, :] = step
        last = cum[GROUP - 1 : GROUP, :]
        start_last = starts_of(first + (GROUP - 1), ints)
        tail = jnp.where(position >= start_last, jnp.exp(last - cum), 0.0) * step
        for block in range(0, conv, LANES):
            lanes = slice(block, block + LANES)
            if block < inner:
                here = pl.ds(pl.multiple_of(c * inner + block, LANES), LANES)
                weight, offset = vecs[0:taps, here], vecs[taps : taps + 1, here]
            else:
                here = slice(block - inner, block - inner + LANES)
                weight, offset = vecs[8 : 8 + taps, here], vecs[8 + taps : 9 + taps, here]
            total = offset + raw[slot, HALO : HALO + GROUP, lanes] * weight[taps - 1 : taps]
            for lag in range(1, taps):
                term = raw[slot, HALO - lag : HALO - lag + GROUP, lanes] * keeps[lag - 1]
                total = total + term * weight[taps - 1 - lag : taps - lag]
            value = silu(total).astype(MM)
            if block < inner:
                xs_ref[rows, lanes] = value
            else:
                bc_ref[rows, here] = value
        b_wide = bc_ref[rows, :state].astype(F32)
        for h in range(0, heads, 2):
            weighted = jnp.concatenate(
                [(b_wide * tail[:, h + i : h + i + 1]).astype(MM) for i in range(2)], axis=1
            )
            both = lax.dot_general(
                xs_ref[rows, h * head_width : (h + 2) * head_width],
                weighted,
                (((0,), (0,)), ((), ())),
                preferred_element_type=F32,
            )
            at = h * head_width
            message[g, at : at + head_width, :] = both[:head_width, :state].astype(MM)
            at = at + head_width
            message[g, at : at + head_width, :] = both[head_width:, state:].astype(MM)
        spread = jnp.broadcast_to(jnp.exp(last), (8, LANES))
        diagonal = lax.broadcasted_iota(jnp.int32, (8, LANES), 0) == lax.broadcasted_iota(
            jnp.int32, (8, LANES), 1
        )
        gates = jnp.sum(jnp.where(diagonal, spread, 0.0), axis=1, keepdims=True)
        gates = jnp.where(start_last < first, jnp.broadcast_to(gates, (8, LANES)), 0.0)
        terms = jnp.concatenate(list(split_terms(gates)) + [jnp.zeros_like(gates)], axis=0)
        message[g, inner : inner + TERMS, :] = terms.astype(MM)

    project(0)
    for g in range(half):
        if g + 1 < half:
            project(g + 1)
        one(g)


def mid_kernel(sizes, ints_ref, floats, xs_ref, bc_ref, cum_ref, step_ref, y_ref, keep_ref):
    inner, heads, prompts, groups, side = sizes
    ints = Ints(ints_ref, prompts)
    state = bc_ref.shape[1] // 2
    head_width = inner // heads
    half = groups // 2
    base = ints.p * (groups * GROUP) + side * half * GROUP
    within_i = lax.broadcasted_iota(jnp.int32, (GROUP, GROUP), 0)
    within_j = lax.broadcasted_iota(jnp.int32, (GROUP, GROUP), 1)
    lane = lax.broadcasted_iota(jnp.int32, (GROUP, LANES), 1)
    skip_at = 4 * heads + ints.c * heads

    @pl.loop(0, half)
    def _(g):
        rows = rows_at(g * GROUP, GROUP)
        first = base + g * GROUP
        start = starts_of(first + within_i, ints)
        seen = (within_j <= within_i) & (first + within_j >= start)
        scores = lax.dot_general(
            bc_ref[rows, state:],
            bc_ref[rows, :state],
            (((1,), (1,)), ((), ())),
            preferred_element_type=F32,
        )
        cum = cum_ref[rows, :]
        cum_t = cum.T
        step_t = step_ref[rows, :].T
        keep = jnp.where(start[:, :LANES] < first, jnp.exp(cum), 0.0)
        for h in range(0, heads, 2):
            lanes = slice(h * head_width, (h + 2) * head_width)
            pair = xs_ref[rows, lanes]
            first_skip, second_skip = (floats[skip_at + h + i] for i in range(2))
            total = jnp.where(lane < head_width, first_skip, second_skip) * pair.astype(F32)
            for i in range(2):
                log_decay = cum[:, h + i : h + i + 1] - cum_t[h + i : h + i + 1, :]
                decay = jnp.exp(jnp.where(seen, log_decay, NEGATIVE))
                mix = (decay * scores * step_t[h + i : h + i + 1, :]).astype(MM)
                own = jnp.where((lane < head_width) == (i == 0), pair, jnp.zeros_like(pair))
                total = total + jnp.dot(mix, own, preferred_element_type=F32)
            y_ref[rows, lanes] = total
            keep_ref[rows, lanes] = jnp.where(
                lane < head_width, keep[:, h : h + 1], keep[:, h + 1 : h + 2]
            )


def gate_kernel(where, depth, last, ints, tok_ref, *refs):
    pieces, refs = refs[: len(where)], refs[len(where) :]
    before, outs = (refs[:2], refs[2:]) if last else ((None, None), refs)
    count = outs[0].shape[0] // GROUP
    for side, (earlier, out) in enumerate(zip(before, outs)):

        @pl.loop(0, count)
        def _(g):
            rows = rows_at(g * GROUP, GROUP)
            total = earlier[rows, :] if last else 0.0
            for piece, (k, first) in zip(pieces, where):
                columns = pl.ds(
                    pl.multiple_of((ints[1] ^ k) * depth + first, LANES), piece.shape[0]
                )
                total = total + jnp.dot(
                    tok_ref[rows_at((side * count + g) * GROUP + HALO, GROUP), columns],
                    piece[...],
                    preferred_element_type=F32,
                )
            out[rows, :] = silu(total.astype(MM).astype(F32)) if last else total


def gating(sizes, ints, low_states, vecs, side, y_ref, keep_ref, gate_ref, bc_ref, out):
    inner, heads, groups = sizes
    half = groups // 2
    state = bc_ref.shape[1] // 2
    lane = lax.broadcasted_iota(jnp.int32, (GROUP, LANES), 1)
    for g in range(half):
        rows = slice(g * GROUP, (g + 1) * GROUP)
        carried = lax.dot_general(
            bc_ref[rows, state:],
            low_states[side * half + g],
            (((1,), (1,)), ((), ())),
            preferred_element_type=F32,
        )
        squares = jnp.zeros((GROUP, LANES), F32)
        for at in range(0, inner, LANES):
            lanes = slice(at, at + LANES)
            y = y_ref[rows, lanes] + carried[:, lanes] * keep_ref[rows, lanes]
            gated = y * gate_ref[rows, lanes]
            squares = squares + gated * gated
            here = pl.ds(pl.multiple_of(ints[2] * inner + at, LANES), LANES)
            out[rows, lanes] = (gated * vecs[5:6, here]).astype(MM)
        total = jnp.broadcast_to(jnp.sum(squares, axis=1, keepdims=True), (GROUP, LANES))
        out[rows, inner:] = spread_terms(total).astype(MM)


def spread_terms(total):
    lane = lax.broadcasted_iota(jnp.int32, total.shape, 1)
    high, mid, low = split_terms(total)
    return jnp.where(lane == 0, high, jnp.where(lane == 1, mid, jnp.where(lane == 2, low, 0.0)))


def added_terms(ref, at):
    value = ref[:, at:].astype(F32)
    return jnp.broadcast_to(jnp.sum(value, axis=1, keepdims=True), value.shape)


def back_kernel(sizes, ints_ref, vecs, *refs):
    inner, heads, prompts, groups, n_pieces, per = sizes
    pieces = refs[:n_pieces]
    sides = (refs[n_pieces : n_pieces + 4], refs[n_pieces + 4 : n_pieces + 8])
    theirs, low_states, asked, own_asked, parts, states, sems = refs[n_pieces + 8 :]
    ints = Ints(ints_ref, prompts)
    p, c = ints.p, ints.c
    head_width = inner // heads
    half = groups // 2
    copies = []
    for i, piece in enumerate(pieces):
        k, side = i // 2, i % 2
        at = (p ^ k) * groups + side * half
        copies.append(pltpu.make_async_copy(piece, parts.at[pl.ds(at, half)], sems.at[i]))
    run_all(copies)
    blocks = parts.shape[0]
    states[0] = jnp.zeros(states.shape[1:], F32)

    @pl.loop(0, blocks)
    def _(b):
        terms = parts[b, inner : inner + TERMS, :].astype(F32)
        gates = terms[0:8] + terms[8:16] + terms[16:24]
        for h in range(heads):
            rows = slice(h * head_width, (h + 1) * head_width)
            states[b + 1, rows, :] = gates[h : h + 1, :] * states[b, rows, :] + parts[
                b, rows, :
            ].astype(F32)

    for g in range(groups):
        low_states[g] = states[p * groups + g].astype(MM)
    for side in range(2):

        @pl.when(c != side)
        def _():
            gating((inner, heads, groups), ints_ref, low_states, vecs, side, *sides[side], theirs)

    for i in range(per):
        own_asked[i] = states[ints.wanted((p * 2 + c) * per + i) + 1]
        asked[i] = states[ints.wanted((p * 2 + 1 - c) * per + i) + 1].astype(MM)


def back_own_kernel(sizes, ints_ref, vecs, low_states, *refs):
    sides = (refs[:4], refs[4:8])
    mine = refs[8]
    for side in range(2):

        @pl.when(ints_ref[2] == side)
        def _():
            gating(sizes, ints_ref, low_states, vecs, side, *sides[side], mine)


def goes_whole(i, tp_count):
    return tp_count == 4 and i == 2


def is_inner(t):
    return (t == 1) | (t == 2)


def block_places(t, tp_count):
    if tp_count == 4:
        inside = is_inner(t)
        first = jnp.where(inside, t ^ 1, 3 - t)
        return [first, lax.rem(t + 2, 4), jnp.where(inside, 3 - t, t ^ 1), t]
    return [lax.rem(t + j, tp_count) for j in range(1, tp_count)] + [t]


def out_kernel(sizes, ints, mine, theirs, *refs):
    inner, tp_count, chosen, where = sizes
    t, p, c = ints[0], ints[1], ints[2]
    if where:
        pieces = refs[: len(where)]
        outs = refs[len(where) : len(where) + 2 * len(chosen)]
        weights, sems = refs[len(where) + 2 * len(chosen) :]
        copies = []
        for i, (piece, (k, other, first)) in enumerate(zip(pieces, where)):
            rows, columns = piece.shape
            core = 1 - c if other else c
            at = pl.multiple_of(((p ^ k) * 2 + core) * columns, LANES)
            copies.append(
                pltpu.make_async_copy(
                    piece, weights.at[pl.ds(first, rows), pl.ds(at, columns)], sems.at[i]
                )
            )
        run_all(copies)
    else:
        weights, outs = refs[0], refs[1:]
    width = weights.shape[1]
    piece_rows = mine.shape[0] // tp_count
    own_rows = rows_at(c * inner, inner)
    other_rows = rows_at((1 - c) * inner, inner)
    outs = list(outs)
    for i in chosen:
        sides = [(outs.pop(0), 0)] if goes_whole(i, tp_count) else []
        sides = sides * 2 or [(outs.pop(0), 0), (outs.pop(0), width // 2)]
        last, last_at = sides[1]
        rows = rows_at(block_places(t, tp_count)[i] * piece_rows, piece_rows)
        sums = jnp.sum(
            mine[rows, inner:].astype(F32) + theirs[rows, inner:].astype(F32), axis=1, keepdims=True
        )
        sums = spread_terms(jnp.broadcast_to(sums, (piece_rows, LANES)))
        last[:, width - last_at :] = sums.astype(last.dtype)
        for at in range(0, width, width // 4):
            lanes = slice(at, at + width // 4)
            value = jnp.dot(mine[rows, :inner], weights[own_rows, lanes], preferred_element_type=F32)
            value = value + jnp.dot(
                theirs[rows, :inner], weights[other_rows, lanes], preferred_element_type=F32
            )
            out, start = sides[at // (width // 2)]
            out[:, at - start : at - start + width // 4] = value.astype(out.dtype)


def add_kernel(width, ints, got, own, out):
    inside = is_inner(ints[0])
    came = jnp.where(inside, got[:, :width].astype(F32), 0.0)
    out[:, :width] = (came + own[:, :width].astype(F32)).astype(MM)
    if out.shape[1] > width:
        came = jnp.where(inside, added_terms(got, width), 0.0)
        out[:, width:] = spread_terms(came + added_terms(own, width)).astype(MM)


def final_kernel(channels, takers, ints, *refs):
    own, refs, out = refs[:2], list(refs[2:-1]), refs[-1]
    width = out.shape[1]
    half = width // 2
    inside = is_inner(ints[0])
    received = []
    for whole, inner in takers:
        low = refs.pop(0)
        received.append((low, low if whole else refs.pop(0), half if whole else 0, inner))

    def taken(value, inner):
        if inner is None:
            return value
        return jnp.where(inside, value, 0.0) if inner else jnp.where(inside, 0.0, value)

    squares = added_terms(own[1], half)
    for _, high, skipped, inner in received:
        squares = squares + taken(added_terms(high, skipped + half), inner)
    factor = lax.rsqrt(squares[:, :1] / channels + epsilon)
    for side in range(2):
        total = own[side][:, :half]
        for low, high, skipped, inner in received:
            got = high[:, skipped : skipped + half] if side else low[:, :half]
            total = total + taken(got.astype(F32), inner)
        out[:, side * half : (side + 1) * half] = (total * factor).astype(out.dtype)


def sum_over_tp(ints, blocks, own, later):
    tp_count = lax.axis_size("tp")
    if tp_count != 4:
        received = [[shift(x, j + 1) for x in block] for j, block in enumerate(blocks)]
        return own, received, ((False, None),) * (tp_count - 1), later

    def send(block, pairs):
        return [lax.ppermute(x, "tp", pairs) for x in block]

    def add(got, x, name):
        kernel = functools.partial(add_kernel, own[0].shape[1])
        specs = [SMEM, VMEM, VMEM]
        return call(kernel, [sds(x.shape, MM)], specs, moved=100_000, name=name)(ints, got, x)[0]

    first, second, third = blocks
    beside = send(first, [(0, 1), (1, 0), (2, 3), (3, 2)])
    to_inner = send(third, [(0, 1), (3, 2)])
    to_middle = send(third, [(1, 2), (2, 1), (0, 0), (3, 3)])
    joined = lax.optimization_barrier((*beside, *second, *own, later))
    beside, second, own, later = list(joined[:2]), joined[2:4], list(joined[4:6]), joined[6]
    second = [add(got, x, "add_far") for got, x in zip(beside, second)]
    across = [shift(x, 2) for x in second]
    takers = ((False, False), (False, None), (True, True), (True, True))
    return own, [beside, across, to_middle, to_inner], takers, later


def on_device(
    tokens,
    w_zx,
    w_dt,
    w_bc,
    conv_x_weight,
    conv_x_bias,
    conv_bc_weight,
    conv_bc_bias,
    dt_bias,
    a_log,
    skip,
    norm_weight,
    w_out,
    lengths,
    request_group,
):
    tp_count, seq_count = lax.axis_size("tp"), lax.axis_size("seq")
    t, s = lax.axis_index("tp"), lax.axis_index("seq")
    chips = seq_count // 2
    p, c = s // 2, s % 2
    tok_dev, width = tokens.shape
    rows = w_zx.shape[0]
    inner_all = w_zx.shape[1] // 2
    pair = conv_x_weight.shape[1]
    inner = pair // 2
    heads = dt_bias.shape[0] // 2
    head_width = inner // heads
    bc_width = w_bc.shape[1]
    state = bc_width // 2
    tok = 2 * tok_dev
    groups = tok // GROUP
    half = groups // 2
    conv = inner + bc_width
    prompts = lengths.shape[0]
    x_width = 2 * inner + bc_width + LANES
    depth = tp_count * rows

    ints = jnp.concatenate([jnp.stack([t, p, c]).astype(jnp.int32), lengths, request_group])
    floats = jnp.concatenate([dt_bias, a_log, skip])
    vecs = jnp.concatenate(
        [
            conv_x_weight,
            conv_x_bias[None, :],
            norm_weight[None, :],
            jnp.zeros((2, pair), F32),
            jnp.pad(conv_bc_weight, ((0, 0), (0, pair - bc_width))),
            jnp.pad(conv_bc_bias[None, :], ((0, 3), (0, pair - bc_width))),
        ],
        axis=0,
    )

    def packed(kernel, operands, specs, wide, name):
        return pl.pallas_call(
            functools.partial(kernel, tp_count),
            grid=(1,),
            out_shape=[sds((rows, wide), MM)] * tp_count,
            in_specs=specs,
            out_specs=[pl.BlockSpec((rows, wide), lambda i: (0, 0))] * tp_count,
            compiler_params=pltpu.CompilerParams(vmem_limit_bytes=VMEM_BYTES),
            name=name,
        )(*operands)

    def whole(x):
        return pl.BlockSpec(x.shape, lambda i: (0, 0))

    def sent_over_tp(pieces):
        return [pieces[0]] + [shift(x, j) for j, x in enumerate(pieces) if j]

    def assembled(kernel, outs, pieces, name):
        return call(
            functools.partial(kernel, tp_count), outs, [SMEM] + [VMEM] * tp_count, name=name
        )(ints, *pieces)

    def together(*lists):
        joined = lax.optimization_barrier(tuple(tuple(one) for one in lists))
        return [list(one) for one in joined]

    x_sent = packed(
        pack_x_kernel,
        (ints, w_zx, w_bc, w_dt),
        [SMEM, pl.BlockSpec((rows, inner_all), lambda i: (0, 1)), whole(w_bc), whole(w_dt)],
        x_width,
        "pack_x",
    )
    x_got = sent_over_tp(x_sent)

    out_near = plane_near(w_out.astype(MM))
    keys = list(out_near)
    other = flip(tokens, 1)
    first_tok = jnp.where(c == 0, tokens, other)
    second_tok = jnp.where(c == 0, other, tokens)
    out_got, (first_tok, second_tok) = together(
        [out_near[k][0] for k in keys], [first_tok, second_tok]
    )
    out_blocks = plane_far({k: (piece,) for k, piece in zip(keys, out_got)})
    out_own = [piece for k in out_blocks for piece in out_blocks[k]]
    out_where = [
        (k, 0, i * (w_out.shape[0] // 2)) for k in out_blocks for i in range(len(out_blocks[k]))
    ]
    x_got, out_own = together(x_got, out_own)
    (x_block,) = assembled(assemble_x_kernel, [sds((depth, x_width), MM)], x_got, "assemble_x")

    before = lax.ppermute(
        second_tok[tok_dev - HALO :], "seq", [(i, i + 2) for i in range(seq_count - 2)]
    )
    all_tok = jnp.concatenate([before, first_tok, second_tok], axis=0)

    ((x_block, all_tok, ints, floats, vecs),) = together([x_block, all_tok, ints, floats, vecs])
    near = plane_near(x_block)
    z_sent = packed(
        pack_z_kernel,
        (ints, w_zx),
        [SMEM, pl.BlockSpec((rows, inner_all), lambda i: (0, 0))],
        2 * inner,
        "pack_z",
    )
    z_got = sent_over_tp(z_sent)
    blocks, z_got, (x_own,) = together([near[k][0] for k in near if k], z_got, [x_block])
    own_other = flip(x_own, 1)
    far = plane_far({k: (block,) for k, block in zip(near, [x_block] + blocks)})
    z_mine, z_theirs = assembled(
        assemble_z_kernel, [sds((depth, inner), MM)] * 2, z_got, "assemble_z"
    )
    (z_block,) = call(
        merge_kernel, [sds((2 * depth, inner), MM)], [SMEM, VMEM, VMEM], name="merge_z"
    )(ints, z_mine, flip(z_theirs, 1))
    near_other = [flip(far[k][0], 1) for k in near if k]
    order = [k for k in far if k not in near]
    near_other, (z_block,) = together(near_other, [z_block])
    x_far, near_other = together([piece for k in order for piece in far[k]], near_other)
    far_other = [flip(piece, 1) for piece in x_far]
    where = [(k, 0) for k in near] + [(k, i * depth // 2) for k in order for i in range(2)]
    where = tuple((k, other, first) for other in range(2) for k, first in where)
    x_pieces = [far[k][0] for k in near] + x_far + [own_other] + near_other + far_other

    def front(side, where, operands):
        outs = [
            sds((tok_dev, inner), MM),
            sds((tok_dev, bc_width), MM),
            sds((tok_dev, LANES), F32),
            sds((tok_dev, LANES), F32),
            sds((half, inner + TERMS, state), MM),
        ]
        scratch = [pltpu.VMEM((2, HALO + GROUP, conv + LANES), F32)]
        if where:
            outs.append(sds((width, conv + LANES), MM))
            scratch.append(pltpu.SemaphoreType.DMA((2 * len(where),)))
        return call(
            functools.partial(
                front_kernel, (inner, bc_width, heads, prompts, where, depth, groups, side)
            ),
            outs,
            [SMEM, SMEM, VMEM, VMEM] + ([ANY] * len(where) if where else [VMEM]),
            scratch,
            flops=0,
            moved=1_000_000,
            name="front_%d" % side,
        )(ints, floats, vecs, all_tok, *operands)

    z_near = plane_near(z_block)
    *first, weights = front(0, where, x_pieces)
    ((*first, weights),) = together([*first, weights])

    low_near = plane_near(first[4])
    second = front(1, (), [weights])
    out_other = [flip(piece, 1) for piece in out_own]
    second, lows, z_blocks, out_other = together(
        second,
        [low_near[k][0] for k in low_near],
        [z_near[k][0] for k in z_near],
        out_other,
    )
    out_pieces = out_own + out_other
    out_where = tuple(out_where + [(k, 1, first_row) for k, _, first_row in out_where])
    z_far = plane_far({k: (block,) for k, block in zip(z_near, z_blocks)})
    z_order = [k for k in z_far if k in z_near] + [k for k in z_far if k not in z_near]
    z_where = tuple((k, i * depth) for k in z_order for i in range(len(z_far[k])))
    z_pieces = [piece for k in z_order for piece in z_far[k]]

    def mid(side, xs, bc, cum, step, message):
        return call(
            functools.partial(mid_kernel, (inner, heads, prompts, groups, side)),
            [sds((tok_dev, inner), F32)] * 2,
            [SMEM, SMEM] + [VMEM] * 4,
            flops=2 * tok_dev * GROUP * inner,
            moved=1_000_000,
            name="mid_%d" % side,
        )(ints, floats, xs, bc, cum, step)

    parts = {k: (block, None) for k, block in zip(low_near, lows)}
    high_near = plane_near(second[4])
    first_y = mid(0, *first)
    highs, first_y = together([high_near[k][0] for k in parts], first_y)
    parts = {k: (parts[k][0], high) for k, high in zip(parts, highs)}
    for k in range(1, chips):
        if k not in parts:
            low, high = k & -k, 1 << (k.bit_length() - 1)
            parts[k] = (flip(parts[k ^ low][0], 2 * low), flip(parts[k ^ high][1], 2 * high))
    parts = [piece for k in range(chips) for piece in parts[k]]

    y = [first_y, mid(1, *second)]
    near_count = len(z_near)
    gate = []
    for part in (slice(0, near_count), slice(near_count, None)):
        chosen = z_where[part]
        gate = call(
            functools.partial(gate_kernel, chosen, 2 * depth, len(gate) > 0),
            [sds((tok_dev, inner), F32)] * 2,
            [SMEM, VMEM] + [VMEM] * (len(chosen) + len(gate)),
            flops=tok * width * inner // 4,
            moved=1_000_000,
            name="gate_%d" % (len(gate) > 0),
        )(ints, all_tok, *z_pieces[part], *gate)
    sides = [*y[0], gate[0], first[1], *y[1], gate[1], second[1]]
    parts, sides = together(parts, sides)

    per = request_group.shape[0] // seq_count
    sent = sds((tok_dev, inner + LANES), MM)
    theirs, low_states, asked, own_asked = call(
        functools.partial(back_kernel, (inner, heads, prompts, groups, len(parts), per)),
        [
            sent,
            sds((groups, inner, state), MM),
            sds((per, inner, state), MM),
            sds((per, inner, state), F32),
        ],
        [SMEM, VMEM] + [ANY] * len(parts) + [VMEM] * 8,
        [
            pltpu.VMEM((chips * groups, inner + TERMS, state), MM),
            pltpu.VMEM((chips * groups + 1, inner, state), F32),
            pltpu.SemaphoreType.DMA((len(parts),)),
        ],
        flops=2 * tok * state * inner,
        moved=8_000_000,
        name="back",
    )(ints, vecs, *parts, *sides)
    theirs = flip(theirs, 1)
    (mine,) = call(
        functools.partial(back_own_kernel, (inner, heads, groups)),
        [sent],
        [SMEM] + [VMEM] * 10,
        flops=2 * tok_dev * state * inner,
        moved=4_000_000,
        name="back_own",
    )(ints, vecs, low_states, *sides)

    out_width = seq_count * w_out.shape[1]
    piece = tok_dev // tp_count
    ahead = 1 if tp_count == 4 else tp_count - 2

    def project_out(chosen, outs, where, operands):
        scratch, extra = [], []
        shapes = []
        for i, kind in zip(chosen, outs):
            if goes_whole(i, tp_count):
                shapes.append(sds((piece, out_width + LANES), kind))
            else:
                shapes += [sds((piece, out_width // 2 + side * LANES), kind) for side in range(2)]
        outs = shapes
        if where:
            extra = [sds((2 * inner, out_width), MM)]
            scratch = [pltpu.SemaphoreType.DMA((len(where),))]
        return call(
            functools.partial(out_kernel, (inner, tp_count, chosen, where)),
            outs + extra,
            [SMEM, VMEM, VMEM] + ([ANY] * len(where) if where else [VMEM]),
            scratch,
            flops=len(outs) * piece * inner * out_width,
            moved=1_000_000,
            name="out_%d" % len(chosen),
        )(ints, mine, theirs, *operands)

    *sent_first, out_weights = project_out(tuple(range(ahead)), [MM] * ahead, out_where, out_pieces)
    *sent_next, own_low, own_high = project_out(
        tuple(range(ahead, tp_count)), [MM] * (tp_count - 1 - ahead) + [F32], (), [out_weights]
    )
    sent_all, blocks = [*sent_first, *sent_next], []
    for i in range(tp_count - 1):
        size = 1 if goes_whole(i, tp_count) else 2
        blocks, sent_all = blocks + [sent_all[:size]], sent_all[size:]
    own, received, takers, asked = sum_over_tp(ints, blocks, [own_low, own_high], asked)
    received = [half for block in received for half in block]
    (mixed,) = call(
        functools.partial(final_kernel, float(inner_all), takers),
        [sds((piece, out_width), MM)],
        [SMEM] + [VMEM] * (2 + len(received)),
        name="final",
    )(ints, *own, *received)

    other_asked = flip(asked, 1).astype(F32)
    states = jnp.where(
        c == 0,
        jnp.concatenate([own_asked, other_asked], axis=1),
        jnp.concatenate([other_asked, own_asked], axis=1),
    )
    return (mixed, states.reshape(per, 2 * heads, head_width, state))


def solution(mesh):
    return jax.shard_map(
        on_device,
        mesh=mesh,
        in_specs=(
            P("seq", None),
            P(("seq", "tp"), None),
            P(("seq", "tp"), None),
            P(("seq", "tp"), None),
            P(None, "tp"),
            P("tp"),
            P(),
            P(),
            P("tp"),
            P("tp"),
            P("tp"),
            P("tp"),
            P("tp", "seq"),
            P(),
            P(),
        ),
        out_specs=(P(("seq", "tp"), None), P("seq", "tp", None, None)),
        check_vma=False,
    )
```

```python
import functools

import jax
import jax.numpy as jnp
from jax import lax
from jax.experimental import pallas as pl
from jax.experimental.pallas import tpu as pltpu
from jax.sharding import PartitionSpec as P

GROUP = 256
HALO = 16
LANES = 128
TERMS = 32
MM = jnp.bfloat16
F32 = jnp.float32
NEGATIVE = -1e30
sds = jax.ShapeDtypeStruct
VMEM_BYTES = 20 * 1024 * 1024

epsilon = 1e-05

ANY = pl.BlockSpec(memory_space=pl.ANY)
SMEM = pl.BlockSpec(memory_space=pltpu.SMEM)
VMEM = pl.BlockSpec(memory_space=pltpu.VMEM)


def flip(x, bits):
    count = lax.axis_size("seq")
    return lax.ppermute(x, "seq", [(i, i ^ bits) for i in range(count)])


def shift(x, by):
    count = lax.axis_size("tp")
    return lax.ppermute(x, "tp", [(i, (i + by) % count) for i in range(count)])


def plane_near(block):
    chips = lax.axis_size("seq") // 2
    return {k: (block if k == 0 else flip(block, 2 * k),) for k in range(chips) if k & (k - 1) == 0}


def plane_far(blocks):
    chips = lax.axis_size("seq") // 2
    blocks = dict(blocks)

    def half(k, side):
        if len(blocks[k]) == 2:
            return blocks[k][side]
        size = blocks[k][0].shape[0] // 2
        return blocks[k][0][side * size : (side + 1) * size]

    for k in range(1, chips):
        if k not in blocks:
            low = k & -k
            high = 1 << (k.bit_length() - 1)
            first = flip(half(k ^ low, 0), 2 * low)
            second = flip(half(k ^ high, 1), 2 * high)
            blocks[k] = (first, second)
    return blocks


def call(kernel, outs, in_specs, scratch=(), flops=0, moved=0, out_specs=None, name=None):
    return pl.pallas_call(
        kernel,
        out_shape=outs,
        in_specs=in_specs,
        out_specs=[VMEM] * len(outs) if out_specs is None else out_specs,
        scratch_shapes=list(scratch),
        compiler_params=pltpu.CompilerParams(vmem_limit_bytes=VMEM_BYTES),
        cost_estimate=pl.CostEstimate(flops=flops, bytes_accessed=moved, transcendentals=0),
        name=name,
    )


def split_terms(x):
    high = x.astype(MM).astype(F32)
    rest = x - high
    mid = rest.astype(MM).astype(F32)
    return high, mid, (rest - mid).astype(MM).astype(F32)


def silu(x):
    half = 0.5 * x
    return half + half * jnp.tanh(half)


def run_all(copies):
    for copy in copies:
        copy.start()
    for copy in copies:
        copy.wait()


def starts_of(position, ints):
    start, end = jnp.zeros_like(position), 0
    for i in range(ints.prompts):
        end = end + ints.ref[3 + i]
        start = jnp.where(position >= end, end, start)
    return start


class Ints:
    def __init__(self, ref, prompts):
        self.ref, self.prompts = ref, prompts
        self.t, self.p, self.c = ref[0], ref[1], ref[2]

    def wanted(self, i):
        return self.ref[3 + self.prompts + i]


def rows_at(first, size):
    return pl.ds(pl.multiple_of(first, 16), size)


def pack_x_kernel(tp_count, ints, w_ref, bc_ref, dt_ref, *outs):
    t = ints[0]
    pair = w_ref.shape[1] // tp_count
    inner = pair // 2
    bc_width = bc_ref.shape[1]
    heads = dt_ref.shape[1] // tp_count
    low_bc = bc_ref[...].astype(MM)
    for j, out in enumerate(outs):
        owner = lax.rem(t + j, tp_count)
        at = pl.multiple_of(owner * pair, LANES)
        out[:, :inner] = w_ref[:, pl.ds(at, inner)].astype(MM)
        out[:, inner : inner + bc_width] = low_bc
        steps = jnp.zeros((dt_ref.shape[0], heads), F32)
        for u in range(tp_count):
            steps = jnp.where(owner == u, dt_ref[:, u * heads : (u + 1) * heads], steps)
        steps = jnp.concatenate(
            [steps, jnp.zeros((dt_ref.shape[0], LANES - heads), F32)], axis=1
        )
        out[:, inner + bc_width : inner + bc_width + LANES] = steps.astype(MM)
        at = pl.multiple_of(owner * pair + inner, LANES)
        out[:, inner + bc_width + LANES :] = w_ref[:, pl.ds(at, inner)].astype(MM)


def pack_z_kernel(tp_count, ints, w_ref, *outs):
    pair = w_ref.shape[1] // tp_count
    for j, out in enumerate(outs):
        at = pl.multiple_of(lax.rem(ints[0] + j, tp_count) * pair, LANES)
        out[...] = w_ref[:, pl.ds(at, pair)].astype(MM)


def assemble_x_kernel(tp_count, ints, *refs):
    pieces, out = refs[:tp_count], refs[tp_count]
    rows = pieces[0].shape[0]
    for j, piece in enumerate(pieces):
        source = lax.rem(ints[0] + tp_count - j, tp_count)
        out[rows_at(source * rows, rows), :] = piece[...]


def assemble_z_kernel(tp_count, ints, *refs):
    pieces, (mine, theirs) = refs[:tp_count], refs[tp_count:]
    rows, inner = pieces[0].shape[0], mine.shape[1]
    c = ints[2]
    for j, piece in enumerate(pieces):
        at = rows_at(lax.rem(ints[0] + tp_count - j, tp_count) * rows, rows)
        mine[at, :] = piece[:, pl.ds(pl.multiple_of(c * inner, LANES), inner)]
        theirs[at, :] = piece[:, pl.ds(pl.multiple_of((1 - c) * inner, LANES), inner)]


def merge_kernel(ints, mine, theirs, out):
    rows = mine.shape[0]
    out[rows_at(ints[2] * rows, rows), :] = mine[...]
    out[rows_at((1 - ints[2]) * rows, rows), :] = theirs[...]


def lane_row(ref, first, count):
    lane = lax.broadcasted_iota(jnp.int32, (1, LANES), 1)
    row = jnp.zeros((1, LANES), F32)
    for i in range(count):
        row = jnp.where(lane == i, ref[first + i], row)
    return row


def front_kernel(sizes, ints_ref, floats, vecs, tok_ref, *refs):
    inner, bc_width, heads, prompts, where, depth, groups, side = sizes
    ints = Ints(ints_ref, prompts)
    c = ints.c
    conv = inner + bc_width
    state = bc_width // 2
    head_width = inner // heads
    half = groups // 2
    if where:
        pieces = refs[: len(where)]
        xs_ref, bc_ref, cum_ref, step_ref, message, weights, raw, sems = refs[len(where) :]
        start_x = pl.multiple_of(c * (conv + LANES), LANES)
        copies = []
        for piece, (k, other, first) in zip(pieces, where):
            core = 1 - c if other else c
            rows = rows_at(((ints.p ^ k) * 2 + core) * depth + first, piece.shape[0])
            for source, goal, size in ((start_x, 0, inner), (inner, inner, bc_width + LANES)):
                copies.append(
                    pltpu.make_async_copy(
                        piece.at[:, pl.ds(source, size)],
                        weights.at[rows, pl.ds(goal, size)],
                        sems.at[len(copies)],
                    )
                )
        run_all(copies)
    else:
        weights, xs_ref, bc_ref, cum_ref, step_ref, message, raw = refs
    taps = 4
    lower = (
        lax.broadcasted_iota(jnp.int32, (GROUP, GROUP), 0)
        >= lax.broadcasted_iota(jnp.int32, (GROUP, GROUP), 1)
    ).astype(F32)
    within = lax.broadcasted_iota(jnp.int32, (GROUP, LANES), 0)
    base = ints.p * (groups * GROUP) + side * half * GROUP
    all_heads = 2 * heads
    bias = lane_row(floats, c * heads, heads)
    rate = -jnp.exp(lane_row(floats, all_heads + c * heads, heads))

    def project(g):
        at = (side * half + g) * GROUP
        value = jnp.dot(
            tok_ref[at : at + GROUP + HALO, :], weights[...], preferred_element_type=F32
        )
        raw[g % 2, :, :conv] = value[:, :conv].astype(MM).astype(F32)
        raw[g % 2, :, conv:] = value[:, conv:]

    def one(g):
        rows = slice(g * GROUP, (g + 1) * GROUP)
        slot = g % 2
        first = base + g * GROUP
        position = first + within
        behind = position - starts_of(position, ints)
        keeps = [(behind >= lag).astype(F32) for lag in range(1, taps)]
        dt = raw[slot, HALO : HALO + GROUP, conv:]
        dt = jnp.where(c == 0, dt, pltpu.roll(dt, LANES - heads, 1)) + bias
        step = jnp.maximum(dt, 0.0) + jnp.log1p(jnp.exp(-jnp.abs(dt)))
        cum = jnp.dot(
            lower, step * rate, precision=lax.Precision.HIGHEST, preferred_element_type=F32
        )
        cum_ref[rows, :] = cum
        step_ref[rows, :] = step
        last = cum[GROUP - 1 : GROUP, :]
        start_last = starts_of(first + (GROUP - 1), ints)
        tail = jnp.where(position >= start_last, jnp.exp(last - cum), 0.0) * step
        for block in range(0, conv, LANES):
            lanes = slice(block, block + LANES)
            if block < inner:
                here = pl.ds(pl.multiple_of(c * inner + block, LANES), LANES)
                weight, offset = vecs[0:taps, here], vecs[taps : taps + 1, here]
            else:
                here = slice(block - inner, block - inner + LANES)
                weight, offset = vecs[8 : 8 + taps, here], vecs[8 + taps : 9 + taps, here]
            total = offset + raw[slot, HALO : HALO + GROUP, lanes] * weight[taps - 1 : taps]
            for lag in range(1, taps):
                term = raw[slot, HALO - lag : HALO - lag + GROUP, lanes] * keeps[lag - 1]
                total = total + term * weight[taps - 1 - lag : taps - lag]
            value = silu(total).astype(MM)
            if block < inner:
                xs_ref[rows, lanes] = value
            else:
                bc_ref[rows, here] = value
        b_wide = bc_ref[rows, :state].astype(F32)
        for h in range(0, heads, 2):
            weighted = jnp.concatenate(
                [(b_wide * tail[:, h + i : h + i + 1]).astype(MM) for i in range(2)], axis=1
            )
            both = lax.dot_general(
                xs_ref[rows, h * head_width : (h + 2) * head_width],
                weighted,
                (((0,), (0,)), ((), ())),
                preferred_element_type=F32,
            )
            at = h * head_width
            message[g, at : at + head_width, :] = both[:head_width, :state].astype(MM)
            at = at + head_width
            message[g, at : at + head_width, :] = both[head_width:, state:].astype(MM)
        spread = jnp.broadcast_to(jnp.exp(last), (8, LANES))
        diagonal = lax.broadcasted_iota(jnp.int32, (8, LANES), 0) == lax.broadcasted_iota(
            jnp.int32, (8, LANES), 1
        )
        gates = jnp.sum(jnp.where(diagonal, spread, 0.0), axis=1, keepdims=True)
        gates = jnp.where(start_last < first, jnp.broadcast_to(gates, (8, LANES)), 0.0)
        terms = jnp.concatenate(list(split_terms(gates)) + [jnp.zeros_like(gates)], axis=0)
        message[g, inner : inner + TERMS, :] = terms.astype(MM)

    project(0)
    for g in range(half):
        if g + 1 < half:
            project(g + 1)
        one(g)


def mid_kernel(sizes, ints_ref, floats, xs_ref, bc_ref, cum_ref, step_ref, y_ref, keep_ref):
    inner, heads, prompts, groups, side = sizes
    ints = Ints(ints_ref, prompts)
    state = bc_ref.shape[1] // 2
    head_width = inner // heads
    half = groups // 2
    base = ints.p * (groups * GROUP) + side * half * GROUP
    within_i = lax.broadcasted_iota(jnp.int32, (GROUP, GROUP), 0)
    within_j = lax.broadcasted_iota(jnp.int32, (GROUP, GROUP), 1)
    lane = lax.broadcasted_iota(jnp.int32, (GROUP, LANES), 1)
    skip_at = 4 * heads + ints.c * heads

    @pl.loop(0, half)
    def _(g):
        rows = rows_at(g * GROUP, GROUP)
        first = base + g * GROUP
        start = starts_of(first + within_i, ints)
        seen = (within_j <= within_i) & (first + within_j >= start)
        scores = lax.dot_general(
            bc_ref[rows, state:],
            bc_ref[rows, :state],
            (((1,), (1,)), ((), ())),
            preferred_element_type=F32,
        )
        cum = cum_ref[rows, :]
        cum_t = cum.T
        step_t = step_ref[rows, :].T
        keep = jnp.where(start[:, :LANES] < first, jnp.exp(cum), 0.0)
        for h in range(0, heads, 2):
            lanes = slice(h * head_width, (h + 2) * head_width)
            pair = xs_ref[rows, lanes]
            first_skip, second_skip = (floats[skip_at + h + i] for i in range(2))
            total = jnp.where(lane < head_width, first_skip, second_skip) * pair.astype(F32)
            for i in range(2):
                log_decay = cum[:, h + i : h + i + 1] - cum_t[h + i : h + i + 1, :]
                decay = jnp.exp(jnp.where(seen, log_decay, NEGATIVE))
                mix = (decay * scores * step_t[h + i : h + i + 1, :]).astype(MM)
                own = jnp.where((lane < head_width) == (i == 0), pair, jnp.zeros_like(pair))
                total = total + jnp.dot(mix, own, preferred_element_type=F32)
            y_ref[rows, lanes] = total
            keep_ref[rows, lanes] = jnp.where(
                lane < head_width, keep[:, h : h + 1], keep[:, h + 1 : h + 2]
            )


def gate_kernel(where, depth, last, ints, tok_ref, *refs):
    pieces, refs = refs[: len(where)], refs[len(where) :]
    before, outs = (refs[:2], refs[2:]) if last else ((None, None), refs)
    count = outs[0].shape[0] // GROUP
    for side, (earlier, out) in enumerate(zip(before, outs)):

        @pl.loop(0, count)
        def _(g):
            rows = rows_at(g * GROUP, GROUP)
            total = earlier[rows, :] if last else 0.0
            for piece, (k, first) in zip(pieces, where):
                columns = pl.ds(
                    pl.multiple_of((ints[1] ^ k) * depth + first, LANES), piece.shape[0]
                )
                total = total + jnp.dot(
                    tok_ref[rows_at((side * count + g) * GROUP + HALO, GROUP), columns],
                    piece[...],
                    preferred_element_type=F32,
                )
            out[rows, :] = silu(total.astype(MM).astype(F32)) if last else total


def gating(sizes, ints, low_states, vecs, side, y_ref, keep_ref, gate_ref, bc_ref, out):
    inner, heads, groups = sizes
    half = groups // 2
    state = bc_ref.shape[1] // 2
    lane = lax.broadcasted_iota(jnp.int32, (GROUP, LANES), 1)
    for g in range(half):
        rows = slice(g * GROUP, (g + 1) * GROUP)
        carried = lax.dot_general(
            bc_ref[rows, state:],
            low_states[side * half + g],
            (((1,), (1,)), ((), ())),
            preferred_element_type=F32,
        )
        squares = jnp.zeros((GROUP, LANES), F32)
        for at in range(0, inner, LANES):
            lanes = slice(at, at + LANES)
            y = y_ref[rows, lanes] + carried[:, lanes] * keep_ref[rows, lanes]
            gated = y * gate_ref[rows, lanes]
            squares = squares + gated * gated
            here = pl.ds(pl.multiple_of(ints[2] * inner + at, LANES), LANES)
            out[rows, lanes] = (gated * vecs[5:6, here]).astype(MM)
        total = jnp.broadcast_to(jnp.sum(squares, axis=1, keepdims=True), (GROUP, LANES))
        out[rows, inner:] = spread_terms(total).astype(MM)


def spread_terms(total):
    lane = lax.broadcasted_iota(jnp.int32, total.shape, 1)
    high, mid, low = split_terms(total)
    return jnp.where(lane == 0, high, jnp.where(lane == 1, mid, jnp.where(lane == 2, low, 0.0)))


def added_terms(ref, at):
    value = ref[:, at:].astype(F32)
    return jnp.broadcast_to(jnp.sum(value, axis=1, keepdims=True), value.shape)


def back_kernel(sizes, ints_ref, vecs, *refs):
    inner, heads, prompts, groups, n_pieces, per = sizes
    pieces = refs[:n_pieces]
    sides = (refs[n_pieces : n_pieces + 4], refs[n_pieces + 4 : n_pieces + 8])
    theirs, low_states, asked, own_asked, parts, states, sems = refs[n_pieces + 8 :]
    ints = Ints(ints_ref, prompts)
    p, c = ints.p, ints.c
    head_width = inner // heads
    half = groups // 2
    copies = []
    for i, piece in enumerate(pieces):
        k, side = i // 2, i % 2
        at = (p ^ k) * groups + side * half
        copies.append(pltpu.make_async_copy(piece, parts.at[pl.ds(at, half)], sems.at[i]))
    run_all(copies)
    blocks = parts.shape[0]
    states[0] = jnp.zeros(states.shape[1:], F32)

    @pl.loop(0, blocks)
    def _(b):
        terms = parts[b, inner : inner + TERMS, :].astype(F32)
        gates = terms[0:8] + terms[8:16] + terms[16:24]
        for h in range(heads):
            rows = slice(h * head_width, (h + 1) * head_width)
            states[b + 1, rows, :] = gates[h : h + 1, :] * states[b, rows, :] + parts[
                b, rows, :
            ].astype(F32)

    for g in range(groups):
        low_states[g] = states[p * groups + g].astype(MM)
    for side in range(2):

        @pl.when(c != side)
        def _():
            gating((inner, heads, groups), ints_ref, low_states, vecs, side, *sides[side], theirs)

    for i in range(per):
        own_asked[i] = states[ints.wanted((p * 2 + c) * per + i) + 1]
        asked[i] = states[ints.wanted((p * 2 + 1 - c) * per + i) + 1].astype(MM)


def back_own_kernel(sizes, ints_ref, vecs, low_states, *refs):
    sides = (refs[:4], refs[4:8])
    mine = refs[8]
    for side in range(2):

        @pl.when(ints_ref[2] == side)
        def _():
            gating(sizes, ints_ref, low_states, vecs, side, *sides[side], mine)


def block_order(tp_count):
    far = tp_count // 2
    return [far] + [j for j in range(1, tp_count) if j != far] + [0]


def in_halves(by, tp_count):
    return by not in (0, tp_count // 2)


def out_kernel(sizes, ints, mine, theirs, *refs):
    inner, tp_count, chosen, where = sizes
    t, p, c = ints[0], ints[1], ints[2]
    if where:
        pieces = refs[: len(where)]
        outs = refs[len(where) : len(where) + len(chosen)]
        weights, sems = refs[len(where) + len(chosen) :]
        copies = []
        for i, (piece, (k, other, first)) in enumerate(zip(pieces, where)):
            rows, columns = piece.shape
            core = 1 - c if other else c
            at = pl.multiple_of(((p ^ k) * 2 + core) * columns, LANES)
            copies.append(
                pltpu.make_async_copy(
                    piece, weights.at[pl.ds(first, rows), pl.ds(at, columns)], sems.at[i]
                )
            )
        run_all(copies)
    else:
        weights, outs = refs[0], refs[1:]
    width = weights.shape[1]
    piece_rows = mine.shape[0] // tp_count
    own_rows = rows_at(c * inner, inner)
    other_rows = rows_at((1 - c) * inner, inner)
    outs = list(outs)
    for by in chosen:
        sides = [(outs.pop(0), 0)]
        if in_halves(by, tp_count):
            sides.append((outs.pop(0), width // 2))
        rows = rows_at(lax.rem(t + by, tp_count) * piece_rows, piece_rows)
        sums = jnp.sum(
            mine[rows, inner:].astype(F32) + theirs[rows, inner:].astype(F32), axis=1, keepdims=True
        )
        out, start = sides[-1]
        terms = spread_terms(jnp.broadcast_to(sums, (piece_rows, LANES)))
        out[:, width - start :] = terms.astype(out.dtype)
        for at in range(0, width, width // 4):
            lanes = slice(at, at + width // 4)
            value = jnp.dot(mine[rows, :inner], weights[own_rows, lanes], preferred_element_type=F32)
            value = value + jnp.dot(
                theirs[rows, :inner], weights[other_rows, lanes], preferred_element_type=F32
            )
            out, start = sides[at * len(sides) // width]
            out[:, at - start : at - start + width // 4] = value.astype(out.dtype)


def final_kernel(channels, sizes, own, *refs):
    refs, out = list(refs[:-1]), refs[-1]
    width = out.shape[1]
    received = []
    for size in sizes:
        low = refs.pop(0)
        received.append(((low, 0), (refs.pop(0), width // 2)) if size == 2 else ((low, 0),) * 2)
    squares = added_terms(own, width)
    for _, (high, start) in received:
        squares = squares + added_terms(high, width - start)
    factor = lax.rsqrt(squares[:, :1] / channels + epsilon)
    for at in range(0, width, width // 4):
        total = own[:, at : at + width // 4]
        for sides in received:
            got, start = sides[at * 2 // width]
            total = total + got[:, at - start : at - start + width // 4].astype(F32)
        out[:, at : at + width // 4] = (total * factor).astype(out.dtype)


def on_device(
    tokens,
    w_zx,
    w_dt,
    w_bc,
    conv_x_weight,
    conv_x_bias,
    conv_bc_weight,
    conv_bc_bias,
    dt_bias,
    a_log,
    skip,
    norm_weight,
    w_out,
    lengths,
    request_group,
):
    tp_count, seq_count = lax.axis_size("tp"), lax.axis_size("seq")
    t, s = lax.axis_index("tp"), lax.axis_index("seq")
    chips = seq_count // 2
    p, c = s // 2, s % 2
    tok_dev, width = tokens.shape
    rows = w_zx.shape[0]
    inner_all = w_zx.shape[1] // 2
    pair = conv_x_weight.shape[1]
    inner = pair // 2
    heads = dt_bias.shape[0] // 2
    head_width = inner // heads
    bc_width = w_bc.shape[1]
    state = bc_width // 2
    tok = 2 * tok_dev
    groups = tok // GROUP
    half = groups // 2
    conv = inner + bc_width
    prompts = lengths.shape[0]
    x_width = 2 * inner + bc_width + LANES
    depth = tp_count * rows

    ints = jnp.concatenate([jnp.stack([t, p, c]).astype(jnp.int32), lengths, request_group])
    floats = jnp.concatenate([dt_bias, a_log, skip])
    vecs = jnp.concatenate(
        [
            conv_x_weight,
            conv_x_bias[None, :],
            norm_weight[None, :],
            jnp.zeros((2, pair), F32),
            jnp.pad(conv_bc_weight, ((0, 0), (0, pair - bc_width))),
            jnp.pad(conv_bc_bias[None, :], ((0, 3), (0, pair - bc_width))),
        ],
        axis=0,
    )

    def packed(kernel, operands, specs, wide, name):
        return pl.pallas_call(
            functools.partial(kernel, tp_count),
            grid=(1,),
            out_shape=[sds((rows, wide), MM)] * tp_count,
            in_specs=specs,
            out_specs=[pl.BlockSpec((rows, wide), lambda i: (0, 0))] * tp_count,
            compiler_params=pltpu.CompilerParams(vmem_limit_bytes=VMEM_BYTES),
            name=name,
        )(*operands)

    def whole(x):
        return pl.BlockSpec(x.shape, lambda i: (0, 0))

    def sent_over_tp(pieces):
        return [pieces[0]] + [shift(x, j) for j, x in enumerate(pieces) if j]

    def assembled(kernel, outs, pieces, name):
        return call(
            functools.partial(kernel, tp_count), outs, [SMEM] + [VMEM] * tp_count, name=name
        )(ints, *pieces)

    def together(*lists):
        joined = lax.optimization_barrier(tuple(tuple(one) for one in lists))
        return [list(one) for one in joined]

    x_sent = packed(
        pack_x_kernel,
        (ints, w_zx, w_bc, w_dt),
        [SMEM, pl.BlockSpec((rows, inner_all), lambda i: (0, 1)), whole(w_bc), whole(w_dt)],
        x_width,
        "pack_x",
    )
    x_got = sent_over_tp(x_sent)

    out_near = plane_near(w_out.astype(MM))
    keys = list(out_near)
    other = flip(tokens, 1)
    first_tok = jnp.where(c == 0, tokens, other)
    second_tok = jnp.where(c == 0, other, tokens)
    out_got, (first_tok, second_tok) = together(
        [out_near[k][0] for k in keys], [first_tok, second_tok]
    )
    out_blocks = plane_far({k: (piece,) for k, piece in zip(keys, out_got)})
    out_own = [piece for k in out_blocks for piece in out_blocks[k]]
    out_where = [
        (k, 0, i * (w_out.shape[0] // 2)) for k in out_blocks for i in range(len(out_blocks[k]))
    ]
    x_got, out_own = together(x_got, out_own)
    (x_block,) = assembled(assemble_x_kernel, [sds((depth, x_width), MM)], x_got, "assemble_x")

    before = lax.ppermute(
        second_tok[tok_dev - HALO :], "seq", [(i, i + 2) for i in range(seq_count - 2)]
    )
    all_tok = jnp.concatenate([before, first_tok, second_tok], axis=0)

    ((x_block, all_tok, ints, floats, vecs),) = together([x_block, all_tok, ints, floats, vecs])
    near = plane_near(x_block)
    z_sent = packed(
        pack_z_kernel,
        (ints, w_zx),
        [SMEM, pl.BlockSpec((rows, inner_all), lambda i: (0, 0))],
        2 * inner,
        "pack_z",
    )
    z_got = sent_over_tp(z_sent)
    blocks, z_got, (x_own,) = together([near[k][0] for k in near if k], z_got, [x_block])
    own_other = flip(x_own, 1)
    far = plane_far({k: (block,) for k, block in zip(near, [x_block] + blocks)})
    z_mine, z_theirs = assembled(
        assemble_z_kernel, [sds((depth, inner), MM)] * 2, z_got, "assemble_z"
    )
    (z_block,) = call(
        merge_kernel, [sds((2 * depth, inner), MM)], [SMEM, VMEM, VMEM], name="merge_z"
    )(ints, z_mine, flip(z_theirs, 1))
    near_other = [flip(far[k][0], 1) for k in near if k]
    order = [k for k in far if k not in near]
    near_other, (z_block,) = together(near_other, [z_block])
    x_far, near_other = together([piece for k in order for piece in far[k]], near_other)
    far_other = [flip(piece, 1) for piece in x_far]
    where = [(k, 0) for k in near] + [(k, i * depth // 2) for k in order for i in range(2)]
    where = tuple((k, other, first) for other in range(2) for k, first in where)
    x_pieces = [far[k][0] for k in near] + x_far + [own_other] + near_other + far_other

    def front(side, where, operands):
        outs = [
            sds((tok_dev, inner), MM),
            sds((tok_dev, bc_width), MM),
            sds((tok_dev, LANES), F32),
            sds((tok_dev, LANES), F32),
            sds((half, inner + TERMS, state), MM),
        ]
        scratch = [pltpu.VMEM((2, HALO + GROUP, conv + LANES), F32)]
        if where:
            outs.append(sds((width, conv + LANES), MM))
            scratch.append(pltpu.SemaphoreType.DMA((2 * len(where),)))
        return call(
            functools.partial(
                front_kernel, (inner, bc_width, heads, prompts, where, depth, groups, side)
            ),
            outs,
            [SMEM, SMEM, VMEM, VMEM] + ([ANY] * len(where) if where else [VMEM]),
            scratch,
            flops=0,
            moved=1_000_000,
            name="front_%d" % side,
        )(ints, floats, vecs, all_tok, *operands)

    z_near = plane_near(z_block)
    *first, weights = front(0, where, x_pieces)
    ((*first, weights),) = together([*first, weights])

    low_near = plane_near(first[4])
    second = front(1, (), [weights])
    out_other = [flip(piece, 1) for piece in out_own]
    second, lows, z_blocks, out_other = together(
        second,
        [low_near[k][0] for k in low_near],
        [z_near[k][0] for k in z_near],
        out_other,
    )
    out_pieces = out_own + out_other
    out_where = tuple(out_where + [(k, 1, first_row) for k, _, first_row in out_where])
    z_far = plane_far({k: (block,) for k, block in zip(z_near, z_blocks)})
    z_order = [k for k in z_far if k in z_near] + [k for k in z_far if k not in z_near]
    z_where = tuple((k, i * depth) for k in z_order for i in range(len(z_far[k])))
    z_pieces = [piece for k in z_order for piece in z_far[k]]

    def mid(side, xs, bc, cum, step, message):
        return call(
            functools.partial(mid_kernel, (inner, heads, prompts, groups, side)),
            [sds((tok_dev, inner), F32)] * 2,
            [SMEM, SMEM] + [VMEM] * 4,
            flops=2 * tok_dev * GROUP * inner,
            moved=1_000_000,
            name="mid_%d" % side,
        )(ints, floats, xs, bc, cum, step)

    parts = {k: (block, None) for k, block in zip(low_near, lows)}
    high_near = plane_near(second[4])
    first_y = mid(0, *first)
    highs, first_y = together([high_near[k][0] for k in parts], first_y)
    parts = {k: (parts[k][0], high) for k, high in zip(parts, highs)}
    for k in range(1, chips):
        if k not in parts:
            low, high = k & -k, 1 << (k.bit_length() - 1)
            parts[k] = (flip(parts[k ^ low][0], 2 * low), flip(parts[k ^ high][1], 2 * high))
    parts = [piece for k in range(chips) for piece in parts[k]]

    y = [first_y, mid(1, *second)]
    near_count = len(z_near)
    gate = []
    for part in (slice(0, near_count), slice(near_count, None)):
        chosen = z_where[part]
        gate = call(
            functools.partial(gate_kernel, chosen, 2 * depth, len(gate) > 0),
            [sds((tok_dev, inner), F32)] * 2,
            [SMEM, VMEM] + [VMEM] * (len(chosen) + len(gate)),
            flops=tok * width * inner // 4,
            moved=1_000_000,
            name="gate_%d" % (len(gate) > 0),
        )(ints, all_tok, *z_pieces[part], *gate)
    sides = [*y[0], gate[0], first[1], *y[1], gate[1], second[1]]
    parts, sides = together(parts, sides)

    per = request_group.shape[0] // seq_count
    sent = sds((tok_dev, inner + LANES), MM)
    theirs, low_states, asked, own_asked = call(
        functools.partial(back_kernel, (inner, heads, prompts, groups, len(parts), per)),
        [
            sent,
            sds((groups, inner, state), MM),
            sds((per, inner, state), MM),
            sds((per, inner, state), F32),
        ],
        [SMEM, VMEM] + [ANY] * len(parts) + [VMEM] * 8,
        [
            pltpu.VMEM((chips * groups, inner + TERMS, state), MM),
            pltpu.VMEM((chips * groups + 1, inner, state), F32),
            pltpu.SemaphoreType.DMA((len(parts),)),
        ],
        flops=2 * tok * state * inner,
        moved=8_000_000,
        name="back",
    )(ints, vecs, *parts, *sides)
    theirs = flip(theirs, 1)
    (mine,) = call(
        functools.partial(back_own_kernel, (inner, heads, groups)),
        [sent],
        [SMEM] + [VMEM] * 10,
        flops=2 * tok_dev * state * inner,
        moved=4_000_000,
        name="back_own",
    )(ints, vecs, low_states, *sides)

    out_width = seq_count * w_out.shape[1]
    piece = tok_dev // tp_count

    def project_out(chosen, where, operands):
        scratch, extra = [], []
        outs = []
        for by in chosen:
            if in_halves(by, tp_count):
                outs += [sds((piece, out_width // 2 + side * LANES), MM) for side in range(2)]
            else:
                outs.append(sds((piece, out_width + LANES), MM if by else F32))
        if where:
            extra = [sds((2 * inner, out_width), MM)]
            scratch = [pltpu.SemaphoreType.DMA((len(where),))]
        return call(
            functools.partial(out_kernel, (inner, tp_count, tuple(chosen), where)),
            outs + extra,
            [SMEM, VMEM, VMEM] + ([ANY] * len(where) if where else [VMEM]),
            scratch,
            flops=len(outs) * piece * inner * out_width,
            moved=1_000_000,
            name="out_%d" % len(chosen),
        )(ints, mine, theirs, *operands)

    order = block_order(tp_count)
    far_block, out_weights = project_out(order[:1], out_where, out_pieces)
    received = [shift(far_block, order[0])]
    *blocks, own = project_out(order[1:], (), [out_weights])
    received += [shift(x, order[1 + i // 2]) for i, x in enumerate(blocks)]
    sizes = (1,) + (2,) * (len(blocks) // 2)
    own, asked = lax.optimization_barrier((own, asked))
    (mixed,) = call(
        functools.partial(final_kernel, float(inner_all), sizes),
        [sds((piece, out_width), MM)],
        [VMEM] * (1 + len(received)),
        name="final",
    )(own, *received)

    other_asked = flip(asked, 1).astype(F32)
    states = jnp.where(
        c == 0,
        jnp.concatenate([own_asked, other_asked], axis=1),
        jnp.concatenate([other_asked, own_asked], axis=1),
    )
    return (mixed, states.reshape(per, 2 * heads, head_width, state))


def solution(mesh):
    return jax.shard_map(
        on_device,
        mesh=mesh,
        in_specs=(
            P("seq", None),
            P(("seq", "tp"), None),
            P(("seq", "tp"), None),
            P(("seq", "tp"), None),
            P(None, "tp"),
            P("tp"),
            P(),
            P(),
            P("tp"),
            P("tp"),
            P("tp"),
            P("tp"),
            P("tp", "seq"),
            P(),
            P(),
        ),
        out_specs=(P(("seq", "tp"), None), P("seq", "tp", None, None)),
        check_vma=False,
    )
```

```python
import functools

import jax
import jax.numpy as jnp
from jax import lax
from jax.experimental import pallas as pl
from jax.experimental.pallas import tpu as pltpu
from jax.sharding import PartitionSpec as P

GROUP = 256
HALO = 16
LANES = 128
TERMS = 32
MM = jnp.bfloat16
F32 = jnp.float32
NEGATIVE = -1e30
sds = jax.ShapeDtypeStruct
VMEM_BYTES = 20 * 1024 * 1024

epsilon = 1e-05

ANY = pl.BlockSpec(memory_space=pl.ANY)
SMEM = pl.BlockSpec(memory_space=pltpu.SMEM)
VMEM = pl.BlockSpec(memory_space=pltpu.VMEM)


def flip(x, bits):
    count = lax.axis_size("seq")
    return lax.ppermute(x, "seq", [(i, i ^ bits) for i in range(count)])


def shift(x, by):
    count = lax.axis_size("tp")
    return lax.ppermute(x, "tp", [(i, (i + by) % count) for i in range(count)])


def plane_near(block):
    chips = lax.axis_size("seq") // 2
    return {k: (block if k == 0 else flip(block, 2 * k),) for k in range(chips) if k & (k - 1) == 0}


def plane_far(blocks):
    chips = lax.axis_size("seq") // 2
    blocks = dict(blocks)

    def half(k, side):
        if len(blocks[k]) == 2:
            return blocks[k][side]
        size = blocks[k][0].shape[0] // 2
        return blocks[k][0][side * size : (side + 1) * size]

    for k in range(1, chips):
        if k not in blocks:
            low = k & -k
            high = 1 << (k.bit_length() - 1)
            first = flip(half(k ^ low, 0), 2 * low)
            second = flip(half(k ^ high, 1), 2 * high)
            blocks[k] = (first, second)
    return blocks


def call(kernel, outs, in_specs, scratch=(), flops=0, moved=0, out_specs=None, name=None):
    return pl.pallas_call(
        kernel,
        out_shape=outs,
        in_specs=in_specs,
        out_specs=[VMEM] * len(outs) if out_specs is None else out_specs,
        scratch_shapes=list(scratch),
        compiler_params=pltpu.CompilerParams(vmem_limit_bytes=VMEM_BYTES),
        cost_estimate=pl.CostEstimate(flops=flops, bytes_accessed=moved, transcendentals=0),
        name=name,
    )


def split_terms(x):
    high = x.astype(MM).astype(F32)
    rest = x - high
    mid = rest.astype(MM).astype(F32)
    return high, mid, (rest - mid).astype(MM).astype(F32)


def silu(x):
    half = 0.5 * x
    return half + half * jnp.tanh(half)


def run_all(copies):
    for copy in copies:
        copy.start()
    for copy in copies:
        copy.wait()


def starts_of(position, ints):
    start, end = jnp.zeros_like(position), 0
    for i in range(ints.prompts):
        end = end + ints.ref[3 + i]
        start = jnp.where(position >= end, end, start)
    return start


class Ints:
    def __init__(self, ref, prompts):
        self.ref, self.prompts = ref, prompts
        self.t, self.p, self.c = ref[0], ref[1], ref[2]

    def wanted(self, i):
        return self.ref[3 + self.prompts + i]


def rows_at(first, size):
    return pl.ds(pl.multiple_of(first, 16), size)


def pack_x_kernel(tp_count, ints, w_ref, bc_ref, dt_ref, *outs):
    t = ints[0]
    pair = w_ref.shape[1] // tp_count
    inner = pair // 2
    bc_width = bc_ref.shape[1]
    heads = dt_ref.shape[1] // tp_count
    low_bc = bc_ref[...].astype(MM)
    for j, out in enumerate(outs):
        owner = lax.rem(t + j, tp_count)
        at = pl.multiple_of(owner * pair, LANES)
        out[:, :inner] = w_ref[:, pl.ds(at, inner)].astype(MM)
        out[:, inner : inner + bc_width] = low_bc
        steps = jnp.zeros((dt_ref.shape[0], heads), F32)
        for u in range(tp_count):
            steps = jnp.where(owner == u, dt_ref[:, u * heads : (u + 1) * heads], steps)
        steps = jnp.concatenate(
            [steps, jnp.zeros((dt_ref.shape[0], LANES - heads), F32)], axis=1
        )
        out[:, inner + bc_width : inner + bc_width + LANES] = steps.astype(MM)
        at = pl.multiple_of(owner * pair + inner, LANES)
        out[:, inner + bc_width + LANES :] = w_ref[:, pl.ds(at, inner)].astype(MM)


def pack_z_kernel(tp_count, ints, w_ref, *outs):
    pair = w_ref.shape[1] // tp_count
    for j, out in enumerate(outs):
        at = pl.multiple_of(lax.rem(ints[0] + j, tp_count) * pair, LANES)
        out[...] = w_ref[:, pl.ds(at, pair)].astype(MM)


def assemble_x_kernel(tp_count, ints, *refs):
    pieces, out = refs[:tp_count], refs[tp_count]
    rows = pieces[0].shape[0]
    for j, piece in enumerate(pieces):
        source = lax.rem(ints[0] + tp_count - j, tp_count)
        out[rows_at(source * rows, rows), :] = piece[...]


def assemble_z_kernel(tp_count, ints, *refs):
    pieces, (mine, theirs) = refs[:tp_count], refs[tp_count:]
    rows, inner = pieces[0].shape[0], mine.shape[1]
    c = ints[2]
    for j, piece in enumerate(pieces):
        at = rows_at(lax.rem(ints[0] + tp_count - j, tp_count) * rows, rows)
        mine[at, :] = piece[:, pl.ds(pl.multiple_of(c * inner, LANES), inner)]
        theirs[at, :] = piece[:, pl.ds(pl.multiple_of((1 - c) * inner, LANES), inner)]


def merge_kernel(ints, mine, theirs, out):
    rows = mine.shape[0]
    out[rows_at(ints[2] * rows, rows), :] = mine[...]
    out[rows_at((1 - ints[2]) * rows, rows), :] = theirs[...]


def lane_row(ref, first, count):
    lane = lax.broadcasted_iota(jnp.int32, (1, LANES), 1)
    row = jnp.zeros((1, LANES), F32)
    for i in range(count):
        row = jnp.where(lane == i, ref[first + i], row)
    return row


def front_kernel(sizes, ints_ref, floats, vecs, tok_ref, *refs):
    inner, bc_width, heads, prompts, where, depth, groups, side = sizes
    ints = Ints(ints_ref, prompts)
    c = ints.c
    conv = inner + bc_width
    state = bc_width // 2
    head_width = inner // heads
    half = groups // 2
    if where:
        pieces = refs[: len(where)]
        xs_ref, bc_ref, cum_ref, step_ref, message, weights, raw, sems = refs[len(where) :]
        start_x = pl.multiple_of(c * (conv + LANES), LANES)
        copies = []
        for piece, (k, other, first) in zip(pieces, where):
            core = 1 - c if other else c
            rows = rows_at(((ints.p ^ k) * 2 + core) * depth + first, piece.shape[0])
            for source, goal, size in ((start_x, 0, inner), (inner, inner, bc_width + LANES)):
                copies.append(
                    pltpu.make_async_copy(
                        piece.at[:, pl.ds(source, size)],
                        weights.at[rows, pl.ds(goal, size)],
                        sems.at[len(copies)],
                    )
                )
        run_all(copies)
    else:
        weights, xs_ref, bc_ref, cum_ref, step_ref, message, raw = refs
    taps = 4
    lower = (
        lax.broadcasted_iota(jnp.int32, (GROUP, GROUP), 0)
        >= lax.broadcasted_iota(jnp.int32, (GROUP, GROUP), 1)
    ).astype(F32)
    within = lax.broadcasted_iota(jnp.int32, (GROUP, LANES), 0)
    base = ints.p * (groups * GROUP) + side * half * GROUP
    all_heads = 2 * heads
    bias = lane_row(floats, c * heads, heads)
    rate = -jnp.exp(lane_row(floats, all_heads + c * heads, heads))

    def project(g):
        at = (side * half + g) * GROUP
        value = jnp.dot(
            tok_ref[at : at + GROUP + HALO, :], weights[...], preferred_element_type=F32
        )
        raw[g % 2, :, :conv] = value[:, :conv].astype(MM).astype(F32)
        raw[g % 2, :, conv:] = value[:, conv:]

    def one(g):
        rows = slice(g * GROUP, (g + 1) * GROUP)
        slot = g % 2
        first = base + g * GROUP
        position = first + within
        behind = position - starts_of(position, ints)
        keeps = [(behind >= lag).astype(F32) for lag in range(1, taps)]
        dt = raw[slot, HALO : HALO + GROUP, conv:]
        dt = jnp.where(c == 0, dt, pltpu.roll(dt, LANES - heads, 1)) + bias
        step = jnp.maximum(dt, 0.0) + jnp.log1p(jnp.exp(-jnp.abs(dt)))
        cum = jnp.dot(
            lower, step * rate, precision=lax.Precision.HIGHEST, preferred_element_type=F32
        )
        cum_ref[rows, :] = cum
        step_ref[rows, :] = step
        last = cum[GROUP - 1 : GROUP, :]
        start_last = starts_of(first + (GROUP - 1), ints)
        tail = jnp.where(position >= start_last, jnp.exp(last - cum), 0.0) * step
        for block in range(0, conv, LANES):
            lanes = slice(block, block + LANES)
            if block < inner:
                here = pl.ds(pl.multiple_of(c * inner + block, LANES), LANES)
                weight, offset = vecs[0:taps, here], vecs[taps : taps + 1, here]
            else:
                here = slice(block - inner, block - inner + LANES)
                weight, offset = vecs[8 : 8 + taps, here], vecs[8 + taps : 9 + taps, here]
            total = offset + raw[slot, HALO : HALO + GROUP, lanes] * weight[taps - 1 : taps]
            for lag in range(1, taps):
                term = raw[slot, HALO - lag : HALO - lag + GROUP, lanes] * keeps[lag - 1]
                total = total + term * weight[taps - 1 - lag : taps - lag]
            value = silu(total).astype(MM)
            if block < inner:
                xs_ref[rows, lanes] = value
            else:
                bc_ref[rows, here] = value
        b_wide = bc_ref[rows, :state].astype(F32)
        for h in range(0, heads, 2):
            weighted = jnp.concatenate(
                [(b_wide * tail[:, h + i : h + i + 1]).astype(MM) for i in range(2)], axis=1
            )
            both = lax.dot_general(
                xs_ref[rows, h * head_width : (h + 2) * head_width],
                weighted,
                (((0,), (0,)), ((), ())),
                preferred_element_type=F32,
            )
            at = h * head_width
            message[g, at : at + head_width, :] = both[:head_width, :state].astype(MM)
            at = at + head_width
            message[g, at : at + head_width, :] = both[head_width:, state:].astype(MM)
        spread = jnp.broadcast_to(jnp.exp(last), (8, LANES))
        diagonal = lax.broadcasted_iota(jnp.int32, (8, LANES), 0) == lax.broadcasted_iota(
            jnp.int32, (8, LANES), 1
        )
        gates = jnp.sum(jnp.where(diagonal, spread, 0.0), axis=1, keepdims=True)
        gates = jnp.where(start_last < first, jnp.broadcast_to(gates, (8, LANES)), 0.0)
        terms = jnp.concatenate(list(split_terms(gates)) + [jnp.zeros_like(gates)], axis=0)
        message[g, inner : inner + TERMS, :] = terms.astype(MM)

    project(0)
    for g in range(half):
        if g + 1 < half:
            project(g + 1)
        one(g)


def mid_kernel(sizes, ints_ref, floats, xs_ref, bc_ref, cum_ref, step_ref, y_ref, keep_ref):
    inner, heads, prompts, groups, side = sizes
    ints = Ints(ints_ref, prompts)
    state = bc_ref.shape[1] // 2
    head_width = inner // heads
    half = groups // 2
    base = ints.p * (groups * GROUP) + side * half * GROUP
    within_i = lax.broadcasted_iota(jnp.int32, (GROUP, GROUP), 0)
    within_j = lax.broadcasted_iota(jnp.int32, (GROUP, GROUP), 1)
    lane = lax.broadcasted_iota(jnp.int32, (GROUP, LANES), 1)
    skip_at = 4 * heads + ints.c * heads

    @pl.loop(0, half)
    def _(g):
        rows = rows_at(g * GROUP, GROUP)
        first = base + g * GROUP
        start = starts_of(first + within_i, ints)
        seen = (within_j <= within_i) & (first + within_j >= start)
        scores = lax.dot_general(
            bc_ref[rows, state:],
            bc_ref[rows, :state],
            (((1,), (1,)), ((), ())),
            preferred_element_type=F32,
        )
        cum = cum_ref[rows, :]
        cum_t = cum.T
        step_t = step_ref[rows, :].T
        keep = jnp.where(start[:, :LANES] < first, jnp.exp(cum), 0.0)
        for h in range(0, heads, 2):
            lanes = slice(h * head_width, (h + 2) * head_width)
            pair = xs_ref[rows, lanes]
            first_skip, second_skip = (floats[skip_at + h + i] for i in range(2))
            total = jnp.where(lane < head_width, first_skip, second_skip) * pair.astype(F32)
            for i in range(2):
                log_decay = cum[:, h + i : h + i + 1] - cum_t[h + i : h + i + 1, :]
                decay = jnp.exp(jnp.where(seen, log_decay, NEGATIVE))
                mix = (decay * scores * step_t[h + i : h + i + 1, :]).astype(MM)
                own = jnp.where((lane < head_width) == (i == 0), pair, jnp.zeros_like(pair))
                total = total + jnp.dot(mix, own, preferred_element_type=F32)
            y_ref[rows, lanes] = total
            keep_ref[rows, lanes] = jnp.where(
                lane < head_width, keep[:, h : h + 1], keep[:, h + 1 : h + 2]
            )


def gate_kernel(where, depth, last, ints, tok_ref, *refs):
    pieces, refs = refs[: len(where)], refs[len(where) :]
    before, outs = (refs[:2], refs[2:]) if last else ((None, None), refs)
    count = outs[0].shape[0] // GROUP
    for side, (earlier, out) in enumerate(zip(before, outs)):

        @pl.loop(0, count)
        def _(g):
            rows = rows_at(g * GROUP, GROUP)
            total = earlier[rows, :] if last else 0.0
            for piece, (k, first) in zip(pieces, where):
                columns = pl.ds(
                    pl.multiple_of((ints[1] ^ k) * depth + first, LANES), piece.shape[0]
                )
                total = total + jnp.dot(
                    tok_ref[rows_at((side * count + g) * GROUP + HALO, GROUP), columns],
                    piece[...],
                    preferred_element_type=F32,
                )
            out[rows, :] = silu(total.astype(MM).astype(F32)) if last else total


def gating(sizes, ints, low_states, vecs, side, y_ref, keep_ref, gate_ref, bc_ref, out):
    inner, heads, groups = sizes
    half = groups // 2
    state = bc_ref.shape[1] // 2
    lane = lax.broadcasted_iota(jnp.int32, (GROUP, LANES), 1)
    for g in range(half):
        rows = slice(g * GROUP, (g + 1) * GROUP)
        carried = lax.dot_general(
            bc_ref[rows, state:],
            low_states[side * half + g],
            (((1,), (1,)), ((), ())),
            preferred_element_type=F32,
        )
        squares = jnp.zeros((GROUP, LANES), F32)
        for at in range(0, inner, LANES):
            lanes = slice(at, at + LANES)
            y = y_ref[rows, lanes] + carried[:, lanes] * keep_ref[rows, lanes]
            gated = y * gate_ref[rows, lanes]
            squares = squares + gated * gated
            here = pl.ds(pl.multiple_of(ints[2] * inner + at, LANES), LANES)
            out[rows, lanes] = (gated * vecs[5:6, here]).astype(MM)
        total = jnp.broadcast_to(jnp.sum(squares, axis=1, keepdims=True), (GROUP, LANES))
        out[rows, inner:] = spread_terms(total).astype(MM)


def spread_terms(total):
    lane = lax.broadcasted_iota(jnp.int32, total.shape, 1)
    high, mid, low = split_terms(total)
    return jnp.where(lane == 0, high, jnp.where(lane == 1, mid, jnp.where(lane == 2, low, 0.0)))


def added_terms(ref, at):
    value = ref[:, at:].astype(F32)
    return jnp.broadcast_to(jnp.sum(value, axis=1, keepdims=True), value.shape)


def back_kernel(sizes, ints_ref, vecs, *refs):
    inner, heads, prompts, groups, n_pieces, per = sizes
    pieces = refs[:n_pieces]
    sides = (refs[n_pieces : n_pieces + 4], refs[n_pieces + 4 : n_pieces + 8])
    theirs, low_states, asked, own_asked, parts, states, sems = refs[n_pieces + 8 :]
    ints = Ints(ints_ref, prompts)
    p, c = ints.p, ints.c
    head_width = inner // heads
    half = groups // 2
    copies = []
    for i, piece in enumerate(pieces):
        k, side = i // 2, i % 2
        at = (p ^ k) * groups + side * half
        copies.append(pltpu.make_async_copy(piece, parts.at[pl.ds(at, half)], sems.at[i]))
    run_all(copies)
    blocks = parts.shape[0]
    states[0] = jnp.zeros(states.shape[1:], F32)

    @pl.loop(0, blocks)
    def _(b):
        terms = parts[b, inner : inner + TERMS, :].astype(F32)
        gates = terms[0:8] + terms[8:16] + terms[16:24]
        for h in range(heads):
            rows = slice(h * head_width, (h + 1) * head_width)
            states[b + 1, rows, :] = gates[h : h + 1, :] * states[b, rows, :] + parts[
                b, rows, :
            ].astype(F32)

    for g in range(groups):
        low_states[g] = states[p * groups + g].astype(MM)
    for side in range(2):

        @pl.when(c != side)
        def _():
            gating((inner, heads, groups), ints_ref, low_states, vecs, side, *sides[side], theirs)

    for i in range(per):
        own_asked[i] = states[ints.wanted((p * 2 + c) * per + i) + 1]
        asked[i] = states[ints.wanted((p * 2 + 1 - c) * per + i) + 1].astype(MM)


def back_own_kernel(sizes, ints_ref, vecs, low_states, *refs):
    sides = (refs[:4], refs[4:8])
    mine = refs[8]
    for side in range(2):

        @pl.when(ints_ref[2] == side)
        def _():
            gating(sizes, ints_ref, low_states, vecs, side, *sides[side], mine)


def block_order(tp_count):
    return [2, 1, 3, 0] if tp_count == 4 else list(range(1, tp_count)) + [0]


def out_kernel(sizes, ints, mine, theirs, *refs):
    inner, tp_count, chosen, where = sizes
    t, p, c = ints[0], ints[1], ints[2]
    if where:
        pieces = refs[: len(where)]
        outs = refs[len(where) : len(where) + 2 * len(chosen)]
        weights, sems = refs[len(where) + 2 * len(chosen) :]
        copies = []
        for i, (piece, (k, other, first)) in enumerate(zip(pieces, where)):
            rows, columns = piece.shape
            core = 1 - c if other else c
            at = pl.multiple_of(((p ^ k) * 2 + core) * columns, LANES)
            copies.append(
                pltpu.make_async_copy(
                    piece, weights.at[pl.ds(first, rows), pl.ds(at, columns)], sems.at[i]
                )
            )
        run_all(copies)
    else:
        weights, outs = refs[0], refs[1:]
    width = weights.shape[1]
    piece_rows = mine.shape[0] // tp_count
    own_rows = rows_at(c * inner, inner)
    other_rows = rows_at((1 - c) * inner, inner)
    for i, low, high in zip(chosen, outs[::2], outs[1::2]):
        rows = rows_at(lax.rem(t + block_order(tp_count)[i], tp_count) * piece_rows, piece_rows)
        sums = jnp.sum(
            mine[rows, inner:].astype(F32) + theirs[rows, inner:].astype(F32), axis=1, keepdims=True
        )
        sums = spread_terms(jnp.broadcast_to(sums, (piece_rows, LANES)))
        high[:, width // 2 :] = sums.astype(high.dtype)
        for at in range(0, width, width // 4):
            lanes = slice(at, at + width // 4)
            value = jnp.dot(mine[rows, :inner], weights[own_rows, lanes], preferred_element_type=F32)
            value = value + jnp.dot(
                theirs[rows, :inner], weights[other_rows, lanes], preferred_element_type=F32
            )
            out, first = (low, at) if at < width // 2 else (high, at - width // 2)
            out[:, first : first + width // 4] = value.astype(out.dtype)


def add_kernel(width, got, own, out):
    out[:, :width] = (got[:, :width].astype(F32) + own[:, :width].astype(F32)).astype(MM)
    if out.shape[1] > width:
        out[:, width:] = spread_terms(added_terms(got, width) + added_terms(own, width)).astype(MM)


def final_kernel(channels, *refs):
    own, received, out = refs[:2], refs[2:-1], refs[-1]
    half = out.shape[1] // 2
    squares = added_terms(own[1], half)
    for got in received[1::2]:
        squares = squares + added_terms(got, half)
    factor = lax.rsqrt(squares[:, :1] / channels + epsilon)
    for side in range(2):
        total = own[side][:, :half]
        for got in received[side::2]:
            total = total + got[:, :half].astype(F32)
        out[:, side * half : (side + 1) * half] = (total * factor).astype(out.dtype)


def sum_over_tp(blocks, own):
    tp_count = lax.axis_size("tp")
    if tp_count != 4:
        return own, [[shift(x, j + 1) for x in block] for j, block in enumerate(blocks)]

    def add(got, x, name):
        kernel = functools.partial(add_kernel, own[0].shape[1])
        return call(kernel, [sds(x.shape, MM)], [VMEM] * 2, moved=100_000, name=name)(got, x)[0]

    (far_low, far_high), (next_low, next_high), (last_low, last_high) = blocks
    came_low, came_high = shift(far_low, 1), shift(far_high, 3)
    from_last_high, from_next_low = shift(next_high, 1), shift(last_low, 3)
    came_low, came_high, next_low, last_high, *own = lax.optimization_barrier(
        (came_low, came_high, next_low, last_high, *own)
    )
    from_last_low = shift(add(came_low, next_low, "add_low"), 1)
    from_next_high = shift(add(came_high, last_high, "add_high"), 3)
    return own, [[from_last_low, from_last_high], [from_next_low, from_next_high]]


def on_device(
    tokens,
    w_zx,
    w_dt,
    w_bc,
    conv_x_weight,
    conv_x_bias,
    conv_bc_weight,
    conv_bc_bias,
    dt_bias,
    a_log,
    skip,
    norm_weight,
    w_out,
    lengths,
    request_group,
):
    tp_count, seq_count = lax.axis_size("tp"), lax.axis_size("seq")
    t, s = lax.axis_index("tp"), lax.axis_index("seq")
    chips = seq_count // 2
    p, c = s // 2, s % 2
    tok_dev, width = tokens.shape
    rows = w_zx.shape[0]
    inner_all = w_zx.shape[1] // 2
    pair = conv_x_weight.shape[1]
    inner = pair // 2
    heads = dt_bias.shape[0] // 2
    head_width = inner // heads
    bc_width = w_bc.shape[1]
    state = bc_width // 2
    tok = 2 * tok_dev
    groups = tok // GROUP
    half = groups // 2
    conv = inner + bc_width
    prompts = lengths.shape[0]
    x_width = 2 * inner + bc_width + LANES
    depth = tp_count * rows

    ints = jnp.concatenate([jnp.stack([t, p, c]).astype(jnp.int32), lengths, request_group])
    floats = jnp.concatenate([dt_bias, a_log, skip])
    vecs = jnp.concatenate(
        [
            conv_x_weight,
            conv_x_bias[None, :],
            norm_weight[None, :],
            jnp.zeros((2, pair), F32),
            jnp.pad(conv_bc_weight, ((0, 0), (0, pair - bc_width))),
            jnp.pad(conv_bc_bias[None, :], ((0, 3), (0, pair - bc_width))),
        ],
        axis=0,
    )

    def packed(kernel, operands, specs, wide, name):
        return pl.pallas_call(
            functools.partial(kernel, tp_count),
            grid=(1,),
            out_shape=[sds((rows, wide), MM)] * tp_count,
            in_specs=specs,
            out_specs=[pl.BlockSpec((rows, wide), lambda i: (0, 0))] * tp_count,
            compiler_params=pltpu.CompilerParams(vmem_limit_bytes=VMEM_BYTES),
            name=name,
        )(*operands)

    def whole(x):
        return pl.BlockSpec(x.shape, lambda i: (0, 0))

    def sent_over_tp(pieces):
        return [pieces[0]] + [shift(x, j) for j, x in enumerate(pieces) if j]

    def assembled(kernel, outs, pieces, name):
        return call(
            functools.partial(kernel, tp_count), outs, [SMEM] + [VMEM] * tp_count, name=name
        )(ints, *pieces)

    def together(*lists):
        joined = lax.optimization_barrier(tuple(tuple(one) for one in lists))
        return [list(one) for one in joined]

    x_sent = packed(
        pack_x_kernel,
        (ints, w_zx, w_bc, w_dt),
        [SMEM, pl.BlockSpec((rows, inner_all), lambda i: (0, 1)), whole(w_bc), whole(w_dt)],
        x_width,
        "pack_x",
    )
    x_got = sent_over_tp(x_sent)

    out_near = plane_near(w_out.astype(MM))
    keys = list(out_near)
    other = flip(tokens, 1)
    first_tok = jnp.where(c == 0, tokens, other)
    second_tok = jnp.where(c == 0, other, tokens)
    out_got, (first_tok, second_tok) = together(
        [out_near[k][0] for k in keys], [first_tok, second_tok]
    )
    out_blocks = plane_far({k: (piece,) for k, piece in zip(keys, out_got)})
    out_own = [piece for k in out_blocks for piece in out_blocks[k]]
    out_where = [
        (k, 0, i * (w_out.shape[0] // 2)) for k in out_blocks for i in range(len(out_blocks[k]))
    ]
    x_got, out_own = together(x_got, out_own)
    (x_block,) = assembled(assemble_x_kernel, [sds((depth, x_width), MM)], x_got, "assemble_x")

    before = lax.ppermute(
        second_tok[tok_dev - HALO :], "seq", [(i, i + 2) for i in range(seq_count - 2)]
    )
    all_tok = jnp.concatenate([before, first_tok, second_tok], axis=0)

    ((x_block, all_tok, ints, floats, vecs),) = together([x_block, all_tok, ints, floats, vecs])
    near = plane_near(x_block)
    z_sent = packed(
        pack_z_kernel,
        (ints, w_zx),
        [SMEM, pl.BlockSpec((rows, inner_all), lambda i: (0, 0))],
        2 * inner,
        "pack_z",
    )
    z_got = sent_over_tp(z_sent)
    blocks, z_got, (x_own,) = together([near[k][0] for k in near if k], z_got, [x_block])
    own_other = flip(x_own, 1)
    far = plane_far({k: (block,) for k, block in zip(near, [x_block] + blocks)})
    z_mine, z_theirs = assembled(
        assemble_z_kernel, [sds((depth, inner), MM)] * 2, z_got, "assemble_z"
    )
    (z_block,) = call(
        merge_kernel, [sds((2 * depth, inner), MM)], [SMEM, VMEM, VMEM], name="merge_z"
    )(ints, z_mine, flip(z_theirs, 1))
    near_other = [flip(far[k][0], 1) for k in near if k]
    order = [k for k in far if k not in near]
    near_other, (z_block,) = together(near_other, [z_block])
    x_far, near_other = together([piece for k in order for piece in far[k]], near_other)
    far_other = [flip(piece, 1) for piece in x_far]
    where = [(k, 0) for k in near] + [(k, i * depth // 2) for k in order for i in range(2)]
    where = tuple((k, other, first) for other in range(2) for k, first in where)
    x_pieces = [far[k][0] for k in near] + x_far + [own_other] + near_other + far_other

    def front(side, where, operands):
        outs = [
            sds((tok_dev, inner), MM),
            sds((tok_dev, bc_width), MM),
            sds((tok_dev, LANES), F32),
            sds((tok_dev, LANES), F32),
            sds((half, inner + TERMS, state), MM),
        ]
        scratch = [pltpu.VMEM((2, HALO + GROUP, conv + LANES), F32)]
        if where:
            outs.append(sds((width, conv + LANES), MM))
            scratch.append(pltpu.SemaphoreType.DMA((2 * len(where),)))
        return call(
            functools.partial(
                front_kernel, (inner, bc_width, heads, prompts, where, depth, groups, side)
            ),
            outs,
            [SMEM, SMEM, VMEM, VMEM] + ([ANY] * len(where) if where else [VMEM]),
            scratch,
            flops=0,
            moved=1_000_000,
            name="front_%d" % side,
        )(ints, floats, vecs, all_tok, *operands)

    z_near = plane_near(z_block)
    *first, weights = front(0, where, x_pieces)
    ((*first, weights),) = together([*first, weights])

    low_near = plane_near(first[4])
    second = front(1, (), [weights])
    out_other = [flip(piece, 1) for piece in out_own]
    second, lows, z_blocks, out_other = together(
        second,
        [low_near[k][0] for k in low_near],
        [z_near[k][0] for k in z_near],
        out_other,
    )
    out_pieces = out_own + out_other
    out_where = tuple(out_where + [(k, 1, first_row) for k, _, first_row in out_where])
    z_far = plane_far({k: (block,) for k, block in zip(z_near, z_blocks)})
    z_order = [k for k in z_far if k in z_near] + [k for k in z_far if k not in z_near]
    z_where = tuple((k, i * depth) for k in z_order for i in range(len(z_far[k])))
    z_pieces = [piece for k in z_order for piece in z_far[k]]

    def mid(side, xs, bc, cum, step, message):
        return call(
            functools.partial(mid_kernel, (inner, heads, prompts, groups, side)),
            [sds((tok_dev, inner), F32)] * 2,
            [SMEM, SMEM] + [VMEM] * 4,
            flops=2 * tok_dev * GROUP * inner,
            moved=1_000_000,
            name="mid_%d" % side,
        )(ints, floats, xs, bc, cum, step)

    parts = {k: (block, None) for k, block in zip(low_near, lows)}
    high_near = plane_near(second[4])
    first_y = mid(0, *first)
    highs, first_y = together([high_near[k][0] for k in parts], first_y)
    parts = {k: (parts[k][0], high) for k, high in zip(parts, highs)}
    for k in range(1, chips):
        if k not in parts:
            low, high = k & -k, 1 << (k.bit_length() - 1)
            parts[k] = (flip(parts[k ^ low][0], 2 * low), flip(parts[k ^ high][1], 2 * high))
    parts = [piece for k in range(chips) for piece in parts[k]]

    y = [first_y, mid(1, *second)]
    near_count = len(z_near)
    gate = []
    for part in (slice(0, near_count), slice(near_count, None)):
        chosen = z_where[part]
        gate = call(
            functools.partial(gate_kernel, chosen, 2 * depth, len(gate) > 0),
            [sds((tok_dev, inner), F32)] * 2,
            [SMEM, VMEM] + [VMEM] * (len(chosen) + len(gate)),
            flops=tok * width * inner // 4,
            moved=1_000_000,
            name="gate_%d" % (len(gate) > 0),
        )(ints, all_tok, *z_pieces[part], *gate)
    sides = [*y[0], gate[0], first[1], *y[1], gate[1], second[1]]
    parts, sides = together(parts, sides)

    per = request_group.shape[0] // seq_count
    sent = sds((tok_dev, inner + LANES), MM)
    theirs, low_states, asked, own_asked = call(
        functools.partial(back_kernel, (inner, heads, prompts, groups, len(parts), per)),
        [
            sent,
            sds((groups, inner, state), MM),
            sds((per, inner, state), MM),
            sds((per, inner, state), F32),
        ],
        [SMEM, VMEM] + [ANY] * len(parts) + [VMEM] * 8,
        [
            pltpu.VMEM((chips * groups, inner + TERMS, state), MM),
            pltpu.VMEM((chips * groups + 1, inner, state), F32),
            pltpu.SemaphoreType.DMA((len(parts),)),
        ],
        flops=2 * tok * state * inner,
        moved=8_000_000,
        name="back",
    )(ints, vecs, *parts, *sides)
    theirs = flip(theirs, 1)
    (mine,) = call(
        functools.partial(back_own_kernel, (inner, heads, groups)),
        [sent],
        [SMEM] + [VMEM] * 10,
        flops=2 * tok_dev * state * inner,
        moved=4_000_000,
        name="back_own",
    )(ints, vecs, low_states, *sides)

    out_width = seq_count * w_out.shape[1]
    piece = tok_dev // tp_count
    ahead = 1 if tp_count == 4 else tp_count - 2

    def project_out(chosen, outs, where, operands):
        scratch, extra = [], []
        outs = [
            sds((piece, out_width // 2 + side * LANES), kind) for kind in outs for side in range(2)
        ]
        if where:
            extra = [sds((2 * inner, out_width), MM)]
            scratch = [pltpu.SemaphoreType.DMA((len(where),))]
        return call(
            functools.partial(out_kernel, (inner, tp_count, chosen, where)),
            outs + extra,
            [SMEM, VMEM, VMEM] + ([ANY] * len(where) if where else [VMEM]),
            scratch,
            flops=len(outs) * piece * inner * out_width,
            moved=1_000_000,
            name="out_%d" % len(chosen),
        )(ints, mine, theirs, *operands)

    *sent_first, out_weights = project_out(tuple(range(ahead)), [MM] * ahead, out_where, out_pieces)
    *sent_next, own_low, own_high = project_out(
        tuple(range(ahead, tp_count)), [MM] * (tp_count - 1 - ahead) + [F32], (), [out_weights]
    )
    halves = [*sent_first, *sent_next]
    own, received = sum_over_tp(
        [halves[i : i + 2] for i in range(0, len(halves), 2)], [own_low, own_high]
    )
    received = [half for block in received for half in block]
    (mixed,) = call(
        functools.partial(final_kernel, float(inner_all)),
        [sds((piece, out_width), MM)],
        [VMEM] * (2 + len(received)),
        name="final",
    )(*own, *received)

    other_asked = flip(asked, 1).astype(F32)
    states = jnp.where(
        c == 0,
        jnp.concatenate([own_asked, other_asked], axis=1),
        jnp.concatenate([other_asked, own_asked], axis=1),
    )
    return (mixed, states.reshape(per, 2 * heads, head_width, state))


def solution(mesh):
    return jax.shard_map(
        on_device,
        mesh=mesh,
        in_specs=(
            P("seq", None),
            P(("seq", "tp"), None),
            P(("seq", "tp"), None),
            P(("seq", "tp"), None),
            P(None, "tp"),
            P("tp"),
            P(),
            P(),
            P("tp"),
            P("tp"),
            P("tp"),
            P("tp"),
            P("tp", "seq"),
            P(),
            P(),
        ),
        out_specs=(P(("seq", "tp"), None), P("seq", "tp", None, None)),
        check_vma=False,
    )
```

```python
import functools

import jax
import jax.numpy as jnp
from jax import lax
from jax.experimental import pallas as pl
from jax.experimental.pallas import tpu as pltpu
from jax.sharding import PartitionSpec as P

GROUP = 256
HALO = 16
LANES = 128
TERMS = 32
MM = jnp.bfloat16
F32 = jnp.float32
NEGATIVE = -1e30
sds = jax.ShapeDtypeStruct
VMEM_BYTES = 20 * 1024 * 1024

epsilon = 1e-05

ANY = pl.BlockSpec(memory_space=pl.ANY)
SMEM = pl.BlockSpec(memory_space=pltpu.SMEM)
VMEM = pl.BlockSpec(memory_space=pltpu.VMEM)


def flip(x, bits):
    count = lax.axis_size("seq")
    return lax.ppermute(x, "seq", [(i, i ^ bits) for i in range(count)])


def shift(x, by):
    count = lax.axis_size("tp")
    return lax.ppermute(x, "tp", [(i, (i + by) % count) for i in range(count)])


def plane_near(block):
    chips = lax.axis_size("seq") // 2
    return {k: (block if k == 0 else flip(block, 2 * k),) for k in range(chips) if k & (k - 1) == 0}


def plane_far(blocks):
    chips = lax.axis_size("seq") // 2
    blocks = dict(blocks)

    def half(k, side):
        if len(blocks[k]) == 2:
            return blocks[k][side]
        size = blocks[k][0].shape[0] // 2
        return blocks[k][0][side * size : (side + 1) * size]

    for k in range(1, chips):
        if k not in blocks:
            low = k & -k
            high = 1 << (k.bit_length() - 1)
            first = flip(half(k ^ low, 0), 2 * low)
            second = flip(half(k ^ high, 1), 2 * high)
            blocks[k] = (first, second)
    return blocks


def call(kernel, outs, in_specs, scratch=(), flops=0, moved=0, out_specs=None, name=None):
    return pl.pallas_call(
        kernel,
        out_shape=outs,
        in_specs=in_specs,
        out_specs=[VMEM] * len(outs) if out_specs is None else out_specs,
        scratch_shapes=list(scratch),
        compiler_params=pltpu.CompilerParams(vmem_limit_bytes=VMEM_BYTES),
        cost_estimate=pl.CostEstimate(flops=flops, bytes_accessed=moved, transcendentals=0),
        name=name,
    )


def split_terms(x):
    high = x.astype(MM).astype(F32)
    rest = x - high
    mid = rest.astype(MM).astype(F32)
    return high, mid, (rest - mid).astype(MM).astype(F32)


def silu(x):
    half = 0.5 * x
    return half + half * jnp.tanh(half)


def run_all(copies):
    for copy in copies:
        copy.start()
    for copy in copies:
        copy.wait()


def starts_of(position, ints):
    start, end = jnp.zeros_like(position), 0
    for i in range(ints.prompts):
        end = end + ints.ref[3 + i]
        start = jnp.where(position >= end, end, start)
    return start


class Ints:
    def __init__(self, ref, prompts):
        self.ref, self.prompts = ref, prompts
        self.t, self.p, self.c = ref[0], ref[1], ref[2]

    def wanted(self, i):
        return self.ref[3 + self.prompts + i]


def rows_at(first, size):
    return pl.ds(pl.multiple_of(first, 16), size)


def pack_x_kernel(tp_count, ints, w_ref, bc_ref, dt_ref, *outs):
    t = ints[0]
    pair = w_ref.shape[1] // tp_count
    inner = pair // 2
    bc_width = bc_ref.shape[1]
    heads = dt_ref.shape[1] // tp_count
    low_bc = bc_ref[...].astype(MM)
    for j, out in enumerate(outs):
        owner = lax.rem(t + j, tp_count)
        at = pl.multiple_of(owner * pair, LANES)
        out[:, :inner] = w_ref[:, pl.ds(at, inner)].astype(MM)
        out[:, inner : inner + bc_width] = low_bc
        steps = jnp.zeros((dt_ref.shape[0], heads), F32)
        for u in range(tp_count):
            steps = jnp.where(owner == u, dt_ref[:, u * heads : (u + 1) * heads], steps)
        steps = jnp.concatenate(
            [steps, jnp.zeros((dt_ref.shape[0], LANES - heads), F32)], axis=1
        )
        out[:, inner + bc_width : inner + bc_width + LANES] = steps.astype(MM)
        at = pl.multiple_of(owner * pair + inner, LANES)
        out[:, inner + bc_width + LANES :] = w_ref[:, pl.ds(at, inner)].astype(MM)


def pack_z_kernel(tp_count, ints, w_ref, *outs):
    pair = w_ref.shape[1] // tp_count
    for j, out in enumerate(outs):
        at = pl.multiple_of(lax.rem(ints[0] + j, tp_count) * pair, LANES)
        out[...] = w_ref[:, pl.ds(at, pair)].astype(MM)


def assemble_x_kernel(tp_count, ints, *refs):
    pieces, out = refs[:tp_count], refs[tp_count]
    rows = pieces[0].shape[0]
    for j, piece in enumerate(pieces):
        source = lax.rem(ints[0] + tp_count - j, tp_count)
        out[rows_at(source * rows, rows), :] = piece[...]


def assemble_z_kernel(tp_count, ints, *refs):
    pieces, (mine, theirs) = refs[:tp_count], refs[tp_count:]
    rows, inner = pieces[0].shape[0], mine.shape[1]
    c = ints[2]
    for j, piece in enumerate(pieces):
        at = rows_at(lax.rem(ints[0] + tp_count - j, tp_count) * rows, rows)
        mine[at, :] = piece[:, pl.ds(pl.multiple_of(c * inner, LANES), inner)]
        theirs[at, :] = piece[:, pl.ds(pl.multiple_of((1 - c) * inner, LANES), inner)]


def merge_kernel(ints, mine, theirs, out):
    rows = mine.shape[0]
    out[rows_at(ints[2] * rows, rows), :] = mine[...]
    out[rows_at((1 - ints[2]) * rows, rows), :] = theirs[...]


def lane_row(ref, first, count):
    lane = lax.broadcasted_iota(jnp.int32, (1, LANES), 1)
    row = jnp.zeros((1, LANES), F32)
    for i in range(count):
        row = jnp.where(lane == i, ref[first + i], row)
    return row


def front_kernel(sizes, ints_ref, floats, vecs, tok_ref, *refs):
    inner, bc_width, heads, prompts, where, depth, groups, side = sizes
    ints = Ints(ints_ref, prompts)
    c = ints.c
    conv = inner + bc_width
    state = bc_width // 2
    head_width = inner // heads
    half = groups // 2
    if where:
        pieces = refs[: len(where)]
        xs_ref, bc_ref, cum_ref, step_ref, message, weights, raw, sems = refs[len(where) :]
        start_x = pl.multiple_of(c * (conv + LANES), LANES)
        copies = []
        for piece, (k, other, first) in zip(pieces, where):
            core = 1 - c if other else c
            rows = rows_at(((ints.p ^ k) * 2 + core) * depth + first, piece.shape[0])
            for source, goal, size in ((start_x, 0, inner), (inner, inner, bc_width + LANES)):
                copies.append(
                    pltpu.make_async_copy(
                        piece.at[:, pl.ds(source, size)],
                        weights.at[rows, pl.ds(goal, size)],
                        sems.at[len(copies)],
                    )
                )
        run_all(copies)
    else:
        weights, xs_ref, bc_ref, cum_ref, step_ref, message, raw = refs
    taps = 4
    lower = (
        lax.broadcasted_iota(jnp.int32, (GROUP, GROUP), 0)
        >= lax.broadcasted_iota(jnp.int32, (GROUP, GROUP), 1)
    ).astype(F32)
    within = lax.broadcasted_iota(jnp.int32, (GROUP, LANES), 0)
    base = ints.p * (groups * GROUP) + side * half * GROUP
    all_heads = 2 * heads
    bias = lane_row(floats, c * heads, heads)
    rate = -jnp.exp(lane_row(floats, all_heads + c * heads, heads))

    def project(g):
        at = (side * half + g) * GROUP
        value = jnp.dot(
            tok_ref[at : at + GROUP + HALO, :], weights[...], preferred_element_type=F32
        )
        raw[g % 2, :, :conv] = value[:, :conv].astype(MM).astype(F32)
        raw[g % 2, :, conv:] = value[:, conv:]

    def one(g):
        rows = slice(g * GROUP, (g + 1) * GROUP)
        slot = g % 2
        first = base + g * GROUP
        position = first + within
        behind = position - starts_of(position, ints)
        keeps = [(behind >= lag).astype(F32) for lag in range(1, taps)]
        dt = raw[slot, HALO : HALO + GROUP, conv:]
        dt = jnp.where(c == 0, dt, pltpu.roll(dt, LANES - heads, 1)) + bias
        step = jnp.maximum(dt, 0.0) + jnp.log1p(jnp.exp(-jnp.abs(dt)))
        cum = jnp.dot(
            lower, step * rate, precision=lax.Precision.HIGHEST, preferred_element_type=F32
        )
        cum_ref[rows, :] = cum
        step_ref[rows, :] = step
        last = cum[GROUP - 1 : GROUP, :]
        start_last = starts_of(first + (GROUP - 1), ints)
        tail = jnp.where(position >= start_last, jnp.exp(last - cum), 0.0) * step
        for block in range(0, conv, LANES):
            lanes = slice(block, block + LANES)
            if block < inner:
                here = pl.ds(pl.multiple_of(c * inner + block, LANES), LANES)
                weight, offset = vecs[0:taps, here], vecs[taps : taps + 1, here]
            else:
                here = slice(block - inner, block - inner + LANES)
                weight, offset = vecs[8 : 8 + taps, here], vecs[8 + taps : 9 + taps, here]
            total = offset + raw[slot, HALO : HALO + GROUP, lanes] * weight[taps - 1 : taps]
            for lag in range(1, taps):
                term = raw[slot, HALO - lag : HALO - lag + GROUP, lanes] * keeps[lag - 1]
                total = total + term * weight[taps - 1 - lag : taps - lag]
            value = silu(total).astype(MM)
            if block < inner:
                xs_ref[rows, lanes] = value
            else:
                bc_ref[rows, here] = value
        b_wide = bc_ref[rows, :state].astype(F32)
        for h in range(0, heads, 2):
            weighted = jnp.concatenate(
                [(b_wide * tail[:, h + i : h + i + 1]).astype(MM) for i in range(2)], axis=1
            )
            both = lax.dot_general(
                xs_ref[rows, h * head_width : (h + 2) * head_width],
                weighted,
                (((0,), (0,)), ((), ())),
                preferred_element_type=F32,
            )
            at = h * head_width
            message[g, at : at + head_width, :] = both[:head_width, :state].astype(MM)
            at = at + head_width
            message[g, at : at + head_width, :] = both[head_width:, state:].astype(MM)
        spread = jnp.broadcast_to(jnp.exp(last), (8, LANES))
        diagonal = lax.broadcasted_iota(jnp.int32, (8, LANES), 0) == lax.broadcasted_iota(
            jnp.int32, (8, LANES), 1
        )
        gates = jnp.sum(jnp.where(diagonal, spread, 0.0), axis=1, keepdims=True)
        gates = jnp.where(start_last < first, jnp.broadcast_to(gates, (8, LANES)), 0.0)
        terms = jnp.concatenate(list(split_terms(gates)) + [jnp.zeros_like(gates)], axis=0)
        message[g, inner : inner + TERMS, :] = terms.astype(MM)

    project(0)
    for g in range(half):
        if g + 1 < half:
            project(g + 1)
        one(g)


def mid_kernel(sizes, ints_ref, floats, xs_ref, bc_ref, cum_ref, step_ref, y_ref, keep_ref):
    inner, heads, prompts, groups, side = sizes
    ints = Ints(ints_ref, prompts)
    state = bc_ref.shape[1] // 2
    head_width = inner // heads
    half = groups // 2
    base = ints.p * (groups * GROUP) + side * half * GROUP
    within_i = lax.broadcasted_iota(jnp.int32, (GROUP, GROUP), 0)
    within_j = lax.broadcasted_iota(jnp.int32, (GROUP, GROUP), 1)
    lane = lax.broadcasted_iota(jnp.int32, (GROUP, LANES), 1)
    skip_at = 4 * heads + ints.c * heads

    @pl.loop(0, half)
    def _(g):
        rows = rows_at(g * GROUP, GROUP)
        first = base + g * GROUP
        start = starts_of(first + within_i, ints)
        seen = (within_j <= within_i) & (first + within_j >= start)
        scores = lax.dot_general(
            bc_ref[rows, state:],
            bc_ref[rows, :state],
            (((1,), (1,)), ((), ())),
            preferred_element_type=F32,
        )
        cum = cum_ref[rows, :]
        cum_t = cum.T
        step_t = step_ref[rows, :].T
        keep = jnp.where(start[:, :LANES] < first, jnp.exp(cum), 0.0)
        for h in range(0, heads, 2):
            lanes = slice(h * head_width, (h + 2) * head_width)
            pair = xs_ref[rows, lanes]
            first_skip, second_skip = (floats[skip_at + h + i] for i in range(2))
            total = jnp.where(lane < head_width, first_skip, second_skip) * pair.astype(F32)
            for i in range(2):
                log_decay = cum[:, h + i : h + i + 1] - cum_t[h + i : h + i + 1, :]
                decay = jnp.exp(jnp.where(seen, log_decay, NEGATIVE))
                mix = (decay * scores * step_t[h + i : h + i + 1, :]).astype(MM)
                own = jnp.where((lane < head_width) == (i == 0), pair, jnp.zeros_like(pair))
                total = total + jnp.dot(mix, own, preferred_element_type=F32)
            y_ref[rows, lanes] = total
            keep_ref[rows, lanes] = jnp.where(
                lane < head_width, keep[:, h : h + 1], keep[:, h + 1 : h + 2]
            )


def gate_kernel(where, depth, last, ints, tok_ref, *refs):
    pieces, refs = refs[: len(where)], refs[len(where) :]
    before, outs = (refs[:2], refs[2:]) if last else ((None, None), refs)
    count = outs[0].shape[0] // GROUP
    for side, (earlier, out) in enumerate(zip(before, outs)):

        @pl.loop(0, count)
        def _(g):
            rows = rows_at(g * GROUP, GROUP)
            total = earlier[rows, :] if last else 0.0
            for piece, (k, first) in zip(pieces, where):
                columns = pl.ds(
                    pl.multiple_of((ints[1] ^ k) * depth + first, LANES), piece.shape[0]
                )
                total = total + jnp.dot(
                    tok_ref[rows_at((side * count + g) * GROUP + HALO, GROUP), columns],
                    piece[...],
                    preferred_element_type=F32,
                )
            out[rows, :] = silu(total.astype(MM).astype(F32)) if last else total


def gating(sizes, ints, low_states, vecs, side, y_ref, keep_ref, gate_ref, bc_ref, out):
    inner, heads, groups = sizes
    half = groups // 2
    state = bc_ref.shape[1] // 2
    lane = lax.broadcasted_iota(jnp.int32, (GROUP, LANES), 1)
    for g in range(half):
        rows = slice(g * GROUP, (g + 1) * GROUP)
        carried = lax.dot_general(
            bc_ref[rows, state:],
            low_states[side * half + g],
            (((1,), (1,)), ((), ())),
            preferred_element_type=F32,
        )
        squares = jnp.zeros((GROUP, LANES), F32)
        for at in range(0, inner, LANES):
            lanes = slice(at, at + LANES)
            y = y_ref[rows, lanes] + carried[:, lanes] * keep_ref[rows, lanes]
            gated = y * gate_ref[rows, lanes]
            squares = squares + gated * gated
            here = pl.ds(pl.multiple_of(ints[2] * inner + at, LANES), LANES)
            out[rows, lanes] = (gated * vecs[5:6, here]).astype(MM)
        total = jnp.broadcast_to(jnp.sum(squares, axis=1, keepdims=True), (GROUP, LANES))
        out[rows, inner:] = spread_terms(total).astype(MM)


def spread_terms(total):
    lane = lax.broadcasted_iota(jnp.int32, total.shape, 1)
    high, mid, low = split_terms(total)
    return jnp.where(lane == 0, high, jnp.where(lane == 1, mid, jnp.where(lane == 2, low, 0.0)))


def added_terms(ref, at):
    value = ref[:, at:].astype(F32)
    return jnp.broadcast_to(jnp.sum(value, axis=1, keepdims=True), value.shape)


def back_kernel(sizes, ints_ref, vecs, *refs):
    inner, heads, prompts, groups, n_pieces, per = sizes
    pieces = refs[:n_pieces]
    sides = (refs[n_pieces : n_pieces + 4], refs[n_pieces + 4 : n_pieces + 8])
    theirs, low_states, asked, own_asked, parts, states, sems = refs[n_pieces + 8 :]
    ints = Ints(ints_ref, prompts)
    p, c = ints.p, ints.c
    head_width = inner // heads
    half = groups // 2
    copies = []
    for i, piece in enumerate(pieces):
        k, side = i // 2, i % 2
        at = (p ^ k) * groups + side * half
        copies.append(pltpu.make_async_copy(piece, parts.at[pl.ds(at, half)], sems.at[i]))
    run_all(copies)
    blocks = parts.shape[0]
    states[0] = jnp.zeros(states.shape[1:], F32)

    @pl.loop(0, blocks)
    def _(b):
        terms = parts[b, inner : inner + TERMS, :].astype(F32)
        gates = terms[0:8] + terms[8:16] + terms[16:24]
        for h in range(heads):
            rows = slice(h * head_width, (h + 1) * head_width)
            states[b + 1, rows, :] = gates[h : h + 1, :] * states[b, rows, :] + parts[
                b, rows, :
            ].astype(F32)

    for g in range(groups):
        low_states[g] = states[p * groups + g].astype(MM)
    for side in range(2):

        @pl.when(c != side)
        def _():
            gating((inner, heads, groups), ints_ref, low_states, vecs, side, *sides[side], theirs)

    for i in range(per):
        own_asked[i] = states[ints.wanted((p * 2 + c) * per + i) + 1]
        asked[i] = states[ints.wanted((p * 2 + 1 - c) * per + i) + 1].astype(MM)


def back_own_kernel(sizes, ints_ref, vecs, low_states, *refs):
    sides = (refs[:4], refs[4:8])
    mine = refs[8]
    for side in range(2):

        @pl.when(ints_ref[2] == side)
        def _():
            gating(sizes, ints_ref, low_states, vecs, side, *sides[side], mine)


def block_order(tp_count):
    return [2, 1, 3, 0] if tp_count == 4 else list(range(1, tp_count)) + [0]


def out_kernel(sizes, ints, mine, theirs, *refs):
    inner, tp_count, chosen, where = sizes
    t, p, c = ints[0], ints[1], ints[2]
    if where:
        pieces = refs[: len(where)]
        outs = refs[len(where) : len(where) + 2 * len(chosen)]
        weights, sems = refs[len(where) + 2 * len(chosen) :]
        copies = []
        for i, (piece, (k, other, first)) in enumerate(zip(pieces, where)):
            rows, columns = piece.shape
            core = 1 - c if other else c
            at = pl.multiple_of(((p ^ k) * 2 + core) * columns, LANES)
            copies.append(
                pltpu.make_async_copy(
                    piece, weights.at[pl.ds(first, rows), pl.ds(at, columns)], sems.at[i]
                )
            )
        run_all(copies)
    else:
        weights, outs = refs[0], refs[1:]
    width = weights.shape[1]
    piece_rows = mine.shape[0] // tp_count
    own_rows = rows_at(c * inner, inner)
    other_rows = rows_at((1 - c) * inner, inner)
    for i, low, high in zip(chosen, outs[::2], outs[1::2]):
        rows = rows_at(lax.rem(t + block_order(tp_count)[i], tp_count) * piece_rows, piece_rows)
        sums = jnp.sum(
            mine[rows, inner:].astype(F32) + theirs[rows, inner:].astype(F32), axis=1, keepdims=True
        )
        sums = spread_terms(jnp.broadcast_to(sums, (piece_rows, LANES)))
        high[:, width // 2 :] = sums.astype(high.dtype)
        for at in range(0, width, width // 4):
            lanes = slice(at, at + width // 4)
            value = jnp.dot(mine[rows, :inner], weights[own_rows, lanes], preferred_element_type=F32)
            value = value + jnp.dot(
                theirs[rows, :inner], weights[other_rows, lanes], preferred_element_type=F32
            )
            out, first = (low, at) if at < width // 2 else (high, at - width // 2)
            out[:, first : first + width // 4] = value.astype(out.dtype)


def add_kernel(width, got, own, out):
    out[:, :width] = (got[:, :width].astype(F32) + own[:, :width].astype(F32)).astype(MM)
    if out.shape[1] > width:
        out[:, width:] = spread_terms(added_terms(got, width) + added_terms(own, width)).astype(MM)


def final_kernel(channels, *refs):
    own, received, out = refs[:2], refs[2:-1], refs[-1]
    half = out.shape[1] // 2
    squares = added_terms(own[1], half)
    for got in received[1::2]:
        squares = squares + added_terms(got, half)
    factor = lax.rsqrt(squares[:, :1] / channels + epsilon)
    for side in range(2):
        total = own[side][:, :half]
        for got in received[side::2]:
            total = total + got[:, :half].astype(F32)
        out[:, side * half : (side + 1) * half] = (total * factor).astype(out.dtype)


def sum_over_tp(blocks, own):
    tp_count = lax.axis_size("tp")
    if tp_count != 4:
        return own, [[shift(x, j + 1) for x in block] for j, block in enumerate(blocks)]

    def add(got, x, name):
        kernel = functools.partial(add_kernel, own[0].shape[1])
        return call(kernel, [sds(x.shape, MM)], [VMEM] * 2, moved=100_000, name=name)(got, x)[0]

    (far_low, far_high), (next_low, next_high), (last_low, last_high) = blocks
    came_low, came_high = shift(far_low, 1), shift(far_high, 3)
    from_last_high, from_next_low = shift(next_high, 1), shift(last_low, 3)
    came_low, came_high, next_low, last_high, *own = lax.optimization_barrier(
        (came_low, came_high, next_low, last_high, *own)
    )
    from_last_low = shift(add(came_low, next_low, "add_low"), 1)
    from_next_high = shift(add(came_high, last_high, "add_high"), 3)
    return own, [[from_last_low, from_last_high], [from_next_low, from_next_high]]


def on_device(
    tokens,
    w_zx,
    w_dt,
    w_bc,
    conv_x_weight,
    conv_x_bias,
    conv_bc_weight,
    conv_bc_bias,
    dt_bias,
    a_log,
    skip,
    norm_weight,
    w_out,
    lengths,
    request_group,
):
    tp_count, seq_count = lax.axis_size("tp"), lax.axis_size("seq")
    t, s = lax.axis_index("tp"), lax.axis_index("seq")
    chips = seq_count // 2
    p, c = s // 2, s % 2
    tok_dev, width = tokens.shape
    rows = w_zx.shape[0]
    inner_all = w_zx.shape[1] // 2
    pair = conv_x_weight.shape[1]
    inner = pair // 2
    heads = dt_bias.shape[0] // 2
    head_width = inner // heads
    bc_width = w_bc.shape[1]
    state = bc_width // 2
    tok = 2 * tok_dev
    groups = tok // GROUP
    half = groups // 2
    conv = inner + bc_width
    prompts = lengths.shape[0]
    x_width = 2 * inner + bc_width + LANES
    depth = tp_count * rows

    ints = jnp.concatenate([jnp.stack([t, p, c]).astype(jnp.int32), lengths, request_group])
    floats = jnp.concatenate([dt_bias, a_log, skip])
    vecs = jnp.concatenate(
        [
            conv_x_weight,
            conv_x_bias[None, :],
            norm_weight[None, :],
            jnp.zeros((2, pair), F32),
            jnp.pad(conv_bc_weight, ((0, 0), (0, pair - bc_width))),
            jnp.pad(conv_bc_bias[None, :], ((0, 3), (0, pair - bc_width))),
        ],
        axis=0,
    )

    def packed(kernel, operands, specs, wide, name):
        return pl.pallas_call(
            functools.partial(kernel, tp_count),
            grid=(1,),
            out_shape=[sds((rows, wide), MM)] * tp_count,
            in_specs=specs,
            out_specs=[pl.BlockSpec((rows, wide), lambda i: (0, 0))] * tp_count,
            compiler_params=pltpu.CompilerParams(vmem_limit_bytes=VMEM_BYTES),
            name=name,
        )(*operands)

    def whole(x):
        return pl.BlockSpec(x.shape, lambda i: (0, 0))

    def sent_over_tp(pieces):
        return [pieces[0]] + [shift(x, j) for j, x in enumerate(pieces) if j]

    def assembled(kernel, outs, pieces, name):
        return call(
            functools.partial(kernel, tp_count), outs, [SMEM] + [VMEM] * tp_count, name=name
        )(ints, *pieces)

    def together(*lists):
        joined = lax.optimization_barrier(tuple(tuple(one) for one in lists))
        return [list(one) for one in joined]

    x_sent = packed(
        pack_x_kernel,
        (ints, w_zx, w_bc, w_dt),
        [SMEM, pl.BlockSpec((rows, inner_all), lambda i: (0, 1)), whole(w_bc), whole(w_dt)],
        x_width,
        "pack_x",
    )
    x_got = sent_over_tp(x_sent)

    out_near = plane_near(w_out.astype(MM))
    keys = list(out_near)
    other = flip(tokens, 1)
    last_rows = jnp.where(c == 0, other[tok_dev - HALO :], tokens[tok_dev - HALO :])
    before = lax.ppermute(last_rows, "seq", [(i, i + 2) for i in range(seq_count - 2)])
    first_tok = jnp.where(c == 0, tokens, other)
    second_tok = jnp.where(c == 0, other, tokens)
    out_got, (first_tok, second_tok, before) = together(
        [out_near[k][0] for k in keys], [first_tok, second_tok, before]
    )
    out_blocks = plane_far({k: (piece,) for k, piece in zip(keys, out_got)})
    out_own = [piece for k in out_blocks for piece in out_blocks[k]]
    out_where = [
        (k, 0, i * (w_out.shape[0] // 2)) for k in out_blocks for i in range(len(out_blocks[k]))
    ]
    x_got, out_own = together(x_got, out_own)
    (x_block,) = assembled(assemble_x_kernel, [sds((depth, x_width), MM)], x_got, "assemble_x")

    all_tok = jnp.concatenate([before, first_tok, second_tok], axis=0)

    ((x_block, all_tok, ints, floats, vecs),) = together([x_block, all_tok, ints, floats, vecs])
    near = plane_near(x_block)
    z_sent = packed(
        pack_z_kernel,
        (ints, w_zx),
        [SMEM, pl.BlockSpec((rows, inner_all), lambda i: (0, 0))],
        2 * inner,
        "pack_z",
    )
    z_got = sent_over_tp(z_sent)
    blocks, z_got, (x_own,) = together([near[k][0] for k in near if k], z_got, [x_block])
    own_other = flip(x_own, 1)
    far = plane_far({k: (block,) for k, block in zip(near, [x_block] + blocks)})
    z_mine, z_theirs = assembled(
        assemble_z_kernel, [sds((depth, inner), MM)] * 2, z_got, "assemble_z"
    )
    (z_block,) = call(
        merge_kernel, [sds((2 * depth, inner), MM)], [SMEM, VMEM, VMEM], name="merge_z"
    )(ints, z_mine, flip(z_theirs, 1))
    near_other = [flip(far[k][0], 1) for k in near if k]
    order = [k for k in far if k not in near]
    near_other, (z_block,) = together(near_other, [z_block])
    x_far, near_other = together([piece for k in order for piece in far[k]], near_other)
    far_other = [flip(piece, 1) for piece in x_far]
    where = [(k, 0) for k in near] + [(k, i * depth // 2) for k in order for i in range(2)]
    where = tuple((k, other, first) for other in range(2) for k, first in where)
    x_pieces = [far[k][0] for k in near] + x_far + [own_other] + near_other + far_other

    def front(side, where, operands):
        outs = [
            sds((tok_dev, inner), MM),
            sds((tok_dev, bc_width), MM),
            sds((tok_dev, LANES), F32),
            sds((tok_dev, LANES), F32),
            sds((half, inner + TERMS, state), MM),
        ]
        scratch = [pltpu.VMEM((2, HALO + GROUP, conv + LANES), F32)]
        if where:
            outs.append(sds((width, conv + LANES), MM))
            scratch.append(pltpu.SemaphoreType.DMA((2 * len(where),)))
        return call(
            functools.partial(
                front_kernel, (inner, bc_width, heads, prompts, where, depth, groups, side)
            ),
            outs,
            [SMEM, SMEM, VMEM, VMEM] + ([ANY] * len(where) if where else [VMEM]),
            scratch,
            flops=0,
            moved=1_000_000,
            name="front_%d" % side,
        )(ints, floats, vecs, all_tok, *operands)

    z_near = plane_near(z_block)
    *first, weights = front(0, where, x_pieces)
    ((*first, weights),) = together([*first, weights])

    low_near = plane_near(first[4])
    second = front(1, (), [weights])
    out_other = [flip(piece, 1) for piece in out_own]
    second, lows, z_blocks, out_other = together(
        second,
        [low_near[k][0] for k in low_near],
        [z_near[k][0] for k in z_near],
        out_other,
    )
    out_pieces = out_own + out_other
    out_where = tuple(out_where + [(k, 1, first_row) for k, _, first_row in out_where])
    z_far = plane_far({k: (block,) for k, block in zip(z_near, z_blocks)})
    z_order = [k for k in z_far if k in z_near] + [k for k in z_far if k not in z_near]
    z_where = tuple((k, i * depth) for k in z_order for i in range(len(z_far[k])))
    z_pieces = [piece for k in z_order for piece in z_far[k]]

    def mid(side, xs, bc, cum, step, message):
        return call(
            functools.partial(mid_kernel, (inner, heads, prompts, groups, side)),
            [sds((tok_dev, inner), F32)] * 2,
            [SMEM, SMEM] + [VMEM] * 4,
            flops=2 * tok_dev * GROUP * inner,
            moved=1_000_000,
            name="mid_%d" % side,
        )(ints, floats, xs, bc, cum, step)

    parts = {k: (block, None) for k, block in zip(low_near, lows)}
    high_near = plane_near(second[4])
    first_y = mid(0, *first)
    highs, first_y = together([high_near[k][0] for k in parts], first_y)
    parts = {k: (parts[k][0], high) for k, high in zip(parts, highs)}
    for k in range(1, chips):
        if k not in parts:
            low, high = k & -k, 1 << (k.bit_length() - 1)
            parts[k] = (flip(parts[k ^ low][0], 2 * low), flip(parts[k ^ high][1], 2 * high))
    parts = [piece for k in range(chips) for piece in parts[k]]

    y = [first_y, mid(1, *second)]
    near_count = len(z_near)
    gate = []
    for part in (slice(0, near_count), slice(near_count, None)):
        chosen = z_where[part]
        gate = call(
            functools.partial(gate_kernel, chosen, 2 * depth, len(gate) > 0),
            [sds((tok_dev, inner), F32)] * 2,
            [SMEM, VMEM] + [VMEM] * (len(chosen) + len(gate)),
            flops=tok * width * inner // 4,
            moved=1_000_000,
            name="gate_%d" % (len(gate) > 0),
        )(ints, all_tok, *z_pieces[part], *gate)
    sides = [*y[0], gate[0], first[1], *y[1], gate[1], second[1]]
    parts, sides = together(parts, sides)

    per = request_group.shape[0] // seq_count
    sent = sds((tok_dev, inner + LANES), MM)
    theirs, low_states, asked, own_asked = call(
        functools.partial(back_kernel, (inner, heads, prompts, groups, len(parts), per)),
        [
            sent,
            sds((groups, inner, state), MM),
            sds((per, inner, state), MM),
            sds((per, inner, state), F32),
        ],
        [SMEM, VMEM] + [ANY] * len(parts) + [VMEM] * 8,
        [
            pltpu.VMEM((chips * groups, inner + TERMS, state), MM),
            pltpu.VMEM((chips * groups + 1, inner, state), F32),
            pltpu.SemaphoreType.DMA((len(parts),)),
        ],
        flops=2 * tok * state * inner,
        moved=8_000_000,
        name="back",
    )(ints, vecs, *parts, *sides)
    theirs = flip(theirs, 1)
    (mine,) = call(
        functools.partial(back_own_kernel, (inner, heads, groups)),
        [sent],
        [SMEM] + [VMEM] * 10,
        flops=2 * tok_dev * state * inner,
        moved=4_000_000,
        name="back_own",
    )(ints, vecs, low_states, *sides)

    out_width = seq_count * w_out.shape[1]
    piece = tok_dev // tp_count
    ahead = 1 if tp_count == 4 else tp_count - 2

    def project_out(chosen, outs, where, operands):
        scratch, extra = [], []
        outs = [
            sds((piece, out_width // 2 + side * LANES), kind) for kind in outs for side in range(2)
        ]
        if where:
            extra = [sds((2 * inner, out_width), MM)]
            scratch = [pltpu.SemaphoreType.DMA((len(where),))]
        return call(
            functools.partial(out_kernel, (inner, tp_count, chosen, where)),
            outs + extra,
            [SMEM, VMEM, VMEM] + ([ANY] * len(where) if where else [VMEM]),
            scratch,
            flops=len(outs) * piece * inner * out_width,
            moved=1_000_000,
            name="out_%d" % len(chosen),
        )(ints, mine, theirs, *operands)

    *sent_first, out_weights = project_out(tuple(range(ahead)), [MM] * ahead, out_where, out_pieces)
    *sent_next, own_low, own_high = project_out(
        tuple(range(ahead, tp_count)), [MM] * (tp_count - 1 - ahead) + [F32], (), [out_weights]
    )
    halves = [*sent_first, *sent_next]
    own, received = sum_over_tp(
        [halves[i : i + 2] for i in range(0, len(halves), 2)], [own_low, own_high]
    )
    received = [half for block in received for half in block]
    (mixed,) = call(
        functools.partial(final_kernel, float(inner_all)),
        [sds((piece, out_width), MM)],
        [VMEM] * (2 + len(received)),
        name="final",
    )(*own, *received)

    other_asked = flip(asked, 1).astype(F32)
    states = jnp.where(
        c == 0,
        jnp.concatenate([own_asked, other_asked], axis=1),
        jnp.concatenate([other_asked, own_asked], axis=1),
    )
    return (mixed, states.reshape(per, 2 * heads, head_width, state))


def solution(mesh):
    return jax.shard_map(
        on_device,
        mesh=mesh,
        in_specs=(
            P("seq", None),
            P(("seq", "tp"), None),
            P(("seq", "tp"), None),
            P(("seq", "tp"), None),
            P(None, "tp"),
            P("tp"),
            P(),
            P(),
            P("tp"),
            P("tp"),
            P("tp"),
            P("tp"),
            P("tp", "seq"),
            P(),
            P(),
        ),
        out_specs=(P(("seq", "tp"), None), P("seq", "tp", None, None)),
        check_vma=False,
    )
```
